32 devices in a mesh: ctx: 4 (over y, core), enc: 8 (over z, x).
Axes of the slice: x: 2, y: 2, z: 4, core: 2. Of those that a mesh axis runs over, the one named last changes fastest.
Arguments:
- queries: bfloat16 [8, 512, 4096], P('enc', 'ctx'), may hold values from -200 to 200
- d_out: bfloat16 [8, 512, 4096], P('enc', 'ctx'), may hold values from -24 to 24
- text_sample: int32 [8, 512], P('enc', 'ctx'), may hold values from 0 to 1, as said below
- tiles: int32 [8, 2], P('enc'), may hold values from 1 to 4
- img_k: bfloat16 [8, 512, 1024], P(None, ('ctx', 'enc')), may hold values from -20 to 20
- img_v: bfloat16 [8, 512, 1024], P(None, ('ctx', 'enc')), may hold values from -6 to 6
Outputs:
- d_queries: bfloat16 [8, 512, 4096], P('enc', 'ctx')
- d_img_k: bfloat16 [8, 512, 1024], P(None, ('ctx', 'enc'))
- d_img_v: bfloat16 [8, 512, 1024], P(None, ('ctx', 'enc'))
The draws below stay inside these ranges and needn't reach their ends.
Inputs may be any that keep to these rules, and one draw needn't show every extreme that they name: `text_sample`: within each group the sample numbers never fall along the text, and each of the 2 samples has at least one token.
All inputs are finite; a program needn't handle non-finite values.
Results may differ from the reference program's by a relative error of at most 0.022.
Values may be sent and summed in bfloat16 or wider, within the bound.
No kernel may reach another device: no remote copies, remote signals or barrier semaphores. Data moves between devices by JAX's collectives and lax.ppermute only.
A program may use at most 128 MiB of HBM per device.

```python
import jax
import jax.numpy as jnp
from jax import lax

H = 32
KVH = 8
HD = 128
SAMP = 2
MAX_TILES = 4
TILE_TOK = 64
TEXT_GRP = 512
KEYS_GRP = 512
N_ENC = 8


def shared_draw(key):
    sample_key = jax.random.fold_in(key, 101)
    base_key = jax.random.fold_in(key, 102)
    group_keys = jax.random.split(sample_key, N_ENC)
    cuts = jax.vmap(lambda one_key: jax.random.permutation(one_key, TEXT_GRP - 1)[:SAMP - 1] + 1)(group_keys)
    positions = jnp.arange(TEXT_GRP, dtype=jnp.int32)
    samples = jnp.sum((positions[None, :, None] >= cuts[:, None, :]).astype(jnp.int32), axis=-1).astype(jnp.int32)
    base = jax.random.truncated_normal(base_key, -6.0, 6.0, (N_ENC, KEYS_GRP, KVH * HD), jnp.float32)
    return (samples, base)


def draw_text_sample(key, part):
    samples, base = shared_draw(key)
    return samples


def draw_img_k(key, part):
    samples, base = shared_draw(key)
    result = base
    return result.astype(jnp.bfloat16)


def draw_queries(key, part):
    key = jax.random.fold_in(key, 9)
    normal_key = jax.random.fold_in(key, 0)
    values = jax.random.truncated_normal(normal_key, -6.0, 6.0, (N_ENC, TEXT_GRP, H, HD), jnp.float32)
    return values.reshape(N_ENC, TEXT_GRP, H * HD).astype(jnp.bfloat16)


def place_ends(array, own_key, smallest, high):
    spot = [jax.random.randint(jax.random.fold_in(own_key, axis), (), 0, length) for axis, length in enumerate(array.shape)]
    longest = array.shape.index(max(array.shape))
    beside = spot[:longest] + [(spot[longest] + 1) % array.shape[longest]] + spot[longest + 1:]
    return array.at[tuple(spot)].set(smallest).at[tuple(beside)].set(high)


def block_levels(own_key, extent, pieces, low, largest):
    def one(position, parts):
        heights = jax.random.uniform(jax.random.fold_in(jax.random.fold_in(own_key, 6), position), (parts,), jnp.float32, low / len(pieces), largest / len(pieces))
        return jnp.repeat(jnp.exp(heights), extent[position] // parts).reshape((-1,) + (1,) * (len(extent) - position - 1))

    level = one(*pieces[0])
    for cut in pieces[1:]:
        level = level * one(*cut)
    return level


def bell_draw(rng, dims, width, bound, pieces=(), held_as=jnp.bfloat16):
    gain = block_levels(rng, dims, pieces, -0.22, 0.18) if pieces else 1.0
    drawn = jax.random.normal(rng, dims, jnp.float32) * width * gain
    return jnp.minimum(jnp.maximum(drawn, -bound), bound).astype(held_as)


def setup_inputs(seed: int = 0) -> dict:
    key_of = jax.random.split(jax.random.key(seed), 7)
    queries = draw_queries(jax.random.fold_in(key_of[6], 71), 0)
    d_out = bell_draw(key_of[1], (N_ENC, TEXT_GRP, H * HD), 4.0, 24.0, ((0, 8), (1, 4)))
    text_sample = draw_text_sample(jax.random.fold_in(key_of[6], 71), 0)
    tiles = place_ends(jax.random.randint(key_of[3], (N_ENC, SAMP), 1, MAX_TILES + 1), jax.random.fold_in(key_of[3], 1), 1, MAX_TILES).astype(jnp.int32)
    img_k = draw_img_k(jax.random.fold_in(key_of[6], 71), 0)
    img_v = bell_draw(key_of[5], (N_ENC, KEYS_GRP, KVH * HD), 1.0, 6.0, ((1, 32),))
    return dict(queries=queries, d_out=d_out, text_sample=text_sample, tiles=tiles, img_k=img_k, img_v=img_v)


big_negative = -1e30


def reference(queries, d_out, text_sample, tiles, img_k, img_v):
    group_ratio = H // KVH
    score_scale = HD ** -0.5
    slot_rows = MAX_TILES * TILE_TOK

    def one_group(items):
        query_rows, grad_rows, sample_rows, tile_row, key_rows, value_rows = items
        token_count = query_rows.shape[0]
        query_heads = query_rows.astype(jnp.float32).reshape(token_count, KVH, group_ratio, HD)
        grad_heads = grad_rows.astype(jnp.float32).reshape(token_count, KVH, group_ratio, HD)
        key_heads = key_rows.astype(jnp.float32).reshape(KEYS_GRP, KVH, HD)
        value_heads = value_rows.astype(jnp.float32).reshape(KEYS_GRP, KVH, HD)
        key_index = jnp.arange(KEYS_GRP, dtype=jnp.int32)
        key_sample = key_index // slot_rows
        key_tile = (key_index % slot_rows) // TILE_TOK
        valid = key_tile < tile_row[key_sample]
        allowed = (sample_rows[:, None] == key_sample[None, :]) & valid[None, :]
        scores = jnp.einsum("tagd,kad->agtk", query_heads, key_heads) * score_scale
        scores = jnp.where(allowed, scores, big_negative)
        row_max = jnp.max(scores, axis=-1)
        weights = jnp.where(allowed, jnp.exp(scores - row_max[..., None]), 0.0)
        log_total = row_max + jnp.log(jnp.sum(weights, axis=-1))
        probs = jnp.where(allowed, jnp.exp(scores - log_total[..., None]), 0.0)
        grad_probs = jnp.einsum("tagd,kad->agtk", grad_heads, value_heads)
        row_dot = jnp.sum(probs * grad_probs, axis=-1)
        grad_scores = (probs * (grad_probs - row_dot[..., None]) * score_scale).astype(jnp.bfloat16)
        probs_half = probs.astype(jnp.bfloat16)
        grad_query = jnp.einsum("agtk,kad->tagd", grad_scores.astype(jnp.float32), key_heads)
        grad_key = jnp.einsum("agtk,tagd->kad", grad_scores.astype(jnp.float32), query_heads)
        grad_value = jnp.einsum("agtk,tagd->kad", probs_half.astype(jnp.float32), grad_heads)
        return (grad_query.reshape(token_count, H * HD).astype(jnp.bfloat16),
                grad_key.reshape(KEYS_GRP, KVH * HD).astype(jnp.bfloat16),
                grad_value.reshape(KEYS_GRP, KVH * HD).astype(jnp.bfloat16))

    d_queries, d_img_k, d_img_v = lax.map(one_group, (queries, d_out, text_sample, tiles, img_k, img_v))
    return (d_queries, d_img_k, d_img_v)
```

```python
import functools

import jax
import jax.numpy as jnp
from jax import lax
from jax.experimental import pallas as pl
from jax.experimental.pallas import tpu as pltpu
from jax.sharding import PartitionSpec as P

H = 32
KVH = 8
HD = 128
SAMP = 2
MAX_TILES = 4
TILE_TOK = 64
RATIO = H // KVH
CORES = 2
SLOT_ROWS = MAX_TILES * TILE_TOK
HALF_KV = KVH // CORES
HALF_KCOLS = HALF_KV * HD
HALF_QCOLS = HALF_KCOLS * RATIO
SCALE = HD ** (-0.5)
LOG2E = 1.4426950408889634
BIG_NEGATIVE = -1e30


def stack_heads(block):
    return jnp.concatenate([block[:, r * HD : (r + 1) * HD] for r in range(RATIO)], axis=0)


def spread_heads(rows, tokens):
    return jnp.concatenate([rows[r * tokens : (r + 1) * tokens] for r in range(RATIO)], axis=1)


def pass_kernel(
    with_prev,
    meta,
    samp_a,
    samp_b,
    row_a,
    row_b,
    q_a,
    q_b,
    g_a,
    g_b,
    k_ref,
    v_ref,
    *rest,
):
    if with_prev:
        prev_a, prev_b, dq_a, dq_b, dk_ref, dv_ref, dk_acc, dv_acc = rest
    else:
        prev_a = prev_b = None
        dq_a, dq_b, dk_ref, dv_ref, dk_acc, dv_acc = rest
    sample = meta[1]
    key_count = meta[2]
    tokens = q_a.shape[0]
    dk_acc[...] = jnp.zeros_like(dk_acc)
    dv_acc[...] = jnp.zeros_like(dv_acc)
    for samp, row, q_ref, g_ref, prev, dq_ref in (
        (samp_a, row_a, q_a, g_a, prev_a, dq_a),
        (samp_b, row_b, q_b, g_b, prev_b, dq_b),
    ):
        present = (samp[0, 0] <= sample) & (samp[0, tokens - 1] >= sample)

        @pl.when(present)
        def _():
            q = stack_heads(q_ref[...])
            g = stack_heads(g_ref[...])
            k = k_ref[...]
            v = v_ref[...]
            mine = jnp.concatenate([row[...] == sample] * RATIO, axis=1)
            nt = (((1,), (1,)), ((), ()))
            s = lax.dot_general(k, q, nt, preferred_element_type=jnp.float32)
            slot = lax.broadcasted_iota(jnp.int32, s.shape, 0)
            s = jnp.where(slot < key_count, s, BIG_NEGATIVE)
            top = jnp.max(s, axis=0, keepdims=True)
            e = jnp.exp2((s - top) * (SCALE * LOG2E))
            total = jnp.sum(e, axis=0, keepdims=True)
            p = e * jnp.where(mine, 1.0 / total, 0.0)
            gp = lax.dot_general(v, g, nt, preferred_element_type=jnp.float32)
            row_dot = jnp.sum(p * gp, axis=0, keepdims=True)
            ds = (p * (gp - row_dot) * SCALE).astype(jnp.bfloat16)
            ph = p.astype(jnp.bfloat16)
            dv_acc[...] += jnp.dot(ph, g, preferred_element_type=jnp.float32)
            dk_acc[...] += jnp.dot(ds, q, preferred_element_type=jnp.float32)
            dq = lax.dot_general(
                ds, k, (((0,), (0,)), ((), ())), preferred_element_type=jnp.float32
            )
            dq = spread_heads(dq, tokens)
            if prev is not None:
                dq = dq + prev[...].astype(jnp.float32)
            dq_ref[...] = dq.astype(dq_ref.dtype)

        @pl.when(jnp.logical_not(present))
        def _():
            dq_ref[...] = jnp.zeros_like(dq_ref) if prev is None else prev[...]

    dk_ref[...] = dk_acc[...].astype(dk_ref.dtype)
    dv_ref[...] = dv_acc[...].astype(dv_ref.dtype)


def sample_pass(meta, samp_a, samp_b, q_full, q_other, g_full, g_other, k, v, prev, grad_dtype):
    tokens = q_full.shape[0]
    wide = RATIO * HD
    smem = pl.BlockSpec(memory_space=pltpu.SMEM)
    row = pl.BlockSpec((1, tokens), lambda i, m: (0, 0))
    own = pl.BlockSpec((tokens, wide), lambda i, m: (0, m[0] * HALF_KV + i))
    half = pl.BlockSpec((tokens, wide), lambda i, m: (0, i))
    keys = pl.BlockSpec((SLOT_ROWS, HD), lambda i, m: (0, i))
    with_prev = prev is not None
    pairs = tokens * wide * SLOT_ROWS * CORES * HALF_KV
    return pl.pallas_call(
        functools.partial(pass_kernel, with_prev),
        grid_spec=pltpu.PrefetchScalarGridSpec(
            num_scalar_prefetch=1,
            grid=(HALF_KV,),
            in_specs=[smem, smem, row, row, own, half, own, half, keys, keys]
            + [half, half] * with_prev,
            out_specs=[half, half, keys, keys],
            scratch_shapes=[pltpu.VMEM((SLOT_ROWS, HD), jnp.float32)] * 2,
        ),
        out_shape=[
            jax.ShapeDtypeStruct((tokens, HALF_QCOLS), jnp.bfloat16),
            jax.ShapeDtypeStruct((tokens, HALF_QCOLS), jnp.bfloat16),
            jax.ShapeDtypeStruct((SLOT_ROWS, HALF_KCOLS), grad_dtype),
            jax.ShapeDtypeStruct((SLOT_ROWS, HALF_KCOLS), grad_dtype),
        ],
        compiler_params=pltpu.CompilerParams(vmem_limit_bytes=32 * 2**20),
        cost_estimate=pl.CostEstimate(
            flops=10 * pairs, bytes_accessed=8 * 2**20, transcendentals=pairs // HD
        ),
    )(
        meta,
        samp_a,
        samp_b,
        samp_a,
        samp_b,
        q_full,
        q_other,
        g_full,
        g_other,
        k,
        v,
        *(prev or ()),
    )


def shards(n_ctx, n_enc, queries, d_out, text_sample, tiles, img_k, img_v):
    n_y = n_ctx // CORES
    slots = img_k.shape[1]
    both = ("ctx", "enc")
    ctx = lax.axis_index("ctx")
    core = ctx % CORES
    y = ctx // CORES
    swap_core = [(i, i ^ 1) for i in range(n_ctx)]
    same_y = [
        [yy * CORES * n_enc + i for i in range(CORES * n_enc)] for yy in range(n_y)
    ]
    same_column = [
        [(yy * CORES + c) * n_enc + e for yy in range(n_y)]
        for c in range(CORES)
        for e in range(n_enc)
    ]

    q_full = queries[0]
    g_full = d_out[0]
    samp_a = text_sample
    samp_b = lax.ppermute(samp_a, "ctx", swap_core)
    q_other = lax.ppermute(
        lax.dynamic_slice_in_dim(q_full, (1 - core) * HALF_QCOLS, HALF_QCOLS, 1),
        "ctx",
        swap_core,
    )
    g_other = lax.ppermute(
        lax.dynamic_slice_in_dim(g_full, (1 - core) * HALF_QCOLS, HALF_QCOLS, 1),
        "ctx",
        swap_core,
    )

    def to_groups(owned):
        parts = owned.reshape(n_enc, slots, CORES, HALF_KCOLS).transpose(2, 0, 1, 3)
        parts = parts.reshape(CORES * n_enc, slots, HALF_KCOLS)
        got = lax.all_to_all(
            parts, both, split_axis=0, concat_axis=0, axis_index_groups=same_y, tiled=True
        )
        return got.reshape(CORES * n_enc * slots, HALF_KCOLS)

    def to_owners(grads):
        parts = grads.reshape(CORES * n_enc, slots, HALF_KCOLS)
        got = lax.all_to_all(
            parts, both, split_axis=0, concat_axis=0, axis_index_groups=same_y, tiled=True
        )
        got = got.reshape(CORES, n_enc, slots, HALF_KCOLS).transpose(1, 2, 0, 3)
        return got.reshape(n_enc, slots, CORES * HALF_KCOLS)

    def meta_of(sample):
        count = jnp.where(sample == 0, tiles[0, 0], tiles[0, 1]) * TILE_TOK
        return jnp.stack([core, sample, count]).astype(jnp.int32)

    own_k = to_groups(img_k)
    own_v = to_groups(img_v)
    text = (samp_a, samp_b, q_full, q_other, g_full, g_other)
    if n_y == SAMP:
        swap_y = [(i, (i + CORES) % n_ctx) for i in range(n_ctx)]
        far_k = lax.ppermute(own_k, "ctx", swap_y)
        far_v = lax.ppermute(own_v, "ctx", swap_y)
        dq_a, dq_b, dk, dv = sample_pass(
            meta_of(y), *text, own_k, own_v, None, jnp.float32
        )
        dq_a, dq_b, far_dk, far_dv = sample_pass(
            meta_of(1 - y), *text, far_k, far_v, (dq_a, dq_b), jnp.bfloat16
        )
        back_k = lax.ppermute(far_dk, "ctx", swap_y)
        back_v = lax.ppermute(far_dv, "ctx", swap_y)
        dk = (dk + back_k.astype(jnp.float32)).astype(jnp.bfloat16)
        dv = (dv + back_v.astype(jnp.float32)).astype(jnp.bfloat16)
    else:
        all_k, all_v = (
            lax.all_gather(part, both, axis=0, axis_index_groups=same_column, tiled=True)
            for part in (own_k, own_v)
        )
        prev = None
        dks, dvs = [], []
        for sample in range(SAMP):
            rows = slice(sample * SLOT_ROWS, (sample + 1) * SLOT_ROWS)
            dq_a, dq_b, dk, dv = sample_pass(
                meta_of(sample), *text, all_k[rows], all_v[rows], prev, jnp.bfloat16
            )
            prev = (dq_a, dq_b)
            dks.append(dk)
            dvs.append(dv)
        dk, dv = (
            lax.psum_scatter(
                jnp.concatenate(part, axis=0),
                both,
                scatter_dimension=0,
                axis_index_groups=same_column,
                tiled=True,
            )
            for part in (dks, dvs)
        )
    d_img_k = to_owners(dk)
    d_img_v = to_owners(dv)
    dq_got = lax.ppermute(dq_b, "ctx", swap_core)
    first = jnp.where(core == 0, dq_a, dq_got)
    second = jnp.where(core == 0, dq_got, dq_a)
    d_queries = jnp.concatenate([first, second], axis=1)[None]
    return (d_queries, d_img_k, d_img_v)


def solution(mesh):
    in_specs = (
        P("enc", "ctx", None),
        P("enc", "ctx", None),
        P("enc", "ctx"),
        P("enc", None),
        P(None, ("ctx", "enc"), None),
        P(None, ("ctx", "enc"), None),
    )
    out_specs = (
        P("enc", "ctx", None),
        P(None, ("ctx", "enc"), None),
        P(None, ("ctx", "enc"), None),
    )
    body = functools.partial(shards, mesh.shape["ctx"], mesh.shape["enc"])
    return jax.shard_map(body, mesh=mesh, in_specs=in_specs, out_specs=out_specs, check_vma=False)
```

```python
import functools

import jax
import jax.numpy as jnp
from jax import lax
from jax.experimental import pallas as pl
from jax.experimental.pallas import tpu as pltpu
from jax.sharding import PartitionSpec as P

H = 32
KVH = 8
HD = 128
SAMP = 2
MAX_TILES = 4
TILE_TOK = 64
RATIO = H // KVH
CORES = 2
SLOT_ROWS = MAX_TILES * TILE_TOK
HALF_KV = KVH // CORES
HALF_KCOLS = HALF_KV * HD
HALF_QCOLS = HALF_KCOLS * RATIO
WIDE = RATIO * HD
SCALE = HD ** (-0.5)
LOG2E = 1.4426950408889634
BIG_NEGATIVE = -1e30
NT = (((1,), (1,)), ((), ()))
TN = (((0,), (0,)), ((), ()))

IN_VMEM = pl.BlockSpec(memory_space=pltpu.VMEM)
IN_SMEM = pl.BlockSpec(memory_space=pltpu.SMEM)
PARAMS = pltpu.CompilerParams(vmem_limit_bytes=40 * 2**20)


def local_call(body, outs, scratch=(), flops=0, moved=2**20):
    def call(meta, *args):
        return pl.pallas_call(
            body,
            in_specs=[IN_SMEM] + [IN_VMEM] * len(args),
            out_specs=[IN_VMEM] * len(outs),
            out_shape=[jax.ShapeDtypeStruct(s, d) for s, d in outs],
            scratch_shapes=list(scratch),
            compiler_params=PARAMS,
            cost_estimate=pl.CostEstimate(
                flops=flops, bytes_accessed=moved, transcendentals=flops // 1280
            ),
        )(meta, *args)

    return call


def pack_swap_kernel(n_enc, slots, meta, k_ref, v_ref, out):
    cols = pl.ds(pl.multiple_of((1 - meta[0]) * HALF_KCOLS, HALF_KCOLS), HALF_KCOLS)
    for d in range(n_enc):
        group = meta[2] ^ d
        out[2 * d * slots : (2 * d + 1) * slots, :] = k_ref[group, :, cols]
        out[(2 * d + 1) * slots : (2 * d + 2) * slots, :] = v_ref[group, :, cols]


def pack_blocks_kernel(n_enc, slots, meta, k_ref, v_ref, got, *outs):
    core = meta[0]
    cols = pl.ds(pl.multiple_of(core * HALF_KCOLS, HALF_KCOLS), HALF_KCOLS)
    mine = pl.multiple_of(core * slots, slots)
    theirs = pl.multiple_of((1 - core) * slots, slots)
    for d, out in enumerate(outs):
        group = meta[2] ^ d
        out[pl.ds(mine, slots), :] = k_ref[group, :, cols]
        out[pl.ds(theirs, slots), :] = got[2 * d * slots : (2 * d + 1) * slots, :]
        out[pl.ds(CORES * slots + mine, slots), :] = v_ref[group, :, cols]
        out[pl.ds(CORES * slots + theirs, slots), :] = got[(2 * d + 1) * slots : (2 * d + 2) * slots, :]


def pack_text_kernel(meta, q_ref, g_ref, q_out, g_out):
    cols = pl.ds(pl.multiple_of((1 - meta[0]) * HALF_QCOLS, HALF_QCOLS), HALF_QCOLS)
    q_out[...] = q_ref[:, cols]
    g_out[...] = g_ref[:, cols]


def pack_back_kernel(slots, meta, *refs):
    blocks, out = refs[:-1], refs[-1]
    theirs = pl.multiple_of((1 - meta[0]) * slots, slots)
    for d, block in enumerate(blocks):
        out[2 * d * slots : (2 * d + 1) * slots, :] = block[pl.ds(theirs, slots), :]
        out[(2 * d + 1) * slots : (2 * d + 2) * slots, :] = block[
            pl.ds(CORES * slots + theirs, slots), :
        ]


def finish_kernel(slots, meta, *refs):
    got, dk, dv = refs[-3:]
    blocks = refs[:-3]
    core = meta[0]
    mine = pl.multiple_of(core * slots, slots)
    own_cols = pl.ds(pl.multiple_of(core * HALF_KCOLS, HALF_KCOLS), HALF_KCOLS)
    got_cols = pl.ds(pl.multiple_of((1 - core) * HALF_KCOLS, HALF_KCOLS), HALF_KCOLS)
    for d, block in enumerate(blocks):
        group = meta[2] ^ d
        dk[group, :, own_cols] = block[pl.ds(mine, slots), :]
        dv[group, :, own_cols] = block[pl.ds(CORES * slots + mine, slots), :]
        dk[group, :, got_cols] = got[2 * d * slots : (2 * d + 1) * slots, :]
        dv[group, :, got_cols] = got[(2 * d + 1) * slots : (2 * d + 2) * slots, :]


def finish_text_kernel(meta, mine, got, out):
    core = meta[0]
    own_cols = pl.ds(pl.multiple_of(core * HALF_QCOLS, HALF_QCOLS), HALF_QCOLS)
    got_cols = pl.ds(pl.multiple_of((1 - core) * HALF_QCOLS, HALF_QCOLS), HALF_QCOLS)
    out[0, :, own_cols] = mine[...]
    out[0, :, got_cols] = got[...]


def pass_kernel(n_blocks, pieces, with_prev, meta, tiles, samp_a, samp_b, q_a, q_b, g_a, g_b, *rest):
    blocks, rest = rest[:n_blocks], rest[n_blocks:]
    prev_a = prev_b = None
    if with_prev:
        (prev_a, prev_b), rest = rest[:2], rest[2:]
    (dq_a, dq_b), rest = rest[:2], rest[2:]
    grads, (bias, dk_acc, dv_acc) = rest[:n_blocks], rest[n_blocks:]
    core, sample, enc = meta[0], meta[1], meta[2]
    tokens = q_a.shape[0]
    block_rows = SLOT_ROWS // n_blocks
    slots = block_rows // pieces

    row = lax.broadcasted_iota(jnp.int32, (SLOT_ROWS, HD), 0)
    block = lax.div(row, block_rows)
    piece = lax.rem(lax.div(row, slots), pieces)
    slot = piece * (SLOT_ROWS // pieces) + (block ^ enc) * slots + lax.rem(row, slots)
    count = jnp.where(sample == 0, tiles[0:1, 0:1], tiles[0:1, 1:2])
    bias[...] = jnp.where(slot < count * TILE_TOK, 0.0, BIG_NEGATIVE)

    def present_in(samp):
        has = samp[...] == sample
        return jnp.max(has.astype(jnp.int32)) > 0

    here = [present_in(samp_a), present_in(samp_b)]

    def head(h, carry):
        dk_acc[...] = jnp.zeros_like(dk_acc)
        dv_acc[...] = jnp.zeros_like(dv_acc)
        kcols = pl.ds(pl.multiple_of(h * HD, HD), HD)
        cols = pl.ds(pl.multiple_of(h * WIDE, WIDE), WIDE)
        own_cols = pl.ds(pl.multiple_of(core * HALF_QCOLS + h * WIDE, WIDE), WIDE)
        for present, samp, q_ref, g_ref, from_cols, prev, dq_ref in (
            (here[0], samp_a, q_a, g_a, own_cols, prev_a, dq_a),
            (here[1], samp_b, q_b, g_b, cols, prev_b, dq_b),
        ):

            @pl.when(present)
            def _():
                def stacked(ref):
                    wide = ref[:, from_cols]
                    return jnp.concatenate(
                        [wide[:, r * HD : (r + 1) * HD] for r in range(RATIO)], axis=0
                    )

                q = stacked(q_ref)
                g = stacked(g_ref)
                k = jnp.concatenate([b[:block_rows, kcols] for b in blocks], axis=0)
                v = jnp.concatenate([b[block_rows:, kcols] for b in blocks], axis=0)
                mine = jnp.concatenate([samp[...] == sample] * RATIO, axis=1)
                s = lax.dot_general(k, q, NT, preferred_element_type=jnp.float32)
                s = s + jnp.concatenate([bias[...]] * (s.shape[1] // HD), axis=1)
                top = jnp.max(s, axis=0, keepdims=True)
                e = jnp.exp2((s - top) * (SCALE * LOG2E))
                total = jnp.sum(e, axis=0, keepdims=True)
                p = e * jnp.where(mine, 1.0 / total, 0.0)
                gp = lax.dot_general(v, g, NT, preferred_element_type=jnp.float32)
                row_dot = jnp.sum(p * gp, axis=0, keepdims=True)
                ds = (p * (gp - row_dot)).astype(jnp.bfloat16)
                ph = p.astype(jnp.bfloat16)
                dv_acc[...] += jnp.dot(ph, g, preferred_element_type=jnp.float32)
                dk_acc[...] += jnp.dot(ds, q, preferred_element_type=jnp.float32)
                dq = lax.dot_general(ds, k, TN, preferred_element_type=jnp.float32) * SCALE
                dq = jnp.concatenate(
                    [dq[r * tokens : (r + 1) * tokens] for r in range(RATIO)], axis=1
                )
                if prev is not None:
                    dq = dq + prev[:, cols].astype(jnp.float32)
                dq_ref[:, cols] = dq.astype(dq_ref.dtype)

            @pl.when(jnp.logical_not(present))
            def _():
                if prev is None:
                    dq_ref[:, cols] = jnp.zeros((tokens, WIDE), dq_ref.dtype)
                else:
                    dq_ref[:, cols] = prev[:, cols]

        for b, out in enumerate(grads):
            rows = slice(b * block_rows, (b + 1) * block_rows)
            out[:block_rows, kcols] = (dk_acc[rows, :] * SCALE).astype(out.dtype)
            out[block_rows:, kcols] = dv_acc[rows, :].astype(out.dtype)
        return carry

    lax.fori_loop(0, HALF_KV, head, 0)


def sample_pass(meta, tiles, text, blocks, pieces, prev, grad_dtype):
    tokens = text[0].shape[1]
    n_blocks = len(blocks)
    dq = ((tokens, HALF_QCOLS), jnp.bfloat16)
    pairs = tokens * WIDE * SLOT_ROWS * CORES * HALF_KV
    call = local_call(
        functools.partial(pass_kernel, n_blocks, pieces, prev is not None),
        [dq, dq] + [(blocks[0].shape, grad_dtype)] * n_blocks,
        [pltpu.VMEM((SLOT_ROWS, HD), jnp.float32)] * 3,
        flops=10 * pairs,
        moved=8 * 2**20,
    )
    dq_a, dq_b, *grads = call(meta, tiles, *text, *blocks, *(prev or ()))
    return (dq_a, dq_b), grads


def shards(n_ctx, n_enc, queries, d_out, text_sample, tiles, img_k, img_v):
    n_y = n_ctx // CORES
    slots = img_k.shape[1]
    ctx = lax.axis_index("ctx")
    enc = lax.axis_index("enc")
    core = ctx % CORES
    y = ctx // CORES
    swap_core = [(i, i ^ 1) for i in range(n_ctx)]

    def meta_of(sample):
        return jnp.stack([core, sample, enc]).astype(jnp.int32)

    q_full = queries[0]
    g_full = d_out[0]
    meta = meta_of(y)
    near = n_y == SAMP and slots % 16 == 0 and n_enc & (n_enc - 1) == 0
    order = sorted(range(1, n_enc), reverse=True)

    if near:
        half_rows = n_enc * 2 * slots
        (for_peer,) = local_call(
            functools.partial(pack_swap_kernel, n_enc, slots),
            [((half_rows, HALF_KCOLS), img_k.dtype)],
        )(meta, img_k, img_v)
        from_peer = lax.ppermute(for_peer, "ctx", swap_core)

    q_send, g_send = local_call(
        pack_text_kernel, [((q_full.shape[0], HALF_QCOLS), q_full.dtype)] * 2
    )(meta, q_full, g_full)
    samp_b = lax.ppermute(text_sample, "ctx", swap_core)
    q_other = lax.ppermute(q_send, "ctx", swap_core)
    g_other = lax.ppermute(g_send, "ctx", swap_core)
    text = (text_sample, samp_b, q_full, q_other, g_full, g_other)

    if near:
        swap_y = [(i, (i + CORES) % n_ctx) for i in range(n_ctx)]

        def across(block, d):
            return lax.ppermute(block, "enc", [(i, i ^ d) for i in range(n_enc)])

        block_shape = (2 * CORES * slots, HALF_KCOLS)
        mine = local_call(
            functools.partial(pack_blocks_kernel, n_enc, slots),
            [(block_shape, img_k.dtype)] * n_enc,
        )(meta, img_k, img_v, from_peer)
        own = {0: mine[0]}
        for d in order:
            own[d] = across(mine[d], d)
        far = {d: lax.ppermute(own[d], "ctx", swap_y) for d in [0] + order}
        own = [own[d] for d in range(n_enc)]
        far = [far[d] for d in range(n_enc)]
        dq, far_grads = sample_pass(
            meta_of(1 - y), tiles, text, far, CORES, None, jnp.bfloat16
        )
        back = {d: lax.ppermute(far_grads[d], "ctx", swap_y) for d in order + [0]}
        dq, own_grads = sample_pass(
            meta, tiles, text, own, CORES, dq, jnp.float32
        )
        dq_got = lax.ppermute(dq[1], "ctx", swap_core)
        done = {}
        for d in order + [0]:
            total = (own_grads[d] + back[d].astype(jnp.float32)).astype(jnp.bfloat16)
            done[d] = across(total, d) if d else total
        done = [done[d] for d in range(n_enc)]
        (for_peer,) = local_call(
            functools.partial(pack_back_kernel, slots),
            [((half_rows, HALF_KCOLS), jnp.bfloat16)],
        )(meta, *done)
        from_peer = lax.ppermute(for_peer, "ctx", swap_core)
        d_img_k, d_img_v = local_call(
            functools.partial(finish_kernel, slots),
            [(img_k.shape, jnp.bfloat16)] * 2,
        )(meta, *done, from_peer)
    else:
        both = ("ctx", "enc")
        same_y = [
            [yy * CORES * n_enc + i for i in range(CORES * n_enc)] for yy in range(n_y)
        ]
        same_column = [
            [(yy * CORES + c) * n_enc + e for yy in range(n_y)]
            for c in range(CORES)
            for e in range(n_enc)
        ]

        def exchange(parts):
            return lax.all_to_all(
                parts, both, split_axis=0, concat_axis=0, axis_index_groups=same_y, tiled=True
            )

        def to_groups(owned):
            parts = owned.reshape(n_enc, slots, CORES, HALF_KCOLS).transpose(2, 0, 1, 3)
            got = exchange(parts.reshape(CORES * n_enc, slots, HALF_KCOLS))
            got = got.reshape(CORES * n_enc * slots, HALF_KCOLS)
            return lax.all_gather(got, both, axis=0, axis_index_groups=same_column, tiled=True)

        def to_owners(grads):
            grads = lax.psum_scatter(
                grads, both, scatter_dimension=0, axis_index_groups=same_column, tiled=True
            )
            got = exchange(grads.reshape(CORES * n_enc, slots, HALF_KCOLS))
            got = got.reshape(CORES, n_enc, slots, HALF_KCOLS).transpose(1, 2, 0, 3)
            return got.reshape(n_enc, slots, CORES * HALF_KCOLS)

        all_k = to_groups(img_k)
        all_v = to_groups(img_v)
        dq = None
        dks, dvs = [], []
        for sample in range(SAMP):
            rows = slice(sample * SLOT_ROWS, (sample + 1) * SLOT_ROWS)
            block = jnp.concatenate([all_k[rows], all_v[rows]], axis=0)
            where = jnp.stack([core, jnp.int32(sample), jnp.int32(0)]).astype(jnp.int32)
            dq, (grad,) = sample_pass(where, tiles, text, [block], 1, dq, jnp.bfloat16)
            dks.append(grad[:SLOT_ROWS])
            dvs.append(grad[SLOT_ROWS:])
        d_img_k = to_owners(jnp.concatenate(dks, axis=0))
        d_img_v = to_owners(jnp.concatenate(dvs, axis=0))
        dq_got = lax.ppermute(dq[1], "ctx", swap_core)
    (d_queries,) = local_call(finish_text_kernel, [(queries.shape, jnp.bfloat16)])(
        meta, dq[0], dq_got
    )
    return (d_queries, d_img_k, d_img_v)


def solution(mesh):
    in_specs = (
        P("enc", "ctx", None),
        P("enc", "ctx", None),
        P("enc", "ctx"),
        P("enc", None),
        P(None, ("ctx", "enc"), None),
        P(None, ("ctx", "enc"), None),
    )
    out_specs = (
        P("enc", "ctx", None),
        P(None, ("ctx", "enc"), None),
        P(None, ("ctx", "enc"), None),
    )
    body = functools.partial(shards, mesh.shape["ctx"], mesh.shape["enc"])
    return jax.shard_map(body, mesh=mesh, in_specs=in_specs, out_specs=out_specs, check_vma=False)
```

```python
import functools

import jax
import jax.numpy as jnp
from jax import lax
from jax.experimental import pallas as pl
from jax.experimental.pallas import tpu as pltpu
from jax.sharding import PartitionSpec as P

H = 32
KVH = 8
HD = 128
SAMP = 2
MAX_TILES = 4
TILE_TOK = 64
RATIO = H // KVH
CORES = 2
SLOT_ROWS = MAX_TILES * TILE_TOK
HALF_KV = KVH // CORES
HALF_KCOLS = HALF_KV * HD
HALF_QCOLS = HALF_KCOLS * RATIO
WIDE = RATIO * HD
CHUNKS = 2
CHUNK_KV = HALF_KV // CHUNKS
CHUNK_KCOLS = CHUNK_KV * HD
CHUNK_QCOLS = CHUNK_KV * WIDE
SCALE = HD ** (-0.5)
LOG2E = 1.4426950408889634
BIG_NEGATIVE = -1e30
NT = (((1,), (1,)), ((), ()))
TN = (((0,), (0,)), ((), ()))
BF16 = jnp.bfloat16
F32 = jnp.float32

IN_VMEM = pl.BlockSpec(memory_space=pltpu.VMEM)
ANYWHERE = pl.BlockSpec(memory_space=pl.ANY)


def local_call(body, ins, outs, scratch=(), flops=0, moved=2**19, limit=8):
    return pl.pallas_call(
        body,
        in_specs=ins,
        out_specs=[spec for _, _, spec in outs],
        out_shape=[jax.ShapeDtypeStruct(s, d) for s, d, _ in outs],
        scratch_shapes=list(scratch),
        compiler_params=pltpu.CompilerParams(vmem_limit_bytes=limit * 2**20),
        cost_estimate=pl.CostEstimate(
            flops=flops, bytes_accessed=moved, transcendentals=flops // 1280
        ),
    )


def in_vmem(body, outs, **more):
    def call(*args):
        spec = [(shape, dtype, IN_VMEM) for shape, dtype in outs]
        return local_call(body, [IN_VMEM] * len(args), spec, **more)(*args)

    return call


def core_of():
    return lax.rem(lax.axis_index("ctx"), CORES)


def run_copies(pairs, sems):
    copies = [pltpu.make_async_copy(src, dst, sems.at[i]) for i, (src, dst) in enumerate(pairs)]
    for copy in copies:
        copy.start()
    for copy in copies:
        copy.wait()


def at_cols(first, width, step):
    return pl.ds(pl.multiple_of(first, step), width)


def split_kernel(k_ref, v_ref, q_ref, g_ref, kv_peer, kv_own, q_peer, g_peer, q_own, g_own, sems):
    core = core_of()
    pairs = []
    for half, kv_out in ((1 - core, kv_peer), (core, kv_own)):
        for c in range(CHUNKS):
            cols = at_cols(half * HALF_KCOLS + c * CHUNK_KCOLS, CHUNK_KCOLS, CHUNK_KCOLS)
            for i, ref in enumerate((k_ref, v_ref)):
                pairs.append((ref.at[:, :, cols], kv_out.at[c, i]))
    for half, outs in ((1 - core, (q_peer, g_peer)), (core, (q_own, g_own))):
        cols = at_cols(half * HALF_QCOLS, HALF_QCOLS, HALF_QCOLS)
        for ref, out in zip((q_ref, g_ref), outs):
            pairs.append((ref.at[0, :, cols], out))
    run_copies(pairs, sems)


def group_blocks_kernel(slots, own, got, *outs):
    core = core_of()
    enc = lax.axis_index("enc")
    for c in range(CHUNKS):
        for dx in range(2):
            out = outs[CHUNKS * (1 - dx) + c]
            for dz in range(out.shape[0]):
                group = enc ^ (2 * dz + dx)
                for i in range(2):
                    first = i * CORES * slots
                    mine = pl.ds(pl.multiple_of(first + core * slots, slots), slots)
                    theirs = pl.ds(pl.multiple_of(first + (1 - core) * slots, slots), slots)
                    out[dz, mine, :] = own[c, i, group]
                    out[dz, theirs, :] = got[c, i, group]


def pair_kernel(near, far, *outs):
    rows = near.shape[1]
    for dz, out in enumerate(outs):
        out[:rows, :] = near[dz]
        out[rows:, :] = far[dz]


def join_kernel(*refs):
    parts, out = refs[:-1], refs[-1]
    rows = parts[0].shape[0]
    for i, part in enumerate(parts):
        out[i * rows : (i + 1) * rows, :] = part[...]


def add_kernel(own, back, *outs):
    rows = outs[0].shape[0]
    for i, out in enumerate(outs):
        part = slice(i * rows, (i + 1) * rows)
        out[...] = (own[part, :] + back[part, :].astype(F32)).astype(out.dtype)


def pick_kernel(*refs):
    parts, out = refs[:-1], refs[-1]
    rows = out.shape[1]
    for dz, part in enumerate(parts):
        out[dz] = part[rows:, :]


def owner_rows_kernel(slots, *refs):
    core = core_of()
    enc = lax.axis_index("enc")
    refs, (mine_out, peer_out) = refs[:-2], refs[-2:]
    each = len(refs) // CHUNKS
    for c in range(CHUNKS):
        parts, got = refs[c * each : (c + 1) * each - 1], refs[(c + 1) * each - 1]
        for dz, part in enumerate(parts):
            for dx in range(2):
                group = enc ^ (2 * dz + dx)
                for i in range(2):
                    first = i * CORES * slots
                    for who, out in ((core, mine_out), (1 - core, peer_out)):
                        rows = pl.ds(pl.multiple_of(first + who * slots, slots), slots)
                        out[c, i, group] = got[dz, rows, :] if dx else part[rows, :]


def finish_kernel(mine, got, dk, dv, sems):
    core = core_of()
    pairs = []
    for half, ref in ((core, mine), (1 - core, got)):
        for c in range(CHUNKS):
            cols = at_cols(half * HALF_KCOLS + c * CHUNK_KCOLS, CHUNK_KCOLS, CHUNK_KCOLS)
            for i, out in enumerate((dk, dv)):
                pairs.append((ref.at[c, i], out.at[:, :, cols]))
    run_copies(pairs, sems)


def finish_text_kernel(*refs):
    refs, (out, sems) = refs[:-2], refs[-2:]
    core = core_of()
    pairs = []
    for c in range(CHUNKS):
        for half, ref in ((core, refs[2 * c]), (1 - core, refs[2 * c + 1])):
            cols = at_cols(half * HALF_QCOLS + c * CHUNK_QCOLS, CHUNK_QCOLS, CHUNK_QCOLS)
            pairs.append((ref, out.at[0, :, cols]))
    run_copies(pairs, sems)


def pass_kernel(chunk, n_blocks, pieces, with_prev, where, tiles, samp_a, samp_b, q_a, q_b, g_a, g_b, kv, *rest):
    prev_a = prev_b = None
    if with_prev:
        (prev_a, prev_b), rest = rest[:2], rest[2:]
    dq_a, dq_b, grads, bias, dk_acc, dv_acc = rest
    sample, enc = where()
    tokens = q_a.shape[0]
    block_rows = SLOT_ROWS // n_blocks
    slots = block_rows // pieces

    row = lax.broadcasted_iota(jnp.int32, (SLOT_ROWS, HD), 0)
    block = lax.div(row, block_rows)
    piece = lax.rem(lax.div(row, slots), pieces)
    slot = piece * (SLOT_ROWS // pieces) + (block ^ enc) * slots + lax.rem(row, slots)
    count = jnp.where(sample == 0, tiles[0:1, 0:1], tiles[0:1, 1:2])
    bias[...] = jnp.where(slot < count * TILE_TOK, 0.0, BIG_NEGATIVE)

    def present_in(samp):
        has = samp[...] == sample
        return jnp.max(has.astype(jnp.int32)) > 0

    here = [present_in(samp_a), present_in(samp_b)]

    def head(h, carry):
        dk_acc[...] = jnp.zeros_like(dk_acc)
        dv_acc[...] = jnp.zeros_like(dv_acc)
        kcols = at_cols(h * HD, HD, HD)
        cols = at_cols(h * WIDE, WIDE, WIDE)
        from_cols = at_cols(chunk * CHUNK_QCOLS + h * WIDE, WIDE, WIDE)

        def rows_of(first):
            parts = [
                kv[b * 2 * block_rows + first : b * 2 * block_rows + first + block_rows, kcols]
                for b in range(n_blocks)
            ]
            return jnp.concatenate(parts, axis=0)

        for present, samp, q_ref, g_ref, prev, dq_ref in (
            (here[0], samp_a, q_a, g_a, prev_a, dq_a),
            (here[1], samp_b, q_b, g_b, prev_b, dq_b),
        ):

            @pl.when(present)
            def _():
                def stacked(ref):
                    wide = ref[:, from_cols]
                    return jnp.concatenate(
                        [wide[:, r * HD : (r + 1) * HD] for r in range(RATIO)], axis=0
                    )

                q = stacked(q_ref)
                g = stacked(g_ref)
                k = rows_of(0)
                v = rows_of(block_rows)
                mine = jnp.concatenate([samp[...] == sample] * RATIO, axis=1)
                s = lax.dot_general(k, q, NT, preferred_element_type=F32)
                s = s + jnp.concatenate([bias[...]] * (s.shape[1] // HD), axis=1)
                top = jnp.max(s, axis=0, keepdims=True)
                e = jnp.exp2((s - top) * (SCALE * LOG2E))
                total = jnp.sum(e, axis=0, keepdims=True)
                p = e * jnp.where(mine, 1.0 / total, 0.0)
                gp = lax.dot_general(v, g, NT, preferred_element_type=F32)
                row_dot = jnp.sum(p * gp, axis=0, keepdims=True)
                ds = (p * (gp - row_dot)).astype(BF16)
                ph = p.astype(BF16)
                dv_acc[...] += jnp.dot(ph, g, preferred_element_type=F32)
                dk_acc[...] += jnp.dot(ds, q, preferred_element_type=F32)
                dq = lax.dot_general(ds, k, TN, preferred_element_type=F32) * SCALE
                dq = jnp.concatenate(
                    [dq[r * tokens : (r + 1) * tokens] for r in range(RATIO)], axis=1
                )
                if prev is not None:
                    dq = dq + prev[:, cols].astype(F32)
                dq_ref[:, cols] = dq.astype(dq_ref.dtype)

            @pl.when(jnp.logical_not(present))
            def _():
                if prev is None:
                    dq_ref[:, cols] = jnp.zeros((tokens, WIDE), dq_ref.dtype)
                else:
                    dq_ref[:, cols] = prev[:, cols]

        for b in range(n_blocks):
            rows = slice(b * block_rows, (b + 1) * block_rows)
            first = b * 2 * block_rows
            grads[first : first + block_rows, kcols] = (dk_acc[rows, :] * SCALE).astype(grads.dtype)
            grads[first + block_rows : first + 2 * block_rows, kcols] = dv_acc[rows, :].astype(grads.dtype)
        return carry

    lax.fori_loop(0, CHUNK_KV, head, 0)


def sample_pass(where, chunk, n_blocks, pieces, tiles, text, kv, prev, grad_dtype):
    tokens = text[0].shape[1]
    dq = ((tokens, CHUNK_QCOLS), BF16)
    pairs = tokens * WIDE * SLOT_ROWS * CORES * CHUNK_KV
    dq_a, dq_b, grads = in_vmem(
        functools.partial(pass_kernel, chunk, n_blocks, pieces, prev is not None, where),
        [dq, dq, (kv.shape, grad_dtype)],
        scratch=[pltpu.VMEM((SLOT_ROWS, HD), F32)] * 3,
        flops=10 * pairs,
        moved=8 * 2**20,
    )(tiles, *text, kv, *(prev or ()))
    return (dq_a, dq_b), grads


def shards(n_ctx, n_enc, queries, d_out, text_sample, tiles, img_k, img_v):
    n_y = n_ctx // CORES
    n_z = n_enc // 2
    slots = img_k.shape[1]
    tokens = queries.shape[1]
    swap_core = [(i, i ^ 1) for i in range(n_ctx)]
    near = n_y == SAMP and slots % 16 == 0 and n_enc & (n_enc - 1) == 0

    halves = (CHUNKS, 2, n_enc, slots, CHUNK_KCOLS)
    text_half = ((tokens, HALF_QCOLS), BF16, IN_VMEM)
    kv_peer, kv_own, q_peer, g_peer, q_own, g_own = local_call(
        split_kernel,
        [ANYWHERE] * 4,
        [(halves, BF16, IN_VMEM)] * 2 + [text_half] * 4,
        [pltpu.SemaphoreType.DMA((4 * CHUNKS + 4,))],
        moved=4 * 2**20,
        limit=56,
    )(img_k, img_v, queries, d_out)
    kv_got = lax.ppermute(kv_peer, "ctx", swap_core)
    q_got = lax.ppermute(q_peer, "ctx", swap_core)
    g_got = lax.ppermute(g_peer, "ctx", swap_core)
    samp_got = lax.ppermute(text_sample, "ctx", swap_core)
    text = (text_sample, samp_got, q_own, q_got, g_own, g_got)
    dqs = [None] * CHUNKS

    if near:
        swap_y = [(i, (i + CORES) % n_ctx) for i in range(n_ctx)]
        block = (2 * CORES * slots, CHUNK_KCOLS)
        blocks = (n_z, *block)
        pair = (2 * block[0], CHUNK_KCOLS)
        whole = (n_enc * block[0], CHUNK_KCOLS)

        def across(part, d):
            return lax.ppermute(part, "enc", [(i, i ^ d) for i in range(n_enc)]) if d else part

        def around_z(parts):
            moved = {dz: across(parts[dz], 2 * dz) for dz in reversed(range(n_z))}
            return [moved[dz] for dz in range(n_z)]

        def own_place():
            return lax.div(lax.axis_index("ctx"), CORES), lax.axis_index("enc")

        def far_place():
            return 1 - lax.div(lax.axis_index("ctx"), CORES), lax.axis_index("enc")

        packed = in_vmem(
            functools.partial(group_blocks_kernel, slots), [(blocks, BF16)] * 2 * CHUNKS
        )(kv_own, kv_got)
        over_x = [across(packed[c], 1) for c in range(CHUNKS)]
        own = []
        for c in range(CHUNKS):
            pairs = in_vmem(pair_kernel, [(pair, BF16)] * n_z)(packed[CHUNKS + c], over_x[c])
            own += in_vmem(join_kernel, [(whole, BF16)])(*around_z(pairs))
        far = [lax.ppermute(own[c], "ctx", swap_y) for c in range(CHUNKS)]

        def near_pass(c, prev):
            return sample_pass(own_place, c, n_enc, CORES, tiles, text, own[c], prev, F32)

        def far_pass(c, prev):
            return sample_pass(far_place, c, n_enc, CORES, tiles, text, far[c], prev, BF16)

        own_grads, back = [None] * CHUNKS, [None] * CHUNKS
        dqs[0], own_grads[0] = near_pass(0, None)
        dqs[0], grads = far_pass(0, dqs[0])
        back[0] = lax.ppermute(grads, "ctx", swap_y)
        for c in range(1, CHUNKS):
            dqs[c], grads = far_pass(c, None)
            back[c] = lax.ppermute(grads, "ctx", swap_y)
            dqs[c], own_grads[c] = near_pass(c, dqs[c])
        returned = []
        for c in range(CHUNKS):
            totals = in_vmem(add_kernel, [(pair, BF16)] * n_z)(own_grads[c], back[c])
            parts = around_z(totals)
            (for_x,) = in_vmem(pick_kernel, [(blocks, BF16)])(*parts)
            returned += [*parts, across(for_x, 1)]
        mine, peer = in_vmem(
            functools.partial(owner_rows_kernel, slots), [(halves, BF16)] * 2
        )(*returned)
        got = lax.ppermute(peer, "ctx", swap_core)
        d_img_k, d_img_v = local_call(
            finish_kernel,
            [IN_VMEM] * 2,
            [(img_k.shape, BF16, ANYWHERE)] * 2,
            [pltpu.SemaphoreType.DMA((4 * CHUNKS,))],
        )(mine, got)
    else:
        both = ("ctx", "enc")
        same_y = [
            [yy * CORES * n_enc + i for i in range(CORES * n_enc)] for yy in range(n_y)
        ]
        same_column = [
            [(yy * CORES + c) * n_enc + e for yy in range(n_y)]
            for c in range(CORES)
            for e in range(n_enc)
        ]
        core = core_of()

        def exchange(parts):
            return lax.all_to_all(
                parts, both, split_axis=0, concat_axis=0, axis_index_groups=same_y, tiled=True
            )

        def to_groups(owned):
            parts = owned.reshape(n_enc, slots, CORES, HALF_KCOLS).transpose(2, 0, 1, 3)
            got = exchange(parts.reshape(CORES * n_enc, slots, HALF_KCOLS))
            got = got.reshape(CORES * n_enc * slots, HALF_KCOLS)
            return lax.all_gather(got, both, axis=0, axis_index_groups=same_column, tiled=True)

        def to_owners(grads):
            grads = lax.psum_scatter(
                grads, both, scatter_dimension=0, axis_index_groups=same_column, tiled=True
            )
            got = exchange(grads.reshape(CORES * n_enc, slots, HALF_KCOLS))
            got = got.reshape(CORES, n_enc, slots, HALF_KCOLS).transpose(1, 2, 0, 3)
            return got.reshape(n_enc, slots, CORES * HALF_KCOLS)

        all_k = to_groups(img_k)
        all_v = to_groups(img_v)
        dks = [[None] * CHUNKS for _ in range(SAMP)]
        dvs = [[None] * CHUNKS for _ in range(SAMP)]
        for sample in range(SAMP):
            rows = slice(sample * SLOT_ROWS, (sample + 1) * SLOT_ROWS)
            for c in range(CHUNKS):
                cols = slice(c * CHUNK_KCOLS, (c + 1) * CHUNK_KCOLS)
                kv = jnp.concatenate([all_k[rows, cols], all_v[rows, cols]], axis=0)
                place = functools.partial(lambda s: (jnp.int32(s), jnp.int32(0)), sample)
                dqs[c], grads = sample_pass(place, c, 1, 1, tiles, text, kv, dqs[c], BF16)
                dks[sample][c] = grads[:SLOT_ROWS]
                dvs[sample][c] = grads[SLOT_ROWS:]
        d_img_k = to_owners(jnp.block(dks))
        d_img_v = to_owners(jnp.block(dvs))

    ends = []
    for c in range(CHUNKS):
        ends += [dqs[c][0], lax.ppermute(dqs[c][1], "ctx", swap_core)]
    (d_queries,) = local_call(
        finish_text_kernel,
        [IN_VMEM] * len(ends),
        [(queries.shape, BF16, ANYWHERE)],
        [pltpu.SemaphoreType.DMA((2 * CHUNKS,))],
    )(*ends)
    return (d_queries, d_img_k, d_img_v)


def solution(mesh):
    in_specs = (
        P("enc", "ctx", None),
        P("enc", "ctx", None),
        P("enc", "ctx"),
        P("enc", None),
        P(None, ("ctx", "enc"), None),
        P(None, ("ctx", "enc"), None),
    )
    out_specs = (
        P("enc", "ctx", None),
        P(None, ("ctx", "enc"), None),
        P(None, ("ctx", "enc"), None),
    )
    body = functools.partial(shards, mesh.shape["ctx"], mesh.shape["enc"])
    return jax.shard_map(body, mesh=mesh, in_specs=in_specs, out_specs=out_specs, check_vma=False)
```

```python
import functools

import jax
import jax.numpy as jnp
from jax import lax
from jax.experimental import pallas as pl
from jax.experimental.pallas import tpu as pltpu
from jax.sharding import PartitionSpec as P

H = 32
KVH = 8
HD = 128
SAMP = 2
MAX_TILES = 4
TILE_TOK = 64
RATIO = H // KVH
CORES = 2
SLOT_ROWS = MAX_TILES * TILE_TOK
HALF_KV = KVH // CORES
HALF_KCOLS = HALF_KV * HD
HALF_QCOLS = HALF_KCOLS * RATIO
WIDE = RATIO * HD
CHUNKS = 2
CHUNK_KV = HALF_KV // CHUNKS
CHUNK_KCOLS = CHUNK_KV * HD
CHUNK_QCOLS = CHUNK_KV * WIDE
SCALE = HD ** (-0.5)
LOG2E = 1.4426950408889634
BIG_NEGATIVE = -1e30
NT = (((1,), (1,)), ((), ()))
TN = (((0,), (0,)), ((), ()))
BF16 = jnp.bfloat16
F32 = jnp.float32

IN_VMEM = pl.BlockSpec(memory_space=pltpu.VMEM)
IN_HBM = pl.BlockSpec(memory_space=pltpu.HBM)


def local_call(body, ins, outs, scratch=(), flops=0, moved=2**19, limit=8):
    return pl.pallas_call(
        body,
        in_specs=ins,
        out_specs=[spec for _, _, spec in outs],
        out_shape=[jax.ShapeDtypeStruct(s, d) for s, d, _ in outs],
        scratch_shapes=list(scratch),
        compiler_params=pltpu.CompilerParams(vmem_limit_bytes=limit * 2**20),
        cost_estimate=pl.CostEstimate(
            flops=flops, bytes_accessed=moved, transcendentals=flops // 1280
        ),
    )


def in_vmem(body, outs, **more):
    def call(*args):
        spec = [(shape, dtype, IN_VMEM) for shape, dtype in outs]
        return local_call(body, [IN_VMEM] * len(args), spec, **more)(*args)

    return call


def core_of():
    return lax.rem(lax.axis_index("ctx"), CORES)


def run_copies(pairs, sems):
    copies = [pltpu.make_async_copy(src, dst, sems.at[i]) for i, (src, dst) in enumerate(pairs)]
    for copy in copies:
        copy.start()
    for copy in copies:
        copy.wait()


def at_cols(first, width, step):
    return pl.ds(pl.multiple_of(first, step), width)


def split_kv_kernel(k_ref, v_ref, kv_peer, kv_own, sems):
    core = core_of()
    pairs = []
    for half, kv_out in ((1 - core, kv_peer), (core, kv_own)):
        cols = at_cols(half * HALF_KCOLS, HALF_KCOLS, HALF_KCOLS)
        for i, ref in enumerate((k_ref, v_ref)):
            pairs.append((ref.at[:, :, cols], kv_out.at[i]))
    run_copies(pairs, sems)


def split_text_kernel(q_ref, g_ref, q_peer, g_peer, q_own, g_own, sems):
    core = core_of()
    pairs = []
    for half, outs in ((1 - core, (q_peer, g_peer)), (core, (q_own, g_own))):
        cols = at_cols(half * HALF_QCOLS, HALF_QCOLS, HALF_QCOLS)
        for ref, out in zip((q_ref, g_ref), outs):
            pairs.append((ref.at[0, :, cols], out))
    run_copies(pairs, sems)


def group_blocks_kernel(slots, own, got, *outs):
    core = core_of()
    enc = lax.axis_index("enc")
    for d, out in enumerate(outs):
        for i in range(2):
            first = i * CORES * slots
            mine = pl.ds(pl.multiple_of(first + core * slots, slots), slots)
            theirs = pl.ds(pl.multiple_of(first + (1 - core) * slots, slots), slots)
            out[mine, :] = own[i, enc ^ d]
            out[theirs, :] = got[i, enc ^ d]


def join_kernel(*refs):
    parts, out = refs[:-1], refs[-1]
    rows = parts[0].shape[0]
    for i, part in enumerate(parts):
        out[i * rows : (i + 1) * rows, :] = part[...]


def add_kernel(*refs):
    own, back, outs = refs[:CHUNKS], refs[CHUNKS : 2 * CHUNKS], refs[2 * CHUNKS :]
    rows = outs[0].shape[0]
    for i, out in enumerate(outs):
        part = slice(i * rows, (i + 1) * rows)
        for c in range(CHUNKS):
            cols = slice(c * CHUNK_KCOLS, (c + 1) * CHUNK_KCOLS)
            out[:, cols] = (own[c][part, :] + back[c][part, :].astype(F32)).astype(out.dtype)


def owner_rows_kernel(slots, *refs):
    core = core_of()
    enc = lax.axis_index("enc")
    parts, (mine_out, peer_out) = refs[:-2], refs[-2:]
    for d, part in enumerate(parts):
        for i in range(2):
            first = i * CORES * slots
            for who, out in ((core, mine_out), (1 - core, peer_out)):
                rows = pl.ds(pl.multiple_of(first + who * slots, slots), slots)
                out[i, enc ^ d] = part[rows, :]


def finish_kernel(mine, got, dk, dv, sems):
    core = core_of()
    pairs = []
    for half, ref in ((core, mine), (1 - core, got)):
        cols = at_cols(half * HALF_KCOLS, HALF_KCOLS, HALF_KCOLS)
        for i, out in enumerate((dk, dv)):
            pairs.append((ref.at[i], out.at[:, :, cols]))
    run_copies(pairs, sems)


def finish_text_kernel(*refs):
    refs, (out, sems) = refs[:-2], refs[-2:]
    core = core_of()
    pairs = []
    for c in range(CHUNKS):
        for half, ref in ((core, refs[2 * c]), (1 - core, refs[2 * c + 1])):
            cols = at_cols(half * HALF_QCOLS + c * CHUNK_QCOLS, CHUNK_QCOLS, CHUNK_QCOLS)
            pairs.append((ref, out.at[0, :, cols]))
    run_copies(pairs, sems)


def pass_kernel(chunk, n_blocks, pieces, n_kv, with_prev, where, tiles, samp_a, samp_b, q_a, q_b, g_a, g_b, *rest):
    kvs, rest = rest[:n_kv], rest[n_kv:]
    prev_a = prev_b = None
    if with_prev:
        (prev_a, prev_b), rest = rest[:2], rest[2:]
    dq_a, dq_b, grads, bias, dk_acc, dv_acc = rest
    sample, enc = where()
    tokens = q_a.shape[0]
    block_rows = SLOT_ROWS // n_blocks
    slots = block_rows // pieces

    row = lax.broadcasted_iota(jnp.int32, (SLOT_ROWS, HD), 0)
    block = lax.div(row, block_rows)
    piece = lax.rem(lax.div(row, slots), pieces)
    slot = piece * (SLOT_ROWS // pieces) + (block ^ enc) * slots + lax.rem(row, slots)
    count = jnp.where(sample == 0, tiles[0:1, 0:1], tiles[0:1, 1:2])
    bias[...] = jnp.where(slot < count * TILE_TOK, 0.0, BIG_NEGATIVE)

    def present_in(samp):
        has = samp[...] == sample
        return jnp.max(has.astype(jnp.int32)) > 0

    here = [present_in(samp_a), present_in(samp_b)]

    def head(h, carry):
        dk_acc[...] = jnp.zeros_like(dk_acc)
        dv_acc[...] = jnp.zeros_like(dv_acc)
        kcols = at_cols(h * HD, HD, HD)
        kv_cols = at_cols(chunk * CHUNK_KCOLS + h * HD, HD, HD)
        cols = at_cols(h * WIDE, WIDE, WIDE)
        from_cols = at_cols(chunk * CHUNK_QCOLS + h * WIDE, WIDE, WIDE)

        def rows_of(first):
            each = n_blocks // n_kv
            parts = [
                kv[b * 2 * block_rows + first : b * 2 * block_rows + first + block_rows, kv_cols]
                for kv in kvs
                for b in range(each)
            ]
            return jnp.concatenate(parts, axis=0)

        for present, samp, q_ref, g_ref, prev, dq_ref in (
            (here[0], samp_a, q_a, g_a, prev_a, dq_a),
            (here[1], samp_b, q_b, g_b, prev_b, dq_b),
        ):

            @pl.when(present)
            def _():
                def stacked(ref):
                    wide = ref[:, from_cols]
                    return jnp.concatenate(
                        [wide[:, r * HD : (r + 1) * HD] for r in range(RATIO)], axis=0
                    )

                q = stacked(q_ref)
                g = stacked(g_ref)
                k = rows_of(0)
                v = rows_of(block_rows)
                mine = jnp.concatenate([samp[...] == sample] * RATIO, axis=1)
                s = lax.dot_general(k, q, NT, preferred_element_type=F32)
                s = s + jnp.concatenate([bias[...]] * (s.shape[1] // HD), axis=1)
                top = jnp.max(s, axis=0, keepdims=True)
                e = jnp.exp2((s - top) * (SCALE * LOG2E))
                total = jnp.sum(e, axis=0, keepdims=True)
                p = e * jnp.where(mine, 1.0 / total, 0.0)
                gp = lax.dot_general(v, g, NT, preferred_element_type=F32)
                row_dot = jnp.sum(p * gp, axis=0, keepdims=True)
                ds = (p * (gp - row_dot)).astype(BF16)
                ph = p.astype(BF16)
                dv_acc[...] += jnp.dot(ph, g, preferred_element_type=F32)
                dk_acc[...] += jnp.dot(ds, q, preferred_element_type=F32)
                dq = lax.dot_general(ds, k, TN, preferred_element_type=F32) * SCALE
                dq = jnp.concatenate(
                    [dq[r * tokens : (r + 1) * tokens] for r in range(RATIO)], axis=1
                )
                if prev is not None:
                    dq = dq + prev[:, cols].astype(F32)
                dq_ref[:, cols] = dq.astype(dq_ref.dtype)

            @pl.when(jnp.logical_not(present))
            def _():
                if prev is None:
                    dq_ref[:, cols] = jnp.zeros((tokens, WIDE), dq_ref.dtype)
                else:
                    dq_ref[:, cols] = prev[:, cols]

        for b in range(n_blocks):
            rows = slice(b * block_rows, (b + 1) * block_rows)
            first = b * 2 * block_rows
            grads[first : first + block_rows, kcols] = (dk_acc[rows, :] * SCALE).astype(grads.dtype)
            grads[first + block_rows : first + 2 * block_rows, kcols] = dv_acc[rows, :].astype(grads.dtype)
        return carry

    lax.fori_loop(0, CHUNK_KV, head, 0)


def sample_pass(where, chunk, n_blocks, pieces, tiles, text, kvs, prev, grad_dtype):
    tokens = text[0].shape[1]
    dq = ((tokens, CHUNK_QCOLS), BF16)
    pairs = tokens * WIDE * SLOT_ROWS * CORES * CHUNK_KV
    dq_a, dq_b, grads = in_vmem(
        functools.partial(
            pass_kernel, chunk, n_blocks, pieces, len(kvs), prev is not None, where
        ),
        [dq, dq, ((2 * SLOT_ROWS, CHUNK_KCOLS), grad_dtype)],
        scratch=[pltpu.VMEM((SLOT_ROWS, HD), F32)] * 3,
        flops=10 * pairs,
        moved=8 * 2**20,
    )(tiles, *text, *kvs, *(prev or ()))
    return (dq_a, dq_b), grads


def shards(n_ctx, n_enc, queries, d_out, text_sample, tiles, img_k, img_v):
    n_y = n_ctx // CORES
    slots = img_k.shape[1]
    tokens = queries.shape[1]
    swap_core = [(i, i ^ 1) for i in range(n_ctx)]
    near = n_y == SAMP and slots % 16 == 0 and n_enc & (n_enc - 1) == 0

    halves = (2, n_enc, slots, HALF_KCOLS)
    text_half = ((tokens, HALF_QCOLS), BF16, IN_VMEM)
    q_peer, g_peer, q_own, g_own = local_call(
        split_text_kernel,
        [IN_HBM] * 2,
        [text_half] * 4,
        [pltpu.SemaphoreType.DMA((4,))],
        moved=4 * 2**20,
    )(queries, d_out)
    q_got = lax.ppermute(q_peer, "ctx", swap_core)
    g_got = lax.ppermute(g_peer, "ctx", swap_core)
    samp_got = lax.ppermute(text_sample, "ctx", swap_core)
    text = (text_sample, samp_got, q_own, q_got, g_own, g_got)
    dqs = [None] * CHUNKS

    if near:
        swap_y = [(i, (i + CORES) % n_ctx) for i in range(n_ctx)]
        block = (2 * CORES * slots, HALF_KCOLS)

        def around(parts):
            moved = {
                d: lax.ppermute(parts[d], "enc", [(i, i ^ d) for i in range(n_enc)])
                for d in reversed(range(1, n_enc))
            }
            return [parts[0]] + [moved[d] for d in range(1, n_enc)]

        def own_place():
            return lax.div(lax.axis_index("ctx"), CORES), lax.axis_index("enc")

        def far_place():
            return 1 - lax.div(lax.axis_index("ctx"), CORES), lax.axis_index("enc")

        kv_peer, kv_own = local_call(
            split_kv_kernel,
            [IN_HBM] * 2,
            [(halves, BF16, IN_VMEM)] * 2,
            [pltpu.SemaphoreType.DMA((4,))],
        )(img_k, img_v)
        kv_got = lax.ppermute(kv_peer, "ctx", swap_core)
        blocks = in_vmem(
            functools.partial(group_blocks_kernel, slots), [(block, BF16)] * n_enc
        )(kv_own, kv_got)
        blocks = around(blocks)
        half = n_enc // 2
        own, far = [], []
        for part in (blocks[half:], blocks[:half]):
            (joined,) = in_vmem(join_kernel, [((half * block[0], block[1]), BF16)])(*part)
            own.insert(0, joined)
            far.insert(0, lax.ppermute(joined, "ctx", swap_y))

        def near_pass(c, prev):
            return sample_pass(own_place, c, n_enc, CORES, tiles, text, own, prev, F32)

        def far_pass(c, prev):
            return sample_pass(far_place, c, n_enc, CORES, tiles, text, far, prev, BF16)

        own_grads, back = [None] * CHUNKS, [None] * CHUNKS
        for c in range(CHUNKS):
            dqs[c], own_grads[c] = near_pass(c, None)
        for c in range(CHUNKS):
            dqs[c], grads = far_pass(c, dqs[c])
            back[c] = lax.ppermute(grads, "ctx", swap_y)
        totals = in_vmem(add_kernel, [(block, BF16)] * n_enc)(*own_grads, *back)
        mine, peer = in_vmem(
            functools.partial(owner_rows_kernel, slots), [(halves, BF16)] * 2
        )(*around(totals))
        got = lax.ppermute(peer, "ctx", swap_core)
        d_img_k, d_img_v = local_call(
            finish_kernel,
            [IN_VMEM] * 2,
            [(img_k.shape, BF16, IN_HBM)] * 2,
            [pltpu.SemaphoreType.DMA((4,))],
        )(mine, got)
    else:
        both = ("ctx", "enc")
        same_y = [
            [yy * CORES * n_enc + i for i in range(CORES * n_enc)] for yy in range(n_y)
        ]
        same_column = [
            [(yy * CORES + c) * n_enc + e for yy in range(n_y)]
            for c in range(CORES)
            for e in range(n_enc)
        ]
        core = core_of()

        def exchange(parts):
            return lax.all_to_all(
                parts, both, split_axis=0, concat_axis=0, axis_index_groups=same_y, tiled=True
            )

        def to_groups(owned):
            parts = owned.reshape(n_enc, slots, CORES, HALF_KCOLS).transpose(2, 0, 1, 3)
            got = exchange(parts.reshape(CORES * n_enc, slots, HALF_KCOLS))
            got = got.reshape(CORES * n_enc * slots, HALF_KCOLS)
            return lax.all_gather(got, both, axis=0, axis_index_groups=same_column, tiled=True)

        def to_owners(grads):
            grads = lax.psum_scatter(
                grads, both, scatter_dimension=0, axis_index_groups=same_column, tiled=True
            )
            got = exchange(grads.reshape(CORES * n_enc, slots, HALF_KCOLS))
            got = got.reshape(CORES, n_enc, slots, HALF_KCOLS).transpose(1, 2, 0, 3)
            return got.reshape(n_enc, slots, CORES * HALF_KCOLS)

        all_k = to_groups(img_k)
        all_v = to_groups(img_v)
        dks = [[None] * CHUNKS for _ in range(SAMP)]
        dvs = [[None] * CHUNKS for _ in range(SAMP)]
        for sample in range(SAMP):
            rows = slice(sample * SLOT_ROWS, (sample + 1) * SLOT_ROWS)
            for c in range(CHUNKS):
                kv = jnp.concatenate([all_k[rows], all_v[rows]], axis=0)
                place = functools.partial(lambda s: (jnp.int32(s), jnp.int32(0)), sample)
                dqs[c], grads = sample_pass(place, c, 1, 1, tiles, text, [kv], dqs[c], BF16)
                dks[sample][c] = grads[:SLOT_ROWS]
                dvs[sample][c] = grads[SLOT_ROWS:]
        d_img_k = to_owners(jnp.block(dks))
        d_img_v = to_owners(jnp.block(dvs))

    ends = []
    for c in range(CHUNKS):
        ends += [dqs[c][0], lax.ppermute(dqs[c][1], "ctx", swap_core)]
    (d_queries,) = local_call(
        finish_text_kernel,
        [IN_VMEM] * len(ends),
        [(queries.shape, BF16, IN_HBM)],
        [pltpu.SemaphoreType.DMA((2 * CHUNKS,))],
    )(*ends)
    return (d_queries, d_img_k, d_img_v)


def solution(mesh):
    in_specs = (
        P("enc", "ctx", None),
        P("enc", "ctx", None),
        P("enc", "ctx"),
        P("enc", None),
        P(None, ("ctx", "enc"), None),
        P(None, ("ctx", "enc"), None),
    )
    out_specs = (
        P("enc", "ctx", None),
        P(None, ("ctx", "enc"), None),
        P(None, ("ctx", "enc"), None),
    )
    body = functools.partial(shards, mesh.shape["ctx"], mesh.shape["enc"])
    return jax.shard_map(body, mesh=mesh, in_specs=in_specs, out_specs=out_specs, check_vma=False)
```

```python
import functools

import jax
import jax.numpy as jnp
from jax import lax
from jax.experimental import pallas as pl
from jax.experimental.pallas import tpu as pltpu
from jax.sharding import PartitionSpec as P

H = 32
KVH = 8
HD = 128
SAMP = 2
MAX_TILES = 4
TILE_TOK = 64
RATIO = H // KVH
CORES = 2
SLOT_ROWS = MAX_TILES * TILE_TOK
HALF_KV = KVH // CORES
HALF_KCOLS = HALF_KV * HD
HALF_QCOLS = HALF_KCOLS * RATIO
WIDE = RATIO * HD
CHUNKS = 2
CHUNK_KV = HALF_KV // CHUNKS
CHUNK_KCOLS = CHUNK_KV * HD
CHUNK_QCOLS = CHUNK_KV * WIDE
BLOCKS = 4
SAMP_ROWS = 16
SCALE = HD ** (-0.5)
LOG2E = 1.4426950408889634
BIG_NEGATIVE = -1e30
NT = (((1,), (1,)), ((), ()))
TN = (((0,), (0,)), ((), ()))
BF16 = jnp.bfloat16
F32 = jnp.float32

IN_VMEM = pl.BlockSpec(memory_space=pltpu.VMEM)
IN_HBM = pl.BlockSpec(memory_space=pltpu.HBM)


def local_call(body, ins, outs, scratch=(), flops=0, moved=2**19, aliases={}):
    return pl.pallas_call(
        body,
        in_specs=ins,
        out_specs=[spec for _, _, spec in outs],
        out_shape=[jax.ShapeDtypeStruct(s, d) for s, d, _ in outs],
        scratch_shapes=list(scratch),
        compiler_params=pltpu.CompilerParams(vmem_limit_bytes=8 * 2**20),
        input_output_aliases=aliases,
        cost_estimate=pl.CostEstimate(
            flops=flops, bytes_accessed=moved, transcendentals=flops // 1280
        ),
    )


def in_vmem(body, outs, **more):
    def call(*args):
        spec = [(shape, dtype, IN_VMEM) for shape, dtype in outs]
        return local_call(body, [IN_VMEM] * len(args), spec, **more)(*args)

    return call


def core_of():
    return lax.rem(lax.axis_index("ctx"), CORES)


def at_rows(first, count):
    return pl.ds(pl.multiple_of(first, count), count)


def at_cols(first, width, step):
    return pl.ds(pl.multiple_of(first, step), width)


def start_copies(pairs, sems):
    copies = [pltpu.make_async_copy(src, dst, sems.at[i]) for i, (src, dst) in enumerate(pairs)]
    for copy in copies:
        copy.start()
    return copies


def run_copies(pairs, sems):
    for copy in start_copies(pairs, sems):
        copy.wait()


def in_hbm(*arrays):
    return [pltpu.with_memory_space_constraint(a, pltpu.HBM) for a in arrays]


def carried(j, core):
    return BLOCKS * (1 - core) + j


def split_kernel(*refs):
    k_ref, v_ref, q_ref, g_ref, samp_hbm, tiles_hbm, mine, peer = refs[:8]
    text_refs, (samp, tiles, sems, small_sems) = refs[8:-4], refs[-4:]
    core = core_of()
    enc = lax.axis_index("enc")
    pairs = []
    for who, out in ((1 - core, peer), (core, mine)):
        for j in range(BLOCKS):
            for i, ref in enumerate((k_ref, v_ref)):
                pairs.append((ref.at[enc ^ carried(j, who)], out.at[i, j]))
    copies = start_copies(pairs, sems)
    split_text(
        2 * BLOCKS, CORES, near_place, q_ref, g_ref, samp_hbm, tiles_hbm, *text_refs, samp, tiles, small_sems
    )
    for copy in copies:
        copy.wait()


def near_place():
    y = lax.div(lax.axis_index("ctx"), CORES)
    return y, lax.axis_index("enc") ^ carried(0, core_of())


def split_text(n_blocks, pieces, where, q_ref, g_ref, samp_hbm, tiles_hbm, peer, q_own, g_own, bias, samp, tiles, sems):
    core = core_of()
    tokens = q_ref.shape[1]
    own_cols = at_cols(core * HALF_QCOLS, HALF_QCOLS, HALF_QCOLS)
    peer_cols = at_cols((1 - core) * HALF_QCOLS, HALF_QCOLS, HALF_QCOLS)
    copies = start_copies(
        [
            (samp_hbm, samp),
            (tiles_hbm, tiles),
            (q_ref.at[0, :, peer_cols], peer.at[:tokens]),
            (g_ref.at[0, :, peer_cols], peer.at[tokens : 2 * tokens]),
            (q_ref.at[0, :, own_cols], q_own.at[:tokens]),
            (g_ref.at[0, :, own_cols], g_own),
        ],
        sems,
    )
    for copy in copies[:2]:
        copy.wait()
    row = jnp.broadcast_to(samp[...].astype(F32), (SAMP_ROWS, tokens)).astype(BF16)
    for out, first in ((q_own, tokens), (peer, 2 * tokens)):
        out[first:, :] = jnp.zeros((SAMP_ROWS, HALF_QCOLS), BF16)
        out[first:, :tokens] = row

    sample, offset = where()
    block_rows = SLOT_ROWS // n_blocks
    slots = block_rows // pieces
    line = lax.broadcasted_iota(jnp.int32, (SLOT_ROWS, HD), 0)
    owner = lax.div(line, block_rows) ^ offset
    piece = lax.rem(lax.div(line, slots), pieces)
    slot = piece * (SLOT_ROWS // pieces) + owner * slots + lax.rem(line, slots)
    for i in range(SAMP):
        count = jnp.where((sample ^ i) == 0, tiles[0:1, 0:1], tiles[0:1, 1:2])
        bias[i] = jnp.where(slot < count * TILE_TOK, 0.0, BIG_NEGATIVE)
    for copy in copies[2:]:
        copy.wait()


def carry_kernel(slots, mine, got, text, *outs):
    core = core_of()
    for j, out in enumerate(outs[:-1]):
        for i in range(2):
            first = i * CORES * slots
            out[at_rows(first + core * slots, slots), :] = mine[i, j]
            out[at_rows(first + (1 - core) * slots, slots), :] = got[i, j]


def join_kernel(*refs):
    parts, out = refs[:-1], refs[-1]
    rows = parts[0].shape[0]
    for i, part in enumerate(parts):
        out[i * rows : (i + 1) * rows, :] = part[...]


def split_cols_kernel(*refs):
    parts, out = refs[: BLOCKS // 2], refs[-1]
    rows = parts[0].shape[0]
    cols = at_cols((1 - core_of()) * HALF_KCOLS, HALF_KCOLS, HALF_KCOLS)
    for i, part in enumerate(parts):
        out[i * rows : (i + 1) * rows, :] = part[:, cols]


def add_kernel(*refs):
    own, back, outs = refs[:CHUNKS], refs[CHUNKS : 2 * CHUNKS], refs[2 * CHUNKS :]
    rows = outs[0].shape[0]
    for i, out in enumerate(outs):
        part = slice(i * rows, (i + 1) * rows)
        for c in range(CHUNKS):
            cols = slice(c * CHUNK_KCOLS, (c + 1) * CHUNK_KCOLS)
            out[:, cols] = (own[c][part, :] + back[c][part, :].astype(F32)).astype(out.dtype)


def back_kernel(mine, got, *outs):
    core = core_of()
    rows = outs[0].shape[0]
    own_cols = at_cols(core * HALF_KCOLS, HALF_KCOLS, HALF_KCOLS)
    got_cols = at_cols((1 - core) * HALF_KCOLS, HALF_KCOLS, HALF_KCOLS)
    for j, out in enumerate(outs):
        out[:, own_cols] = mine[j * rows : (j + 1) * rows, :]
        out[:, got_cols] = got[j * rows : (j + 1) * rows, :]


def owner_rows_kernel(slots, *refs):
    blocks, (mine, peer) = refs[: BLOCKS], refs[-2:]
    core = core_of()
    for j, block in enumerate(blocks):
        for i in range(2):
            first = i * CORES * slots
            mine[i, j] = block[at_rows(first + core * slots, slots), :]
            peer[i, j] = block[at_rows(first + (1 - core) * slots, slots), :]


def finish_kernel(mine, got, dk, dv, sems):
    core = core_of()
    enc = lax.axis_index("enc")
    pairs = []
    for who, ref in ((core, mine), (1 - core, got)):
        for j in range(BLOCKS):
            for i, out in enumerate((dk, dv)):
                pairs.append((ref.at[i, j], out.at[enc ^ carried(j, who)]))
    run_copies(pairs, sems)


def finish_text_kernel(*refs):
    refs, (out, token, sems) = refs[:-3], refs[-3:]
    core = core_of()
    token[...] = jnp.zeros_like(token)
    pairs = []
    for c in range(CHUNKS):
        for half, ref in ((core, refs[2 * c]), (1 - core, refs[2 * c + 1])):
            cols = at_cols(half * HALF_QCOLS + c * CHUNK_QCOLS, CHUNK_QCOLS, CHUNK_QCOLS)
            pairs.append((ref, out.at[0, :, cols]))
    run_copies(pairs, sems)


def pass_kernel(role, chunk, n_blocks, n_kv, with_prev, where, bias, q_a, g_a, got, *rest):
    kvs, rest = rest[:n_kv], rest[n_kv:]
    prev = None
    if with_prev:
        prev, rest = rest[:2], rest[2:]
    *dqs, grads = rest
    sample = where()[0] ^ role
    tokens = g_a.shape[0]
    block_rows = SLOT_ROWS // n_blocks
    row_a = q_a[tokens : tokens + 1, :tokens].astype(F32)
    row_b = got[2 * tokens : 2 * tokens + 1, :tokens].astype(F32)
    wanted = sample.astype(F32)
    has = jnp.where(row_a == wanted, 1.0, jnp.where(row_b == wanted, 1.0, 0.0))
    present = jnp.max(has) > 0.5

    @pl.when(present)
    def _():
        mine = jnp.concatenate([row_a] * RATIO + [row_b] * RATIO, axis=1) == wanted
        for h in range(CHUNK_KV):
            first_q = chunk * CHUNK_QCOLS + h * WIDE
            first_k = chunk * CHUNK_KCOLS + h * HD

            def stacked(ref_a, first_b):
                parts = [
                    ref[first : first + tokens, first_q + r * HD : first_q + (r + 1) * HD]
                    for ref, first in ((ref_a, 0), (got, first_b))
                    for r in range(RATIO)
                ]
                return jnp.concatenate(parts, axis=0)

            def rows_of(first):
                parts = []
                for kv in kvs:
                    if kv.shape[1] == HALF_KCOLS:
                        cols = slice(first_k, first_k + HD)
                    else:
                        cols = at_cols(core_of() * HALF_KCOLS + first_k, HD, HD)
                    for at in range(first, kv.shape[0], 2 * block_rows):
                        parts.append(kv[at : at + block_rows, cols])
                return jnp.concatenate(parts, axis=0)

            q = stacked(q_a, 0)
            g = stacked(g_a, tokens)
            k = rows_of(0)
            v = rows_of(block_rows)
            s = lax.dot_general(k, q, NT, preferred_element_type=F32)
            s = s + jnp.concatenate([bias[role]] * (s.shape[1] // HD), axis=1)
            top = jnp.max(s, axis=0, keepdims=True)
            e = jnp.exp2((s - top) * (SCALE * LOG2E))
            total = jnp.sum(e, axis=0, keepdims=True)
            p = e * jnp.where(mine, 1.0 / total, 0.0)
            gp = lax.dot_general(v, g, NT, preferred_element_type=F32)
            row_dot = jnp.sum(p * gp, axis=0, keepdims=True)
            ds = (p * (gp - row_dot)).astype(BF16)
            dv = jnp.dot(p.astype(BF16), g, preferred_element_type=F32)
            dk = jnp.dot(ds, q, preferred_element_type=F32) * SCALE
            dq = lax.dot_general(ds, k, TN, preferred_element_type=F32) * SCALE
            for t, dq_ref in enumerate(dqs):
                for r in range(RATIO):
                    at = (t * RATIO + r) * tokens
                    cols = slice(h * WIDE + r * HD, h * WIDE + (r + 1) * HD)
                    part = dq[at : at + tokens]
                    if with_prev:
                        part = part + prev[t][:, cols].astype(F32)
                    dq_ref[:, cols] = part.astype(dq_ref.dtype)
            cols = slice(h * HD, (h + 1) * HD)
            for b in range(n_blocks):
                rows = slice(b * block_rows, (b + 1) * block_rows)
                first = b * 2 * block_rows
                grads[first : first + block_rows, cols] = dk[rows].astype(grads.dtype)
                grads[first + block_rows : first + 2 * block_rows, cols] = dv[rows].astype(grads.dtype)

    @pl.when(jnp.logical_not(present))
    def _():
        grads[...] = jnp.zeros_like(grads)
        for t, dq_ref in enumerate(dqs):
            dq_ref[...] = prev[t][...] if with_prev else jnp.zeros_like(dq_ref)


def sample_pass(where, role, chunk, n_blocks, bias, text, kvs, prev, grad_dtype):
    tokens = text[1].shape[0]
    dq = ((tokens, CHUNK_QCOLS), BF16)
    pairs = tokens * WIDE * SLOT_ROWS * CORES * CHUNK_KV
    dq_a, dq_b, grads = in_vmem(
        functools.partial(
            pass_kernel, role, chunk, n_blocks, len(kvs), prev is not None, where
        ),
        [dq, dq, ((2 * SLOT_ROWS, CHUNK_KCOLS), grad_dtype)],
        flops=10 * pairs,
        moved=8 * 2**20,
    )(bias, *text, *kvs, *(prev or ()))
    return (dq_a, dq_b), grads


def shards(n_ctx, n_enc, queries, d_out, text_sample, tiles, img_k, img_v):
    n_y = n_ctx // CORES
    slots = img_k.shape[1]
    tokens = queries.shape[1]
    swap_core = [(i, i ^ 1) for i in range(n_ctx)]
    near = n_y == SAMP and slots % 16 == 0 and n_enc == 2 * BLOCKS
    dqs = [None] * CHUNKS
    text_outs = [
        ((2 * tokens + SAMP_ROWS, HALF_QCOLS), BF16, IN_VMEM),
        ((tokens + SAMP_ROWS, HALF_QCOLS), BF16, IN_VMEM),
        ((tokens, HALF_QCOLS), BF16, IN_VMEM),
        ((SAMP, SLOT_ROWS, HD), F32, IN_VMEM),
    ]
    text_scratch = [
        pltpu.VMEM(text_sample.shape, jnp.int32),
        pltpu.VMEM(tiles.shape, jnp.int32),
    ]
    text_sems = pltpu.SemaphoreType.DMA((6,))

    if near:
        swap_y = [(i, (i + CORES) % n_ctx) for i in range(n_ctx)]
        block = (2 * CORES * slots, KVH * HD)
        pair = (2 * block[0], block[1])
        half = (BLOCKS * block[0], HALF_KCOLS)
        slabs = (2, BLOCKS, slots, KVH * HD)

        def around(parts):
            return [
                lax.ppermute(
                    part,
                    ("ctx", "enc"),
                    [
                        (i * n_enc + e, i * n_enc + (e ^ carried(j, i % CORES)))
                        for i in range(n_ctx)
                        for e in range(n_enc)
                    ],
                )
                for j, part in enumerate(parts)
            ]

        mine, for_peer, text_peer, q_own, g_own, bias = local_call(
            split_kernel,
            [IN_HBM] * 6,
            [(slabs, BF16, IN_VMEM)] * 2 + text_outs,
            text_scratch + [pltpu.SemaphoreType.DMA((4 * BLOCKS,)), text_sems],
            moved=4 * 2**20,
        )(*in_hbm(img_k, img_v, queries, d_out, text_sample, tiles))
        *carry, text_peer = in_vmem(
            functools.partial(carry_kernel, slots),
            [(block, BF16)] * BLOCKS + [(text_peer.shape, BF16)],
            aliases={2: BLOCKS},
        )(mine, lax.ppermute(for_peer, "ctx", swap_core), text_peer)
        text = (q_own, g_own, lax.ppermute(text_peer, "ctx", swap_core))
        brought = around(carry)

        def with_other_core(parts, after=()):
            (for_peer,) = in_vmem(split_cols_kernel, [(half, BF16)])(*parts, *after)
            return [*parts, lax.ppermute(for_peer, "ctx", swap_core)]

        own, far = [], []
        for j in range(0, BLOCKS, 2):
            own += in_vmem(join_kernel, [(pair, BF16)])(*brought[j : j + 2])
            far.append(lax.ppermute(own[-1], "ctx", swap_y))
        own = with_other_core(own)

        own_grads, back = [None] * CHUNKS, [None] * CHUNKS
        for c in range(CHUNKS):
            dqs[c], own_grads[c] = sample_pass(
                near_place, 0, c, n_enc, bias, text, own, None, F32
            )
        far = with_other_core(far, [pair[0] for pair in dqs])
        for c in range(CHUNKS):
            dqs[c], grads = sample_pass(
                near_place, 1, c, n_enc, bias, text, far, dqs[c], BF16
            )
            back[c] = lax.ppermute(grads, "ctx", swap_y)
        mine, for_peer = in_vmem(add_kernel, [(half, BF16)] * 2)(*own_grads, *back)
        carry = in_vmem(back_kernel, [(block, BF16)] * BLOCKS)(
            mine, lax.ppermute(for_peer, "ctx", swap_core)
        )
        brought = around(carry)
    else:
        both = ("ctx", "enc")
        same_y = [
            [yy * CORES * n_enc + i for i in range(CORES * n_enc)] for yy in range(n_y)
        ]
        same_column = [
            [(yy * CORES + c) * n_enc + e for yy in range(n_y)]
            for c in range(CORES)
            for e in range(n_enc)
        ]
        core = core_of()

        def exchange(parts):
            return lax.all_to_all(
                parts, both, split_axis=0, concat_axis=0, axis_index_groups=same_y, tiled=True
            )

        def to_groups(owned):
            parts = owned.reshape(n_enc, slots, CORES, HALF_KCOLS).transpose(2, 0, 1, 3)
            got = exchange(parts.reshape(CORES * n_enc, slots, HALF_KCOLS))
            got = got.reshape(CORES * n_enc * slots, HALF_KCOLS)
            return lax.all_gather(got, both, axis=0, axis_index_groups=same_column, tiled=True)

        def to_owners(grads):
            grads = lax.psum_scatter(
                grads, both, scatter_dimension=0, axis_index_groups=same_column, tiled=True
            )
            got = exchange(grads.reshape(CORES * n_enc, slots, HALF_KCOLS))
            got = got.reshape(CORES, n_enc, slots, HALF_KCOLS).transpose(1, 2, 0, 3)
            return got.reshape(n_enc, slots, CORES * HALF_KCOLS)

        def no_place():
            return jnp.int32(0), jnp.int32(0)

        all_k = to_groups(img_k)
        all_v = to_groups(img_v)
        text_peer, q_own, g_own, bias = local_call(
            functools.partial(split_text, 1, 1, no_place),
            [IN_HBM] * 4,
            text_outs,
            text_scratch + [text_sems],
            moved=4 * 2**20,
        )(*in_hbm(queries, d_out, text_sample, tiles))
        text = (q_own, g_own, lax.ppermute(text_peer, "ctx", swap_core))
        dks = [[None] * CHUNKS for _ in range(SAMP)]
        dvs = [[None] * CHUNKS for _ in range(SAMP)]
        for sample in range(SAMP):
            rows = slice(sample * SLOT_ROWS, (sample + 1) * SLOT_ROWS)
            kv = jnp.concatenate([all_k[rows], all_v[rows]], axis=0)
            for c in range(CHUNKS):
                dqs[c], grads = sample_pass(no_place, sample, c, 1, bias, text, [kv], dqs[c], BF16)
                dks[sample][c] = grads[:SLOT_ROWS]
                dvs[sample][c] = grads[SLOT_ROWS:]
        d_img_k = to_owners(jnp.block(dks))
        d_img_v = to_owners(jnp.block(dvs))

    ends = []
    for c in range(CHUNKS):
        ends += [dqs[c][0], lax.ppermute(dqs[c][1], "ctx", swap_core)]
    d_queries, token = local_call(
        finish_text_kernel,
        [IN_VMEM] * len(ends),
        [(queries.shape, BF16, IN_HBM), ((8, HD), F32, IN_VMEM)],
        [pltpu.SemaphoreType.DMA((2 * CHUNKS,))],
    )(*ends)
    if near:
        mine, for_peer = in_vmem(
            functools.partial(owner_rows_kernel, slots), [(slabs, BF16)] * 2
        )(*brought, token)
        d_img_k, d_img_v = local_call(
            finish_kernel,
            [IN_VMEM] * 2,
            [(img_k.shape, BF16, IN_HBM)] * 2,
            [pltpu.SemaphoreType.DMA((4 * BLOCKS,))],
        )(mine, lax.ppermute(for_peer, "ctx", swap_core))
    return (d_queries, d_img_k, d_img_v)


def solution(mesh):
    in_specs = (
        P("enc", "ctx", None),
        P("enc", "ctx", None),
        P("enc", "ctx"),
        P("enc", None),
        P(None, ("ctx", "enc"), None),
        P(None, ("ctx", "enc"), None),
    )
    out_specs = (
        P("enc", "ctx", None),
        P(None, ("ctx", "enc"), None),
        P(None, ("ctx", "enc"), None),
    )
    body = functools.partial(shards, mesh.shape["ctx"], mesh.shape["enc"])
    return jax.shard_map(body, mesh=mesh, in_specs=in_specs, out_specs=out_specs, check_vma=False)
```

```python
import functools

import jax
import jax.numpy as jnp
from jax import lax
from jax.experimental import pallas as pl
from jax.experimental.pallas import tpu as pltpu
from jax.sharding import PartitionSpec as P

H = 32
KVH = 8
HD = 128
SAMP = 2
MAX_TILES = 4
TILE_TOK = 64
RATIO = H // KVH
CORES = 2
SLOT_ROWS = MAX_TILES * TILE_TOK
HALF_KV = KVH // CORES
HALF_KCOLS = HALF_KV * HD
HALF_QCOLS = HALF_KCOLS * RATIO
WIDE = RATIO * HD
CHUNKS = 2
CHUNK_KV = HALF_KV // CHUNKS
CHUNK_KCOLS = CHUNK_KV * HD
CHUNK_QCOLS = CHUNK_KV * WIDE
SAMP_ROWS = 16
SCALE = HD ** (-0.5)
LOG2E = 1.4426950408889634
BIG_NEGATIVE = -1e30
NT = (((1,), (1,)), ((), ()))
TN = (((0,), (0,)), ((), ()))
BF16 = jnp.bfloat16
F32 = jnp.float32

IN_VMEM = pl.BlockSpec(memory_space=pltpu.VMEM)
IN_HBM = pl.BlockSpec(memory_space=pltpu.HBM)


def local_call(body, ins, outs, scratch=(), flops=0, moved=2**19, aliases={}):
    return pl.pallas_call(
        body,
        in_specs=ins,
        out_specs=[spec for _, _, spec in outs],
        out_shape=[jax.ShapeDtypeStruct(s, d) for s, d, _ in outs],
        scratch_shapes=list(scratch),
        compiler_params=pltpu.CompilerParams(vmem_limit_bytes=8 * 2**20),
        input_output_aliases=aliases,
        cost_estimate=pl.CostEstimate(
            flops=flops, bytes_accessed=moved, transcendentals=flops // 1280
        ),
    )


def in_vmem(body, outs, **more):
    def call(*args):
        spec = [(shape, dtype, IN_VMEM) for shape, dtype in outs]
        return local_call(body, [IN_VMEM] * len(args), spec, **more)(*args)

    return call


def core_of():
    return lax.rem(lax.axis_index("ctx"), CORES)


def at_rows(first, count):
    return pl.ds(pl.multiple_of(first, count), count)


def at_cols(first, width, step):
    return pl.ds(pl.multiple_of(first, step), width)


def start_copies(pairs, sems):
    copies = [pltpu.make_async_copy(src, dst, sems.at[i]) for i, (src, dst) in enumerate(pairs)]
    for copy in copies:
        copy.start()
    return copies


def run_copies(pairs, sems):
    for copy in start_copies(pairs, sems):
        copy.wait()


def in_hbm(*arrays):
    return [pltpu.with_memory_space_constraint(a, pltpu.HBM) for a in arrays]


def split_kernel(*refs):
    k_ref, v_ref, q_ref, g_ref, samp_hbm, tiles_hbm, mine, peer = refs[:8]
    text_refs, (samp, tiles, sems, small_sems) = refs[8:-4], refs[-4:]
    core = core_of()
    pairs = []
    for half, out in ((1 - core, peer), (core, mine)):
        for c in range(CHUNKS):
            cols = at_cols(half * HALF_KCOLS + c * CHUNK_KCOLS, CHUNK_KCOLS, CHUNK_KCOLS)
            for i, ref in enumerate((k_ref, v_ref)):
                pairs.append((ref.at[:, :, cols], out.at[c, i]))
    copies = start_copies(pairs, sems)
    split_text(
        k_ref.shape[0], CORES, near_place, q_ref, g_ref, samp_hbm, tiles_hbm, *text_refs, samp, tiles, small_sems
    )
    for copy in copies:
        copy.wait()


def near_place():
    return lax.div(lax.axis_index("ctx"), CORES), lax.axis_index("enc")


def split_text(n_blocks, pieces, where, q_ref, g_ref, samp_hbm, tiles_hbm, peer, q_own, g_own, bias, samp, tiles, sems):
    core = core_of()
    tokens = q_ref.shape[1]
    own_cols = at_cols(core * HALF_QCOLS, HALF_QCOLS, HALF_QCOLS)
    peer_cols = at_cols((1 - core) * HALF_QCOLS, HALF_QCOLS, HALF_QCOLS)
    copies = start_copies(
        [
            (samp_hbm, samp),
            (tiles_hbm, tiles),
            (q_ref.at[0, :, peer_cols], peer.at[:tokens]),
            (g_ref.at[0, :, peer_cols], peer.at[tokens : 2 * tokens]),
            (q_ref.at[0, :, own_cols], q_own.at[:tokens]),
            (g_ref.at[0, :, own_cols], g_own),
        ],
        sems,
    )
    for copy in copies[:2]:
        copy.wait()
    row = jnp.broadcast_to(samp[...].astype(F32), (SAMP_ROWS, tokens)).astype(BF16)
    for out, first in ((q_own, tokens), (peer, 2 * tokens)):
        out[first:, :] = jnp.zeros((SAMP_ROWS, HALF_QCOLS), BF16)
        out[first:, :tokens] = row

    sample, enc = where()
    block_rows = SLOT_ROWS // n_blocks
    slots = block_rows // pieces
    line = lax.broadcasted_iota(jnp.int32, (SLOT_ROWS, HD), 0)
    block = lax.div(line, block_rows)
    if n_blocks > 1:
        n_z = n_blocks // 2
        block = 2 * lax.rem(block, n_z) + lax.div(block, n_z)
    owner = block ^ enc
    piece = lax.rem(lax.div(line, slots), pieces)
    slot = piece * (SLOT_ROWS // pieces) + owner * slots + lax.rem(line, slots)
    for i in range(SAMP):
        count = jnp.where((sample ^ i) == 0, tiles[0:1, 0:1], tiles[0:1, 1:2])
        bias[i] = jnp.where(slot < count * TILE_TOK, 0.0, BIG_NEGATIVE)
    for copy in copies[2:]:
        copy.wait()


def carry_kernel(slots, own, got, text, *outs):
    core = core_of()
    enc = lax.axis_index("enc")
    n_z = (len(outs) - 1) // CHUNKS
    for c in range(CHUNKS):
        for dz in range(n_z):
            out = outs[c * n_z + dz]
            for dx in range(2):
                group = enc ^ (2 * dz + dx)
                for i in range(2):
                    first = i * CORES * slots
                    out[dx, at_rows(first + core * slots, slots), :] = own[c, i, group]
                    out[dx, at_rows(first + (1 - core) * slots, slots), :] = got[c, i, group]


def join_kernel(*refs):
    parts, outs = refs[:-2], refs[-2:]
    rows = parts[0].shape[1]
    for dx, out in enumerate(outs):
        for dz, part in enumerate(parts):
            out[dz * rows : (dz + 1) * rows, :] = part[dx]


def add_kernel(own, back_y, back_x, back_xy, *outs):
    rows = outs[0].shape[1]
    for dz, out in enumerate(outs):
        part = slice(dz * rows, (dz + 1) * rows)
        out[0] = (own[part, :] + back_y[part, :].astype(F32)).astype(out.dtype)
        out[1] = (back_x[part, :].astype(F32) + back_xy[part, :].astype(F32)).astype(out.dtype)


def owner_rows_kernel(slots, n_z, *refs):
    core = core_of()
    enc = lax.axis_index("enc")
    parts, (mine_out, peer_out) = refs[: CHUNKS * n_z], refs[-2:]
    for c in range(CHUNKS):
        for dz in range(n_z):
            part = parts[c * n_z + dz]
            for dx in range(2):
                group = enc ^ (2 * dz + dx)
                for i in range(2):
                    first = i * CORES * slots
                    mine_out[c, i, group] = part[dx, at_rows(first + core * slots, slots), :]
                    peer_out[c, i, group] = part[dx, at_rows(first + (1 - core) * slots, slots), :]


def finish_kernel(mine, got, dk, dv, sems):
    core = core_of()
    pairs = []
    for half, ref in ((core, mine), (1 - core, got)):
        for c in range(CHUNKS):
            cols = at_cols(half * HALF_KCOLS + c * CHUNK_KCOLS, CHUNK_KCOLS, CHUNK_KCOLS)
            for i, out in enumerate((dk, dv)):
                pairs.append((ref.at[c, i], out.at[:, :, cols]))
    run_copies(pairs, sems)


def finish_text_kernel(*refs):
    refs, (out, token, sems) = refs[:-3], refs[-3:]
    core = core_of()
    token[...] = jnp.zeros_like(token)
    pairs = []
    for c in range(CHUNKS):
        for half, ref in ((core, refs[2 * c]), (1 - core, refs[2 * c + 1])):
            cols = at_cols(half * HALF_QCOLS + c * CHUNK_QCOLS, CHUNK_QCOLS, CHUNK_QCOLS)
            pairs.append((ref, out.at[0, :, cols]))
    run_copies(pairs, sems)


def pass_kernel(role, chunk, n_blocks, n_kv, with_prev, where, bias, q_a, g_a, got, *rest):
    kvs, rest = rest[:n_kv], rest[n_kv:]
    prev = None
    if with_prev:
        prev, rest = rest[:2], rest[2:]
    dqs, grads = rest[:2], rest[2:]
    sample = where()[0] ^ role
    tokens = g_a.shape[0]
    block_rows = SLOT_ROWS // n_blocks
    row_a = q_a[tokens : tokens + 1, :tokens].astype(F32)
    row_b = got[2 * tokens : 2 * tokens + 1, :tokens].astype(F32)
    wanted = sample.astype(F32)
    has = jnp.where(row_a == wanted, 1.0, jnp.where(row_b == wanted, 1.0, 0.0))
    present = jnp.max(has) > 0.5

    @pl.when(present)
    def _():
        mine = jnp.concatenate([row_a] * RATIO + [row_b] * RATIO, axis=1) == wanted
        for h in range(CHUNK_KV):
            first_q = chunk * CHUNK_QCOLS + h * WIDE

            def stacked(ref_a, first_b):
                parts = [
                    ref[first : first + tokens, first_q + r * HD : first_q + (r + 1) * HD]
                    for ref, first in ((ref_a, 0), (got, first_b))
                    for r in range(RATIO)
                ]
                return jnp.concatenate(parts, axis=0)

            def rows_of(first):
                parts = []
                for kv in kvs:
                    for at in range(first, kv.shape[0], 2 * block_rows):
                        parts.append(kv[at : at + block_rows, h * HD : (h + 1) * HD])
                return jnp.concatenate(parts, axis=0)

            q = stacked(q_a, 0)
            g = stacked(g_a, tokens)
            k = rows_of(0)
            v = rows_of(block_rows)
            s = lax.dot_general(k, q, NT, preferred_element_type=F32)
            s = s + jnp.concatenate([bias[role]] * (s.shape[1] // HD), axis=1)
            top = jnp.max(s, axis=0, keepdims=True)
            e = jnp.exp2((s - top) * (SCALE * LOG2E))
            total = jnp.sum(e, axis=0, keepdims=True)
            p = e * jnp.where(mine, 1.0 / total, 0.0)
            gp = lax.dot_general(v, g, NT, preferred_element_type=F32)
            row_dot = jnp.sum(p * gp, axis=0, keepdims=True)
            ds = (p * (gp - row_dot)).astype(BF16)
            dv = jnp.dot(p.astype(BF16), g, preferred_element_type=F32)
            dk = jnp.dot(ds, q, preferred_element_type=F32) * SCALE
            dq = lax.dot_general(ds, k, TN, preferred_element_type=F32) * SCALE
            for t, dq_ref in enumerate(dqs):
                for r in range(RATIO):
                    at = (t * RATIO + r) * tokens
                    cols = slice(h * WIDE + r * HD, h * WIDE + (r + 1) * HD)
                    part = dq[at : at + tokens]
                    if with_prev:
                        part = part + prev[t][:, cols].astype(F32)
                    dq_ref[:, cols] = part.astype(dq_ref.dtype)
            cols = slice(h * HD, (h + 1) * HD)
            each = n_blocks // len(grads)
            for b in range(n_blocks):
                rows = slice(b * block_rows, (b + 1) * block_rows)
                out, first = grads[b // each], b % each * 2 * block_rows
                out[first : first + block_rows, cols] = dk[rows].astype(out.dtype)
                out[first + block_rows : first + 2 * block_rows, cols] = dv[rows].astype(out.dtype)

    @pl.when(jnp.logical_not(present))
    def _():
        for out in grads:
            out[...] = jnp.zeros_like(out)
        for t, dq_ref in enumerate(dqs):
            dq_ref[...] = prev[t][...] if with_prev else jnp.zeros_like(dq_ref)


def sample_pass(where, role, chunk, n_blocks, bias, text, kvs, prev, grad_dtypes):
    tokens = text[1].shape[0]
    dq = ((tokens, CHUNK_QCOLS), BF16)
    pairs = tokens * WIDE * SLOT_ROWS * CORES * CHUNK_KV
    dq_a, dq_b, *grads = in_vmem(
        functools.partial(
            pass_kernel, role, chunk, n_blocks, len(kvs), prev is not None, where
        ),
        [dq, dq] + [(kv.shape, dtype) for kv, dtype in zip(kvs, grad_dtypes)],
        flops=10 * pairs,
        moved=8 * 2**20,
    )(bias, *text, *kvs, *(prev or ()))
    return (dq_a, dq_b), grads


def shards(n_ctx, n_enc, queries, d_out, text_sample, tiles, img_k, img_v):
    n_y = n_ctx // CORES
    slots = img_k.shape[1]
    tokens = queries.shape[1]
    swap_core = [(i, i ^ 1) for i in range(n_ctx)]
    near = n_y == SAMP and slots % 16 == 0 and n_enc == 8
    dqs = [None] * CHUNKS
    text_outs = [
        ((2 * tokens + SAMP_ROWS, HALF_QCOLS), BF16, IN_VMEM),
        ((tokens + SAMP_ROWS, HALF_QCOLS), BF16, IN_VMEM),
        ((tokens, HALF_QCOLS), BF16, IN_VMEM),
        ((SAMP, SLOT_ROWS, HD), F32, IN_VMEM),
    ]
    text_scratch = [
        pltpu.VMEM(text_sample.shape, jnp.int32),
        pltpu.VMEM(tiles.shape, jnp.int32),
    ]
    text_sems = pltpu.SemaphoreType.DMA((6,))

    if near:
        swap_y = [(i, (i + CORES) % n_ctx) for i in range(n_ctx)]
        n_z = n_enc // 2
        pair = (2, 2 * CORES * slots, CHUNK_KCOLS)
        half = (SLOT_ROWS, CHUNK_KCOLS)
        halves = (CHUNKS, 2, n_enc, slots, CHUNK_KCOLS)
        swap_x = [(i, i ^ 1) for i in range(n_enc)]
        swap_xy = [
            (i * n_enc + e, (i + CORES) % n_ctx * n_enc + (e ^ 1))
            for i in range(n_ctx)
            for e in range(n_enc)
        ]

        def around_z(parts):
            moved = [
                lax.ppermute(parts[dz], "enc", [(i, i ^ (2 * dz)) for i in range(n_enc)])
                for dz in range(1, n_z)
            ]
            return [parts[0], *moved]

        def along_x(part):
            return lax.ppermute(part, "enc", swap_x)

        def along_y(part):
            return lax.ppermute(part, "ctx", swap_y)

        def along_xy(part):
            return lax.ppermute(part, ("ctx", "enc"), swap_xy)

        mine, for_peer, text_peer, q_own, g_own, bias = local_call(
            split_kernel,
            [IN_HBM] * 6,
            [(halves, BF16, IN_VMEM)] * 2 + text_outs,
            text_scratch + [pltpu.SemaphoreType.DMA((4 * CHUNKS,)), text_sems],
            moved=4 * 2**20,
        )(*in_hbm(img_k, img_v, queries, d_out, text_sample, tiles))
        *carry, text_peer = in_vmem(
            functools.partial(carry_kernel, slots),
            [(pair, BF16)] * CHUNKS * n_z + [(text_peer.shape, BF16)],
            aliases={2: CHUNKS * n_z},
        )(mine, lax.ppermute(for_peer, "ctx", swap_core), text_peer)
        text = (q_own, g_own, lax.ppermute(text_peer, "ctx", swap_core))

        returned = []
        for c in range(CHUNKS):
            came = around_z(carry[c * n_z : (c + 1) * n_z])
            here, beside = in_vmem(join_kernel, [(half, BF16)] * 2)(*came)
            own = [here, along_x(beside)]
            far = [along_y(here), along_xy(beside)]
            dqs[c], (own_here, own_beside) = sample_pass(
                near_place, 0, c, n_enc, bias, text, own, None, (F32, BF16)
            )
            back_x = along_x(own_beside)
            dqs[c], (far_here, far_beside) = sample_pass(
                near_place, 1, c, n_enc, bias, text, far, dqs[c], (BF16, BF16)
            )
            totals = in_vmem(add_kernel, [(pair, BF16)] * n_z)(
                own_here, along_y(far_here), back_x, along_xy(far_beside)
            )
            returned += around_z(totals)
    else:
        both = ("ctx", "enc")
        same_y = [
            [yy * CORES * n_enc + i for i in range(CORES * n_enc)] for yy in range(n_y)
        ]
        same_column = [
            [(yy * CORES + c) * n_enc + e for yy in range(n_y)]
            for c in range(CORES)
            for e in range(n_enc)
        ]
        core = core_of()

        def exchange(parts):
            return lax.all_to_all(
                parts, both, split_axis=0, concat_axis=0, axis_index_groups=same_y, tiled=True
            )

        def to_groups(owned):
            parts = owned.reshape(n_enc, slots, CORES, HALF_KCOLS).transpose(2, 0, 1, 3)
            got = exchange(parts.reshape(CORES * n_enc, slots, HALF_KCOLS))
            got = got.reshape(CORES * n_enc * slots, HALF_KCOLS)
            return lax.all_gather(got, both, axis=0, axis_index_groups=same_column, tiled=True)

        def to_owners(grads):
            grads = lax.psum_scatter(
                grads, both, scatter_dimension=0, axis_index_groups=same_column, tiled=True
            )
            got = exchange(grads.reshape(CORES * n_enc, slots, HALF_KCOLS))
            got = got.reshape(CORES, n_enc, slots, HALF_KCOLS).transpose(1, 2, 0, 3)
            return got.reshape(n_enc, slots, CORES * HALF_KCOLS)

        def no_place():
            return jnp.int32(0), jnp.int32(0)

        all_k = to_groups(img_k)
        all_v = to_groups(img_v)
        text_peer, q_own, g_own, bias = local_call(
            functools.partial(split_text, 1, 1, no_place),
            [IN_HBM] * 4,
            text_outs,
            text_scratch + [text_sems],
            moved=4 * 2**20,
        )(*in_hbm(queries, d_out, text_sample, tiles))
        text = (q_own, g_own, lax.ppermute(text_peer, "ctx", swap_core))
        dks = [[None] * CHUNKS for _ in range(SAMP)]
        dvs = [[None] * CHUNKS for _ in range(SAMP)]
        for sample in range(SAMP):
            rows = slice(sample * SLOT_ROWS, (sample + 1) * SLOT_ROWS)
            kv = jnp.concatenate([all_k[rows], all_v[rows]], axis=0)
            kv = jnp.split(kv, CHUNKS, axis=1)
            for c in range(CHUNKS):
                dqs[c], (grads,) = sample_pass(no_place, sample, c, 1, bias, text, [kv[c]], dqs[c], (BF16,))
                dks[sample][c] = grads[:SLOT_ROWS]
                dvs[sample][c] = grads[SLOT_ROWS:]
        d_img_k = to_owners(jnp.block(dks))
        d_img_v = to_owners(jnp.block(dvs))

    ends = []
    for c in range(CHUNKS):
        ends += [dqs[c][0], lax.ppermute(dqs[c][1], "ctx", swap_core)]
    d_queries, token = local_call(
        finish_text_kernel,
        [IN_VMEM] * len(ends),
        [(queries.shape, BF16, IN_HBM), ((8, HD), F32, IN_VMEM)],
        [pltpu.SemaphoreType.DMA((2 * CHUNKS,))],
    )(*ends)
    if near:
        mine, for_peer = in_vmem(
            functools.partial(owner_rows_kernel, slots, n_z), [(halves, BF16)] * 2
        )(*returned, token)
        d_img_k, d_img_v = local_call(
            finish_kernel,
            [IN_VMEM] * 2,
            [(img_k.shape, BF16, IN_HBM)] * 2,
            [pltpu.SemaphoreType.DMA((4 * CHUNKS,))],
        )(mine, lax.ppermute(for_peer, "ctx", swap_core))
    return (d_queries, d_img_k, d_img_v)


def solution(mesh):
    in_specs = (
        P("enc", "ctx", None),
        P("enc", "ctx", None),
        P("enc", "ctx"),
        P("enc", None),
        P(None, ("ctx", "enc"), None),
        P(None, ("ctx", "enc"), None),
    )
    out_specs = (
        P("enc", "ctx", None),
        P(None, ("ctx", "enc"), None),
        P(None, ("ctx", "enc"), None),
    )
    body = functools.partial(shards, mesh.shape["ctx"], mesh.shape["enc"])
    return jax.shard_map(body, mesh=mesh, in_specs=in_specs, out_specs=out_specs, check_vma=False)
```

```python
import functools

import jax
import jax.numpy as jnp
from jax import lax
from jax.experimental import pallas as pl
from jax.experimental.pallas import tpu as pltpu
from jax.sharding import PartitionSpec as P

H = 32
KVH = 8
HD = 128
SAMP = 2
MAX_TILES = 4
TILE_TOK = 64
RATIO = H // KVH
CORES = 2
SLOT_ROWS = MAX_TILES * TILE_TOK
HALF_KV = KVH // CORES
HALF_KCOLS = HALF_KV * HD
HALF_QCOLS = HALF_KCOLS * RATIO
WIDE = RATIO * HD
CHUNKS = 2
CHUNK_KV = HALF_KV // CHUNKS
CHUNK_KCOLS = CHUNK_KV * HD
CHUNK_QCOLS = CHUNK_KV * WIDE
SAMP_ROWS = 16
SCALE = HD ** (-0.5)
LOG2E = 1.4426950408889634
BIG_NEGATIVE = -1e30
NT = (((1,), (1,)), ((), ()))
TN = (((0,), (0,)), ((), ()))
BF16 = jnp.bfloat16
F32 = jnp.float32

IN_VMEM = pl.BlockSpec(memory_space=pltpu.VMEM)
IN_HBM = pl.BlockSpec(memory_space=pltpu.HBM)


def local_call(body, ins, outs, scratch=(), flops=0, moved=2**19, aliases={}):
    return pl.pallas_call(
        body,
        in_specs=ins,
        out_specs=[spec for _, _, spec in outs],
        out_shape=[jax.ShapeDtypeStruct(s, d) for s, d, _ in outs],
        scratch_shapes=list(scratch),
        compiler_params=pltpu.CompilerParams(vmem_limit_bytes=8 * 2**20),
        input_output_aliases=aliases,
        cost_estimate=pl.CostEstimate(
            flops=flops, bytes_accessed=moved, transcendentals=flops // 1280
        ),
    )


def in_vmem(body, outs, **more):
    def call(*args):
        spec = [(shape, dtype, IN_VMEM) for shape, dtype in outs]
        return local_call(body, [IN_VMEM] * len(args), spec, **more)(*args)

    return call


def core_of():
    return lax.rem(lax.axis_index("ctx"), CORES)


def at_rows(first, count):
    return pl.ds(pl.multiple_of(first, count), count)


def at_cols(first, width, step):
    return pl.ds(pl.multiple_of(first, step), width)


def start_copies(pairs, sems):
    copies = [pltpu.make_async_copy(src, dst, sems.at[i]) for i, (src, dst) in enumerate(pairs)]
    for copy in copies:
        copy.start()
    return copies


def run_copies(pairs, sems):
    for copy in start_copies(pairs, sems):
        copy.wait()


def in_hbm(*arrays):
    return [pltpu.with_memory_space_constraint(a, pltpu.HBM) for a in arrays]


def split_kernel(*refs):
    k_ref, v_ref, q_ref, g_ref, samp_hbm, tiles_hbm, mine, peer = refs[:8]
    text_refs, (samp, tiles, sems, small_sems) = refs[8:-4], refs[-4:]
    core = core_of()
    pairs = []
    for half, out in ((1 - core, peer), (core, mine)):
        cols = at_cols(half * HALF_KCOLS, HALF_KCOLS, HALF_KCOLS)
        for i, ref in enumerate((k_ref, v_ref)):
            pairs.append((ref.at[:, :, cols], out.at[i]))
    copies = start_copies(pairs, sems)
    split_text(
        k_ref.shape[0], CORES, near_place, q_ref, g_ref, samp_hbm, tiles_hbm, *text_refs, samp, tiles, small_sems
    )
    for copy in copies:
        copy.wait()


def near_place():
    return lax.div(lax.axis_index("ctx"), CORES), lax.axis_index("enc")


def split_text(n_blocks, pieces, where, q_ref, g_ref, samp_hbm, tiles_hbm, peer, q_own, g_own, bias, samp, tiles, sems):
    core = core_of()
    tokens = q_ref.shape[1]
    own_cols = at_cols(core * HALF_QCOLS, HALF_QCOLS, HALF_QCOLS)
    peer_cols = at_cols((1 - core) * HALF_QCOLS, HALF_QCOLS, HALF_QCOLS)
    copies = start_copies(
        [
            (samp_hbm, samp),
            (tiles_hbm, tiles),
            (q_ref.at[0, :, peer_cols], peer.at[:tokens]),
            (g_ref.at[0, :, peer_cols], peer.at[tokens : 2 * tokens]),
            (q_ref.at[0, :, own_cols], q_own.at[:tokens]),
            (g_ref.at[0, :, own_cols], g_own),
        ],
        sems,
    )
    for copy in copies[:2]:
        copy.wait()
    row = jnp.broadcast_to(samp[...].astype(F32), (SAMP_ROWS, tokens)).astype(BF16)
    for out, first in ((q_own, tokens), (peer, 2 * tokens)):
        out[first:, :] = jnp.zeros((SAMP_ROWS, HALF_QCOLS), BF16)
        out[first:, :tokens] = row

    sample, enc = where()
    block_rows = SLOT_ROWS // n_blocks
    slots = block_rows // pieces
    line = lax.broadcasted_iota(jnp.int32, (SLOT_ROWS, HD), 0)
    block = lax.div(line, block_rows)
    if n_blocks > 1:
        low, high = block & 1, lax.div(block, 2) & 1
        block = block - low - 2 * high + 2 * low + high
    owner = block ^ enc
    piece = lax.rem(lax.div(line, slots), pieces)
    slot = piece * (SLOT_ROWS // pieces) + owner * slots + lax.rem(line, slots)
    for i in range(SAMP):
        count = jnp.where((sample ^ i) == 0, tiles[0:1, 0:1], tiles[0:1, 1:2])
        bias[i] = jnp.where(slot < count * TILE_TOK, 0.0, BIG_NEGATIVE)
    for copy in copies[2:]:
        copy.wait()


def carry_kernel(slots, own, got, text, *outs):
    core = core_of()
    enc = lax.axis_index("enc")
    for dz, out in enumerate(outs[:-1]):
        for dx in range(2):
            group = enc ^ (2 * dz + dx)
            for i in range(2):
                first = i * CORES * slots
                out[dx, at_rows(first + core * slots, slots), :] = own[i, group]
                out[dx, at_rows(first + (1 - core) * slots, slots), :] = got[i, group]


def join_kernel(*refs):
    parts, outs = refs[:2], refs[-2:]
    rows = parts[0].shape[1]
    for dx, out in enumerate(outs):
        for dz, part in enumerate(parts):
            out[dz * rows : (dz + 1) * rows, :] = part[dx]


def join_cols_kernel(*refs):
    parts, out = refs[:CHUNKS], refs[-1]
    for c, part in enumerate(parts):
        out[:, c * CHUNK_QCOLS : (c + 1) * CHUNK_QCOLS] = part[...]


def block_place(b, n_outs):
    return (b // 2 % 2, b // 4 * 2 + b % 2) if n_outs > 1 else (0, b)


def add_kernel(chunk, n_z, own, back_y, back_x, back_xy, *rest):
    outs = rest[-n_z:]
    rows = outs[0].shape[1]
    cols = slice(chunk * CHUNK_KCOLS, (chunk + 1) * CHUNK_KCOLS)
    for dz, out in enumerate(outs):
        part = slice(dz * rows, (dz + 1) * rows)
        out[0] = (own[part, cols] + back_y[part, :].astype(F32)).astype(out.dtype)
        out[1] = (back_x[part, cols].astype(F32) + back_xy[part, :].astype(F32)).astype(out.dtype)


def owner_rows_kernel(slots, n_z, *refs):
    core = core_of()
    enc = lax.axis_index("enc")
    parts, (mine_out, peer_out) = refs[: CHUNKS * n_z], refs[-2:]
    for c in range(CHUNKS):
        for dz in range(n_z):
            part = parts[c * n_z + dz]
            for dx in range(2):
                group = enc ^ (2 * dz + dx)
                for i in range(2):
                    first = i * CORES * slots
                    mine_out[c, i, group] = part[dx, at_rows(first + core * slots, slots), :]
                    peer_out[c, i, group] = part[dx, at_rows(first + (1 - core) * slots, slots), :]


def finish_kernel(mine, got, dk, dv, sems):
    core = core_of()
    pairs = []
    for half, ref in ((core, mine), (1 - core, got)):
        for c in range(CHUNKS):
            cols = at_cols(half * HALF_KCOLS + c * CHUNK_KCOLS, CHUNK_KCOLS, CHUNK_KCOLS)
            for i, out in enumerate((dk, dv)):
                pairs.append((ref.at[c, i], out.at[:, :, cols]))
    run_copies(pairs, sems)


def finish_text_kernel(*refs):
    parts, got, (out, token, sems) = refs[:CHUNKS], refs[CHUNKS], refs[-3:]
    core = core_of()
    token[...] = jnp.zeros_like(token)
    pairs = [(got, out.at[0, :, at_cols((1 - core) * HALF_QCOLS, HALF_QCOLS, HALF_QCOLS)])]
    for c, part in enumerate(parts):
        cols = at_cols(core * HALF_QCOLS + c * CHUNK_QCOLS, CHUNK_QCOLS, CHUNK_QCOLS)
        pairs.append((part, out.at[0, :, cols]))
    run_copies(pairs, sems)


def pass_kernel(role, first_head, n_heads, n_blocks, n_kv, with_prev, n_after, n_grads, where, bias, q_a, g_a, got, *rest):
    kvs, rest = rest[:n_kv], rest[n_kv:]
    prev = None
    if with_prev:
        prev, rest = rest[:2], rest[2:]
    rest = rest[n_after:]
    dqs, grads = rest[:2], rest[2 : 2 + n_grads]
    sample = where()[0] ^ role
    tokens = g_a.shape[0]
    block_rows = SLOT_ROWS // n_blocks
    row_a = q_a[tokens : tokens + 1, :tokens].astype(F32)
    row_b = got[2 * tokens : 2 * tokens + 1, :tokens].astype(F32)
    wanted = sample.astype(F32)
    has = jnp.where(row_a == wanted, 1.0, jnp.where(row_b == wanted, 1.0, 0.0))
    present = jnp.max(has) > 0.5

    @pl.when(present)
    def _():
        mine = jnp.concatenate([row_a] * RATIO + [row_b] * RATIO, axis=1) == wanted
        for h in range(n_heads):
            first_q = (first_head + h) * WIDE
            first_k = (first_head + h) * HD

            def stacked(ref_a, first_b):
                parts = [
                    ref[first : first + tokens, first_q + r * HD : first_q + (r + 1) * HD]
                    for ref, first in ((ref_a, 0), (got, first_b))
                    for r in range(RATIO)
                ]
                return jnp.concatenate(parts, axis=0)

            def rows_of(first):
                parts = []
                for kv in kvs:
                    for at in range(first, kv.shape[0], 2 * block_rows):
                        parts.append(kv[at : at + block_rows, first_k : first_k + HD])
                return jnp.concatenate(parts, axis=0)

            q = stacked(q_a, 0)
            g = stacked(g_a, tokens)
            k = rows_of(0)
            v = rows_of(block_rows)
            s = lax.dot_general(k, q, NT, preferred_element_type=F32)
            s = s + jnp.concatenate([bias[role]] * (s.shape[1] // HD), axis=1)
            top = jnp.max(s, axis=0, keepdims=True)
            e = jnp.exp2((s - top) * (SCALE * LOG2E))
            total = jnp.sum(e, axis=0, keepdims=True)
            p = e * jnp.where(mine, 1.0 / total, 0.0)
            gp = lax.dot_general(v, g, NT, preferred_element_type=F32)
            row_dot = jnp.sum(p * gp, axis=0, keepdims=True)
            ds = (p * (gp - row_dot)).astype(BF16)
            dv = jnp.dot(p.astype(BF16), g, preferred_element_type=F32)
            dk = jnp.dot(ds, q, preferred_element_type=F32) * SCALE
            dq = lax.dot_general(ds, k, TN, preferred_element_type=F32) * SCALE
            for t, dq_ref in enumerate(dqs):
                for r in range(RATIO):
                    at = (t * RATIO + r) * tokens
                    cols = slice(h * WIDE + r * HD, h * WIDE + (r + 1) * HD)
                    part = dq[at : at + tokens]
                    if with_prev:
                        from_cols = slice(first_q + r * HD, first_q + (r + 1) * HD)
                        part = part + prev[t][:, from_cols].astype(F32)
                    dq_ref[:, cols] = part.astype(dq_ref.dtype)
            cols = slice(h * HD, (h + 1) * HD)
            for b in range(n_blocks):
                rows = slice(b * block_rows, (b + 1) * block_rows)
                dx, at = block_place(b, len(grads))
                out, first = grads[dx], at * 2 * block_rows
                out[first : first + block_rows, cols] = dk[rows].astype(out.dtype)
                out[first + block_rows : first + 2 * block_rows, cols] = dv[rows].astype(out.dtype)

    @pl.when(jnp.logical_not(present))
    def _():
        for out in grads:
            out[...] = jnp.zeros_like(out)
        for t, dq_ref in enumerate(dqs):
            if with_prev:
                dq_ref[...] = prev[t][:, first_head * WIDE : (first_head + n_heads) * WIDE]
            else:
                dq_ref[...] = jnp.zeros_like(dq_ref)


def sample_pass(where, role, first_head, n_heads, n_blocks, bias, text, kvs, prev, grads, after=(), through=()):
    tokens = text[1].shape[0]
    dq = ((tokens, n_heads * WIDE), BF16)
    pairs = tokens * WIDE * SLOT_ROWS * CORES * n_heads
    args = [bias, *text, *kvs, *(prev or ()), *after]
    dq_a, dq_b, *outs = in_vmem(
        functools.partial(
            pass_kernel,
            role,
            first_head,
            n_heads,
            n_blocks,
            len(kvs),
            prev is not None,
            len(after) + len(through),
            len(grads),
            where,
        ),
        [dq, dq, *grads] + [(a.shape, a.dtype) for a in through],
        flops=10 * pairs,
        moved=n_heads * 4 * 2**20,
        aliases={len(args) + i: 2 + len(grads) + i for i in range(len(through))},
    )(*args, *through)
    return (dq_a, dq_b), outs


def shards(n_ctx, n_enc, queries, d_out, text_sample, tiles, img_k, img_v):
    n_y = n_ctx // CORES
    slots = img_k.shape[1]
    tokens = queries.shape[1]
    swap_core = [(i, i ^ 1) for i in range(n_ctx)]
    near = n_y == SAMP and slots % 16 == 0 and n_enc == 8
    dqs = [None] * CHUNKS
    text_outs = [
        ((2 * tokens + SAMP_ROWS, HALF_QCOLS), BF16, IN_VMEM),
        ((tokens + SAMP_ROWS, HALF_QCOLS), BF16, IN_VMEM),
        ((tokens, HALF_QCOLS), BF16, IN_VMEM),
        ((SAMP, SLOT_ROWS, HD), F32, IN_VMEM),
    ]
    text_scratch = [
        pltpu.VMEM(text_sample.shape, jnp.int32),
        pltpu.VMEM(tiles.shape, jnp.int32),
    ]
    text_sems = pltpu.SemaphoreType.DMA((6,))

    if near:
        swap_y = [(i, (i + CORES) % n_ctx) for i in range(n_ctx)]
        n_z = n_enc // 2
        block_rows = 2 * CORES * slots
        pair = (2, block_rows, HALF_KCOLS)
        back_pair = (2, block_rows, CHUNK_KCOLS)
        quarter = (2 * block_rows, HALF_KCOLS)
        half = (SLOT_ROWS, CHUNK_KCOLS)
        whole = (SLOT_ROWS, HALF_KCOLS)
        kv_halves = (2, n_enc, slots, HALF_KCOLS)
        halves = (CHUNKS, 2, n_enc, slots, CHUNK_KCOLS)
        swap_x = [(i, i ^ 1) for i in range(n_enc)]
        swap_xy = [
            (i * n_enc + e, (i + CORES) % n_ctx * n_enc + (e ^ 1))
            for i in range(n_ctx)
            for e in range(n_enc)
        ]

        def around_z(parts):
            moved = [
                lax.ppermute(parts[dz], "enc", [(i, i ^ (2 * dz)) for i in range(n_enc)])
                for dz in range(1, n_z)
            ]
            return [parts[0], *moved]

        def along_x(part):
            return lax.ppermute(part, "enc", swap_x)

        def along_y(part):
            return lax.ppermute(part, "ctx", swap_y)

        def along_xy(part):
            return lax.ppermute(part, ("ctx", "enc"), swap_xy)

        mine, for_peer, text_peer, q_own, g_own, bias = local_call(
            split_kernel,
            [IN_HBM] * 6,
            [(kv_halves, BF16, IN_VMEM)] * 2 + text_outs,
            text_scratch + [pltpu.SemaphoreType.DMA((4,)), text_sems],
            moved=4 * 2**20,
        )(*in_hbm(img_k, img_v, queries, d_out, text_sample, tiles))
        *carry, text_peer = in_vmem(
            functools.partial(carry_kernel, slots),
            [(pair, BF16)] * n_z + [(text_peer.shape, BF16)],
            aliases={2: n_z},
        )(mine, lax.ppermute(for_peer, "ctx", swap_core), text_peer)
        text = (q_own, g_own, lax.ppermute(text_peer, "ctx", swap_core))

        came = around_z(carry)
        own, far = [], []
        for z in (0, 2):
            here, beside = in_vmem(join_kernel, [(quarter, BF16)] * 2)(
                *came[z : z + 2], text[2], *far
            )
            own += [here, along_x(beside)]
            far += [along_y(here), along_xy(beside)]
        own_dq, (own_here, own_beside) = sample_pass(
            near_place, 0, 0, HALF_KV, n_enc, bias, text, own, None, [(whole, F32), (whole, BF16)]
        )
        returned, after = [], ()
        for c in range(CHUNKS):
            dqs[c], (far_here, far_beside, *on) = sample_pass(
                near_place,
                1,
                c * CHUNK_KV,
                CHUNK_KV,
                n_enc,
                bias,
                text,
                far,
                own_dq,
                [(half, BF16)] * 2,
                after,
                () if c else (own_beside,),
            )
            if on:
                back_x = along_x(on[0])
            totals = in_vmem(functools.partial(add_kernel, c, n_z), [(back_pair, BF16)] * n_z)(
                own_here, along_y(far_here), back_x, along_xy(far_beside), *returned
            )
            returned += around_z(totals)
            after = dqs[c][:1]
        after = totals[:1]
    else:
        both = ("ctx", "enc")
        same_y = [
            [yy * CORES * n_enc + i for i in range(CORES * n_enc)] for yy in range(n_y)
        ]
        same_column = [
            [(yy * CORES + c) * n_enc + e for yy in range(n_y)]
            for c in range(CORES)
            for e in range(n_enc)
        ]
        core = core_of()

        def exchange(parts):
            return lax.all_to_all(
                parts, both, split_axis=0, concat_axis=0, axis_index_groups=same_y, tiled=True
            )

        def to_groups(owned):
            parts = owned.reshape(n_enc, slots, CORES, HALF_KCOLS).transpose(2, 0, 1, 3)
            got = exchange(parts.reshape(CORES * n_enc, slots, HALF_KCOLS))
            got = got.reshape(CORES * n_enc * slots, HALF_KCOLS)
            return lax.all_gather(got, both, axis=0, axis_index_groups=same_column, tiled=True)

        def to_owners(grads):
            grads = lax.psum_scatter(
                grads, both, scatter_dimension=0, axis_index_groups=same_column, tiled=True
            )
            got = exchange(grads.reshape(CORES * n_enc, slots, HALF_KCOLS))
            got = got.reshape(CORES, n_enc, slots, HALF_KCOLS).transpose(1, 2, 0, 3)
            return got.reshape(n_enc, slots, CORES * HALF_KCOLS)

        def no_place():
            return jnp.int32(0), jnp.int32(0)

        all_k = to_groups(img_k)
        all_v = to_groups(img_v)
        text_peer, q_own, g_own, bias = local_call(
            functools.partial(split_text, 1, 1, no_place),
            [IN_HBM] * 4,
            text_outs,
            text_scratch + [text_sems],
            moved=4 * 2**20,
        )(*in_hbm(queries, d_out, text_sample, tiles))
        text = (q_own, g_own, lax.ppermute(text_peer, "ctx", swap_core))
        kvs = [
            jnp.concatenate([part[s * SLOT_ROWS : (s + 1) * SLOT_ROWS] for part in (all_k, all_v)], axis=0)
            for s in range(SAMP)
        ]
        first_dq, (first,) = sample_pass(
            no_place, 0, 0, HALF_KV, 1, bias, text, kvs[:1], None, [(kvs[0].shape, BF16)]
        )
        chunks = []
        for c in range(CHUNKS):
            dqs[c], chunk = sample_pass(
                no_place, 1, c * CHUNK_KV, CHUNK_KV, 1, bias, text, kvs[1:], first_dq,
                [((2 * SLOT_ROWS, CHUNK_KCOLS), BF16)],
            )
            chunks += chunk
        grads = [first, jnp.concatenate(chunks, axis=1)]
        d_img_k = to_owners(jnp.concatenate([g[:SLOT_ROWS] for g in grads], axis=0))
        d_img_v = to_owners(jnp.concatenate([g[SLOT_ROWS:] for g in grads], axis=0))
        after = ()

    (dq_peer,) = in_vmem(join_cols_kernel, [((tokens, HALF_QCOLS), BF16)])(
        *[dq[1] for dq in dqs], *after
    )
    d_queries, token = local_call(
        finish_text_kernel,
        [IN_VMEM] * (CHUNKS + 1),
        [(queries.shape, BF16, IN_HBM), ((8, HD), F32, IN_VMEM)],
        [pltpu.SemaphoreType.DMA((CHUNKS + 1,))],
    )(*[dq[0] for dq in dqs], lax.ppermute(dq_peer, "ctx", swap_core))
    if near:
        mine, for_peer = in_vmem(
            functools.partial(owner_rows_kernel, slots, n_z), [(halves, BF16)] * 2
        )(*returned, token)
        d_img_k, d_img_v = local_call(
            finish_kernel,
            [IN_VMEM] * 2,
            [(img_k.shape, BF16, IN_HBM)] * 2,
            [pltpu.SemaphoreType.DMA((4 * CHUNKS,))],
        )(mine, lax.ppermute(for_peer, "ctx", swap_core))
    return (d_queries, d_img_k, d_img_v)


def solution(mesh):
    in_specs = (
        P("enc", "ctx", None),
        P("enc", "ctx", None),
        P("enc", "ctx"),
        P("enc", None),
        P(None, ("ctx", "enc"), None),
        P(None, ("ctx", "enc"), None),
    )
    out_specs = (
        P("enc", "ctx", None),
        P(None, ("ctx", "enc"), None),
        P(None, ("ctx", "enc"), None),
    )
    body = functools.partial(shards, mesh.shape["ctx"], mesh.shape["enc"])
    return jax.shard_map(body, mesh=mesh, in_specs=in_specs, out_specs=out_specs, check_vma=False)
```

```python
import functools

import jax
import jax.numpy as jnp
from jax import lax
from jax.experimental import pallas as pl
from jax.experimental.pallas import tpu as pltpu
from jax.sharding import PartitionSpec as P

H = 32
KVH = 8
HD = 128
SAMP = 2
MAX_TILES = 4
TILE_TOK = 64
RATIO = H // KVH
CORES = 2
SLOT_ROWS = MAX_TILES * TILE_TOK
HALF_KV = KVH // CORES
HALF_KCOLS = HALF_KV * HD
HALF_QCOLS = HALF_KCOLS * RATIO
WIDE = RATIO * HD
SAMP_ROWS = 16
SCALE = HD ** (-0.5)
LOG2E = 1.4426950408889634
BIG_NEGATIVE = -1e30
NT = (((1,), (1,)), ((), ()))
TN = (((0,), (0,)), ((), ()))
BF16 = jnp.bfloat16
F32 = jnp.float32

IN_VMEM = pl.BlockSpec(memory_space=pltpu.VMEM)
IN_HBM = pl.BlockSpec(memory_space=pltpu.HBM)


def local_call(body, ins, outs, scratch=(), flops=0, moved=2**19, aliases={}):
    return pl.pallas_call(
        body,
        in_specs=ins,
        out_specs=[spec for _, _, spec in outs],
        out_shape=[jax.ShapeDtypeStruct(s, d) for s, d, _ in outs],
        scratch_shapes=list(scratch),
        compiler_params=pltpu.CompilerParams(vmem_limit_bytes=8 * 2**20),
        input_output_aliases=aliases,
        cost_estimate=pl.CostEstimate(
            flops=flops, bytes_accessed=moved, transcendentals=flops // 1280
        ),
    )


def in_vmem(body, outs, **more):
    def call(*args):
        spec = [(shape, dtype, IN_VMEM) for shape, dtype in outs]
        return local_call(body, [IN_VMEM] * len(args), spec, **more)(*args)

    return call


def core_of():
    return lax.rem(lax.axis_index("ctx"), CORES)


def at_rows(first, count):
    return pl.ds(pl.multiple_of(first, count), count)


def at_cols(first, width, step):
    return pl.ds(pl.multiple_of(first, step), width)


def start_copies(pairs, sems):
    copies = [pltpu.make_async_copy(src, dst, sems.at[i]) for i, (src, dst) in enumerate(pairs)]
    for copy in copies:
        copy.start()
    return copies


def run_copies(pairs, sems):
    for copy in start_copies(pairs, sems):
        copy.wait()


def in_hbm(*arrays):
    return [pltpu.with_memory_space_constraint(a, pltpu.HBM) for a in arrays]


def split_kernel(k_ref, v_ref, mine, peer, sems):
    core = core_of()
    pairs = []
    for half, out in ((1 - core, peer), (core, mine)):
        cols = at_cols(half * HALF_KCOLS, HALF_KCOLS, HALF_KCOLS)
        for i, ref in enumerate((k_ref, v_ref)):
            pairs.append((ref.at[:, :, cols], out.at[i]))
    run_copies(pairs, sems)


def near_place():
    return lax.div(lax.axis_index("ctx"), CORES), lax.axis_index("enc")


def split_text(n_blocks, pieces, where, q_ref, g_ref, samp_hbm, tiles_hbm, peer, q_own, g_own, bias, samp, tiles, sems):
    core = core_of()
    tokens = q_ref.shape[1]
    own_cols = at_cols(core * HALF_QCOLS, HALF_QCOLS, HALF_QCOLS)
    peer_cols = at_cols((1 - core) * HALF_QCOLS, HALF_QCOLS, HALF_QCOLS)
    copies = start_copies(
        [
            (samp_hbm, samp),
            (tiles_hbm, tiles),
            (q_ref.at[0, :, peer_cols], peer.at[:tokens]),
            (g_ref.at[0, :, peer_cols], peer.at[tokens : 2 * tokens]),
            (q_ref.at[0, :, own_cols], q_own.at[:tokens]),
            (g_ref.at[0, :, own_cols], g_own),
        ],
        sems,
    )
    for copy in copies[:2]:
        copy.wait()
    row = jnp.broadcast_to(samp[...].astype(F32), (SAMP_ROWS, tokens)).astype(BF16)
    for out, first in ((q_own, tokens), (peer, 2 * tokens)):
        out[first:, :] = jnp.zeros((SAMP_ROWS, HALF_QCOLS), BF16)
        out[first:, :tokens] = row

    sample, enc = where()
    block_rows = SLOT_ROWS // n_blocks
    slots = block_rows // pieces
    line = lax.broadcasted_iota(jnp.int32, (SLOT_ROWS, HD), 0)
    block = lax.div(line, block_rows)
    if n_blocks > 1:
        low, high = block & 1, lax.div(block, 2) & 1
        block = block - low - 2 * high + 2 * low + high
    owner = block ^ enc
    piece = lax.rem(lax.div(line, slots), pieces)
    slot = piece * (SLOT_ROWS // pieces) + owner * slots + lax.rem(line, slots)
    for i in range(SAMP):
        count = jnp.where((sample ^ i) == 0, tiles[0:1, 0:1], tiles[0:1, 1:2])
        bias[i] = jnp.where(slot < count * TILE_TOK, 0.0, BIG_NEGATIVE)
    for copy in copies[2:]:
        copy.wait()


def carry_kernel(slots, own, got, text, *outs):
    core = core_of()
    enc = lax.axis_index("enc")
    for dz, out in enumerate(outs[:-1]):
        for dx in range(2):
            group = enc ^ (2 * dz + dx)
            for i in range(2):
                first = i * CORES * slots
                out[dx, at_rows(first + core * slots, slots), :] = own[i, group]
                out[dx, at_rows(first + (1 - core) * slots, slots), :] = got[i, group]


def join_kernel(*refs):
    parts, outs = refs[:2], refs[-2:]
    rows = parts[0].shape[1]
    for dx, out in enumerate(outs):
        for dz, part in enumerate(parts):
            out[dz * rows : (dz + 1) * rows, :] = part[dx]


def block_place(b, n_outs):
    return (b // 2 % 2, b // 4 * 2 + b % 2) if n_outs > 1 else (0, b)


def add_kernel(own, back_x, back_y, back_xy, _, *outs):
    rows = outs[0].shape[1]
    for dz, out in enumerate(outs):
        part = slice(dz * rows, (dz + 1) * rows)
        for dx, (here, far) in enumerate(((own, back_y), (back_x, back_xy))):
            out[dx] = (here[part, :].astype(F32) + far[part, :].astype(F32)).astype(out.dtype)


def owner_rows_kernel(slots, n_z, *refs):
    core = core_of()
    enc = lax.axis_index("enc")
    parts, (mine_out, peer_out) = refs[:n_z], refs[-2:]
    for dz, part in enumerate(parts):
        for dx in range(2):
            group = enc ^ (2 * dz + dx)
            for i in range(2):
                first = i * CORES * slots
                mine_out[i, group] = part[dx, at_rows(first + core * slots, slots), :]
                peer_out[i, group] = part[dx, at_rows(first + (1 - core) * slots, slots), :]


def finish_kernel(mine, got, dk, dv, sems):
    core = core_of()
    pairs = []
    for half, ref in ((core, mine), (1 - core, got)):
        cols = at_cols(half * HALF_KCOLS, HALF_KCOLS, HALF_KCOLS)
        for i, out in enumerate((dk, dv)):
            pairs.append((ref.at[i], out.at[:, :, cols]))
    run_copies(pairs, sems)


def finish_text_kernel(mine, got, out, token, sems):
    core = core_of()
    token[...] = jnp.zeros_like(token)
    pairs = []
    for half, ref in ((core, mine), (1 - core, got)):
        pairs.append((ref, out.at[0, :, at_cols(half * HALF_QCOLS, HALF_QCOLS, HALF_QCOLS)]))
    run_copies(pairs, sems)


def pass_kernel(role, n_blocks, n_kv, with_prev, n_through, n_grads, where, bias, q_a, g_a, got, *rest):
    kvs, rest = rest[:n_kv], rest[n_kv:]
    prev = None
    if with_prev:
        prev, rest = rest[:2], rest[2:]
    rest = rest[n_through:]
    dqs, grads = rest[:2], rest[2 : 2 + n_grads]
    sample = where()[0] ^ role
    tokens = g_a.shape[0]
    block_rows = SLOT_ROWS // n_blocks
    row_a = q_a[tokens : tokens + 1, :tokens].astype(F32)
    row_b = got[2 * tokens : 2 * tokens + 1, :tokens].astype(F32)
    wanted = sample.astype(F32)
    has = jnp.where(row_a == wanted, 1.0, jnp.where(row_b == wanted, 1.0, 0.0))
    present = jnp.max(has) > 0.5

    @pl.when(present)
    def _():
        mine = jnp.concatenate([row_a] * RATIO + [row_b] * RATIO, axis=1) == wanted
        for h in range(HALF_KV):
            first_q = h * WIDE
            first_k = h * HD

            def stacked(ref_a, first_b):
                parts = [
                    ref[first : first + tokens, first_q + r * HD : first_q + (r + 1) * HD]
                    for ref, first in ((ref_a, 0), (got, first_b))
                    for r in range(RATIO)
                ]
                return jnp.concatenate(parts, axis=0)

            def rows_of(first):
                parts = []
                for kv in kvs:
                    for at in range(first, kv.shape[0], 2 * block_rows):
                        parts.append(kv[at : at + block_rows, first_k : first_k + HD])
                return jnp.concatenate(parts, axis=0)

            q = stacked(q_a, 0)
            g = stacked(g_a, tokens)
            k = rows_of(0)
            v = rows_of(block_rows)
            s = lax.dot_general(k, q, NT, preferred_element_type=F32)
            s = s + jnp.concatenate([bias[role]] * (s.shape[1] // HD), axis=1)
            top = jnp.max(s, axis=0, keepdims=True)
            e = jnp.exp2((s - top) * (SCALE * LOG2E))
            total = jnp.sum(e, axis=0, keepdims=True)
            p = e * jnp.where(mine, 1.0 / total, 0.0)
            gp = lax.dot_general(v, g, NT, preferred_element_type=F32)
            row_dot = jnp.sum(p * gp, axis=0, keepdims=True)
            ds = (p * (gp - row_dot)).astype(BF16)
            dv = jnp.dot(p.astype(BF16), g, preferred_element_type=F32)
            dk = jnp.dot(ds, q, preferred_element_type=F32) * SCALE
            dq = lax.dot_general(ds, k, TN, preferred_element_type=F32) * SCALE
            for t, dq_ref in enumerate(dqs):
                for r in range(RATIO):
                    at = (t * RATIO + r) * tokens
                    cols = slice(first_q + r * HD, first_q + (r + 1) * HD)
                    part = dq[at : at + tokens]
                    if with_prev:
                        part = part + prev[t][:, cols].astype(F32)
                    dq_ref[:, cols] = part.astype(dq_ref.dtype)
            cols = slice(first_k, first_k + HD)
            for b in range(n_blocks):
                rows = slice(b * block_rows, (b + 1) * block_rows)
                dx, at = block_place(b, len(grads))
                out, first = grads[dx], at * 2 * block_rows
                out[first : first + block_rows, cols] = dk[rows].astype(out.dtype)
                out[first + block_rows : first + 2 * block_rows, cols] = dv[rows].astype(out.dtype)

    @pl.when(jnp.logical_not(present))
    def _():
        for out in grads:
            out[...] = jnp.zeros_like(out)
        for t, dq_ref in enumerate(dqs):
            dq_ref[...] = prev[t][...] if with_prev else jnp.zeros_like(dq_ref)


def sample_pass(where, role, n_blocks, bias, text, kvs, prev, grads, through=()):
    tokens = text[1].shape[0]
    dq = ((tokens, HALF_QCOLS), BF16)
    args = [bias, *text, *kvs, *(prev or ())]
    dq_a, dq_b, *outs = in_vmem(
        functools.partial(
            pass_kernel, role, n_blocks, len(kvs), prev is not None, len(through), len(grads), where
        ),
        [dq, dq, *grads] + [(a.shape, a.dtype) for a in through],
        flops=10 * tokens * WIDE * SLOT_ROWS * CORES * HALF_KV,
        moved=16 * 2**20,
        aliases={len(args) + i: 2 + len(grads) + i for i in range(len(through))},
    )(*args, *through)
    return (dq_a, dq_b), outs


def shards(n_ctx, n_enc, queries, d_out, text_sample, tiles, img_k, img_v):
    n_y = n_ctx // CORES
    slots = img_k.shape[1]
    tokens = queries.shape[1]
    swap_core = [(i, i ^ 1) for i in range(n_ctx)]
    near = n_y == SAMP and slots % 16 == 0 and n_enc == 8
    text_outs = [
        ((2 * tokens + SAMP_ROWS, HALF_QCOLS), BF16, IN_VMEM),
        ((tokens + SAMP_ROWS, HALF_QCOLS), BF16, IN_VMEM),
        ((tokens, HALF_QCOLS), BF16, IN_VMEM),
        ((SAMP, SLOT_ROWS, HD), F32, IN_VMEM),
    ]

    def split_the_text(n_blocks, pieces, where):
        return local_call(
            functools.partial(split_text, n_blocks, pieces, where),
            [IN_HBM] * 4,
            text_outs,
            [
                pltpu.VMEM(text_sample.shape, jnp.int32),
                pltpu.VMEM(tiles.shape, jnp.int32),
                pltpu.SemaphoreType.DMA((6,)),
            ],
            moved=4 * 2**20,
        )(*in_hbm(queries, d_out, text_sample, tiles))

    if near:
        swap_y = [(i, (i + CORES) % n_ctx) for i in range(n_ctx)]
        n_z = n_enc // 2
        block_rows = 2 * CORES * slots
        pair = (2, block_rows, HALF_KCOLS)
        quarter = (2 * block_rows, HALF_KCOLS)
        whole = (SLOT_ROWS, HALF_KCOLS)
        kv_halves = (2, n_enc, slots, HALF_KCOLS)
        swap_x = [(i, i ^ 1) for i in range(n_enc)]
        swap_xy = [
            (i * n_enc + e, (i + CORES) % n_ctx * n_enc + (e ^ 1))
            for i in range(n_ctx)
            for e in range(n_enc)
        ]

        def around_z(parts):
            moved = [
                lax.ppermute(parts[dz], "enc", [(i, i ^ (2 * dz)) for i in range(n_enc)])
                for dz in range(1, n_z)
            ]
            return [parts[0], *moved]

        def along_x(part):
            return lax.ppermute(part, "enc", swap_x)

        def along_y(part):
            return lax.ppermute(part, "ctx", swap_y)

        def along_xy(part):
            return lax.ppermute(part, ("ctx", "enc"), swap_xy)

        mine, for_peer = local_call(
            split_kernel,
            [IN_HBM] * 2,
            [(kv_halves, BF16, IN_VMEM)] * 2,
            [pltpu.SemaphoreType.DMA((4,))],
        )(*in_hbm(img_k, img_v))
        text_peer, q_own, g_own, bias = split_the_text(n_enc, CORES, near_place)
        *carry, text_peer = in_vmem(
            functools.partial(carry_kernel, slots),
            [(pair, BF16)] * n_z + [(text_peer.shape, BF16)],
            aliases={2: n_z},
        )(mine, lax.ppermute(for_peer, "ctx", swap_core), text_peer)
        text = (q_own, g_own, lax.ppermute(text_peer, "ctx", swap_core))

        came = around_z(carry)
        own, far = [], []
        for z in (0, 2):
            here, beside = in_vmem(join_kernel, [(quarter, BF16)] * 2)(
                *came[z : z + 2], text[2], *far
            )
            own += [here, along_x(beside)]
            far += [along_y(here), along_xy(beside)]
        own_dq, (own_here, own_beside) = sample_pass(
            near_place, 0, n_enc, bias, text, own, None, [(whole, F32), (whole, BF16)]
        )
        dq, (far_here, far_beside, own_beside) = sample_pass(
            near_place, 1, n_enc, bias, text, far, own_dq, [(whole, BF16)] * 2, (own_beside,)
        )
        dq_got = lax.ppermute(dq[1], "ctx", swap_core)
        totals = in_vmem(add_kernel, [(pair, BF16)] * n_z)(
            own_here, along_x(own_beside), along_y(far_here), along_xy(far_beside), dq_got
        )
        returned = around_z(totals)
    else:
        both = ("ctx", "enc")
        same_y = [
            [yy * CORES * n_enc + i for i in range(CORES * n_enc)] for yy in range(n_y)
        ]
        same_column = [
            [(yy * CORES + c) * n_enc + e for yy in range(n_y)]
            for c in range(CORES)
            for e in range(n_enc)
        ]
        core = core_of()

        def exchange(parts):
            return lax.all_to_all(
                parts, both, split_axis=0, concat_axis=0, axis_index_groups=same_y, tiled=True
            )

        def to_groups(owned):
            parts = owned.reshape(n_enc, slots, CORES, HALF_KCOLS).transpose(2, 0, 1, 3)
            got = exchange(parts.reshape(CORES * n_enc, slots, HALF_KCOLS))
            got = got.reshape(CORES * n_enc * slots, HALF_KCOLS)
            return lax.all_gather(got, both, axis=0, axis_index_groups=same_column, tiled=True)

        def to_owners(grads):
            grads = lax.psum_scatter(
                grads, both, scatter_dimension=0, axis_index_groups=same_column, tiled=True
            )
            got = exchange(grads.reshape(CORES * n_enc, slots, HALF_KCOLS))
            got = got.reshape(CORES, n_enc, slots, HALF_KCOLS).transpose(1, 2, 0, 3)
            return got.reshape(n_enc, slots, CORES * HALF_KCOLS)

        def no_place():
            return jnp.int32(0), jnp.int32(0)

        all_k = to_groups(img_k)
        all_v = to_groups(img_v)
        text_peer, q_own, g_own, bias = split_the_text(1, 1, no_place)
        text = (q_own, g_own, lax.ppermute(text_peer, "ctx", swap_core))
        kvs = [
            jnp.concatenate([part[s * SLOT_ROWS : (s + 1) * SLOT_ROWS] for part in (all_k, all_v)], axis=0)
            for s in range(SAMP)
        ]
        dq, grads = None, []
        for sample, kv in enumerate(kvs):
            dq, grad = sample_pass(no_place, sample, 1, bias, text, [kv], dq, [(kv.shape, BF16)])
            grads += grad
        d_img_k = to_owners(jnp.concatenate([g[:SLOT_ROWS] for g in grads], axis=0))
        d_img_v = to_owners(jnp.concatenate([g[SLOT_ROWS:] for g in grads], axis=0))
        dq_got = lax.ppermute(dq[1], "ctx", swap_core)

    d_queries, token = local_call(
        finish_text_kernel,
        [IN_VMEM] * 2,
        [(queries.shape, BF16, IN_HBM), ((8, HD), F32, IN_VMEM)],
        [pltpu.SemaphoreType.DMA((2,))],
    )(dq[0], dq_got)
    if near:
        mine, for_peer = in_vmem(
            functools.partial(owner_rows_kernel, slots, n_z), [(kv_halves, BF16)] * 2
        )(*returned, token)
        d_img_k, d_img_v = local_call(
            finish_kernel,
            [IN_VMEM] * 2,
            [(img_k.shape, BF16, IN_HBM)] * 2,
            [pltpu.SemaphoreType.DMA((4,))],
        )(mine, lax.ppermute(for_peer, "ctx", swap_core))
    return (d_queries, d_img_k, d_img_v)


def solution(mesh):
    in_specs = (
        P("enc", "ctx", None),
        P("enc", "ctx", None),
        P("enc", "ctx"),
        P("enc", None),
        P(None, ("ctx", "enc"), None),
        P(None, ("ctx", "enc"), None),
    )
    out_specs = (
        P("enc", "ctx", None),
        P(None, ("ctx", "enc"), None),
        P(None, ("ctx", "enc"), None),
    )
    body = functools.partial(shards, mesh.shape["ctx"], mesh.shape["enc"])
    return jax.shard_map(body, mesh=mesh, in_specs=in_specs, out_specs=out_specs, check_vma=False)
```

```python
import functools

import jax
import jax.numpy as jnp
from jax import lax
from jax.experimental import pallas as pl
from jax.experimental.pallas import tpu as pltpu
from jax.sharding import PartitionSpec as P

H = 32
KVH = 8
HD = 128
SAMP = 2
MAX_TILES = 4
TILE_TOK = 64
RATIO = H // KVH
CORES = 2
SLOT_ROWS = MAX_TILES * TILE_TOK
HALF_KV = KVH // CORES
HALF_KCOLS = HALF_KV * HD
HALF_QCOLS = HALF_KCOLS * RATIO
WIDE = RATIO * HD
SAMP_ROWS = 16
SCALE = HD ** (-0.5)
LOG2E = 1.4426950408889634
BIG_NEGATIVE = -1e30
NT = (((1,), (1,)), ((), ()))
TN = (((0,), (0,)), ((), ()))
BF16 = jnp.bfloat16
F32 = jnp.float32

IN_VMEM = pl.BlockSpec(memory_space=pltpu.VMEM)
IN_HBM = pl.BlockSpec(memory_space=pltpu.HBM)


def local_call(body, ins, outs, scratch=(), flops=0, moved=2**19, aliases={}):
    return pl.pallas_call(
        body,
        in_specs=ins,
        out_specs=[spec for _, _, spec in outs],
        out_shape=[jax.ShapeDtypeStruct(s, d) for s, d, _ in outs],
        scratch_shapes=list(scratch),
        compiler_params=pltpu.CompilerParams(vmem_limit_bytes=8 * 2**20),
        input_output_aliases=aliases,
        cost_estimate=pl.CostEstimate(
            flops=flops, bytes_accessed=moved, transcendentals=flops // 1280
        ),
    )


def in_vmem(body, outs, **more):
    def call(*args):
        spec = [(shape, dtype, IN_VMEM) for shape, dtype in outs]
        return local_call(body, [IN_VMEM] * len(args), spec, **more)(*args)

    return call


def core_of():
    return lax.rem(lax.axis_index("ctx"), CORES)


def at_rows(first, count):
    return pl.ds(pl.multiple_of(first, count), count)


def at_cols(first, width, step):
    return pl.ds(pl.multiple_of(first, step), width)


def start_copies(pairs, sems):
    copies = [pltpu.make_async_copy(src, dst, sems.at[i]) for i, (src, dst) in enumerate(pairs)]
    for copy in copies:
        copy.start()
    return copies


def run_copies(pairs, sems):
    for copy in start_copies(pairs, sems):
        copy.wait()


def in_hbm(*arrays):
    return [pltpu.with_memory_space_constraint(a, pltpu.HBM) for a in arrays]


def split_kernel(k_ref, v_ref, mine, peer, sems):
    core = core_of()
    pairs = []
    for half, out in ((1 - core, peer), (core, mine)):
        cols = at_cols(half * HALF_KCOLS, HALF_KCOLS, HALF_KCOLS)
        for i, ref in enumerate((k_ref, v_ref)):
            pairs.append((ref.at[:, :, cols], out.at[i]))
    run_copies(pairs, sems)


def near_place():
    return lax.div(lax.axis_index("ctx"), CORES), lax.axis_index("enc")


def split_text(n_blocks, pieces, where, q_ref, g_ref, samp_hbm, tiles_hbm, peer, q_own, g_own, bias, samp, tiles, sems):
    core = core_of()
    tokens = q_ref.shape[1]
    own_cols = at_cols(core * HALF_QCOLS, HALF_QCOLS, HALF_QCOLS)
    peer_cols = at_cols((1 - core) * HALF_QCOLS, HALF_QCOLS, HALF_QCOLS)
    copies = start_copies(
        [
            (samp_hbm, samp),
            (tiles_hbm, tiles),
            (q_ref.at[0, :, peer_cols], peer.at[:tokens]),
            (g_ref.at[0, :, peer_cols], peer.at[tokens : 2 * tokens]),
            (q_ref.at[0, :, own_cols], q_own.at[:tokens]),
            (g_ref.at[0, :, own_cols], g_own),
        ],
        sems,
    )
    for copy in copies[:2]:
        copy.wait()
    row = jnp.broadcast_to(samp[...].astype(F32), (SAMP_ROWS, tokens)).astype(BF16)
    for out, first in ((q_own, tokens), (peer, 2 * tokens)):
        out[first:, :] = jnp.zeros((SAMP_ROWS, HALF_QCOLS), BF16)
        out[first:, :tokens] = row

    sample, enc = where()
    block_rows = SLOT_ROWS // n_blocks
    slots = block_rows // pieces
    line = lax.broadcasted_iota(jnp.int32, (SLOT_ROWS, HD), 0)
    block = lax.div(line, block_rows)
    if n_blocks > 1:
        low, high = block & 1, lax.div(block, 2) & 1
        block = block - low - 2 * high + 2 * low + high
    owner = block ^ enc
    piece = lax.rem(lax.div(line, slots), pieces)
    slot = piece * (SLOT_ROWS // pieces) + owner * slots + lax.rem(line, slots)
    for i in range(SAMP):
        count = jnp.where((sample ^ i) == 0, tiles[0:1, 0:1], tiles[0:1, 1:2])
        bias[i] = jnp.where(slot < count * TILE_TOK, 0.0, BIG_NEGATIVE)
    for copy in copies[2:]:
        copy.wait()


def carry_kernel(slots, own, got, text, *outs):
    core = core_of()
    enc = lax.axis_index("enc")
    for dz, out in enumerate(outs[:-1]):
        for dx in range(2):
            group = enc ^ (2 * dz + dx)
            for i in range(2):
                first = i * CORES * slots
                out[dx, at_rows(first + core * slots, slots), :] = own[i, group]
                out[dx, at_rows(first + (1 - core) * slots, slots), :] = got[i, group]


def join_kernel(*refs):
    parts, outs = refs[:2], refs[-2:]
    rows = parts[0].shape[1]
    for dx, out in enumerate(outs):
        for dz, part in enumerate(parts):
            out[dz * rows : (dz + 1) * rows, :] = part[dx]


def block_place(b, n_outs):
    half, x, z = b // 4, b // 2 % 2, b % 2
    return {1: (0, b), 2: (x, 2 * half + z), 4: (2 * half + x, z)}[n_outs]


def add_kernel(z, own, back_x, back_y, back_xy, *outs):
    rows = outs[0].shape[1]
    for dz, out in enumerate(outs):
        near = slice((z + dz) * rows, (z + dz + 1) * rows)
        far = slice(dz * rows, (dz + 1) * rows)
        for dx, (here, back) in enumerate(((own, back_y), (back_x, back_xy))):
            out[dx] = (here[near, :].astype(F32) + back[far, :].astype(F32)).astype(out.dtype)


def nothing_kernel(*refs):
    pass


def hand_on(array, *after):
    return in_vmem(nothing_kernel, [(array.shape, array.dtype)], aliases={0: 0})(array, *after)


def far_rows_kernel(slots, *refs):
    core = core_of()
    parts, outs = refs[:2], refs[-2:]
    for dz, part in enumerate(parts):
        for dx in range(2):
            for i in range(2):
                first = i * CORES * slots
                for who, out in zip((core, 1 - core), outs):
                    out[i, 2 * dz + dx] = part[dx, at_rows(first + who * slots, slots), :]


def owner_rows_kernel(slots, *refs):
    core = core_of()
    enc = lax.axis_index("enc")
    parts, far, outs = refs[:2], refs[2:4], refs[4:]
    for dz, part in enumerate(parts):
        for dx in range(2):
            d = 2 * dz + dx
            for i in range(2):
                first = i * CORES * slots
                for who, from_far, out in zip((core, 1 - core), far, outs):
                    out[i, enc ^ d] = part[dx, at_rows(first + who * slots, slots), :]
                    out[i, enc ^ (2 * len(parts) + d)] = from_far[i, d]


def finish_kernel(mine, got, dk, dv, sems):
    core = core_of()
    pairs = []
    for half, ref in ((core, mine), (1 - core, got)):
        cols = at_cols(half * HALF_KCOLS, HALF_KCOLS, HALF_KCOLS)
        for i, out in enumerate((dk, dv)):
            pairs.append((ref.at[i], out.at[:, :, cols]))
    run_copies(pairs, sems)


def finish_text_kernel(mine, got, out, sems):
    core = core_of()
    pairs = []
    for half, ref in ((core, mine), (1 - core, got)):
        pairs.append((ref, out.at[0, :, at_cols(half * HALF_QCOLS, HALF_QCOLS, HALF_QCOLS)]))
    run_copies(pairs, sems)


def pass_kernel(role, n_blocks, n_kv, with_prev, n_through, n_grads, where, bias, q_a, g_a, got, *rest):
    kvs, rest = rest[:n_kv], rest[n_kv:]
    prev = None
    if with_prev:
        prev, rest = rest[:2], rest[2:]
    rest = rest[n_through:]
    dqs, grads = rest[:2], rest[2 : 2 + n_grads]
    sample = where()[0] ^ role
    tokens = g_a.shape[0]
    block_rows = SLOT_ROWS // n_blocks
    row_a = q_a[tokens : tokens + 1, :tokens].astype(F32)
    row_b = got[2 * tokens : 2 * tokens + 1, :tokens].astype(F32)
    wanted = sample.astype(F32)
    has = jnp.where(row_a == wanted, 1.0, jnp.where(row_b == wanted, 1.0, 0.0))
    present = jnp.max(has) > 0.5

    @pl.when(present)
    def _():
        mine = jnp.concatenate([row_a] * RATIO + [row_b] * RATIO, axis=1) == wanted
        for h in range(HALF_KV):
            first_q = h * WIDE
            first_k = h * HD

            def stacked(ref_a, first_b):
                parts = [
                    ref[first : first + tokens, first_q + r * HD : first_q + (r + 1) * HD]
                    for ref, first in ((ref_a, 0), (got, first_b))
                    for r in range(RATIO)
                ]
                return jnp.concatenate(parts, axis=0)

            def rows_of(first):
                parts = []
                for kv in kvs:
                    for at in range(first, kv.shape[0], 2 * block_rows):
                        parts.append(kv[at : at + block_rows, first_k : first_k + HD])
                return jnp.concatenate(parts, axis=0)

            q = stacked(q_a, 0)
            g = stacked(g_a, tokens)
            k = rows_of(0)
            v = rows_of(block_rows)
            s = lax.dot_general(k, q, NT, preferred_element_type=F32)
            s = s + jnp.concatenate([bias[role]] * (s.shape[1] // HD), axis=1)
            top = jnp.max(s, axis=0, keepdims=True)
            e = jnp.exp2((s - top) * (SCALE * LOG2E))
            total = jnp.sum(e, axis=0, keepdims=True)
            p = e * jnp.where(mine, 1.0 / total, 0.0)
            gp = lax.dot_general(v, g, NT, preferred_element_type=F32)
            row_dot = jnp.sum(p * gp, axis=0, keepdims=True)
            ds = (p * (gp - row_dot)).astype(BF16)
            dv = jnp.dot(p.astype(BF16), g, preferred_element_type=F32)
            dk = jnp.dot(ds, q, preferred_element_type=F32) * SCALE
            dq = lax.dot_general(ds, k, TN, preferred_element_type=F32) * SCALE
            for t, dq_ref in enumerate(dqs):
                for r in range(RATIO):
                    at = (t * RATIO + r) * tokens
                    cols = slice(first_q + r * HD, first_q + (r + 1) * HD)
                    part = dq[at : at + tokens]
                    if with_prev:
                        part = part + prev[t][:, cols].astype(F32)
                    dq_ref[:, cols] = part.astype(dq_ref.dtype)
            cols = slice(first_k, first_k + HD)
            for b in range(n_blocks):
                rows = slice(b * block_rows, (b + 1) * block_rows)
                dx, at = block_place(b, len(grads))
                out, first = grads[dx], at * 2 * block_rows
                out[first : first + block_rows, cols] = dk[rows].astype(out.dtype)
                out[first + block_rows : first + 2 * block_rows, cols] = dv[rows].astype(out.dtype)

    @pl.when(jnp.logical_not(present))
    def _():
        for out in grads:
            out[...] = jnp.zeros_like(out)
        for t, dq_ref in enumerate(dqs):
            dq_ref[...] = prev[t][...] if with_prev else jnp.zeros_like(dq_ref)


def sample_pass(where, role, n_blocks, bias, text, kvs, prev, grads, through=()):
    tokens = text[1].shape[0]
    dq = ((tokens, HALF_QCOLS), BF16)
    args = [bias, *text, *kvs, *(prev or ())]
    dq_a, dq_b, *outs = in_vmem(
        functools.partial(
            pass_kernel, role, n_blocks, len(kvs), prev is not None, len(through), len(grads), where
        ),
        [dq, dq, *grads] + [(a.shape, a.dtype) for a in through],
        flops=10 * tokens * WIDE * SLOT_ROWS * CORES * HALF_KV,
        moved=16 * 2**20,
        aliases={len(args) + i: 2 + len(grads) + i for i in range(len(through))},
    )(*args, *through)
    return (dq_a, dq_b), outs


def shards(n_ctx, n_enc, queries, d_out, text_sample, tiles, img_k, img_v):
    n_y = n_ctx // CORES
    slots = img_k.shape[1]
    tokens = queries.shape[1]
    swap_core = [(i, i ^ 1) for i in range(n_ctx)]
    near = n_y == SAMP and slots % 16 == 0 and n_enc == 8
    text_outs = [
        ((2 * tokens + SAMP_ROWS, HALF_QCOLS), BF16, IN_VMEM),
        ((tokens + SAMP_ROWS, HALF_QCOLS), BF16, IN_VMEM),
        ((tokens, HALF_QCOLS), BF16, IN_VMEM),
        ((SAMP, SLOT_ROWS, HD), F32, IN_VMEM),
    ]

    def split_the_text(n_blocks, pieces, where):
        return local_call(
            functools.partial(split_text, n_blocks, pieces, where),
            [IN_HBM] * 4,
            text_outs,
            [
                pltpu.VMEM(text_sample.shape, jnp.int32),
                pltpu.VMEM(tiles.shape, jnp.int32),
                pltpu.SemaphoreType.DMA((6,)),
            ],
            moved=4 * 2**20,
        )(*in_hbm(queries, d_out, text_sample, tiles))

    if near:
        swap_y = [(i, (i + CORES) % n_ctx) for i in range(n_ctx)]
        n_z = n_enc // 2
        block_rows = 2 * CORES * slots
        pair = (2, block_rows, HALF_KCOLS)
        quarter = (2 * block_rows, HALF_KCOLS)
        whole = (SLOT_ROWS, HALF_KCOLS)
        kv_halves = (2, n_enc, slots, HALF_KCOLS)
        swap_x = [(i, i ^ 1) for i in range(n_enc)]
        swap_xy = [
            (i * n_enc + e, (i + CORES) % n_ctx * n_enc + (e ^ 1))
            for i in range(n_ctx)
            for e in range(n_enc)
        ]

        def along_z(part, dz):
            return lax.ppermute(part, "enc", [(i, i ^ (2 * dz)) for i in range(n_enc)]) if dz else part

        def along_x(part):
            return lax.ppermute(part, "enc", swap_x)

        def along_y(part):
            return lax.ppermute(part, "ctx", swap_y)

        def along_xy(part):
            return lax.ppermute(part, ("ctx", "enc"), swap_xy)

        mine, for_peer = local_call(
            split_kernel,
            [IN_HBM] * 2,
            [(kv_halves, BF16, IN_VMEM)] * 2,
            [pltpu.SemaphoreType.DMA((4,))],
        )(*in_hbm(img_k, img_v))
        text_peer, q_own, g_own, bias = split_the_text(n_enc, CORES, near_place)
        *carry, text_peer = in_vmem(
            functools.partial(carry_kernel, slots),
            [(pair, BF16)] * n_z + [(text_peer.shape, BF16)],
            aliases={2: n_z},
        )(mine, lax.ppermute(for_peer, "ctx", swap_core), text_peer)
        text = (q_own, g_own, lax.ppermute(text_peer, "ctx", swap_core))

        came = [along_z(part, dz) for dz, part in enumerate(carry)]
        own, far = [], []
        for z in (0, 2):
            here, beside = in_vmem(join_kernel, [(quarter, BF16)] * 2)(
                *came[z : z + 2], text[2], *far
            )
            own += [here, along_x(beside)]
            far += [along_y(here), along_xy(beside)]
        own_dq, (own_here, own_beside) = sample_pass(
            near_place, 0, n_enc, bias, text, own, None, [(whole, F32), (whole, BF16)]
        )
        (own_beside,) = hand_on(own_beside, far[2])
        back_x = along_x(own_beside)
        dq, far_grads = sample_pass(
            near_place, 1, n_enc, bias, text, far, own_dq, [(quarter, BF16)] * 4
        )
        dq_got = lax.ppermute(dq[1], "ctx", swap_core)
        returned = [None] * n_z
        for z in (2, 0):
            here, beside = far_grads[z : z + 2]
            totals = in_vmem(functools.partial(add_kernel, z), [(pair, BF16)] * 2)(
                own_here, back_x, along_y(here), along_xy(beside)
            )
            for dz, total in enumerate(totals, z):
                returned[dz] = along_z(total, dz)
    else:
        both = ("ctx", "enc")
        same_y = [
            [yy * CORES * n_enc + i for i in range(CORES * n_enc)] for yy in range(n_y)
        ]
        same_column = [
            [(yy * CORES + c) * n_enc + e for yy in range(n_y)]
            for c in range(CORES)
            for e in range(n_enc)
        ]
        core = core_of()

        def exchange(parts):
            return lax.all_to_all(
                parts, both, split_axis=0, concat_axis=0, axis_index_groups=same_y, tiled=True
            )

        def to_groups(owned):
            parts = owned.reshape(n_enc, slots, CORES, HALF_KCOLS).transpose(2, 0, 1, 3)
            got = exchange(parts.reshape(CORES * n_enc, slots, HALF_KCOLS))
            got = got.reshape(CORES * n_enc * slots, HALF_KCOLS)
            return lax.all_gather(got, both, axis=0, axis_index_groups=same_column, tiled=True)

        def to_owners(grads):
            grads = lax.psum_scatter(
                grads, both, scatter_dimension=0, axis_index_groups=same_column, tiled=True
            )
            got = exchange(grads.reshape(CORES * n_enc, slots, HALF_KCOLS))
            got = got.reshape(CORES, n_enc, slots, HALF_KCOLS).transpose(1, 2, 0, 3)
            return got.reshape(n_enc, slots, CORES * HALF_KCOLS)

        def no_place():
            return jnp.int32(0), jnp.int32(0)

        all_k = to_groups(img_k)
        all_v = to_groups(img_v)
        text_peer, q_own, g_own, bias = split_the_text(1, 1, no_place)
        text = (q_own, g_own, lax.ppermute(text_peer, "ctx", swap_core))
        kvs = [
            jnp.concatenate([part[s * SLOT_ROWS : (s + 1) * SLOT_ROWS] for part in (all_k, all_v)], axis=0)
            for s in range(SAMP)
        ]
        dq, grads = None, []
        for sample, kv in enumerate(kvs):
            dq, grad = sample_pass(no_place, sample, 1, bias, text, [kv], dq, [(kv.shape, BF16)])
            grads += grad
        d_img_k = to_owners(jnp.concatenate([g[:SLOT_ROWS] for g in grads], axis=0))
        d_img_v = to_owners(jnp.concatenate([g[SLOT_ROWS:] for g in grads], axis=0))
        dq_got = lax.ppermute(dq[1], "ctx", swap_core)

    (d_queries,) = local_call(
        finish_text_kernel,
        [IN_VMEM] * 2,
        [(queries.shape, BF16, IN_HBM)],
        [pltpu.SemaphoreType.DMA((2,))],
    )(dq[0], dq_got)
    if near:
        far_rows = in_vmem(
            functools.partial(far_rows_kernel, slots),
            [((2, n_enc // 2, slots, HALF_KCOLS), BF16)] * 2,
        )(*returned[2:])
        mine, for_peer = in_vmem(
            functools.partial(owner_rows_kernel, slots), [(kv_halves, BF16)] * 2
        )(*returned[:2], *far_rows)
        d_img_k, d_img_v = local_call(
            finish_kernel,
            [IN_VMEM] * 2,
            [(img_k.shape, BF16, IN_HBM)] * 2,
            [pltpu.SemaphoreType.DMA((4,))],
        )(mine, lax.ppermute(for_peer, "ctx", swap_core))
    return (d_queries, d_img_k, d_img_v)


def solution(mesh):
    in_specs = (
        P("enc", "ctx", None),
        P("enc", "ctx", None),
        P("enc", "ctx"),
        P("enc", None),
        P(None, ("ctx", "enc"), None),
        P(None, ("ctx", "enc"), None),
    )
    out_specs = (
        P("enc", "ctx", None),
        P(None, ("ctx", "enc"), None),
        P(None, ("ctx", "enc"), None),
    )
    body = functools.partial(shards, mesh.shape["ctx"], mesh.shape["enc"])
    return jax.shard_map(body, mesh=mesh, in_specs=in_specs, out_specs=out_specs, check_vma=False)
```

```python
import functools

import jax
import jax.numpy as jnp
from jax import lax
from jax.experimental import pallas as pl
from jax.experimental.pallas import tpu as pltpu
from jax.sharding import PartitionSpec as P

H = 32
KVH = 8
HD = 128
SAMP = 2
MAX_TILES = 4
TILE_TOK = 64
RATIO = H // KVH
CORES = 2
SLOT_ROWS = MAX_TILES * TILE_TOK
HALF_KV = KVH // CORES
HALF_KCOLS = HALF_KV * HD
HALF_QCOLS = HALF_KCOLS * RATIO
WIDE = RATIO * HD
SAMP_ROWS = 16
TILE = 256
DQ_PARTS = 2
SCALE = HD ** (-0.5)
LOG2E = 1.4426950408889634
BIG_NEGATIVE = -1e30
NT = (((1,), (1,)), ((), ()))
TN = (((0,), (0,)), ((), ()))
BF16 = jnp.bfloat16
F32 = jnp.float32

IN_VMEM = pl.BlockSpec(memory_space=pltpu.VMEM)
IN_HBM = pl.BlockSpec(memory_space=pltpu.HBM)


def local_call(body, ins, outs, scratch=(), flops=0, moved=2**19, aliases={}):
    return pl.pallas_call(
        body,
        in_specs=ins,
        out_specs=[spec for _, _, spec in outs],
        out_shape=[jax.ShapeDtypeStruct(s, d) for s, d, _ in outs],
        scratch_shapes=list(scratch),
        compiler_params=pltpu.CompilerParams(vmem_limit_bytes=8 * 2**20),
        input_output_aliases=aliases,
        cost_estimate=pl.CostEstimate(
            flops=flops, bytes_accessed=moved, transcendentals=flops // 1280
        ),
    )


def in_vmem(body, outs, **more):
    def call(*args):
        spec = [(shape, dtype, IN_VMEM) for shape, dtype in outs]
        return local_call(body, [IN_VMEM] * len(args), spec, **more)(*args)

    return call


def core_of():
    return lax.rem(lax.axis_index("ctx"), CORES)


def at_rows(first, count):
    return pl.ds(pl.multiple_of(first, count), count)


def at_cols(first, width, step):
    return pl.ds(pl.multiple_of(first, step), width)


def start_copies(pairs, sems):
    copies = [pltpu.make_async_copy(src, dst, sems.at[i]) for i, (src, dst) in enumerate(pairs)]
    for copy in copies:
        copy.start()
    return copies


def run_copies(pairs, sems):
    for copy in start_copies(pairs, sems):
        copy.wait()


def in_hbm(*arrays):
    return [pltpu.with_memory_space_constraint(a, pltpu.HBM) for a in arrays]


def split_kernel(k_ref, v_ref, mine, peer, sems):
    core = core_of()
    pairs = []
    for half, out in ((1 - core, peer), (core, mine)):
        cols = at_cols(half * HALF_KCOLS, HALF_KCOLS, HALF_KCOLS)
        for i, ref in enumerate((k_ref, v_ref)):
            pairs.append((ref.at[:, :, cols], out.at[i]))
    run_copies(pairs, sems)


def near_place():
    return lax.div(lax.axis_index("ctx"), CORES), lax.axis_index("enc")


def split_text(n_blocks, pieces, where, q_ref, g_ref, samp_hbm, tiles_hbm, peer, q_own, g_own, bias, samp, tiles, sems):
    core = core_of()
    tokens = q_ref.shape[1]
    own_cols = at_cols(core * HALF_QCOLS, HALF_QCOLS, HALF_QCOLS)
    peer_cols = at_cols((1 - core) * HALF_QCOLS, HALF_QCOLS, HALF_QCOLS)
    copies = start_copies(
        [
            (samp_hbm, samp),
            (tiles_hbm, tiles),
            (q_ref.at[0, :, peer_cols], peer.at[:tokens]),
            (g_ref.at[0, :, peer_cols], peer.at[tokens : 2 * tokens]),
            (q_ref.at[0, :, own_cols], q_own.at[:tokens]),
            (g_ref.at[0, :, own_cols], g_own),
        ],
        sems,
    )
    for copy in copies[:2]:
        copy.wait()
    row = jnp.broadcast_to(samp[...].astype(F32), (SAMP_ROWS, tokens)).astype(BF16)
    for out, first in ((q_own, tokens), (peer, 2 * tokens)):
        out[first:, :] = jnp.zeros((SAMP_ROWS, HALF_QCOLS), BF16)
        out[first:, :tokens] = row

    sample, enc = where()
    block_rows = SLOT_ROWS // n_blocks
    slots = block_rows // pieces
    line = lax.broadcasted_iota(jnp.int32, (SLOT_ROWS, HD), 0)
    block = lax.div(line, block_rows)
    if n_blocks > 1:
        low, high = block & 1, lax.div(block, 2) & 1
        block = block - low - 2 * high + 2 * low + high
    owner = block ^ enc
    piece = lax.rem(lax.div(line, slots), pieces)
    slot = piece * (SLOT_ROWS // pieces) + owner * slots + lax.rem(line, slots)
    for i in range(SAMP):
        count = jnp.where((sample ^ i) == 0, tiles[0:1, 0:1], tiles[0:1, 1:2])
        bias[i] = jnp.where(slot < count * TILE_TOK, 0.0, BIG_NEGATIVE)
    for copy in copies[2:]:
        copy.wait()


def carry_kernel(slots, own, got, text, *outs):
    core = core_of()
    enc = lax.axis_index("enc")
    for dz, out in enumerate(outs[:-1]):
        for dx in range(2):
            group = enc ^ (2 * dz + dx)
            for i in range(2):
                first = i * CORES * slots
                out[dx, at_rows(first + core * slots, slots), :] = own[i, group]
                out[dx, at_rows(first + (1 - core) * slots, slots), :] = got[i, group]


def join_kernel(*refs):
    parts, outs = refs[:2], refs[-2:]
    rows = parts[0].shape[1]
    for dx, out in enumerate(outs):
        for dz, part in enumerate(parts):
            out[dz * rows : (dz + 1) * rows, :] = part[dx]


def block_place(b, n_outs):
    half, x, z = b // 4, b // 2 % 2, b % 2
    return {1: (0, b), 2: (x, 2 * half + z), 4: (2 * half + x, z)}[n_outs]


def add_kernel(z, own, back_x, back_y, back_xy, *outs):
    rows = outs[0].shape[1]
    for dz, out in enumerate(outs):
        near = slice((z + dz) * rows, (z + dz + 1) * rows)
        far = slice(dz * rows, (dz + 1) * rows)
        for dx, (here, back) in enumerate(((own, back_y), (back_x, back_xy))):
            out[dx] = (here[near, :].astype(F32) + back[far, :].astype(F32)).astype(out.dtype)


def nothing_kernel(*refs):
    pass


def hand_on(array, *after):
    return in_vmem(nothing_kernel, [(array.shape, array.dtype)], aliases={0: 0})(array, *after)


def far_rows_kernel(slots, *refs):
    core = core_of()
    parts, outs = refs[:2], refs[-2:]
    for dz, part in enumerate(parts):
        for dx in range(2):
            for i in range(2):
                first = i * CORES * slots
                for who, out in zip((core, 1 - core), outs):
                    out[i, 2 * dz + dx] = part[dx, at_rows(first + who * slots, slots), :]


def owner_rows_kernel(slots, *refs):
    core = core_of()
    enc = lax.axis_index("enc")
    parts, far, outs = refs[:2], refs[2:4], refs[4:]
    for dz, part in enumerate(parts):
        for dx in range(2):
            d = 2 * dz + dx
            for i in range(2):
                first = i * CORES * slots
                for who, from_far, out in zip((core, 1 - core), far, outs):
                    out[i, enc ^ d] = part[dx, at_rows(first + who * slots, slots), :]
                    out[i, enc ^ (2 * len(parts) + d)] = from_far[i, d]


def finish_kernel(mine, got, _, dk, dv, sems):
    core = core_of()
    pairs = []
    for half, ref in ((core, mine), (1 - core, got)):
        cols = at_cols(half * HALF_KCOLS, HALF_KCOLS, HALF_KCOLS)
        for i, out in enumerate((dk, dv)):
            pairs.append((ref.at[i], out.at[:, :, cols]))
    run_copies(pairs, sems)


def split_rows_kernel(whole, *refs):
    outs = refs[-DQ_PARTS:]
    rows = outs[0].shape[0]
    for i, out in enumerate(outs):
        out[...] = whole[i * rows : (i + 1) * rows, :]


def finish_text_kernel(mine, *refs):
    got, (out, token, sems) = refs[:-3], refs[-3:]
    core = core_of()
    token[...] = jnp.zeros_like(token)
    own_cols = at_cols(core * HALF_QCOLS, HALF_QCOLS, HALF_QCOLS)
    got_cols = at_cols((1 - core) * HALF_QCOLS, HALF_QCOLS, HALF_QCOLS)
    pairs = [(mine, out.at[0, :, own_cols])]
    rows = got[0].shape[0]
    for i, ref in enumerate(got):
        pairs.append((ref, out.at[0, i * rows : (i + 1) * rows, got_cols]))
    run_copies(pairs, sems)


def pass_kernel(role, n_blocks, n_kv, with_prev, n_through, n_grads, where, bias, q_a, g_a, got, *rest):
    kvs, rest = rest[:n_kv], rest[n_kv:]
    prev = None
    if with_prev:
        prev, rest = rest[:2], rest[2:]
    rest = rest[n_through:]
    dqs, grads, (ds_all, ph_all) = rest[:2], rest[2 : 2 + n_grads], rest[-2:]
    sample = where()[0] ^ role
    tokens = g_a.shape[0]
    block_rows = SLOT_ROWS // n_blocks
    row_a = q_a[tokens : tokens + 1, :tokens].astype(F32)
    row_b = got[2 * tokens : 2 * tokens + 1, :tokens].astype(F32)
    wanted = sample.astype(F32)
    has = jnp.where(row_a == wanted, 1.0, jnp.where(row_b == wanted, 1.0, 0.0))
    present = jnp.max(has) > 0.5

    @pl.when(present)
    def _():
        mine = jnp.concatenate([row_a] * RATIO + [row_b] * RATIO, axis=1) == wanted
        for h in range(HALF_KV):
            first_q = h * WIDE
            first_k = h * HD
            ds_ref, ph_ref = ds_all.at[h % 2], ph_all.at[h % 2]

            def stacked(ref_a, first_b):
                parts = [
                    ref[first : first + tokens, first_q + r * HD : first_q + (r + 1) * HD]
                    for ref, first in ((ref_a, 0), (got, first_b))
                    for r in range(RATIO)
                ]
                return jnp.concatenate(parts, axis=0)

            def rows_of(first):
                parts = []
                for kv in kvs:
                    for at in range(first, kv.shape[0], 2 * block_rows):
                        parts.append(kv[at : at + block_rows, first_k : first_k + HD])
                return jnp.concatenate(parts, axis=0)

            q = stacked(q_a, 0)
            g = stacked(g_a, tokens)
            k = rows_of(0)
            v = rows_of(block_rows)
            for first in range(0, q.shape[0], TILE):
                many = slice(first, first + TILE)
                s = lax.dot_general(k, q[many], NT, preferred_element_type=F32)
                gp = lax.dot_general(v, g[many], NT, preferred_element_type=F32)
                for at in range(0, TILE, HD):
                    one = slice(at, at + HD)
                    here = slice(first + at, first + at + HD)
                    part = s[:, one] + bias[role]
                    top = jnp.max(part, axis=0, keepdims=True)
                    e = jnp.exp2((part - top) * (SCALE * LOG2E))
                    total = jnp.sum(e, axis=0, keepdims=True)
                    p = e * jnp.where(mine[:, here], 1.0 / total, 0.0)
                    row_dot = jnp.sum(p * gp[:, one], axis=0, keepdims=True)
                    ds_ref[:, here] = (p * (gp[:, one] - row_dot)).astype(BF16)
                    ph_ref[:, here] = p.astype(BF16)
            ds = ds_ref[...]
            dv = jnp.dot(ph_ref[...], g, preferred_element_type=F32)
            dk = jnp.dot(ds, q, preferred_element_type=F32) * SCALE
            dq = lax.dot_general(ds, k, TN, preferred_element_type=F32) * SCALE
            for t, dq_ref in enumerate(dqs):
                for r in range(RATIO):
                    at = (t * RATIO + r) * tokens
                    cols = slice(first_q + r * HD, first_q + (r + 1) * HD)
                    part = dq[at : at + tokens]
                    if with_prev:
                        part = part + prev[t][:, cols].astype(F32)
                    dq_ref[:, cols] = part.astype(dq_ref.dtype)
            cols = slice(first_k, first_k + HD)
            for b in range(n_blocks):
                rows = slice(b * block_rows, (b + 1) * block_rows)
                dx, at = block_place(b, len(grads))
                out, first = grads[dx], at * 2 * block_rows
                out[first : first + block_rows, cols] = dk[rows].astype(out.dtype)
                out[first + block_rows : first + 2 * block_rows, cols] = dv[rows].astype(out.dtype)

    @pl.when(jnp.logical_not(present))
    def _():
        for out in grads:
            out[...] = jnp.zeros_like(out)
        for t, dq_ref in enumerate(dqs):
            dq_ref[...] = prev[t][...] if with_prev else jnp.zeros_like(dq_ref)


def sample_pass(where, role, n_blocks, bias, text, kvs, prev, grads, through=()):
    tokens = text[1].shape[0]
    dq = ((tokens, HALF_QCOLS), BF16)
    args = [bias, *text, *kvs, *(prev or ())]
    dq_a, dq_b, *outs = in_vmem(
        functools.partial(
            pass_kernel, role, n_blocks, len(kvs), prev is not None, len(through), len(grads), where
        ),
        [dq, dq, *grads] + [(a.shape, a.dtype) for a in through],
        scratch=[pltpu.VMEM((2, SLOT_ROWS, CORES * RATIO * tokens), BF16)] * 2,
        flops=10 * tokens * WIDE * SLOT_ROWS * CORES * HALF_KV,
        moved=16 * 2**20,
        aliases={len(args) + i: 2 + len(grads) + i for i in range(len(through))},
    )(*args, *through)
    return (dq_a, dq_b), outs


def shards(n_ctx, n_enc, queries, d_out, text_sample, tiles, img_k, img_v):
    n_y = n_ctx // CORES
    slots = img_k.shape[1]
    tokens = queries.shape[1]
    swap_core = [(i, i ^ 1) for i in range(n_ctx)]
    near = n_y == SAMP and slots % 16 == 0 and n_enc == 8
    text_outs = [
        ((2 * tokens + SAMP_ROWS, HALF_QCOLS), BF16, IN_VMEM),
        ((tokens + SAMP_ROWS, HALF_QCOLS), BF16, IN_VMEM),
        ((tokens, HALF_QCOLS), BF16, IN_VMEM),
        ((SAMP, SLOT_ROWS, HD), F32, IN_VMEM),
    ]

    def split_the_text(n_blocks, pieces, where):
        return local_call(
            functools.partial(split_text, n_blocks, pieces, where),
            [IN_HBM] * 4,
            text_outs,
            [
                pltpu.VMEM(text_sample.shape, jnp.int32),
                pltpu.VMEM(tiles.shape, jnp.int32),
                pltpu.SemaphoreType.DMA((6,)),
            ],
            moved=4 * 2**20,
        )(*in_hbm(queries, d_out, text_sample, tiles))

    if near:
        swap_y = [(i, (i + CORES) % n_ctx) for i in range(n_ctx)]
        n_z = n_enc // 2
        block_rows = 2 * CORES * slots
        pair = (2, block_rows, HALF_KCOLS)
        quarter = (2 * block_rows, HALF_KCOLS)
        whole = (SLOT_ROWS, HALF_KCOLS)
        kv_halves = (2, n_enc, slots, HALF_KCOLS)
        swap_x = [(i, i ^ 1) for i in range(n_enc)]
        swap_xy = [
            (i * n_enc + e, (i + CORES) % n_ctx * n_enc + (e ^ 1))
            for i in range(n_ctx)
            for e in range(n_enc)
        ]

        def along_z(part, dz):
            return lax.ppermute(part, "enc", [(i, i ^ (2 * dz)) for i in range(n_enc)]) if dz else part

        def along_x(part):
            return lax.ppermute(part, "enc", swap_x)

        def along_y(part):
            return lax.ppermute(part, "ctx", swap_y)

        def along_xy(part):
            return lax.ppermute(part, ("ctx", "enc"), swap_xy)

        mine, for_peer = local_call(
            split_kernel,
            [IN_HBM] * 2,
            [(kv_halves, BF16, IN_VMEM)] * 2,
            [pltpu.SemaphoreType.DMA((4,))],
        )(*in_hbm(img_k, img_v))
        text_peer, q_own, g_own, bias = split_the_text(n_enc, CORES, near_place)
        *carry, text_peer = in_vmem(
            functools.partial(carry_kernel, slots),
            [(pair, BF16)] * n_z + [(text_peer.shape, BF16)],
            aliases={2: n_z},
        )(mine, lax.ppermute(for_peer, "ctx", swap_core), text_peer)
        text = (q_own, g_own, lax.ppermute(text_peer, "ctx", swap_core))

        came = [along_z(part, dz) for dz, part in enumerate(carry)]
        own, far = [], []
        for z in (0, 2):
            here, beside = in_vmem(join_kernel, [(quarter, BF16)] * 2)(
                *came[z : z + 2], text[2], *far
            )
            own += [here, along_x(beside)]
            far += [along_y(here), along_xy(beside)]
        own_dq, (own_here, own_beside) = sample_pass(
            near_place, 0, n_enc, bias, text, own, None, [(whole, F32), (whole, BF16)]
        )
        (own_beside,) = hand_on(own_beside, far[2])
        back_x = along_x(own_beside)
        dq, far_grads = sample_pass(
            near_place, 1, n_enc, bias, text, far, own_dq, [(quarter, BF16)] * 4
        )
        returned = [None] * n_z
        for z in (2, 0):
            here, beside = far_grads[z : z + 2]
            back_y = along_y(here)
            totals = in_vmem(functools.partial(add_kernel, z), [(pair, BF16)] * 2)(
                own_here, back_x, back_y, along_xy(beside)
            )
            for dz, total in enumerate(totals, z):
                returned[dz] = along_z(total, dz)
            if z:
                sent = totals[0]
        dq_parts = in_vmem(split_rows_kernel, [((tokens // DQ_PARTS, HALF_QCOLS), BF16)] * DQ_PARTS)(
            dq[1], sent, totals[0]
        )
        dq_got = [lax.ppermute(part, "ctx", swap_core) for part in dq_parts]
    else:
        both = ("ctx", "enc")
        same_y = [
            [yy * CORES * n_enc + i for i in range(CORES * n_enc)] for yy in range(n_y)
        ]
        same_column = [
            [(yy * CORES + c) * n_enc + e for yy in range(n_y)]
            for c in range(CORES)
            for e in range(n_enc)
        ]
        core = core_of()

        def exchange(parts):
            return lax.all_to_all(
                parts, both, split_axis=0, concat_axis=0, axis_index_groups=same_y, tiled=True
            )

        def to_groups(owned):
            parts = owned.reshape(n_enc, slots, CORES, HALF_KCOLS).transpose(2, 0, 1, 3)
            got = exchange(parts.reshape(CORES * n_enc, slots, HALF_KCOLS))
            got = got.reshape(CORES * n_enc * slots, HALF_KCOLS)
            return lax.all_gather(got, both, axis=0, axis_index_groups=same_column, tiled=True)

        def to_owners(grads):
            grads = lax.psum_scatter(
                grads, both, scatter_dimension=0, axis_index_groups=same_column, tiled=True
            )
            got = exchange(grads.reshape(CORES * n_enc, slots, HALF_KCOLS))
            got = got.reshape(CORES, n_enc, slots, HALF_KCOLS).transpose(1, 2, 0, 3)
            return got.reshape(n_enc, slots, CORES * HALF_KCOLS)

        def no_place():
            return jnp.int32(0), jnp.int32(0)

        all_k = to_groups(img_k)
        all_v = to_groups(img_v)
        text_peer, q_own, g_own, bias = split_the_text(1, 1, no_place)
        text = (q_own, g_own, lax.ppermute(text_peer, "ctx", swap_core))
        kvs = [
            jnp.concatenate([part[s * SLOT_ROWS : (s + 1) * SLOT_ROWS] for part in (all_k, all_v)], axis=0)
            for s in range(SAMP)
        ]
        dq, grads = None, []
        for sample, kv in enumerate(kvs):
            dq, grad = sample_pass(no_place, sample, 1, bias, text, [kv], dq, [(kv.shape, BF16)])
            grads += grad
        d_img_k = to_owners(jnp.concatenate([g[:SLOT_ROWS] for g in grads], axis=0))
        d_img_v = to_owners(jnp.concatenate([g[SLOT_ROWS:] for g in grads], axis=0))
        dq_got = [lax.ppermute(dq[1], "ctx", swap_core)]

    d_queries, token = local_call(
        finish_text_kernel,
        [IN_VMEM] * (1 + len(dq_got)),
        [(queries.shape, BF16, IN_HBM), ((8, HD), F32, IN_VMEM)],
        [pltpu.SemaphoreType.DMA((1 + len(dq_got),))],
    )(dq[0], *dq_got)
    if near:
        far_rows = in_vmem(
            functools.partial(far_rows_kernel, slots),
            [((2, n_enc // 2, slots, HALF_KCOLS), BF16)] * 2,
        )(*returned[2:])
        mine, for_peer = in_vmem(
            functools.partial(owner_rows_kernel, slots),
            [(kv_halves, BF16)] * 2,
        )(*returned[:2], *far_rows)
        d_img_k, d_img_v = local_call(
            finish_kernel,
            [IN_VMEM] * 3,
            [(img_k.shape, BF16, IN_HBM)] * 2,
            [pltpu.SemaphoreType.DMA((4,))],
        )(mine, lax.ppermute(for_peer, "ctx", swap_core), token)
    return (d_queries, d_img_k, d_img_v)


def solution(mesh):
    in_specs = (
        P("enc", "ctx", None),
        P("enc", "ctx", None),
        P("enc", "ctx"),
        P("enc", None),
        P(None, ("ctx", "enc"), None),
        P(None, ("ctx", "enc"), None),
    )
    out_specs = (
        P("enc", "ctx", None),
        P(None, ("ctx", "enc"), None),
        P(None, ("ctx", "enc"), None),
    )
    body = functools.partial(shards, mesh.shape["ctx"], mesh.shape["enc"])
    return jax.shard_map(body, mesh=mesh, in_specs=in_specs, out_specs=out_specs, check_vma=False)
```

```python
import functools

import jax
import jax.numpy as jnp
from jax import lax
from jax.experimental import pallas as pl
from jax.experimental.pallas import tpu as pltpu
from jax.sharding import PartitionSpec as P

H = 32
KVH = 8
HD = 128
SAMP = 2
MAX_TILES = 4
TILE_TOK = 64
RATIO = H // KVH
CORES = 2
SLOT_ROWS = MAX_TILES * TILE_TOK
HALF_KV = KVH // CORES
HALF_KCOLS = HALF_KV * HD
HALF_QCOLS = HALF_KCOLS * RATIO
WIDE = RATIO * HD
SAMP_ROWS = 16
DQ_PARTS = 2
SCALE = HD ** (-0.5)
LOG2E = 1.4426950408889634
BIG_NEGATIVE = -1e30
NT = (((1,), (1,)), ((), ()))
TN = (((0,), (0,)), ((), ()))
BF16 = jnp.bfloat16
F32 = jnp.float32

IN_VMEM = pl.BlockSpec(memory_space=pltpu.VMEM)
IN_HBM = pl.BlockSpec(memory_space=pltpu.HBM)


def local_call(body, ins, outs, scratch=(), flops=0, moved=2**19, aliases={}):
    return pl.pallas_call(
        body,
        in_specs=ins,
        out_specs=[spec for _, _, spec in outs],
        out_shape=[jax.ShapeDtypeStruct(s, d) for s, d, _ in outs],
        scratch_shapes=list(scratch),
        compiler_params=pltpu.CompilerParams(vmem_limit_bytes=8 * 2**20),
        input_output_aliases=aliases,
        cost_estimate=pl.CostEstimate(
            flops=flops, bytes_accessed=moved, transcendentals=flops // 1280
        ),
    )


def in_vmem(body, outs, **more):
    def call(*args):
        spec = [(shape, dtype, IN_VMEM) for shape, dtype in outs]
        return local_call(body, [IN_VMEM] * len(args), spec, **more)(*args)

    return call


def core_of():
    return lax.rem(lax.axis_index("ctx"), CORES)


def at_rows(first, count):
    return pl.ds(pl.multiple_of(first, count), count)


def at_cols(first, width, step):
    return pl.ds(pl.multiple_of(first, step), width)


def start_copies(pairs, sems):
    copies = [pltpu.make_async_copy(src, dst, sems.at[i]) for i, (src, dst) in enumerate(pairs)]
    for copy in copies:
        copy.start()
    return copies


def run_copies(pairs, sems):
    for copy in start_copies(pairs, sems):
        copy.wait()


def in_hbm(*arrays):
    return [pltpu.with_memory_space_constraint(a, pltpu.HBM) for a in arrays]


def split_kernel(k_ref, v_ref, mine, peer, sems):
    core = core_of()
    pairs = []
    for half, out in ((1 - core, peer), (core, mine)):
        cols = at_cols(half * HALF_KCOLS, HALF_KCOLS, HALF_KCOLS)
        for i, ref in enumerate((k_ref, v_ref)):
            pairs.append((ref.at[:, :, cols], out.at[i]))
    run_copies(pairs, sems)


def near_place():
    return lax.div(lax.axis_index("ctx"), CORES), lax.axis_index("enc")


def split_text(n_blocks, pieces, where, q_ref, g_ref, samp_hbm, tiles_hbm, peer, q_own, g_own, bias, samp, tiles, sems):
    core = core_of()
    tokens = q_ref.shape[1]
    own_cols = at_cols(core * HALF_QCOLS, HALF_QCOLS, HALF_QCOLS)
    peer_cols = at_cols((1 - core) * HALF_QCOLS, HALF_QCOLS, HALF_QCOLS)
    copies = start_copies(
        [
            (samp_hbm, samp),
            (tiles_hbm, tiles),
            (q_ref.at[0, :, peer_cols], peer.at[:tokens]),
            (g_ref.at[0, :, peer_cols], peer.at[tokens : 2 * tokens]),
            (q_ref.at[0, :, own_cols], q_own.at[:tokens]),
            (g_ref.at[0, :, own_cols], g_own),
        ],
        sems,
    )
    for copy in copies[:2]:
        copy.wait()
    row = jnp.broadcast_to(samp[...].astype(F32), (SAMP_ROWS, tokens)).astype(BF16)
    for out, first in ((q_own, tokens), (peer, 2 * tokens)):
        out[first:, :] = jnp.zeros((SAMP_ROWS, HALF_QCOLS), BF16)
        out[first:, :tokens] = row

    sample, enc = where()
    block_rows = SLOT_ROWS // n_blocks
    slots = block_rows // pieces
    line = lax.broadcasted_iota(jnp.int32, (SLOT_ROWS, HD), 0)
    block = lax.div(line, block_rows)
    if n_blocks > 1:
        low, high = block & 1, lax.div(block, 2) & 1
        block = block - low - 2 * high + 2 * low + high
    owner = block ^ enc
    piece = lax.rem(lax.div(line, slots), pieces)
    slot = piece * (SLOT_ROWS // pieces) + owner * slots + lax.rem(line, slots)
    for i in range(SAMP):
        count = jnp.where((sample ^ i) == 0, tiles[0:1, 0:1], tiles[0:1, 1:2])
        bias[i] = jnp.where(slot < count * TILE_TOK, 0.0, BIG_NEGATIVE)
    for copy in copies[2:]:
        copy.wait()


def carry_kernel(slots, own, got, text, *outs):
    core = core_of()
    enc = lax.axis_index("enc")
    for dz, out in enumerate(outs[:-1]):
        for dx in range(2):
            group = enc ^ (2 * dz + dx)
            for i in range(2):
                first = i * CORES * slots
                out[dx, at_rows(first + core * slots, slots), :] = own[i, group]
                out[dx, at_rows(first + (1 - core) * slots, slots), :] = got[i, group]


def join_kernel(*refs):
    parts, outs = refs[:2], refs[-2:]
    rows = parts[0].shape[1]
    for dx, out in enumerate(outs):
        for dz, part in enumerate(parts):
            out[dz * rows : (dz + 1) * rows, :] = part[dx]


def block_place(b, n_outs):
    half, x, z = b // 4, b // 2 % 2, b % 2
    return {1: (0, b), 2: (x, 2 * half + z), 4: (2 * half + x, z)}[n_outs]


def add_kernel(z, own, back_x, back_y, back_xy, *outs):
    rows = outs[0].shape[1]
    for dz, out in enumerate(outs):
        near = slice((z + dz) * rows, (z + dz + 1) * rows)
        far = slice(dz * rows, (dz + 1) * rows)
        for dx, (here, back) in enumerate(((own, back_y), (back_x, back_xy))):
            out[dx] = (here[near, :].astype(F32) + back[far, :].astype(F32)).astype(out.dtype)


def nothing_kernel(*refs):
    pass


def hand_on(array, *after):
    return in_vmem(nothing_kernel, [(array.shape, array.dtype)], aliases={0: 0})(array, *after)


def far_rows_kernel(slots, *refs):
    core = core_of()
    parts, outs = refs[:2], refs[-2:]
    for dz, part in enumerate(parts):
        for dx in range(2):
            for i in range(2):
                first = i * CORES * slots
                for who, out in zip((core, 1 - core), outs):
                    out[i, 2 * dz + dx] = part[dx, at_rows(first + who * slots, slots), :]


def owner_rows_kernel(slots, *refs):
    core = core_of()
    enc = lax.axis_index("enc")
    parts, far, outs = refs[:2], refs[2:4], refs[4:]
    for dz, part in enumerate(parts):
        for dx in range(2):
            d = 2 * dz + dx
            for i in range(2):
                first = i * CORES * slots
                for who, from_far, out in zip((core, 1 - core), far, outs):
                    out[i, enc ^ d] = part[dx, at_rows(first + who * slots, slots), :]
                    out[i, enc ^ (2 * len(parts) + d)] = from_far[i, d]


def finish_kernel(mine, got, _, dk, dv, sems):
    core = core_of()
    pairs = []
    for half, ref in ((core, mine), (1 - core, got)):
        cols = at_cols(half * HALF_KCOLS, HALF_KCOLS, HALF_KCOLS)
        for i, out in enumerate((dk, dv)):
            pairs.append((ref.at[i], out.at[:, :, cols]))
    run_copies(pairs, sems)


def split_rows_kernel(whole, *refs):
    outs = refs[-DQ_PARTS:]
    rows = outs[0].shape[0]
    for i, out in enumerate(outs):
        out[...] = whole[i * rows : (i + 1) * rows, :]


def finish_text_kernel(mine, *refs):
    got, (out, token, sems) = refs[:-3], refs[-3:]
    core = core_of()
    token[...] = jnp.zeros_like(token)
    own_cols = at_cols(core * HALF_QCOLS, HALF_QCOLS, HALF_QCOLS)
    got_cols = at_cols((1 - core) * HALF_QCOLS, HALF_QCOLS, HALF_QCOLS)
    pairs = [(mine, out.at[0, :, own_cols])]
    rows = got[0].shape[0]
    for i, ref in enumerate(got):
        pairs.append((ref, out.at[0, i * rows : (i + 1) * rows, got_cols]))
    run_copies(pairs, sems)


def pass_kernel(role, n_blocks, n_kv, with_prev, n_through, n_grads, where, bias, q_a, g_a, got, *rest):
    kvs, rest = rest[:n_kv], rest[n_kv:]
    prev = None
    if with_prev:
        prev, rest = rest[:2], rest[2:]
    rest = rest[n_through:]
    dqs, grads = rest[:2], rest[2 : 2 + n_grads]
    sample = where()[0] ^ role
    tokens = g_a.shape[0]
    block_rows = SLOT_ROWS // n_blocks
    row_a = q_a[tokens : tokens + 1, :tokens].astype(F32)
    row_b = got[2 * tokens : 2 * tokens + 1, :tokens].astype(F32)
    wanted = sample.astype(F32)
    rows = (row_a, row_b)
    present = [jnp.max(jnp.where(row == wanted, 1.0, 0.0)) > 0.5 for row in rows]
    sources = ((q_a, 0, g_a, 0), (got, 0, got, tokens))

    def one_pass(which):
        mine = jnp.concatenate([rows[t] for t in which for _ in range(RATIO)], axis=1) == wanted

        def head(h, carry):
            def stacked(part):
                parts = []
                for t in which:
                    ref, first = sources[t][part : part + 2]
                    wide = ref[first : first + tokens, at_cols(h * WIDE, WIDE, WIDE)]
                    parts += [wide[:, r * HD : (r + 1) * HD] for r in range(RATIO)]
                return jnp.concatenate(parts, axis=0)

            def rows_of(first):
                parts = []
                for kv in kvs:
                    for at in range(first, kv.shape[0], 2 * block_rows):
                        parts.append(kv[at : at + block_rows, at_cols(h * HD, HD, HD)])
                return jnp.concatenate(parts, axis=0)

            q = stacked(0)
            g = stacked(2)
            k = rows_of(0)
            v = rows_of(block_rows)
            s = lax.dot_general(k, q, NT, preferred_element_type=F32)
            s = s + jnp.concatenate([bias[role]] * (s.shape[1] // HD), axis=1)
            top = jnp.max(s, axis=0, keepdims=True)
            e = jnp.exp2((s - top) * (SCALE * LOG2E))
            total = jnp.sum(e, axis=0, keepdims=True)
            p = e * jnp.where(mine, 1.0 / total, 0.0)
            gp = lax.dot_general(v, g, NT, preferred_element_type=F32)
            row_dot = jnp.sum(p * gp, axis=0, keepdims=True)
            ds = (p * (gp - row_dot)).astype(BF16)
            dv = jnp.dot(p.astype(BF16), g, preferred_element_type=F32)
            dk = jnp.dot(ds, q, preferred_element_type=F32) * SCALE
            dq = lax.dot_general(ds, k, TN, preferred_element_type=F32) * SCALE
            for i, t in enumerate(which):
                cols = at_cols(h * WIDE, WIDE, WIDE)
                at = i * RATIO * tokens
                part = jnp.concatenate(
                    [dq[at + r * tokens : at + (r + 1) * tokens] for r in range(RATIO)], axis=1
                )
                if with_prev:
                    part = part + prev[t][:, cols].astype(F32)
                dqs[t][:, cols] = part.astype(dqs[t].dtype)
            cols = at_cols(h * HD, HD, HD)
            for b in range(n_blocks):
                block = slice(b * block_rows, (b + 1) * block_rows)
                dx, at = block_place(b, len(grads))
                out, first = grads[dx], at * 2 * block_rows
                out[first : first + block_rows, cols] = dk[block].astype(out.dtype)
                out[first + block_rows : first + 2 * block_rows, cols] = dv[block].astype(out.dtype)
            return carry

        lax.fori_loop(0, HALF_KV, head, 0)

    for which in ((0, 1), (0,), (1,), ()):
        wants = [present[t] if t in which else jnp.logical_not(present[t]) for t in range(2)]

        @pl.when(wants[0] & wants[1])
        def _():
            if which:
                one_pass(which)
            else:
                for out in grads:
                    out[...] = jnp.zeros_like(out)
            for t in range(2):
                if t not in which:
                    dqs[t][...] = prev[t][...] if with_prev else jnp.zeros_like(dqs[t])


def sample_pass(where, role, n_blocks, bias, text, kvs, prev, grads, through=()):
    tokens = text[1].shape[0]
    dq = ((tokens, HALF_QCOLS), BF16)
    args = [bias, *text, *kvs, *(prev or ())]
    dq_a, dq_b, *outs = in_vmem(
        functools.partial(
            pass_kernel, role, n_blocks, len(kvs), prev is not None, len(through), len(grads), where
        ),
        [dq, dq, *grads] + [(a.shape, a.dtype) for a in through],
        flops=10 * tokens * WIDE * SLOT_ROWS * CORES * HALF_KV,
        moved=16 * 2**20,
        aliases={len(args) + i: 2 + len(grads) + i for i in range(len(through))},
    )(*args, *through)
    return (dq_a, dq_b), outs


def shards(n_ctx, n_enc, queries, d_out, text_sample, tiles, img_k, img_v):
    n_y = n_ctx // CORES
    slots = img_k.shape[1]
    tokens = queries.shape[1]
    swap_core = [(i, i ^ 1) for i in range(n_ctx)]
    near = n_y == SAMP and slots % 16 == 0 and n_enc == 8
    text_outs = [
        ((2 * tokens + SAMP_ROWS, HALF_QCOLS), BF16, IN_VMEM),
        ((tokens + SAMP_ROWS, HALF_QCOLS), BF16, IN_VMEM),
        ((tokens, HALF_QCOLS), BF16, IN_VMEM),
        ((SAMP, SLOT_ROWS, HD), F32, IN_VMEM),
    ]

    def split_the_text(n_blocks, pieces, where):
        return local_call(
            functools.partial(split_text, n_blocks, pieces, where),
            [IN_HBM] * 4,
            text_outs,
            [
                pltpu.VMEM(text_sample.shape, jnp.int32),
                pltpu.VMEM(tiles.shape, jnp.int32),
                pltpu.SemaphoreType.DMA((6,)),
            ],
            moved=4 * 2**20,
        )(*in_hbm(queries, d_out, text_sample, tiles))

    if near:
        swap_y = [(i, (i + CORES) % n_ctx) for i in range(n_ctx)]
        n_z = n_enc // 2
        block_rows = 2 * CORES * slots
        pair = (2, block_rows, HALF_KCOLS)
        quarter = (2 * block_rows, HALF_KCOLS)
        whole = (SLOT_ROWS, HALF_KCOLS)
        kv_halves = (2, n_enc, slots, HALF_KCOLS)
        swap_x = [(i, i ^ 1) for i in range(n_enc)]
        swap_xy = [
            (i * n_enc + e, (i + CORES) % n_ctx * n_enc + (e ^ 1))
            for i in range(n_ctx)
            for e in range(n_enc)
        ]

        def along_z(part, dz):
            return lax.ppermute(part, "enc", [(i, i ^ (2 * dz)) for i in range(n_enc)]) if dz else part

        def along_x(part):
            return lax.ppermute(part, "enc", swap_x)

        def along_y(part):
            return lax.ppermute(part, "ctx", swap_y)

        def along_xy(part):
            return lax.ppermute(part, ("ctx", "enc"), swap_xy)

        mine, for_peer = local_call(
            split_kernel,
            [IN_HBM] * 2,
            [(kv_halves, BF16, IN_VMEM)] * 2,
            [pltpu.SemaphoreType.DMA((4,))],
        )(*in_hbm(img_k, img_v))
        text_peer, q_own, g_own, bias = split_the_text(n_enc, CORES, near_place)
        *carry, text_peer = in_vmem(
            functools.partial(carry_kernel, slots),
            [(pair, BF16)] * n_z + [(text_peer.shape, BF16)],
            aliases={2: n_z},
        )(mine, lax.ppermute(for_peer, "ctx", swap_core), text_peer)
        text = (q_own, g_own, lax.ppermute(text_peer, "ctx", swap_core))

        came = [along_z(part, dz) for dz, part in enumerate(carry)]
        own, far = [], []
        for z in (0, 2):
            here, beside = in_vmem(join_kernel, [(quarter, BF16)] * 2)(
                *came[z : z + 2], text[2], *far
            )
            own += [here, along_x(beside)]
            far += [along_y(here), along_xy(beside)]
        own_dq, (own_here, own_beside) = sample_pass(
            near_place, 0, n_enc, bias, text, own, None, [(whole, F32), (whole, BF16)]
        )
        (own_beside,) = hand_on(own_beside, far[2])
        back_x = along_x(own_beside)
        dq, far_grads = sample_pass(
            near_place, 1, n_enc, bias, text, far, own_dq, [(quarter, BF16)] * 4
        )
        returned = [None] * n_z
        for z in (2, 0):
            here, beside = far_grads[z : z + 2]
            back_y = along_y(here)
            totals = in_vmem(functools.partial(add_kernel, z), [(pair, BF16)] * 2)(
                own_here, back_x, back_y, along_xy(beside)
            )
            for dz, total in enumerate(totals, z):
                returned[dz] = along_z(total, dz)
            if z:
                sent = totals[0]
        dq_parts = in_vmem(split_rows_kernel, [((tokens // DQ_PARTS, HALF_QCOLS), BF16)] * DQ_PARTS)(
            dq[1], sent, totals[0]
        )
        dq_got = [lax.ppermute(part, "ctx", swap_core) for part in dq_parts]
    else:
        both = ("ctx", "enc")
        same_y = [
            [yy * CORES * n_enc + i for i in range(CORES * n_enc)] for yy in range(n_y)
        ]
        same_column = [
            [(yy * CORES + c) * n_enc + e for yy in range(n_y)]
            for c in range(CORES)
            for e in range(n_enc)
        ]
        core = core_of()

        def exchange(parts):
            return lax.all_to_all(
                parts, both, split_axis=0, concat_axis=0, axis_index_groups=same_y, tiled=True
            )

        def to_groups(owned):
            parts = owned.reshape(n_enc, slots, CORES, HALF_KCOLS).transpose(2, 0, 1, 3)
            got = exchange(parts.reshape(CORES * n_enc, slots, HALF_KCOLS))
            got = got.reshape(CORES * n_enc * slots, HALF_KCOLS)
            return lax.all_gather(got, both, axis=0, axis_index_groups=same_column, tiled=True)

        def to_owners(grads):
            grads = lax.psum_scatter(
                grads, both, scatter_dimension=0, axis_index_groups=same_column, tiled=True
            )
            got = exchange(grads.reshape(CORES * n_enc, slots, HALF_KCOLS))
            got = got.reshape(CORES, n_enc, slots, HALF_KCOLS).transpose(1, 2, 0, 3)
            return got.reshape(n_enc, slots, CORES * HALF_KCOLS)

        def no_place():
            return jnp.int32(0), jnp.int32(0)

        all_k = to_groups(img_k)
        all_v = to_groups(img_v)
        text_peer, q_own, g_own, bias = split_the_text(1, 1, no_place)
        text = (q_own, g_own, lax.ppermute(text_peer, "ctx", swap_core))
        kvs = [
            jnp.concatenate([part[s * SLOT_ROWS : (s + 1) * SLOT_ROWS] for part in (all_k, all_v)], axis=0)
            for s in range(SAMP)
        ]
        dq, grads = None, []
        for sample, kv in enumerate(kvs):
            dq, grad = sample_pass(no_place, sample, 1, bias, text, [kv], dq, [(kv.shape, BF16)])
            grads += grad
        d_img_k = to_owners(jnp.concatenate([g[:SLOT_ROWS] for g in grads], axis=0))
        d_img_v = to_owners(jnp.concatenate([g[SLOT_ROWS:] for g in grads], axis=0))
        dq_got = [lax.ppermute(dq[1], "ctx", swap_core)]

    d_queries, token = local_call(
        finish_text_kernel,
        [IN_VMEM] * (1 + len(dq_got)),
        [(queries.shape, BF16, IN_HBM), ((8, HD), F32, IN_VMEM)],
        [pltpu.SemaphoreType.DMA((1 + len(dq_got),))],
    )(dq[0], *dq_got)
    if near:
        far_rows = in_vmem(
            functools.partial(far_rows_kernel, slots),
            [((2, n_enc // 2, slots, HALF_KCOLS), BF16)] * 2,
        )(*returned[2:])
        mine, for_peer = in_vmem(
            functools.partial(owner_rows_kernel, slots),
            [(kv_halves, BF16)] * 2,
        )(*returned[:2], *far_rows)
        d_img_k, d_img_v = local_call(
            finish_kernel,
            [IN_VMEM] * 3,
            [(img_k.shape, BF16, IN_HBM)] * 2,
            [pltpu.SemaphoreType.DMA((4,))],
        )(mine, lax.ppermute(for_peer, "ctx", swap_core), token)
    return (d_queries, d_img_k, d_img_v)


def solution(mesh):
    in_specs = (
        P("enc", "ctx", None),
        P("enc", "ctx", None),
        P("enc", "ctx"),
        P("enc", None),
        P(None, ("ctx", "enc"), None),
        P(None, ("ctx", "enc"), None),
    )
    out_specs = (
        P("enc", "ctx", None),
        P(None, ("ctx", "enc"), None),
        P(None, ("ctx", "enc"), None),
    )
    body = functools.partial(shards, mesh.shape["ctx"], mesh.shape["enc"])
    return jax.shard_map(body, mesh=mesh, in_specs=in_specs, out_specs=out_specs, check_vma=False)
```

```python
import functools

import jax
import jax.numpy as jnp
from jax import lax
from jax.experimental import pallas as pl
from jax.experimental.pallas import tpu as pltpu
from jax.sharding import PartitionSpec as P

H = 32
KVH = 8
HD = 128
SAMP = 2
MAX_TILES = 4
TILE_TOK = 64
RATIO = H // KVH
CORES = 2
SLOT_ROWS = MAX_TILES * TILE_TOK
HALF_KV = KVH // CORES
HALF_KCOLS = HALF_KV * HD
HALF_QCOLS = HALF_KCOLS * RATIO
WIDE = RATIO * HD
SAMP_ROWS = 16
DQ_PARTS = 2
SCALE = HD ** (-0.5)
LOG2E = 1.4426950408889634
BIG_NEGATIVE = -1e30
NT = (((1,), (1,)), ((), ()))
TN = (((0,), (0,)), ((), ()))
BF16 = jnp.bfloat16
F32 = jnp.float32

IN_VMEM = pl.BlockSpec(memory_space=pltpu.VMEM)
IN_HBM = pl.BlockSpec(memory_space=pltpu.HBM)


def local_call(body, ins, outs, scratch=(), flops=0, moved=2**19, aliases={}):
    return pl.pallas_call(
        body,
        in_specs=ins,
        out_specs=[spec for _, _, spec in outs],
        out_shape=[jax.ShapeDtypeStruct(s, d) for s, d, _ in outs],
        scratch_shapes=list(scratch),
        compiler_params=pltpu.CompilerParams(vmem_limit_bytes=8 * 2**20),
        input_output_aliases=aliases,
        cost_estimate=pl.CostEstimate(
            flops=flops, bytes_accessed=moved, transcendentals=flops // 1280
        ),
    )


def in_vmem(body, outs, **more):
    def call(*args):
        spec = [(shape, dtype, IN_VMEM) for shape, dtype in outs]
        return local_call(body, [IN_VMEM] * len(args), spec, **more)(*args)

    return call


def core_of():
    return lax.rem(lax.axis_index("ctx"), CORES)


def at_rows(first, count):
    return pl.ds(pl.multiple_of(first, count), count)


def at_cols(first, width, step):
    return pl.ds(pl.multiple_of(first, step), width)


def start_copies(pairs, sems):
    copies = [pltpu.make_async_copy(src, dst, sems.at[i]) for i, (src, dst) in enumerate(pairs)]
    for copy in copies:
        copy.start()
    return copies


def run_copies(pairs, sems):
    for copy in start_copies(pairs, sems):
        copy.wait()


def in_hbm(*arrays):
    return [pltpu.with_memory_space_constraint(a, pltpu.HBM) for a in arrays]


def split_kernel(k_ref, v_ref, mine, peer, sems):
    core = core_of()
    pairs = []
    for half, out in ((1 - core, peer), (core, mine)):
        cols = at_cols(half * HALF_KCOLS, HALF_KCOLS, HALF_KCOLS)
        for i, ref in enumerate((k_ref, v_ref)):
            pairs.append((ref.at[:, :, cols], out.at[i]))
    run_copies(pairs, sems)


def near_place():
    return lax.div(lax.axis_index("ctx"), CORES), lax.axis_index("enc")


def split_text(n_blocks, pieces, where, q_ref, g_ref, samp_hbm, tiles_hbm, peer, q_own, g_own, bias, samp, tiles, sems):
    core = core_of()
    tokens = q_ref.shape[1]
    own_cols = at_cols(core * HALF_QCOLS, HALF_QCOLS, HALF_QCOLS)
    peer_cols = at_cols((1 - core) * HALF_QCOLS, HALF_QCOLS, HALF_QCOLS)
    copies = start_copies(
        [
            (samp_hbm, samp),
            (tiles_hbm, tiles),
            (q_ref.at[0, :, peer_cols], peer.at[:tokens]),
            (g_ref.at[0, :, peer_cols], peer.at[tokens : 2 * tokens]),
            (q_ref.at[0, :, own_cols], q_own.at[:tokens]),
            (g_ref.at[0, :, own_cols], g_own),
        ],
        sems,
    )
    for copy in copies[:2]:
        copy.wait()
    row = jnp.broadcast_to(samp[...].astype(F32), (SAMP_ROWS, tokens)).astype(BF16)
    for out, first in ((q_own, tokens), (peer, 2 * tokens)):
        out[first:, :] = jnp.zeros((SAMP_ROWS, HALF_QCOLS), BF16)
        out[first:, :tokens] = row

    sample, enc = where()
    block_rows = SLOT_ROWS // n_blocks
    slots = block_rows // pieces
    line = lax.broadcasted_iota(jnp.int32, (SLOT_ROWS, HD), 0)
    block = lax.div(line, block_rows)
    if n_blocks > 1:
        low, high = block & 1, lax.div(block, 2) & 1
        block = block - low - 2 * high + 2 * low + high
    owner = block ^ enc
    piece = lax.rem(lax.div(line, slots), pieces)
    slot = piece * (SLOT_ROWS // pieces) + owner * slots + lax.rem(line, slots)
    for i in range(SAMP):
        count = jnp.where((sample ^ i) == 0, tiles[0:1, 0:1], tiles[0:1, 1:2])
        bias[i] = jnp.where(slot < count * TILE_TOK, 0.0, BIG_NEGATIVE)
    for copy in copies[2:]:
        copy.wait()


def carry_kernel(slots, own, got, text, *outs):
    core = core_of()
    enc = lax.axis_index("enc")
    for dz, out in enumerate(outs[:-1]):
        for dx in range(2):
            group = enc ^ (2 * dz + dx)
            for i in range(2):
                first = i * CORES * slots
                out[dx, at_rows(first + core * slots, slots), :] = own[i, group]
                out[dx, at_rows(first + (1 - core) * slots, slots), :] = got[i, group]


def join_kernel(*refs):
    parts, outs = refs[:2], refs[-2:]
    rows = parts[0].shape[1]
    for dx, out in enumerate(outs):
        for dz, part in enumerate(parts):
            out[dz * rows : (dz + 1) * rows, :] = part[dx]


def block_place(b, n_outs):
    half, x, z = b // 4, b // 2 % 2, b % 2
    return {1: (0, b), 2: (x, 2 * half + z), 4: (2 * half + x, z)}[n_outs]


def add_kernel(z, own, back_x, back_y, back_xy, *outs):
    rows = outs[0].shape[1]
    for dz, out in enumerate(outs):
        near = slice((z + dz) * rows, (z + dz + 1) * rows)
        far = slice(dz * rows, (dz + 1) * rows)
        for dx, (here, back) in enumerate(((own, back_y), (back_x, back_xy))):
            out[dx] = (here[near, :].astype(F32) + back[far, :].astype(F32)).astype(out.dtype)


def nothing_kernel(*refs):
    pass


def hand_on(array, *after):
    return in_vmem(nothing_kernel, [(array.shape, array.dtype)], aliases={0: 0})(array, *after)


def far_rows_kernel(slots, *refs):
    core = core_of()
    parts, outs = refs[:2], refs[-2:]
    for dz, part in enumerate(parts):
        for dx in range(2):
            for i in range(2):
                first = i * CORES * slots
                for who, out in zip((core, 1 - core), outs):
                    out[i, 2 * dz + dx] = part[dx, at_rows(first + who * slots, slots), :]


def owner_rows_kernel(slots, *refs):
    core = core_of()
    enc = lax.axis_index("enc")
    parts, far, outs = refs[:2], refs[2:4], refs[4:]
    for dz, part in enumerate(parts):
        for dx in range(2):
            d = 2 * dz + dx
            for i in range(2):
                first = i * CORES * slots
                for who, from_far, out in zip((core, 1 - core), far, outs):
                    out[i, enc ^ d] = part[dx, at_rows(first + who * slots, slots), :]
                    out[i, enc ^ (2 * len(parts) + d)] = from_far[i, d]


def finish_kernel(mine, got, _, dk, dv, sems):
    core = core_of()
    pairs = []
    for half, ref in ((core, mine), (1 - core, got)):
        cols = at_cols(half * HALF_KCOLS, HALF_KCOLS, HALF_KCOLS)
        for i, out in enumerate((dk, dv)):
            pairs.append((ref.at[i], out.at[:, :, cols]))
    run_copies(pairs, sems)


def split_rows_kernel(whole, *refs):
    outs = refs[-DQ_PARTS:]
    rows = outs[0].shape[0]
    for i, out in enumerate(outs):
        out[...] = whole[i * rows : (i + 1) * rows, :]


def finish_text_kernel(mine, *refs):
    got, (out, token, sems) = refs[:-3], refs[-3:]
    core = core_of()
    token[...] = jnp.zeros_like(token)
    own_cols = at_cols(core * HALF_QCOLS, HALF_QCOLS, HALF_QCOLS)
    got_cols = at_cols((1 - core) * HALF_QCOLS, HALF_QCOLS, HALF_QCOLS)
    pairs = [(mine, out.at[0, :, own_cols])]
    rows = got[0].shape[0]
    for i, ref in enumerate(got):
        pairs.append((ref, out.at[0, i * rows : (i + 1) * rows, got_cols]))
    run_copies(pairs, sems)


def pass_kernel(role, n_blocks, n_kv, with_prev, n_through, n_grads, where, bias, q_a, g_a, got, *rest):
    kvs, rest = rest[:n_kv], rest[n_kv:]
    prev = None
    if with_prev:
        prev, rest = rest[:2], rest[2:]
    rest = rest[n_through:]
    dqs, grads = rest[:2], rest[2 : 2 + n_grads]
    sample = where()[0] ^ role
    tokens = g_a.shape[0]
    block_rows = SLOT_ROWS // n_blocks
    row_a = q_a[tokens : tokens + 1, :tokens].astype(F32)
    row_b = got[2 * tokens : 2 * tokens + 1, :tokens].astype(F32)
    wanted = sample.astype(F32)
    rows = (row_a, row_b)
    present = [jnp.max(jnp.where(row == wanted, 1.0, 0.0)) > 0.5 for row in rows]
    sources = ((q_a, 0, g_a, 0), (got, 0, got, tokens))

    def one_pass(which):
        mine = jnp.concatenate([rows[t] for t in which for _ in range(RATIO)], axis=1) == wanted

        def products(h):
            def stacked(part):
                parts = []
                for t in which:
                    ref, first = sources[t][part : part + 2]
                    for r in range(RATIO):
                        at = h * WIDE + r * HD
                        parts.append(ref[first : first + tokens, at : at + HD])
                return jnp.concatenate(parts, axis=0)

            def rows_of(first):
                parts = []
                for kv in kvs:
                    for at in range(first, kv.shape[0], 2 * block_rows):
                        parts.append(kv[at : at + block_rows, h * HD : (h + 1) * HD])
                return jnp.concatenate(parts, axis=0)

            q, g, k, v = stacked(0), stacked(2), rows_of(0), rows_of(block_rows)
            s = lax.dot_general(k, q, NT, preferred_element_type=F32)
            gp = lax.dot_general(v, g, NT, preferred_element_type=F32)
            return q, g, k, s, gp

        masks = jnp.concatenate([bias[role]] * (len(which) * RATIO), axis=1)
        ahead = products(0)
        for h in range(HALF_KV):
            q, g, k, s, gp = ahead
            if h + 1 < HALF_KV:
                ahead = products(h + 1)
            s = s + masks
            top = jnp.max(s, axis=0, keepdims=True)
            e = jnp.exp2((s - top) * (SCALE * LOG2E))
            total = jnp.sum(e, axis=0, keepdims=True)
            p = e * jnp.where(mine, 1.0 / total, 0.0)
            row_dot = jnp.sum(p * gp, axis=0, keepdims=True)
            ds = (p * (gp - row_dot)).astype(BF16)
            dv = jnp.dot(p.astype(BF16), g, preferred_element_type=F32)
            dk = jnp.dot(ds, q, preferred_element_type=F32) * SCALE
            dq = lax.dot_general(ds, k, TN, preferred_element_type=F32) * SCALE
            for i, t in enumerate(which):
                for r in range(RATIO):
                    at = (i * RATIO + r) * tokens
                    cols = slice(h * WIDE + r * HD, h * WIDE + (r + 1) * HD)
                    part = dq[at : at + tokens]
                    if with_prev:
                        part = part + prev[t][:, cols].astype(F32)
                    dqs[t][:, cols] = part.astype(dqs[t].dtype)
            cols = slice(h * HD, (h + 1) * HD)
            for b in range(n_blocks):
                block = slice(b * block_rows, (b + 1) * block_rows)
                dx, at = block_place(b, len(grads))
                out, first = grads[dx], at * 2 * block_rows
                out[first : first + block_rows, cols] = dk[block].astype(out.dtype)
                out[first + block_rows : first + 2 * block_rows, cols] = dv[block].astype(out.dtype)

    for which in ((0, 1), (0,), (1,), ()):
        wants = [present[t] if t in which else jnp.logical_not(present[t]) for t in range(2)]

        @pl.when(wants[0] & wants[1])
        def _():
            if which:
                one_pass(which)
            else:
                for out in grads:
                    out[...] = jnp.zeros_like(out)
            for t in range(2):
                if t not in which:
                    dqs[t][...] = prev[t][...] if with_prev else jnp.zeros_like(dqs[t])


def sample_pass(where, role, n_blocks, bias, text, kvs, prev, grads, through=()):
    tokens = text[1].shape[0]
    dq = ((tokens, HALF_QCOLS), BF16)
    args = [bias, *text, *kvs, *(prev or ())]
    dq_a, dq_b, *outs = in_vmem(
        functools.partial(
            pass_kernel, role, n_blocks, len(kvs), prev is not None, len(through), len(grads), where
        ),
        [dq, dq, *grads] + [(a.shape, a.dtype) for a in through],
        flops=10 * tokens * WIDE * SLOT_ROWS * CORES * HALF_KV,
        moved=16 * 2**20,
        aliases={len(args) + i: 2 + len(grads) + i for i in range(len(through))},
    )(*args, *through)
    return (dq_a, dq_b), outs


def shards(n_ctx, n_enc, queries, d_out, text_sample, tiles, img_k, img_v):
    n_y = n_ctx // CORES
    slots = img_k.shape[1]
    tokens = queries.shape[1]
    swap_core = [(i, i ^ 1) for i in range(n_ctx)]
    near = n_y == SAMP and slots % 16 == 0 and n_enc == 8
    text_outs = [
        ((2 * tokens + SAMP_ROWS, HALF_QCOLS), BF16, IN_VMEM),
        ((tokens + SAMP_ROWS, HALF_QCOLS), BF16, IN_VMEM),
        ((tokens, HALF_QCOLS), BF16, IN_VMEM),
        ((SAMP, SLOT_ROWS, HD), F32, IN_VMEM),
    ]

    def split_the_text(n_blocks, pieces, where):
        return local_call(
            functools.partial(split_text, n_blocks, pieces, where),
            [IN_HBM] * 4,
            text_outs,
            [
                pltpu.VMEM(text_sample.shape, jnp.int32),
                pltpu.VMEM(tiles.shape, jnp.int32),
                pltpu.SemaphoreType.DMA((6,)),
            ],
            moved=4 * 2**20,
        )(*in_hbm(queries, d_out, text_sample, tiles))

    if near:
        swap_y = [(i, (i + CORES) % n_ctx) for i in range(n_ctx)]
        n_z = n_enc // 2
        block_rows = 2 * CORES * slots
        pair = (2, block_rows, HALF_KCOLS)
        quarter = (2 * block_rows, HALF_KCOLS)
        whole = (SLOT_ROWS, HALF_KCOLS)
        kv_halves = (2, n_enc, slots, HALF_KCOLS)
        swap_x = [(i, i ^ 1) for i in range(n_enc)]
        swap_xy = [
            (i * n_enc + e, (i + CORES) % n_ctx * n_enc + (e ^ 1))
            for i in range(n_ctx)
            for e in range(n_enc)
        ]

        def along_z(part, dz):
            return lax.ppermute(part, "enc", [(i, i ^ (2 * dz)) for i in range(n_enc)]) if dz else part

        def along_x(part):
            return lax.ppermute(part, "enc", swap_x)

        def along_y(part):
            return lax.ppermute(part, "ctx", swap_y)

        def along_xy(part):
            return lax.ppermute(part, ("ctx", "enc"), swap_xy)

        mine, for_peer = local_call(
            split_kernel,
            [IN_HBM] * 2,
            [(kv_halves, BF16, IN_VMEM)] * 2,
            [pltpu.SemaphoreType.DMA((4,))],
        )(*in_hbm(img_k, img_v))
        text_peer, q_own, g_own, bias = split_the_text(n_enc, CORES, near_place)
        *carry, text_peer = in_vmem(
            functools.partial(carry_kernel, slots),
            [(pair, BF16)] * n_z + [(text_peer.shape, BF16)],
            aliases={2: n_z},
        )(mine, lax.ppermute(for_peer, "ctx", swap_core), text_peer)
        text = (q_own, g_own, lax.ppermute(text_peer, "ctx", swap_core))

        came = [along_z(part, dz) for dz, part in enumerate(carry)]
        own, far = [], []
        for z in (0, 2):
            here, beside = in_vmem(join_kernel, [(quarter, BF16)] * 2)(
                *came[z : z + 2], text[2], *far
            )
            own += [here, along_x(beside)]
            far += [along_y(here), along_xy(beside)]
        own_dq, (own_here, own_beside) = sample_pass(
            near_place, 0, n_enc, bias, text, own, None, [(whole, F32), (whole, BF16)]
        )
        (own_beside,) = hand_on(own_beside, far[2])
        back_x = along_x(own_beside)
        dq, far_grads = sample_pass(
            near_place, 1, n_enc, bias, text, far, own_dq, [(quarter, BF16)] * 4
        )
        returned = [None] * n_z
        for z in (2, 0):
            here, beside = far_grads[z : z + 2]
            back_y = along_y(here)
            totals = in_vmem(functools.partial(add_kernel, z), [(pair, BF16)] * 2)(
                own_here, back_x, back_y, along_xy(beside)
            )
            for dz, total in enumerate(totals, z):
                returned[dz] = along_z(total, dz)
            if z:
                sent = totals[0]
        dq_parts = in_vmem(split_rows_kernel, [((tokens // DQ_PARTS, HALF_QCOLS), BF16)] * DQ_PARTS)(
            dq[1], sent, totals[0]
        )
        dq_got = [lax.ppermute(part, "ctx", swap_core) for part in dq_parts]
    else:
        both = ("ctx", "enc")
        same_y = [
            [yy * CORES * n_enc + i for i in range(CORES * n_enc)] for yy in range(n_y)
        ]
        same_column = [
            [(yy * CORES + c) * n_enc + e for yy in range(n_y)]
            for c in range(CORES)
            for e in range(n_enc)
        ]
        core = core_of()

        def exchange(parts):
            return lax.all_to_all(
                parts, both, split_axis=0, concat_axis=0, axis_index_groups=same_y, tiled=True
            )

        def to_groups(owned):
            parts = owned.reshape(n_enc, slots, CORES, HALF_KCOLS).transpose(2, 0, 1, 3)
            got = exchange(parts.reshape(CORES * n_enc, slots, HALF_KCOLS))
            got = got.reshape(CORES * n_enc * slots, HALF_KCOLS)
            return lax.all_gather(got, both, axis=0, axis_index_groups=same_column, tiled=True)

        def to_owners(grads):
            grads = lax.psum_scatter(
                grads, both, scatter_dimension=0, axis_index_groups=same_column, tiled=True
            )
            got = exchange(grads.reshape(CORES * n_enc, slots, HALF_KCOLS))
            got = got.reshape(CORES, n_enc, slots, HALF_KCOLS).transpose(1, 2, 0, 3)
            return got.reshape(n_enc, slots, CORES * HALF_KCOLS)

        def no_place():
            return jnp.int32(0), jnp.int32(0)

        all_k = to_groups(img_k)
        all_v = to_groups(img_v)
        text_peer, q_own, g_own, bias = split_the_text(1, 1, no_place)
        text = (q_own, g_own, lax.ppermute(text_peer, "ctx", swap_core))
        kvs = [
            jnp.concatenate([part[s * SLOT_ROWS : (s + 1) * SLOT_ROWS] for part in (all_k, all_v)], axis=0)
            for s in range(SAMP)
        ]
        dq, grads = None, []
        for sample, kv in enumerate(kvs):
            dq, grad = sample_pass(no_place, sample, 1, bias, text, [kv], dq, [(kv.shape, BF16)])
            grads += grad
        d_img_k = to_owners(jnp.concatenate([g[:SLOT_ROWS] for g in grads], axis=0))
        d_img_v = to_owners(jnp.concatenate([g[SLOT_ROWS:] for g in grads], axis=0))
        dq_got = [lax.ppermute(dq[1], "ctx", swap_core)]

    d_queries, token = local_call(
        finish_text_kernel,
        [IN_VMEM] * (1 + len(dq_got)),
        [(queries.shape, BF16, IN_HBM), ((8, HD), F32, IN_VMEM)],
        [pltpu.SemaphoreType.DMA((1 + len(dq_got),))],
    )(dq[0], *dq_got)
    if near:
        far_rows = in_vmem(
            functools.partial(far_rows_kernel, slots),
            [((2, n_enc // 2, slots, HALF_KCOLS), BF16)] * 2,
        )(*returned[2:])
        mine, for_peer = in_vmem(
            functools.partial(owner_rows_kernel, slots),
            [(kv_halves, BF16)] * 2,
        )(*returned[:2], *far_rows)
        d_img_k, d_img_v = local_call(
            finish_kernel,
            [IN_VMEM] * 3,
            [(img_k.shape, BF16, IN_HBM)] * 2,
            [pltpu.SemaphoreType.DMA((4,))],
        )(mine, lax.ppermute(for_peer, "ctx", swap_core), token)
    return (d_queries, d_img_k, d_img_v)


def solution(mesh):
    in_specs = (
        P("enc", "ctx", None),
        P("enc", "ctx", None),
        P("enc", "ctx"),
        P("enc", None),
        P(None, ("ctx", "enc"), None),
        P(None, ("ctx", "enc"), None),
    )
    out_specs = (
        P("enc", "ctx", None),
        P(None, ("ctx", "enc"), None),
        P(None, ("ctx", "enc"), None),
    )
    body = functools.partial(shards, mesh.shape["ctx"], mesh.shape["enc"])
    return jax.shard_map(body, mesh=mesh, in_specs=in_specs, out_specs=out_specs, check_vma=False)
```

```python
import functools

import jax
import jax.numpy as jnp
from jax import lax
from jax.experimental import pallas as pl
from jax.experimental.pallas import tpu as pltpu
from jax.sharding import PartitionSpec as P

H = 32
KVH = 8
HD = 128
SAMP = 2
MAX_TILES = 4
TILE_TOK = 64
RATIO = H // KVH
CORES = 2
SLOT_ROWS = MAX_TILES * TILE_TOK
HALF_KV = KVH // CORES
HALF_KCOLS = HALF_KV * HD
HALF_QCOLS = HALF_KCOLS * RATIO
WIDE = RATIO * HD
SAMP_ROWS = 16
DQ_PARTS = 2
SCALE = HD ** (-0.5)
LOG2E = 1.4426950408889634
BIG_NEGATIVE = -1e30
NT = (((1,), (1,)), ((), ()))
TN = (((0,), (0,)), ((), ()))
BF16 = jnp.bfloat16
F32 = jnp.float32

IN_VMEM = pl.BlockSpec(memory_space=pltpu.VMEM)
IN_HBM = pl.BlockSpec(memory_space=pltpu.HBM)


def local_call(body, ins, outs, scratch=(), flops=0, moved=2**19, aliases={}):
    return pl.pallas_call(
        body,
        in_specs=ins,
        out_specs=[spec for _, _, spec in outs],
        out_shape=[jax.ShapeDtypeStruct(s, d) for s, d, _ in outs],
        scratch_shapes=list(scratch),
        compiler_params=pltpu.CompilerParams(vmem_limit_bytes=8 * 2**20),
        input_output_aliases=aliases,
        cost_estimate=pl.CostEstimate(
            flops=flops, bytes_accessed=moved, transcendentals=flops // 1280
        ),
    )


def in_vmem(body, outs, **more):
    def call(*args):
        spec = [(shape, dtype, IN_VMEM) for shape, dtype in outs]
        return local_call(body, [IN_VMEM] * len(args), spec, **more)(*args)

    return call


def core_of():
    return lax.rem(lax.axis_index("ctx"), CORES)


def at_rows(first, count):
    return pl.ds(pl.multiple_of(first, count), count)


def at_cols(first, width, step):
    return pl.ds(pl.multiple_of(first, step), width)


def start_copies(pairs, sems):
    copies = [pltpu.make_async_copy(src, dst, sems.at[i]) for i, (src, dst) in enumerate(pairs)]
    for copy in copies:
        copy.start()
    return copies


def run_copies(pairs, sems):
    for copy in start_copies(pairs, sems):
        copy.wait()


def in_hbm(*arrays):
    return [pltpu.with_memory_space_constraint(a, pltpu.HBM) for a in arrays]


def split_kernel(k_ref, v_ref, mine, peer, sems):
    core = core_of()
    pairs = []
    for half, out in ((1 - core, peer), (core, mine)):
        cols = at_cols(half * HALF_KCOLS, HALF_KCOLS, HALF_KCOLS)
        for i, ref in enumerate((k_ref, v_ref)):
            pairs.append((ref.at[:, :, cols], out.at[i]))
    run_copies(pairs, sems)


def near_place():
    return lax.div(lax.axis_index("ctx"), CORES), lax.axis_index("enc")


def split_text(n_blocks, pieces, where, q_ref, g_ref, samp_hbm, tiles_hbm, peer, q_own, g_own, bias, samp, tiles, sems):
    core = core_of()
    tokens = q_ref.shape[1]
    own_cols = at_cols(core * HALF_QCOLS, HALF_QCOLS, HALF_QCOLS)
    peer_cols = at_cols((1 - core) * HALF_QCOLS, HALF_QCOLS, HALF_QCOLS)
    copies = start_copies(
        [
            (samp_hbm, samp),
            (tiles_hbm, tiles),
            (q_ref.at[0, :, peer_cols], peer.at[:tokens]),
            (g_ref.at[0, :, peer_cols], peer.at[tokens : 2 * tokens]),
            (q_ref.at[0, :, own_cols], q_own.at[:tokens]),
            (g_ref.at[0, :, own_cols], g_own),
        ],
        sems,
    )
    for copy in copies[:2]:
        copy.wait()
    row = jnp.broadcast_to(samp[...].astype(F32), (SAMP_ROWS, tokens)).astype(BF16)
    for out, first in ((q_own, tokens), (peer, 2 * tokens)):
        out[first:, :] = jnp.zeros((SAMP_ROWS, HALF_QCOLS), BF16)
        out[first:, :tokens] = row

    sample, enc = where()
    block_rows = SLOT_ROWS // n_blocks
    slots = block_rows // pieces
    line = lax.broadcasted_iota(jnp.int32, (SLOT_ROWS, HD), 0)
    block = lax.div(line, block_rows)
    if n_blocks > 1:
        low, high = block & 1, lax.div(block, 2) & 1
        block = block - low - 2 * high + 2 * low + high
    owner = block ^ enc
    piece = lax.rem(lax.div(line, slots), pieces)
    slot = piece * (SLOT_ROWS // pieces) + owner * slots + lax.rem(line, slots)
    for i in range(SAMP):
        count = jnp.where((sample ^ i) == 0, tiles[0:1, 0:1], tiles[0:1, 1:2])
        bias[i] = jnp.where(slot < count * TILE_TOK, 0.0, BIG_NEGATIVE)
    for copy in copies[2:]:
        copy.wait()


def carry_kernel(slots, own, got, text, *outs):
    core = core_of()
    enc = lax.axis_index("enc")
    for dz, out in enumerate(outs[:-1]):
        for dx in range(2):
            group = enc ^ (2 * dz + dx)
            for i in range(2):
                first = i * CORES * slots
                out[dx, at_rows(first + core * slots, slots), :] = own[i, group]
                out[dx, at_rows(first + (1 - core) * slots, slots), :] = got[i, group]


def join_kernel(*refs):
    parts, outs = refs[:2], refs[-2:]
    rows = parts[0].shape[1]
    for dx, out in enumerate(outs):
        for dz, part in enumerate(parts):
            out[dz * rows : (dz + 1) * rows, :] = part[dx]


def block_place(b, n_outs):
    half, x, z = b // 4, b // 2 % 2, b % 2
    return {1: (0, b), 2: (x, 2 * half + z), 4: (2 * half + x, z)}[n_outs]


def add_kernel(z, own, back_x, back_y, back_xy, *outs):
    rows = outs[0].shape[1]
    for dz, out in enumerate(outs):
        near = slice((z + dz) * rows, (z + dz + 1) * rows)
        far = slice(dz * rows, (dz + 1) * rows)
        for dx, (here, back) in enumerate(((own, back_y), (back_x, back_xy))):
            out[dx] = (here[near, :].astype(F32) + back[far, :].astype(F32)).astype(out.dtype)


def nothing_kernel(*refs):
    pass


def hand_on(array, *after):
    return in_vmem(nothing_kernel, [(array.shape, array.dtype)], aliases={0: 0})(array, *after)


def far_rows_kernel(slots, *refs):
    core = core_of()
    parts, outs = refs[:2], refs[-2:]
    for dz, part in enumerate(parts):
        for dx in range(2):
            for i in range(2):
                first = i * CORES * slots
                for who, out in zip((core, 1 - core), outs):
                    out[i, 2 * dz + dx] = part[dx, at_rows(first + who * slots, slots), :]


def owner_rows_kernel(slots, *refs):
    core = core_of()
    enc = lax.axis_index("enc")
    parts, far, outs = refs[:2], refs[2:4], refs[4:]
    for dz, part in enumerate(parts):
        for dx in range(2):
            d = 2 * dz + dx
            for i in range(2):
                first = i * CORES * slots
                for who, from_far, out in zip((core, 1 - core), far, outs):
                    out[i, enc ^ d] = part[dx, at_rows(first + who * slots, slots), :]
                    out[i, enc ^ (2 * len(parts) + d)] = from_far[i, d]


def finish_kernel(mine, got, _, dk, dv, sems):
    core = core_of()
    pairs = []
    for half, ref in ((core, mine), (1 - core, got)):
        cols = at_cols(half * HALF_KCOLS, HALF_KCOLS, HALF_KCOLS)
        for i, out in enumerate((dk, dv)):
            pairs.append((ref.at[i], out.at[:, :, cols]))
    run_copies(pairs, sems)


def split_rows_kernel(whole, *refs):
    outs = refs[-DQ_PARTS:]
    rows = outs[0].shape[0]
    for i, out in enumerate(outs):
        out[...] = whole[i * rows : (i + 1) * rows, :]


def finish_text_kernel(mine, *refs):
    got, (out, token, sems) = refs[:-3], refs[-3:]
    core = core_of()
    token[...] = jnp.zeros_like(token)
    own_cols = at_cols(core * HALF_QCOLS, HALF_QCOLS, HALF_QCOLS)
    got_cols = at_cols((1 - core) * HALF_QCOLS, HALF_QCOLS, HALF_QCOLS)
    pairs = [(mine, out.at[0, :, own_cols])]
    rows = got[0].shape[0]
    for i, ref in enumerate(got):
        pairs.append((ref, out.at[0, i * rows : (i + 1) * rows, got_cols]))
    run_copies(pairs, sems)


def blocks_with(sample, q_own, got):
    tokens = q_own.shape[0] - SAMP_ROWS
    rows = (q_own[tokens : tokens + 1, :tokens], got[2 * tokens : 2 * tokens + 1, :tokens])
    rows = [row.astype(F32) for row in rows]
    wanted = sample.astype(F32)
    return rows, [jnp.max(jnp.where(row == wanted, 1.0, 0.0)) > 0.5 for row in rows]


def key_rows(kvs, block_rows, first, h):
    parts = []
    for kv in kvs:
        for at in range(first, kv.shape[0], 2 * block_rows):
            parts.append(kv[at : at + block_rows, h * HD : (h + 1) * HD])
    return jnp.concatenate(parts, axis=0)


def choose(flags, branch):
    for which in ((0, 1), (0,), (1,), ()):
        wants = [flags[t] if t in which else jnp.logical_not(flags[t]) for t in range(2)]

        @pl.when(wants[0] & wants[1])
        def _():
            branch(which)


def pass_kernel(role, n_blocks, n_kv, n_grads, where, bias, q_a, g_a, got, *rest):
    kvs, (ds_out, *grads) = rest[:n_kv], rest[-1 - n_grads :]
    sample = where()[0] ^ role
    tokens = g_a.shape[0]
    block_rows = SLOT_ROWS // n_blocks
    rows, present = blocks_with(sample, q_a, got)
    sources = ((q_a, 0, g_a, 0), (got, 0, got, tokens))

    def one_pass(which):
        if not which:
            for out in grads:
                out[...] = jnp.zeros_like(out)
            return
        mine = jnp.concatenate([rows[t] for t in which for _ in range(RATIO)], axis=1)
        mine = mine == sample.astype(F32)
        masks = jnp.concatenate([bias[role]] * (len(which) * RATIO), axis=1)

        def products(h):
            def stacked(part):
                parts = []
                for t in which:
                    ref, first = sources[t][part : part + 2]
                    for r in range(RATIO):
                        at = h * WIDE + r * HD
                        parts.append(ref[first : first + tokens, at : at + HD])
                return jnp.concatenate(parts, axis=0)

            q, g = stacked(0), stacked(2)
            k, v = (key_rows(kvs, block_rows, first, h) for first in (0, block_rows))
            s = lax.dot_general(k, q, NT, preferred_element_type=F32)
            gp = lax.dot_general(v, g, NT, preferred_element_type=F32)
            return q, g, s, gp

        early = len(which) == 1
        ahead = products(0)
        for h in range(HALF_KV):
            q, g, s, gp = ahead
            if early and h + 1 < HALF_KV:
                ahead = products(h + 1)
            s = s + masks
            top = jnp.max(s, axis=0, keepdims=True)
            e = jnp.exp2((s - top) * (SCALE * LOG2E))
            total = jnp.sum(e, axis=0, keepdims=True)
            p = e * jnp.where(mine, 1.0 / total, 0.0)
            row_dot = jnp.sum(p * gp, axis=0, keepdims=True)
            ds = (p * (gp - row_dot)).astype(BF16)
            dv = jnp.dot(p.astype(BF16), g, preferred_element_type=F32)
            dk = jnp.dot(ds, q, preferred_element_type=F32) * SCALE
            wide = RATIO * tokens
            for i, t in enumerate(which):
                ds_out[h, :, t * wide : (t + 1) * wide] = ds[:, i * wide : (i + 1) * wide]
            cols = slice(h * HD, (h + 1) * HD)
            for b in range(n_blocks):
                block = slice(b * block_rows, (b + 1) * block_rows)
                dx, at = block_place(b, len(grads))
                out, first = grads[dx], at * 2 * block_rows
                out[first : first + block_rows, cols] = dk[block].astype(out.dtype)
                out[first + block_rows : first + 2 * block_rows, cols] = dv[block].astype(out.dtype)
            if not early and h + 1 < HALF_KV:
                ahead = products(h + 1)

    choose(present, one_pass)


def dq_kernel(n_blocks, n_kv, where, q_a, got, *rest):
    keys = rest[:n_kv], rest[n_kv : 2 * n_kv]
    ds, dqs = rest[2 * n_kv : 2 * n_kv + 2], rest[-2:]
    tokens = dqs[0].shape[0]
    block_rows = SLOT_ROWS // n_blocks
    first = where()[0]
    present = [blocks_with(first ^ role, q_a, got)[1] for role in range(SAMP)]
    wide = RATIO * tokens
    for t, dq_ref in enumerate(dqs):

        def one_block(roles):
            for h in range(HALF_KV):
                total = 0.0
                for role in roles:
                    k = key_rows(keys[role], block_rows, 0, h)
                    part = ds[role][h, :, t * wide : (t + 1) * wide]
                    total += lax.dot_general(part, k, TN, preferred_element_type=F32)
                if roles:
                    for r in range(RATIO):
                        at = h * WIDE + r * HD
                        rows = total[r * tokens : (r + 1) * tokens] * SCALE
                        dq_ref[:, at : at + HD] = rows.astype(dq_ref.dtype)

        choose([present[role][t] for role in range(SAMP)], one_block)


def sample_pass(where, role, n_blocks, bias, text, kvs, grads, after=()):
    tokens = text[1].shape[0]
    ds = ((HALF_KV, SLOT_ROWS, CORES * RATIO * tokens), BF16)
    return in_vmem(
        functools.partial(pass_kernel, role, n_blocks, len(kvs), len(grads), where),
        [ds, *grads],
        flops=8 * tokens * WIDE * SLOT_ROWS * CORES * HALF_KV,
        moved=16 * 2**20,
    )(bias, *text, *kvs, *after)


def text_grads(where, n_blocks, text, keys, ds):
    tokens = text[1].shape[0]
    return in_vmem(
        functools.partial(dq_kernel, n_blocks, len(keys[0]), where),
        [((tokens, HALF_QCOLS), BF16)] * 2,
        flops=4 * tokens * WIDE * SLOT_ROWS * CORES * HALF_KV,
        moved=8 * 2**20,
    )(text[0], text[2], *keys[0], *keys[1], *ds)


def shards(n_ctx, n_enc, queries, d_out, text_sample, tiles, img_k, img_v):
    n_y = n_ctx // CORES
    slots = img_k.shape[1]
    tokens = queries.shape[1]
    swap_core = [(i, i ^ 1) for i in range(n_ctx)]
    near = n_y == SAMP and slots % 16 == 0 and n_enc == 8
    text_outs = [
        ((2 * tokens + SAMP_ROWS, HALF_QCOLS), BF16, IN_VMEM),
        ((tokens + SAMP_ROWS, HALF_QCOLS), BF16, IN_VMEM),
        ((tokens, HALF_QCOLS), BF16, IN_VMEM),
        ((SAMP, SLOT_ROWS, HD), F32, IN_VMEM),
    ]

    def split_the_text(n_blocks, pieces, where):
        return local_call(
            functools.partial(split_text, n_blocks, pieces, where),
            [IN_HBM] * 4,
            text_outs,
            [
                pltpu.VMEM(text_sample.shape, jnp.int32),
                pltpu.VMEM(tiles.shape, jnp.int32),
                pltpu.SemaphoreType.DMA((6,)),
            ],
            moved=4 * 2**20,
        )(*in_hbm(queries, d_out, text_sample, tiles))

    if near:
        swap_y = [(i, (i + CORES) % n_ctx) for i in range(n_ctx)]
        n_z = n_enc // 2
        block_rows = 2 * CORES * slots
        pair = (2, block_rows, HALF_KCOLS)
        quarter = (2 * block_rows, HALF_KCOLS)
        whole = (SLOT_ROWS, HALF_KCOLS)
        kv_halves = (2, n_enc, slots, HALF_KCOLS)
        swap_x = [(i, i ^ 1) for i in range(n_enc)]
        swap_xy = [
            (i * n_enc + e, (i + CORES) % n_ctx * n_enc + (e ^ 1))
            for i in range(n_ctx)
            for e in range(n_enc)
        ]

        def along_z(part, dz):
            return lax.ppermute(part, "enc", [(i, i ^ (2 * dz)) for i in range(n_enc)]) if dz else part

        def along_x(part):
            return lax.ppermute(part, "enc", swap_x)

        def along_y(part):
            return lax.ppermute(part, "ctx", swap_y)

        def along_xy(part):
            return lax.ppermute(part, ("ctx", "enc"), swap_xy)

        mine, for_peer = local_call(
            split_kernel,
            [IN_HBM] * 2,
            [(kv_halves, BF16, IN_VMEM)] * 2,
            [pltpu.SemaphoreType.DMA((4,))],
        )(*in_hbm(img_k, img_v))
        text_peer, q_own, g_own, bias = split_the_text(n_enc, CORES, near_place)
        *carry, text_peer = in_vmem(
            functools.partial(carry_kernel, slots),
            [(pair, BF16)] * n_z + [(text_peer.shape, BF16)],
            aliases={2: n_z},
        )(mine, lax.ppermute(for_peer, "ctx", swap_core), text_peer)
        text = (q_own, g_own, lax.ppermute(text_peer, "ctx", swap_core))

        came = [along_z(part, dz) for dz, part in enumerate(carry)]
        own, far = [], []
        for z in (0, 2):
            here, beside = in_vmem(join_kernel, [(quarter, BF16)] * 2)(
                *came[z : z + 2], text[2], *far
            )
            own += [here, along_x(beside)]
            far += [along_y(here), along_xy(beside)]
        own_ds, own_here, own_beside = sample_pass(
            near_place, 0, n_enc, bias, text, own, [(whole, F32), (whole, BF16)]
        )
        (own_beside,) = hand_on(own_beside, far[2])
        back_x = along_x(own_beside)
        far_ds, *far_grads = sample_pass(
            near_place, 1, n_enc, bias, text, far, [(quarter, BF16)] * 4, (own_beside,)
        )
        dq = text_grads(near_place, n_enc, text, (own, far), (own_ds, far_ds))
        returned = [None] * n_z
        for z in (2, 0):
            here, beside = far_grads[z : z + 2]
            back_y = along_y(here)
            totals = in_vmem(functools.partial(add_kernel, z), [(pair, BF16)] * 2)(
                own_here, back_x, back_y, along_xy(beside)
            )
            for dz, total in enumerate(totals, z):
                returned[dz] = along_z(total, dz)
            if z:
                sent = totals[0]
        dq_parts = in_vmem(split_rows_kernel, [((tokens // DQ_PARTS, HALF_QCOLS), BF16)] * DQ_PARTS)(
            dq[1], sent, totals[0]
        )
        dq_got = [lax.ppermute(part, "ctx", swap_core) for part in dq_parts]
    else:
        both = ("ctx", "enc")
        same_y = [
            [yy * CORES * n_enc + i for i in range(CORES * n_enc)] for yy in range(n_y)
        ]
        same_column = [
            [(yy * CORES + c) * n_enc + e for yy in range(n_y)]
            for c in range(CORES)
            for e in range(n_enc)
        ]
        core = core_of()

        def exchange(parts):
            return lax.all_to_all(
                parts, both, split_axis=0, concat_axis=0, axis_index_groups=same_y, tiled=True
            )

        def to_groups(owned):
            parts = owned.reshape(n_enc, slots, CORES, HALF_KCOLS).transpose(2, 0, 1, 3)
            got = exchange(parts.reshape(CORES * n_enc, slots, HALF_KCOLS))
            got = got.reshape(CORES * n_enc * slots, HALF_KCOLS)
            return lax.all_gather(got, both, axis=0, axis_index_groups=same_column, tiled=True)

        def to_owners(grads):
            grads = lax.psum_scatter(
                grads, both, scatter_dimension=0, axis_index_groups=same_column, tiled=True
            )
            got = exchange(grads.reshape(CORES * n_enc, slots, HALF_KCOLS))
            got = got.reshape(CORES, n_enc, slots, HALF_KCOLS).transpose(1, 2, 0, 3)
            return got.reshape(n_enc, slots, CORES * HALF_KCOLS)

        def no_place():
            return jnp.int32(0), jnp.int32(0)

        all_k = to_groups(img_k)
        all_v = to_groups(img_v)
        text_peer, q_own, g_own, bias = split_the_text(1, 1, no_place)
        text = (q_own, g_own, lax.ppermute(text_peer, "ctx", swap_core))
        kvs = [
            jnp.concatenate([part[s * SLOT_ROWS : (s + 1) * SLOT_ROWS] for part in (all_k, all_v)], axis=0)
            for s in range(SAMP)
        ]
        all_ds, grads = [], []
        for sample, kv in enumerate(kvs):
            ds, grad = sample_pass(no_place, sample, 1, bias, text, [kv], [(kv.shape, BF16)])
            all_ds.append(ds)
            grads.append(grad)
        dq = text_grads(no_place, 1, text, [[kv] for kv in kvs], all_ds)
        d_img_k = to_owners(jnp.concatenate([g[:SLOT_ROWS] for g in grads], axis=0))
        d_img_v = to_owners(jnp.concatenate([g[SLOT_ROWS:] for g in grads], axis=0))
        dq_got = [lax.ppermute(dq[1], "ctx", swap_core)]

    d_queries, token = local_call(
        finish_text_kernel,
        [IN_VMEM] * (1 + len(dq_got)),
        [(queries.shape, BF16, IN_HBM), ((8, HD), F32, IN_VMEM)],
        [pltpu.SemaphoreType.DMA((1 + len(dq_got),))],
    )(dq[0], *dq_got)
    if near:
        far_rows = in_vmem(
            functools.partial(far_rows_kernel, slots),
            [((2, n_enc // 2, slots, HALF_KCOLS), BF16)] * 2,
        )(*returned[2:])
        mine, for_peer = in_vmem(
            functools.partial(owner_rows_kernel, slots),
            [(kv_halves, BF16)] * 2,
        )(*returned[:2], *far_rows)
        d_img_k, d_img_v = local_call(
            finish_kernel,
            [IN_VMEM] * 3,
            [(img_k.shape, BF16, IN_HBM)] * 2,
            [pltpu.SemaphoreType.DMA((4,))],
        )(mine, lax.ppermute(for_peer, "ctx", swap_core), token)
    return (d_queries, d_img_k, d_img_v)


def solution(mesh):
    in_specs = (
        P("enc", "ctx", None),
        P("enc", "ctx", None),
        P("enc", "ctx"),
        P("enc", None),
        P(None, ("ctx", "enc"), None),
        P(None, ("ctx", "enc"), None),
    )
    out_specs = (
        P("enc", "ctx", None),
        P(None, ("ctx", "enc"), None),
        P(None, ("ctx", "enc"), None),
    )
    body = functools.partial(shards, mesh.shape["ctx"], mesh.shape["enc"])
    return jax.shard_map(body, mesh=mesh, in_specs=in_specs, out_specs=out_specs, check_vma=False)
```

```python
import functools

import jax
import jax.numpy as jnp
from jax import lax
from jax.experimental import pallas as pl
from jax.experimental.pallas import tpu as pltpu
from jax.sharding import PartitionSpec as P

H = 32
KVH = 8
HD = 128
SAMP = 2
MAX_TILES = 4
TILE_TOK = 64
RATIO = H // KVH
CORES = 2
SLOT_ROWS = MAX_TILES * TILE_TOK
HALF_KV = KVH // CORES
HALF_KCOLS = HALF_KV * HD
HALF_QCOLS = HALF_KCOLS * RATIO
WIDE = RATIO * HD
SAMP_ROWS = 16
DQ_PARTS = 2
SCALE = HD ** (-0.5)
LOG2E = 1.4426950408889634
BIG_NEGATIVE = -1e30
NT = (((1,), (1,)), ((), ()))
TN = (((0,), (0,)), ((), ()))
BF16 = jnp.bfloat16
F32 = jnp.float32

IN_VMEM = pl.BlockSpec(memory_space=pltpu.VMEM)
IN_HBM = pl.BlockSpec(memory_space=pltpu.HBM)


def local_call(body, ins, outs, scratch=(), flops=0, moved=2**19, aliases={}):
    return pl.pallas_call(
        body,
        in_specs=ins,
        out_specs=[spec for _, _, spec in outs],
        out_shape=[jax.ShapeDtypeStruct(s, d) for s, d, _ in outs],
        scratch_shapes=list(scratch),
        compiler_params=pltpu.CompilerParams(vmem_limit_bytes=8 * 2**20),
        input_output_aliases=aliases,
        cost_estimate=pl.CostEstimate(
            flops=flops, bytes_accessed=moved, transcendentals=flops // 1280
        ),
    )


def in_vmem(body, outs, **more):
    def call(*args):
        spec = [(shape, dtype, IN_VMEM) for shape, dtype in outs]
        return local_call(body, [IN_VMEM] * len(args), spec, **more)(*args)

    return call


def core_of():
    return lax.rem(lax.axis_index("ctx"), CORES)


def at_rows(first, count):
    return pl.ds(pl.multiple_of(first, count), count)


def at_cols(first, width, step):
    return pl.ds(pl.multiple_of(first, step), width)


def start_copies(pairs, sems):
    copies = [pltpu.make_async_copy(src, dst, sems.at[i]) for i, (src, dst) in enumerate(pairs)]
    for copy in copies:
        copy.start()
    return copies


def run_copies(pairs, sems):
    for copy in start_copies(pairs, sems):
        copy.wait()


def in_hbm(*arrays):
    return [pltpu.with_memory_space_constraint(a, pltpu.HBM) for a in arrays]


def split_kernel(k_ref, v_ref, mine, peer, sems):
    core = core_of()
    pairs = []
    for half, out in ((1 - core, peer), (core, mine)):
        cols = at_cols(half * HALF_KCOLS, HALF_KCOLS, HALF_KCOLS)
        for i, ref in enumerate((k_ref, v_ref)):
            pairs.append((ref.at[:, :, cols], out.at[i]))
    run_copies(pairs, sems)


def near_place():
    return lax.div(lax.axis_index("ctx"), CORES), lax.axis_index("enc")


def split_text(n_blocks, pieces, where, q_ref, g_ref, samp_hbm, tiles_hbm, peer, q_own, g_own, bias, samp, tiles, sems):
    core = core_of()
    tokens = q_ref.shape[1]
    own_cols = at_cols(core * HALF_QCOLS, HALF_QCOLS, HALF_QCOLS)
    peer_cols = at_cols((1 - core) * HALF_QCOLS, HALF_QCOLS, HALF_QCOLS)
    copies = start_copies(
        [
            (samp_hbm, samp),
            (tiles_hbm, tiles),
            (q_ref.at[0, :, peer_cols], peer.at[:tokens]),
            (g_ref.at[0, :, peer_cols], peer.at[tokens : 2 * tokens]),
            (q_ref.at[0, :, own_cols], q_own.at[:tokens]),
            (g_ref.at[0, :, own_cols], g_own),
        ],
        sems,
    )
    for copy in copies[:2]:
        copy.wait()
    row = jnp.broadcast_to(samp[...].astype(F32), (SAMP_ROWS, tokens)).astype(BF16)
    for out, first in ((q_own, tokens), (peer, 2 * tokens)):
        out[first:, :] = jnp.zeros((SAMP_ROWS, HALF_QCOLS), BF16)
        out[first:, :tokens] = row

    sample, enc = where()
    block_rows = SLOT_ROWS // n_blocks
    slots = block_rows // pieces
    line = lax.broadcasted_iota(jnp.int32, (SLOT_ROWS, HD), 0)
    block = lax.div(line, block_rows)
    if n_blocks > 1:
        low, high = block & 1, lax.div(block, 2) & 1
        block = block - low - 2 * high + 2 * low + high
    owner = block ^ enc
    piece = lax.rem(lax.div(line, slots), pieces)
    slot = piece * (SLOT_ROWS // pieces) + owner * slots + lax.rem(line, slots)
    for i in range(SAMP):
        count = jnp.where((sample ^ i) == 0, tiles[0:1, 0:1], tiles[0:1, 1:2])
        masked = jnp.where(slot < count * TILE_TOK, 0.0, BIG_NEGATIVE)
        first = lax.broadcasted_iota(jnp.int32, masked.shape, 1) == 0
        bias[i] = jnp.where(first, masked, 0.0).astype(BF16)
    for copy in copies[2:]:
        copy.wait()


def carry_kernel(slots, own, got, text, *outs):
    core = core_of()
    enc = lax.axis_index("enc")
    for dz, out in enumerate(outs[:-1]):
        for dx in range(2):
            group = enc ^ (2 * dz + dx)
            for i in range(2):
                first = i * CORES * slots
                out[dx, at_rows(first + core * slots, slots), :] = own[i, group]
                out[dx, at_rows(first + (1 - core) * slots, slots), :] = got[i, group]


def join_kernel(*refs):
    parts, outs = refs[:2], refs[-2:]
    rows = parts[0].shape[1]
    for dx, out in enumerate(outs):
        for dz, part in enumerate(parts):
            out[dz * rows : (dz + 1) * rows, :] = part[dx]


def block_place(b, n_outs):
    half, x, z = b // 4, b // 2 % 2, b % 2
    whole = 2 * half + z
    return {1: (0, b), 3: (1 + half, z) if x else (0, whole), 4: (2 * half + x, z)}[n_outs]


def add_kernel(z, own, back_y, back_xy, back_x, *outs):
    rows = outs[0].shape[1]
    for dz, out in enumerate(outs):
        whole = slice((z + dz) * rows, (z + dz + 1) * rows)
        part = slice(dz * rows, (dz + 1) * rows)
        out[0] = (own[whole, :] + back_y[part, :].astype(F32)).astype(out.dtype)
        out[1] = (back_x[part, :].astype(F32) + back_xy[part, :].astype(F32)).astype(out.dtype)


def nothing_kernel(*refs):
    pass


def hand_on(array, *after):
    return in_vmem(nothing_kernel, [(array.shape, array.dtype)], aliases={0: 0})(array, *after)


def far_rows_kernel(slots, *refs):
    core = core_of()
    parts, outs = refs[:2], refs[-2:]
    for dz, part in enumerate(parts):
        for dx in range(2):
            for i in range(2):
                first = i * CORES * slots
                for who, out in zip((core, 1 - core), outs):
                    out[i, 2 * dz + dx] = part[dx, at_rows(first + who * slots, slots), :]


def owner_rows_kernel(slots, *refs):
    core = core_of()
    enc = lax.axis_index("enc")
    parts, far, outs = refs[:2], refs[2:4], refs[4:]
    for dz, part in enumerate(parts):
        for dx in range(2):
            d = 2 * dz + dx
            for i in range(2):
                first = i * CORES * slots
                for who, from_far, out in zip((core, 1 - core), far, outs):
                    out[i, enc ^ d] = part[dx, at_rows(first + who * slots, slots), :]
                    out[i, enc ^ (2 * len(parts) + d)] = from_far[i, d]


def finish_kernel(mine, got, _, dk, dv, sems):
    core = core_of()
    pairs = []
    for half, ref in ((core, mine), (1 - core, got)):
        cols = at_cols(half * HALF_KCOLS, HALF_KCOLS, HALF_KCOLS)
        for i, out in enumerate((dk, dv)):
            pairs.append((ref.at[i], out.at[:, :, cols]))
    run_copies(pairs, sems)


def split_rows_kernel(whole, *refs):
    outs = refs[-DQ_PARTS:]
    rows = outs[0].shape[0]
    for i, out in enumerate(outs):
        out[...] = whole[i * rows : (i + 1) * rows, :]


def finish_text_kernel(mine, *refs):
    got, (out, token, sems) = refs[:-3], refs[-3:]
    core = core_of()
    token[...] = jnp.zeros_like(token)
    own_cols = at_cols(core * HALF_QCOLS, HALF_QCOLS, HALF_QCOLS)
    got_cols = at_cols((1 - core) * HALF_QCOLS, HALF_QCOLS, HALF_QCOLS)
    pairs = [(mine, out.at[0, :, own_cols])]
    rows = got[0].shape[0]
    for i, ref in enumerate(got):
        pairs.append((ref, out.at[0, i * rows : (i + 1) * rows, got_cols]))
    run_copies(pairs, sems)


def blocks_with(sample, q_own, got):
    tokens = q_own.shape[0] - SAMP_ROWS
    rows = (q_own[tokens : tokens + 1, :tokens], got[2 * tokens : 2 * tokens + 1, :tokens])
    rows = [row.astype(F32) for row in rows]
    wanted = sample.astype(F32)
    return rows, [jnp.max(jnp.where(row == wanted, 1.0, 0.0)) > 0.5 for row in rows]


def key_rows(kvs, block_rows, first, h):
    parts = []
    for kv in kvs:
        for at in range(first, kv.shape[0], 2 * block_rows):
            parts.append(kv[at : at + block_rows, h * HD : (h + 1) * HD])
    return jnp.concatenate(parts, axis=0)


def choose(flags, branch):
    for which in ((0, 1), (0,), (1,), ()):
        wants = [flags[t] if t in which else jnp.logical_not(flags[t]) for t in range(2)]

        @pl.when(wants[0] & wants[1])
        def _():
            branch(which)


def pass_kernel(role, n_blocks, n_kv, n_grads, where, bias, q_a, g_a, got, *rest):
    kvs, (ds_out, *grads) = rest[:n_kv], rest[-1 - n_grads :]
    sample = where()[0] ^ role
    tokens = g_a.shape[0]
    block_rows = SLOT_ROWS // n_blocks
    rows, present = blocks_with(sample, q_a, got)
    sources = ((q_a, 0, g_a, 0), (got, 0, got, tokens))

    def one_pass(which):
        if not which:
            for out in grads:
                out[...] = jnp.zeros_like(out)
            return
        mine = jnp.concatenate([rows[t] for t in which for _ in range(RATIO)], axis=1)
        mine = mine == sample.astype(F32)
        masks = bias[role]
        ones = jnp.ones((len(which) * RATIO * tokens, HD), BF16)

        def products(h):
            def stacked(part):
                parts = []
                for t in which:
                    ref, first = sources[t][part : part + 2]
                    for r in range(RATIO):
                        at = h * WIDE + r * HD
                        parts.append(ref[first : first + tokens, at : at + HD])
                return jnp.concatenate(parts, axis=0)

            q, g = stacked(0), stacked(2)
            k, v = (key_rows(kvs, block_rows, first, h) for first in (0, block_rows))
            s = lax.dot_general(
                jnp.concatenate([k, masks], axis=1),
                jnp.concatenate([q, ones], axis=1),
                NT,
                preferred_element_type=F32,
            )
            gp = lax.dot_general(v, g, NT, preferred_element_type=F32)
            return q, g, s, gp

        early = len(which) == 1
        ahead = products(0)
        for h in range(HALF_KV):
            q, g, s, gp = ahead
            if early and h + 1 < HALF_KV:
                ahead = products(h + 1)
            top = jnp.max(s, axis=0, keepdims=True)
            e = jnp.exp2((s - top) * (SCALE * LOG2E))
            total = jnp.sum(e, axis=0, keepdims=True)
            p = e * jnp.where(mine, 1.0 / total, 0.0)
            row_dot = jnp.sum(p * gp, axis=0, keepdims=True)
            ph = p.astype(BF16)
            ds = ph * (gp - row_dot).astype(BF16)
            dv = jnp.dot(ph, g, preferred_element_type=F32)
            dk = jnp.dot(ds, q, preferred_element_type=F32) * SCALE
            wide = RATIO * tokens
            for i, t in enumerate(which):
                ds_out[h, :, t * wide : (t + 1) * wide] = ds[:, i * wide : (i + 1) * wide]
            cols = slice(h * HD, (h + 1) * HD)
            for b in range(n_blocks):
                block = slice(b * block_rows, (b + 1) * block_rows)
                dx, at = block_place(b, len(grads))
                out, first = grads[dx], at * 2 * block_rows
                out[first : first + block_rows, cols] = dk[block].astype(out.dtype)
                out[first + block_rows : first + 2 * block_rows, cols] = dv[block].astype(out.dtype)
            if not early and h + 1 < HALF_KV:
                ahead = products(h + 1)

    choose(present, one_pass)


def dq_kernel(n_blocks, n_kv, where, q_a, got, *rest):
    keys = rest[:n_kv], rest[n_kv : 2 * n_kv]
    ds, dqs = rest[2 * n_kv : 2 * n_kv + 2], rest[-2:]
    tokens = dqs[0].shape[0]
    block_rows = SLOT_ROWS // n_blocks
    first = where()[0]
    present = [blocks_with(first ^ role, q_a, got)[1] for role in range(SAMP)]
    wide = RATIO * tokens
    for t, dq_ref in enumerate(dqs):

        def one_block(roles):
            for h in range(HALF_KV):
                total = 0.0
                for role in roles:
                    k = key_rows(keys[role], block_rows, 0, h)
                    part = ds[role][h, :, t * wide : (t + 1) * wide]
                    total += lax.dot_general(part, k, TN, preferred_element_type=F32)
                if roles:
                    for r in range(RATIO):
                        at = h * WIDE + r * HD
                        rows = total[r * tokens : (r + 1) * tokens] * SCALE
                        dq_ref[:, at : at + HD] = rows.astype(dq_ref.dtype)

        choose([present[role][t] for role in range(SAMP)], one_block)


def sample_pass(where, role, n_blocks, bias, text, kvs, grads, after=()):
    tokens = text[1].shape[0]
    ds = ((HALF_KV, SLOT_ROWS, CORES * RATIO * tokens), BF16)
    return in_vmem(
        functools.partial(pass_kernel, role, n_blocks, len(kvs), len(grads), where),
        [ds, *grads],
        flops=8 * tokens * WIDE * SLOT_ROWS * CORES * HALF_KV,
        moved=16 * 2**20,
    )(bias, *text, *kvs, *after)


def text_grads(where, n_blocks, text, keys, ds):
    tokens = text[1].shape[0]
    return in_vmem(
        functools.partial(dq_kernel, n_blocks, len(keys[0]), where),
        [((tokens, HALF_QCOLS), BF16)] * 2,
        flops=4 * tokens * WIDE * SLOT_ROWS * CORES * HALF_KV,
        moved=8 * 2**20,
    )(text[0], text[2], *keys[0], *keys[1], *ds)


def shards(n_ctx, n_enc, queries, d_out, text_sample, tiles, img_k, img_v):
    n_y = n_ctx // CORES
    slots = img_k.shape[1]
    tokens = queries.shape[1]
    swap_core = [(i, i ^ 1) for i in range(n_ctx)]
    near = n_y == SAMP and slots % 16 == 0 and n_enc == 8
    text_outs = [
        ((2 * tokens + SAMP_ROWS, HALF_QCOLS), BF16, IN_VMEM),
        ((tokens + SAMP_ROWS, HALF_QCOLS), BF16, IN_VMEM),
        ((tokens, HALF_QCOLS), BF16, IN_VMEM),
        ((SAMP, SLOT_ROWS, HD), BF16, IN_VMEM),
    ]

    def split_the_text(n_blocks, pieces, where):
        return local_call(
            functools.partial(split_text, n_blocks, pieces, where),
            [IN_HBM] * 4,
            text_outs,
            [
                pltpu.VMEM(text_sample.shape, jnp.int32),
                pltpu.VMEM(tiles.shape, jnp.int32),
                pltpu.SemaphoreType.DMA((6,)),
            ],
            moved=4 * 2**20,
        )(*in_hbm(queries, d_out, text_sample, tiles))

    if near:
        swap_y = [(i, (i + CORES) % n_ctx) for i in range(n_ctx)]
        n_z = n_enc // 2
        block_rows = 2 * CORES * slots
        pair = (2, block_rows, HALF_KCOLS)
        quarter = (2 * block_rows, HALF_KCOLS)
        whole = (SLOT_ROWS, HALF_KCOLS)
        kv_halves = (2, n_enc, slots, HALF_KCOLS)
        swap_x = [(i, i ^ 1) for i in range(n_enc)]
        swap_xy = [
            (i * n_enc + e, (i + CORES) % n_ctx * n_enc + (e ^ 1))
            for i in range(n_ctx)
            for e in range(n_enc)
        ]

        def along_z(part, dz):
            return lax.ppermute(part, "enc", [(i, i ^ (2 * dz)) for i in range(n_enc)]) if dz else part

        def along_x(part):
            return lax.ppermute(part, "enc", swap_x)

        def along_y(part):
            return lax.ppermute(part, "ctx", swap_y)

        def along_xy(part):
            return lax.ppermute(part, ("ctx", "enc"), swap_xy)

        mine, for_peer = local_call(
            split_kernel,
            [IN_HBM] * 2,
            [(kv_halves, BF16, IN_VMEM)] * 2,
            [pltpu.SemaphoreType.DMA((4,))],
        )(*in_hbm(img_k, img_v))
        text_peer, q_own, g_own, bias = split_the_text(n_enc, CORES, near_place)
        *carry, text_peer = in_vmem(
            functools.partial(carry_kernel, slots),
            [(pair, BF16)] * n_z + [(text_peer.shape, BF16)],
            aliases={2: n_z},
        )(mine, lax.ppermute(for_peer, "ctx", swap_core), text_peer)
        text = (q_own, g_own, lax.ppermute(text_peer, "ctx", swap_core))

        came = [along_z(part, dz) for dz, part in enumerate(carry)]
        own, far = [], []
        for z in (0, 2):
            here, beside = in_vmem(join_kernel, [(quarter, BF16)] * 2)(
                *came[z : z + 2], text[2], *far
            )
            own += [here, along_x(beside)]
            far += [along_y(here), along_xy(beside)]
        own_ds, own_here, *own_beside = sample_pass(
            near_place, 0, n_enc, bias, text, own, [(whole, F32)] + [(quarter, BF16)] * 2
        )
        far_ds, *far_grads = sample_pass(
            near_place, 1, n_enc, bias, text, far, [(quarter, BF16)] * 4, (own_here,)
        )
        dq = text_grads(near_place, n_enc, text, (own, far), (own_ds, far_ds))
        returned = [None] * n_z
        for z in (2, 0):
            here, beside = far_grads[z : z + 2]
            (own_part,) = hand_on(own_beside[z // 2], here)
            back_y, back_xy, back_x = along_y(here), along_xy(beside), along_x(own_part)
            totals = in_vmem(functools.partial(add_kernel, z), [(pair, BF16)] * 2)(
                own_here, back_y, back_xy, back_x
            )
            for dz, total in enumerate(totals, z):
                returned[dz] = along_z(total, dz)
            if z:
                sent = totals[0]
        dq_parts = in_vmem(split_rows_kernel, [((tokens // DQ_PARTS, HALF_QCOLS), BF16)] * DQ_PARTS)(
            dq[1], sent, totals[0]
        )
        dq_got = [lax.ppermute(part, "ctx", swap_core) for part in dq_parts]
    else:
        both = ("ctx", "enc")
        same_y = [
            [yy * CORES * n_enc + i for i in range(CORES * n_enc)] for yy in range(n_y)
        ]
        same_column = [
            [(yy * CORES + c) * n_enc + e for yy in range(n_y)]
            for c in range(CORES)
            for e in range(n_enc)
        ]
        core = core_of()

        def exchange(parts):
            return lax.all_to_all(
                parts, both, split_axis=0, concat_axis=0, axis_index_groups=same_y, tiled=True
            )

        def to_groups(owned):
            parts = owned.reshape(n_enc, slots, CORES, HALF_KCOLS).transpose(2, 0, 1, 3)
            got = exchange(parts.reshape(CORES * n_enc, slots, HALF_KCOLS))
            got = got.reshape(CORES * n_enc * slots, HALF_KCOLS)
            return lax.all_gather(got, both, axis=0, axis_index_groups=same_column, tiled=True)

        def to_owners(grads):
            grads = lax.psum_scatter(
                grads, both, scatter_dimension=0, axis_index_groups=same_column, tiled=True
            )
            got = exchange(grads.reshape(CORES * n_enc, slots, HALF_KCOLS))
            got = got.reshape(CORES, n_enc, slots, HALF_KCOLS).transpose(1, 2, 0, 3)
            return got.reshape(n_enc, slots, CORES * HALF_KCOLS)

        def no_place():
            return jnp.int32(0), jnp.int32(0)

        all_k = to_groups(img_k)
        all_v = to_groups(img_v)
        text_peer, q_own, g_own, bias = split_the_text(1, 1, no_place)
        text = (q_own, g_own, lax.ppermute(text_peer, "ctx", swap_core))
        kvs = [
            jnp.concatenate([part[s * SLOT_ROWS : (s + 1) * SLOT_ROWS] for part in (all_k, all_v)], axis=0)
            for s in range(SAMP)
        ]
        all_ds, grads = [], []
        for sample, kv in enumerate(kvs):
            ds, grad = sample_pass(no_place, sample, 1, bias, text, [kv], [(kv.shape, BF16)])
            all_ds.append(ds)
            grads.append(grad)
        dq = text_grads(no_place, 1, text, [[kv] for kv in kvs], all_ds)
        d_img_k = to_owners(jnp.concatenate([g[:SLOT_ROWS] for g in grads], axis=0))
        d_img_v = to_owners(jnp.concatenate([g[SLOT_ROWS:] for g in grads], axis=0))
        dq_got = [lax.ppermute(dq[1], "ctx", swap_core)]

    d_queries, token = local_call(
        finish_text_kernel,
        [IN_VMEM] * (1 + len(dq_got)),
        [(queries.shape, BF16, IN_HBM), ((8, HD), F32, IN_VMEM)],
        [pltpu.SemaphoreType.DMA((1 + len(dq_got),))],
    )(dq[0], *dq_got)
    if near:
        far_rows = in_vmem(
            functools.partial(far_rows_kernel, slots),
            [((2, n_enc // 2, slots, HALF_KCOLS), BF16)] * 2,
        )(*returned[2:])
        mine, for_peer = in_vmem(
            functools.partial(owner_rows_kernel, slots),
            [(kv_halves, BF16)] * 2,
        )(*returned[:2], *far_rows)
        d_img_k, d_img_v = local_call(
            finish_kernel,
            [IN_VMEM] * 3,
            [(img_k.shape, BF16, IN_HBM)] * 2,
            [pltpu.SemaphoreType.DMA((4,))],
        )(mine, lax.ppermute(for_peer, "ctx", swap_core), token)
    return (d_queries, d_img_k, d_img_v)


def solution(mesh):
    in_specs = (
        P("enc", "ctx", None),
        P("enc", "ctx", None),
        P("enc", "ctx"),
        P("enc", None),
        P(None, ("ctx", "enc"), None),
        P(None, ("ctx", "enc"), None),
    )
    out_specs = (
        P("enc", "ctx", None),
        P(None, ("ctx", "enc"), None),
        P(None, ("ctx", "enc"), None),
    )
    body = functools.partial(shards, mesh.shape["ctx"], mesh.shape["enc"])
    return jax.shard_map(body, mesh=mesh, in_specs=in_specs, out_specs=out_specs, check_vma=False)
```

```python
import functools

import jax
import jax.numpy as jnp
from jax import lax
from jax.experimental import pallas as pl
from jax.experimental.pallas import tpu as pltpu
from jax.sharding import PartitionSpec as P

H = 32
KVH = 8
HD = 128
SAMP = 2
MAX_TILES = 4
TILE_TOK = 64
RATIO = H // KVH
CORES = 2
SLOT_ROWS = MAX_TILES * TILE_TOK
HALF_KV = KVH // CORES
HALF_KCOLS = HALF_KV * HD
HALF_QCOLS = HALF_KCOLS * RATIO
WIDE = RATIO * HD
SAMP_ROWS = 16
DQ_PARTS = 2
SCALE = HD ** (-0.5)
LOG2E = 1.4426950408889634
BIG_NEGATIVE = -1e30
NT = (((1,), (1,)), ((), ()))
TN = (((0,), (0,)), ((), ()))
BF16 = jnp.bfloat16
F32 = jnp.float32

IN_VMEM = pl.BlockSpec(memory_space=pltpu.VMEM)
IN_HBM = pl.BlockSpec(memory_space=pltpu.HBM)


def local_call(body, ins, outs, scratch=(), flops=0, moved=2**19, aliases={}):
    return pl.pallas_call(
        body,
        in_specs=ins,
        out_specs=[spec for _, _, spec in outs],
        out_shape=[jax.ShapeDtypeStruct(s, d) for s, d, _ in outs],
        scratch_shapes=list(scratch),
        compiler_params=pltpu.CompilerParams(vmem_limit_bytes=8 * 2**20),
        input_output_aliases=aliases,
        cost_estimate=pl.CostEstimate(
            flops=flops, bytes_accessed=moved, transcendentals=flops // 1280
        ),
    )


def in_vmem(body, outs, **more):
    def call(*args):
        spec = [(shape, dtype, IN_VMEM) for shape, dtype in outs]
        return local_call(body, [IN_VMEM] * len(args), spec, **more)(*args)

    return call


def core_of():
    return lax.rem(lax.axis_index("ctx"), CORES)


def at_rows(first, count):
    return pl.ds(pl.multiple_of(first, count), count)


def at_cols(first, width, step):
    return pl.ds(pl.multiple_of(first, step), width)


def start_copies(pairs, sems):
    copies = [pltpu.make_async_copy(src, dst, sems.at[i]) for i, (src, dst) in enumerate(pairs)]
    for copy in copies:
        copy.start()
    return copies


def run_copies(pairs, sems):
    for copy in start_copies(pairs, sems):
        copy.wait()


def in_hbm(*arrays):
    return [pltpu.with_memory_space_constraint(a, pltpu.HBM) for a in arrays]


def split_kernel(k_ref, v_ref, mine, peer, sems):
    core = core_of()
    pairs = []
    for half, out in ((1 - core, peer), (core, mine)):
        cols = at_cols(half * HALF_KCOLS, HALF_KCOLS, HALF_KCOLS)
        for i, ref in enumerate((k_ref, v_ref)):
            pairs.append((ref.at[:, :, cols], out.at[i]))
    run_copies(pairs, sems)


def near_place():
    return lax.div(lax.axis_index("ctx"), CORES), lax.axis_index("enc")


def split_text(n_blocks, pieces, where, q_ref, g_ref, samp_hbm, tiles_hbm, peer, q_own, g_own, bias, samp, tiles, sems):
    core = core_of()
    tokens = q_ref.shape[1]
    own_cols = at_cols(core * HALF_QCOLS, HALF_QCOLS, HALF_QCOLS)
    peer_cols = at_cols((1 - core) * HALF_QCOLS, HALF_QCOLS, HALF_QCOLS)
    copies = start_copies(
        [
            (samp_hbm, samp),
            (tiles_hbm, tiles),
            (q_ref.at[0, :, peer_cols], peer.at[:tokens]),
            (g_ref.at[0, :, peer_cols], peer.at[tokens : 2 * tokens]),
            (q_ref.at[0, :, own_cols], q_own.at[:tokens]),
            (g_ref.at[0, :, own_cols], g_own),
        ],
        sems,
    )
    for copy in copies[:2]:
        copy.wait()
    row = jnp.broadcast_to(samp[...].astype(F32), (SAMP_ROWS, tokens)).astype(BF16)
    for out, first in ((q_own, tokens), (peer, 2 * tokens)):
        out[first:, :] = jnp.zeros((SAMP_ROWS, HALF_QCOLS), BF16)
        out[first:, :tokens] = row

    sample, enc = where()
    block_rows = SLOT_ROWS // n_blocks
    slots = block_rows // pieces
    line = lax.broadcasted_iota(jnp.int32, (SLOT_ROWS, HD), 0)
    block = lax.div(line, block_rows)
    if n_blocks > 1:
        low, high = block & 1, lax.div(block, 2) & 1
        block = block - low - 2 * high + 2 * low + high
    owner = block ^ enc
    piece = lax.rem(lax.div(line, slots), pieces)
    slot = piece * (SLOT_ROWS // pieces) + owner * slots + lax.rem(line, slots)
    for i in range(SAMP):
        count = jnp.where((sample ^ i) == 0, tiles[0:1, 0:1], tiles[0:1, 1:2])
        masked = jnp.where(slot < count * TILE_TOK, 0.0, BIG_NEGATIVE)
        first = lax.broadcasted_iota(jnp.int32, masked.shape, 1) == 0
        bias[i] = jnp.where(first, masked, 0.0).astype(BF16)
    for copy in copies[2:]:
        copy.wait()


def carry_kernel(slots, own, got, text, *outs):
    core = core_of()
    enc = lax.axis_index("enc")
    for dz, out in enumerate(outs[:-1]):
        for dx in range(2):
            group = enc ^ (2 * dz + dx)
            for i in range(2):
                first = i * CORES * slots
                out[dx, at_rows(first + core * slots, slots), :] = own[i, group]
                out[dx, at_rows(first + (1 - core) * slots, slots), :] = got[i, group]


def join_kernel(*refs):
    parts, outs = refs[:2], refs[-2:]
    rows = parts[0].shape[1]
    for dx, out in enumerate(outs):
        for dz, part in enumerate(parts):
            out[dz * rows : (dz + 1) * rows, :] = part[dx]


def block_place(b, n_outs):
    half, x, z = b // 4, b // 2 % 2, b % 2
    whole = 2 * half + z
    return {1: (0, b), 3: (1 + half, z) if x else (0, whole), 4: (2 * half + x, z)}[n_outs]


def add_kernel(z, own, back_y, back_xy, back_x, *outs):
    rows = outs[0].shape[1]
    for dz, out in enumerate(outs):
        whole = slice((z + dz) * rows, (z + dz + 1) * rows)
        part = slice(dz * rows, (dz + 1) * rows)
        out[0] = (own[whole, :] + back_y[part, :].astype(F32)).astype(out.dtype)
        out[1] = (back_x[part, :].astype(F32) + back_xy[part, :].astype(F32)).astype(out.dtype)


def nothing_kernel(*refs):
    pass


def hand_on(array, *after):
    return in_vmem(nothing_kernel, [(array.shape, array.dtype)], aliases={0: 0})(array, *after)


def far_rows_kernel(slots, *refs):
    core = core_of()
    parts, outs = refs[:2], refs[-2:]
    for dz, part in enumerate(parts):
        for dx in range(2):
            for i in range(2):
                first = i * CORES * slots
                for who, out in zip((core, 1 - core), outs):
                    out[i, 2 * dz + dx] = part[dx, at_rows(first + who * slots, slots), :]


def owner_rows_kernel(slots, *refs):
    core = core_of()
    enc = lax.axis_index("enc")
    parts, far, outs = refs[:2], refs[2:4], refs[4:]
    for dz, part in enumerate(parts):
        for dx in range(2):
            d = 2 * dz + dx
            for i in range(2):
                first = i * CORES * slots
                for who, from_far, out in zip((core, 1 - core), far, outs):
                    out[i, enc ^ d] = part[dx, at_rows(first + who * slots, slots), :]
                    out[i, enc ^ (2 * len(parts) + d)] = from_far[i, d]


def finish_kernel(mine, got, _, dk, dv, sems):
    core = core_of()
    pairs = []
    for half, ref in ((core, mine), (1 - core, got)):
        cols = at_cols(half * HALF_KCOLS, HALF_KCOLS, HALF_KCOLS)
        for i, out in enumerate((dk, dv)):
            pairs.append((ref.at[i], out.at[:, :, cols]))
    run_copies(pairs, sems)


def split_rows_kernel(whole, *refs):
    outs = refs[-DQ_PARTS:]
    rows = outs[0].shape[0]
    for i, out in enumerate(outs):
        out[...] = whole[i * rows : (i + 1) * rows, :]


def finish_text_kernel(mine, *refs):
    got, (out, token, sems) = refs[:-3], refs[-3:]
    core = core_of()
    token[...] = jnp.zeros_like(token)
    own_cols = at_cols(core * HALF_QCOLS, HALF_QCOLS, HALF_QCOLS)
    got_cols = at_cols((1 - core) * HALF_QCOLS, HALF_QCOLS, HALF_QCOLS)
    pairs = [(mine, out.at[0, :, own_cols])]
    rows = got[0].shape[0]
    for i, ref in enumerate(got):
        pairs.append((ref, out.at[0, i * rows : (i + 1) * rows, got_cols]))
    run_copies(pairs, sems)


def blocks_with(sample, q_own, got):
    tokens = q_own.shape[0] - SAMP_ROWS
    rows = (q_own[tokens : tokens + 1, :tokens], got[2 * tokens : 2 * tokens + 1, :tokens])
    rows = [row.astype(F32) for row in rows]
    wanted = sample.astype(F32)
    return rows, [jnp.max(jnp.where(row == wanted, 1.0, 0.0)) > 0.5 for row in rows]


def key_rows(kvs, block_rows, first, h):
    parts = []
    for kv in kvs:
        for at in range(first, kv.shape[0], 2 * block_rows):
            parts.append(kv[at : at + block_rows, h * HD : (h + 1) * HD])
    return jnp.concatenate(parts, axis=0)


def choose(flags, branch):
    for which in ((0, 1), (0,), (1,), ()):
        wants = [flags[t] if t in which else jnp.logical_not(flags[t]) for t in range(2)]

        @pl.when(wants[0] & wants[1])
        def _():
            branch(which)


def pass_kernel(role, n_blocks, n_kv, n_grads, n_through, where, bias, q_a, g_a, got, *rest):
    kvs, (ds_out, *grads) = rest[:n_kv], rest[n_kv + n_through : n_kv + n_through + 1 + n_grads]
    sample = where()[0] ^ role
    tokens = g_a.shape[0]
    block_rows = SLOT_ROWS // n_blocks
    rows, present = blocks_with(sample, q_a, got)
    sources = ((q_a, 0, g_a, 0), (got, 0, got, tokens))

    def one_pass(which):
        if not which:
            for out in grads:
                out[...] = jnp.zeros_like(out)
            return
        mine = jnp.concatenate([rows[t] for t in which for _ in range(RATIO)], axis=1)
        mine = mine == sample.astype(F32)
        masks = bias[role]
        ones = jnp.ones((len(which) * RATIO * tokens, HD), BF16)

        def products(h):
            def stacked(part):
                parts = []
                for t in which:
                    ref, first = sources[t][part : part + 2]
                    for r in range(RATIO):
                        at = h * WIDE + r * HD
                        parts.append(ref[first : first + tokens, at : at + HD])
                return jnp.concatenate(parts, axis=0)

            q, g = stacked(0), stacked(2)
            k, v = (key_rows(kvs, block_rows, first, h) for first in (0, block_rows))
            s = lax.dot_general(
                jnp.concatenate([k, masks], axis=1),
                jnp.concatenate([q, ones], axis=1),
                NT,
                preferred_element_type=F32,
            )
            gp = lax.dot_general(v, g, NT, preferred_element_type=F32)
            return q, g, s, gp

        early = len(which) == 1
        ahead = products(0)
        for h in range(HALF_KV):
            q, g, s, gp = ahead
            if early and h + 1 < HALF_KV:
                ahead = products(h + 1)
            top = jnp.max(s, axis=0, keepdims=True)
            e = jnp.exp2((s - top) * (SCALE * LOG2E))
            total = jnp.sum(e, axis=0, keepdims=True)
            p = e * jnp.where(mine, 1.0 / total, 0.0)
            row_dot = jnp.sum(p * gp, axis=0, keepdims=True)
            ph = p.astype(BF16)
            ds = ph * (gp - row_dot).astype(BF16)
            dv = jnp.dot(ph, g, preferred_element_type=F32)
            dk = jnp.dot(ds, q, preferred_element_type=F32) * SCALE
            wide = RATIO * tokens
            for i, t in enumerate(which):
                ds_out[h, :, t * wide : (t + 1) * wide] = ds[:, i * wide : (i + 1) * wide]
            cols = slice(h * HD, (h + 1) * HD)
            for b in range(n_blocks):
                block = slice(b * block_rows, (b + 1) * block_rows)
                dx, at = block_place(b, len(grads))
                out, first = grads[dx], at * 2 * block_rows
                out[first : first + block_rows, cols] = dk[block].astype(out.dtype)
                out[first + block_rows : first + 2 * block_rows, cols] = dv[block].astype(out.dtype)
            if not early and h + 1 < HALF_KV:
                ahead = products(h + 1)

    choose(present, one_pass)


def dq_kernel(n_blocks, n_kv, where, q_a, got, *rest):
    keys = rest[:n_kv], rest[n_kv : 2 * n_kv]
    ds, dqs = rest[2 * n_kv : 2 * n_kv + 2], rest[-2:]
    tokens = dqs[0].shape[0]
    block_rows = SLOT_ROWS // n_blocks
    first = where()[0]
    present = [blocks_with(first ^ role, q_a, got)[1] for role in range(SAMP)]
    wide = RATIO * tokens
    for t, dq_ref in enumerate(dqs):

        def one_block(roles):
            for h in range(HALF_KV):
                total = 0.0
                for role in roles:
                    k = key_rows(keys[role], block_rows, 0, h)
                    part = ds[role][h, :, t * wide : (t + 1) * wide]
                    total += lax.dot_general(part, k, TN, preferred_element_type=F32)
                if roles:
                    for r in range(RATIO):
                        at = h * WIDE + r * HD
                        rows = total[r * tokens : (r + 1) * tokens] * SCALE
                        dq_ref[:, at : at + HD] = rows.astype(dq_ref.dtype)

        choose([present[role][t] for role in range(SAMP)], one_block)


def sample_pass(where, role, n_blocks, bias, text, kvs, grads, through=()):
    tokens = text[1].shape[0]
    ds = ((HALF_KV, SLOT_ROWS, CORES * RATIO * tokens), BF16)
    return in_vmem(
        functools.partial(pass_kernel, role, n_blocks, len(kvs), len(grads), len(through), where),
        [ds, *grads] + [(part.shape, part.dtype) for part in through],
        aliases={4 + len(kvs) + i: 1 + len(grads) + i for i in range(len(through))},
        flops=8 * tokens * WIDE * SLOT_ROWS * CORES * HALF_KV,
        moved=16 * 2**20,
    )(bias, *text, *kvs, *through)


def text_grads(where, n_blocks, text, keys, ds):
    tokens = text[1].shape[0]
    return in_vmem(
        functools.partial(dq_kernel, n_blocks, len(keys[0]), where),
        [((tokens, HALF_QCOLS), BF16)] * 2,
        flops=4 * tokens * WIDE * SLOT_ROWS * CORES * HALF_KV,
        moved=8 * 2**20,
    )(text[0], text[2], *keys[0], *keys[1], *ds)


def shards(n_ctx, n_enc, queries, d_out, text_sample, tiles, img_k, img_v):
    n_y = n_ctx // CORES
    slots = img_k.shape[1]
    tokens = queries.shape[1]
    swap_core = [(i, i ^ 1) for i in range(n_ctx)]
    near = n_y == SAMP and slots % 16 == 0 and n_enc == 8
    text_outs = [
        ((2 * tokens + SAMP_ROWS, HALF_QCOLS), BF16, IN_VMEM),
        ((tokens + SAMP_ROWS, HALF_QCOLS), BF16, IN_VMEM),
        ((tokens, HALF_QCOLS), BF16, IN_VMEM),
        ((SAMP, SLOT_ROWS, HD), BF16, IN_VMEM),
    ]

    def split_the_text(n_blocks, pieces, where):
        return local_call(
            functools.partial(split_text, n_blocks, pieces, where),
            [IN_HBM] * 4,
            text_outs,
            [
                pltpu.VMEM(text_sample.shape, jnp.int32),
                pltpu.VMEM(tiles.shape, jnp.int32),
                pltpu.SemaphoreType.DMA((6,)),
            ],
            moved=4 * 2**20,
        )(*in_hbm(queries, d_out, text_sample, tiles))

    if near:
        swap_y = [(i, (i + CORES) % n_ctx) for i in range(n_ctx)]
        n_z = n_enc // 2
        block_rows = 2 * CORES * slots
        pair = (2, block_rows, HALF_KCOLS)
        quarter = (2 * block_rows, HALF_KCOLS)
        whole = (SLOT_ROWS, HALF_KCOLS)
        kv_halves = (2, n_enc, slots, HALF_KCOLS)
        swap_x = [(i, i ^ 1) for i in range(n_enc)]
        swap_xy = [
            (i * n_enc + e, (i + CORES) % n_ctx * n_enc + (e ^ 1))
            for i in range(n_ctx)
            for e in range(n_enc)
        ]

        def along_z(part, dz):
            return lax.ppermute(part, "enc", [(i, i ^ (2 * dz)) for i in range(n_enc)]) if dz else part

        def along_x(part):
            return lax.ppermute(part, "enc", swap_x)

        def along_y(part):
            return lax.ppermute(part, "ctx", swap_y)

        def along_xy(part):
            return lax.ppermute(part, ("ctx", "enc"), swap_xy)

        mine, for_peer = local_call(
            split_kernel,
            [IN_HBM] * 2,
            [(kv_halves, BF16, IN_VMEM)] * 2,
            [pltpu.SemaphoreType.DMA((4,))],
        )(*in_hbm(img_k, img_v))
        text_peer, q_own, g_own, bias = split_the_text(n_enc, CORES, near_place)
        *carry, text_peer = in_vmem(
            functools.partial(carry_kernel, slots),
            [(pair, BF16)] * n_z + [(text_peer.shape, BF16)],
            aliases={2: n_z},
        )(mine, lax.ppermute(for_peer, "ctx", swap_core), text_peer)
        text = (q_own, g_own, lax.ppermute(text_peer, "ctx", swap_core))

        came = [along_z(part, dz) for dz, part in enumerate(carry)]
        own, far = [], []
        for z in (0, 2):
            here, beside = in_vmem(join_kernel, [(quarter, BF16)] * 2)(
                *came[z : z + 2], text[2], *far
            )
            own += [here, along_x(beside)]
            far += [along_y(here), along_xy(beside)]
        own_ds, own_here, *own_beside = sample_pass(
            near_place, 0, n_enc, bias, text, own, [(whole, F32)] + [(quarter, BF16)] * 2
        )
        far_ds, *far_grads = sample_pass(
            near_place, 1, n_enc, bias, text, far, [(quarter, BF16)] * 4, own_beside
        )
        own_beside = far_grads[4:]
        dq = text_grads(near_place, n_enc, text, (own, far), (own_ds, far_ds))
        returned = [None] * n_z
        for z in (2, 0):
            here, beside = far_grads[z : z + 2]
            back_y, back_xy, back_x = along_y(here), along_xy(beside), along_x(own_beside[z // 2])
            totals = in_vmem(functools.partial(add_kernel, z), [(pair, BF16)] * 2)(
                own_here, back_y, back_xy, back_x
            )
            for dz, total in enumerate(totals, z):
                returned[dz] = along_z(total, dz)
            if z:
                sent = totals[0]
        dq_parts = in_vmem(split_rows_kernel, [((tokens // DQ_PARTS, HALF_QCOLS), BF16)] * DQ_PARTS)(
            dq[1], sent, totals[0]
        )
        dq_got = [lax.ppermute(part, "ctx", swap_core) for part in dq_parts]
    else:
        both = ("ctx", "enc")
        same_y = [
            [yy * CORES * n_enc + i for i in range(CORES * n_enc)] for yy in range(n_y)
        ]
        same_column = [
            [(yy * CORES + c) * n_enc + e for yy in range(n_y)]
            for c in range(CORES)
            for e in range(n_enc)
        ]
        core = core_of()

        def exchange(parts):
            return lax.all_to_all(
                parts, both, split_axis=0, concat_axis=0, axis_index_groups=same_y, tiled=True
            )

        def to_groups(owned):
            parts = owned.reshape(n_enc, slots, CORES, HALF_KCOLS).transpose(2, 0, 1, 3)
            got = exchange(parts.reshape(CORES * n_enc, slots, HALF_KCOLS))
            got = got.reshape(CORES * n_enc * slots, HALF_KCOLS)
            return lax.all_gather(got, both, axis=0, axis_index_groups=same_column, tiled=True)

        def to_owners(grads):
            grads = lax.psum_scatter(
                grads, both, scatter_dimension=0, axis_index_groups=same_column, tiled=True
            )
            got = exchange(grads.reshape(CORES * n_enc, slots, HALF_KCOLS))
            got = got.reshape(CORES, n_enc, slots, HALF_KCOLS).transpose(1, 2, 0, 3)
            return got.reshape(n_enc, slots, CORES * HALF_KCOLS)

        def no_place():
            return jnp.int32(0), jnp.int32(0)

        all_k = to_groups(img_k)
        all_v = to_groups(img_v)
        text_peer, q_own, g_own, bias = split_the_text(1, 1, no_place)
        text = (q_own, g_own, lax.ppermute(text_peer, "ctx", swap_core))
        kvs = [
            jnp.concatenate([part[s * SLOT_ROWS : (s + 1) * SLOT_ROWS] for part in (all_k, all_v)], axis=0)
            for s in range(SAMP)
        ]
        all_ds, grads = [], []
        for sample, kv in enumerate(kvs):
            ds, grad = sample_pass(no_place, sample, 1, bias, text, [kv], [(kv.shape, BF16)])
            all_ds.append(ds)
            grads.append(grad)
        dq = text_grads(no_place, 1, text, [[kv] for kv in kvs], all_ds)
        d_img_k = to_owners(jnp.concatenate([g[:SLOT_ROWS] for g in grads], axis=0))
        d_img_v = to_owners(jnp.concatenate([g[SLOT_ROWS:] for g in grads], axis=0))
        dq_got = [lax.ppermute(dq[1], "ctx", swap_core)]

    d_queries, token = local_call(
        finish_text_kernel,
        [IN_VMEM] * (1 + len(dq_got)),
        [(queries.shape, BF16, IN_HBM), ((8, HD), F32, IN_VMEM)],
        [pltpu.SemaphoreType.DMA((1 + len(dq_got),))],
    )(dq[0], *dq_got)
    if near:
        far_rows = in_vmem(
            functools.partial(far_rows_kernel, slots),
            [((2, n_enc // 2, slots, HALF_KCOLS), BF16)] * 2,
        )(*returned[2:])
        mine, for_peer = in_vmem(
            functools.partial(owner_rows_kernel, slots),
            [(kv_halves, BF16)] * 2,
        )(*returned[:2], *far_rows)
        d_img_k, d_img_v = local_call(
            finish_kernel,
            [IN_VMEM] * 3,
            [(img_k.shape, BF16, IN_HBM)] * 2,
            [pltpu.SemaphoreType.DMA((4,))],
        )(mine, lax.ppermute(for_peer, "ctx", swap_core), token)
    return (d_queries, d_img_k, d_img_v)


def solution(mesh):
    in_specs = (
        P("enc", "ctx", None),
        P("enc", "ctx", None),
        P("enc", "ctx"),
        P("enc", None),
        P(None, ("ctx", "enc"), None),
        P(None, ("ctx", "enc"), None),
    )
    out_specs = (
        P("enc", "ctx", None),
        P(None, ("ctx", "enc"), None),
        P(None, ("ctx", "enc"), None),
    )
    body = functools.partial(shards, mesh.shape["ctx"], mesh.shape["enc"])
    return jax.shard_map(body, mesh=mesh, in_specs=in_specs, out_specs=out_specs, check_vma=False)
```

```python
import functools

import jax
import jax.numpy as jnp
from jax import lax
from jax.experimental import pallas as pl
from jax.experimental.pallas import tpu as pltpu
from jax.sharding import PartitionSpec as P

H = 32
KVH = 8
HD = 128
SAMP = 2
MAX_TILES = 4
TILE_TOK = 64
RATIO = H // KVH
CORES = 2
SLOT_ROWS = MAX_TILES * TILE_TOK
HALF_KV = KVH // CORES
HALF_KCOLS = HALF_KV * HD
HALF_QCOLS = HALF_KCOLS * RATIO
WIDE = RATIO * HD
SAMP_ROWS = 16
DQ_PARTS = 2
SCALE = HD ** (-0.5)
LOG2E = 1.4426950408889634
BIG_NEGATIVE = -1e30
NT = (((1,), (1,)), ((), ()))
TN = (((0,), (0,)), ((), ()))
BF16 = jnp.bfloat16
F32 = jnp.float32

IN_VMEM = pl.BlockSpec(memory_space=pltpu.VMEM)
IN_HBM = pl.BlockSpec(memory_space=pltpu.HBM)


def local_call(body, ins, outs, scratch=(), flops=0, moved=2**19, aliases={}):
    return pl.pallas_call(
        body,
        in_specs=ins,
        out_specs=[spec for _, _, spec in outs],
        out_shape=[jax.ShapeDtypeStruct(s, d) for s, d, _ in outs],
        scratch_shapes=list(scratch),
        compiler_params=pltpu.CompilerParams(vmem_limit_bytes=8 * 2**20),
        input_output_aliases=aliases,
        cost_estimate=pl.CostEstimate(
            flops=flops, bytes_accessed=moved, transcendentals=flops // 1280
        ),
    )


def in_vmem(body, outs, **more):
    def call(*args):
        spec = [(shape, dtype, IN_VMEM) for shape, dtype in outs]
        return local_call(body, [IN_VMEM] * len(args), spec, **more)(*args)

    return call


def core_of():
    return lax.rem(lax.axis_index("ctx"), CORES)


def at_rows(first, count):
    return pl.ds(pl.multiple_of(first, count), count)


def at_cols(first, width, step):
    return pl.ds(pl.multiple_of(first, step), width)


def start_copies(pairs, sems):
    copies = [pltpu.make_async_copy(src, dst, sems.at[i]) for i, (src, dst) in enumerate(pairs)]
    for copy in copies:
        copy.start()
    return copies


def run_copies(pairs, sems):
    for copy in start_copies(pairs, sems):
        copy.wait()


def in_hbm(*arrays):
    return [pltpu.with_memory_space_constraint(a, pltpu.HBM) for a in arrays]


def split_kernel(k_ref, v_ref, mine, peer, sems):
    core = core_of()
    pairs = []
    for half, out in ((1 - core, peer), (core, mine)):
        cols = at_cols(half * HALF_KCOLS, HALF_KCOLS, HALF_KCOLS)
        for i, ref in enumerate((k_ref, v_ref)):
            pairs.append((ref.at[:, :, cols], out.at[i]))
    run_copies(pairs, sems)


def near_place():
    return lax.div(lax.axis_index("ctx"), CORES), lax.axis_index("enc")


def split_text(n_blocks, pieces, where, q_ref, g_ref, samp_hbm, tiles_hbm, peer, q_own, g_own, bias, samp, tiles, sems):
    core = core_of()
    tokens = q_ref.shape[1]
    own_cols = at_cols(core * HALF_QCOLS, HALF_QCOLS, HALF_QCOLS)
    peer_cols = at_cols((1 - core) * HALF_QCOLS, HALF_QCOLS, HALF_QCOLS)
    copies = start_copies(
        [
            (samp_hbm, samp),
            (tiles_hbm, tiles),
            (q_ref.at[0, :, peer_cols], peer.at[:tokens]),
            (g_ref.at[0, :, peer_cols], peer.at[tokens : 2 * tokens]),
            (q_ref.at[0, :, own_cols], q_own.at[:tokens]),
            (g_ref.at[0, :, own_cols], g_own),
        ],
        sems,
    )
    for copy in copies[:2]:
        copy.wait()
    row = jnp.broadcast_to(samp[...].astype(F32), (SAMP_ROWS, tokens)).astype(BF16)
    for out, first in ((q_own, tokens), (peer, 2 * tokens)):
        out[first:, :] = jnp.zeros((SAMP_ROWS, HALF_QCOLS), BF16)
        out[first:, :tokens] = row

    sample, enc = where()
    block_rows = SLOT_ROWS // n_blocks
    slots = block_rows // pieces
    line = lax.broadcasted_iota(jnp.int32, (SLOT_ROWS, HD), 0)
    block = lax.div(line, block_rows)
    if n_blocks > 1:
        low, high = block & 1, lax.div(block, 2) & 1
        block = block - low - 2 * high + 2 * low + high
    owner = block ^ enc
    piece = lax.rem(lax.div(line, slots), pieces)
    slot = piece * (SLOT_ROWS // pieces) + owner * slots + lax.rem(line, slots)
    for i in range(SAMP):
        count = jnp.where((sample ^ i) == 0, tiles[0:1, 0:1], tiles[0:1, 1:2])
        masked = jnp.where(slot < count * TILE_TOK, 0.0, BIG_NEGATIVE)
        first = lax.broadcasted_iota(jnp.int32, masked.shape, 1) == 0
        bias[i] = jnp.where(first, masked, 0.0).astype(BF16)
    for copy in copies[2:]:
        copy.wait()


def carry_kernel(slots, own, got, text, *outs):
    core = core_of()
    enc = lax.axis_index("enc")
    for dz, out in enumerate(outs[:-1]):
        for dx in range(2):
            group = enc ^ (2 * dz + dx)
            for i in range(2):
                first = i * CORES * slots
                out[dx, at_rows(first + core * slots, slots), :] = own[i, group]
                out[dx, at_rows(first + (1 - core) * slots, slots), :] = got[i, group]


def join_kernel(*refs):
    parts, outs = refs[:2], refs[-2:]
    rows = parts[0].shape[1]
    for dx, out in enumerate(outs):
        for dz, part in enumerate(parts):
            out[dz * rows : (dz + 1) * rows, :] = part[dx]


def block_place(b, n_outs):
    half, x, z = b // 4, b // 2 % 2, b % 2
    whole = 2 * half + z
    return {1: (0, b), 3: (1 + half, z) if x else (0, whole), 4: (2 * half + x, z)}[n_outs]


def add_kernel(z, own, back_y, back_xy, back_x, *outs):
    rows = outs[0].shape[1]
    for dz, out in enumerate(outs):
        whole = slice((z + dz) * rows, (z + dz + 1) * rows)
        part = slice(dz * rows, (dz + 1) * rows)
        out[0] = (own[whole, :] + back_y[part, :].astype(F32)).astype(out.dtype)
        out[1] = (back_x[part, :].astype(F32) + back_xy[part, :].astype(F32)).astype(out.dtype)


def nothing_kernel(*refs):
    pass


def hand_on(array, *after):
    return in_vmem(nothing_kernel, [(array.shape, array.dtype)], aliases={0: 0})(array, *after)


def far_rows_kernel(slots, *refs):
    core = core_of()
    parts, outs = refs[:2], refs[-2:]
    for dz, part in enumerate(parts):
        for dx in range(2):
            for i in range(2):
                first = i * CORES * slots
                for who, out in zip((core, 1 - core), outs):
                    out[i, 2 * dz + dx] = part[dx, at_rows(first + who * slots, slots), :]


def owner_rows_kernel(slots, *refs):
    core = core_of()
    enc = lax.axis_index("enc")
    parts, far, outs = refs[:2], refs[2:4], refs[4:]
    for dz, part in enumerate(parts):
        for dx in range(2):
            d = 2 * dz + dx
            for i in range(2):
                first = i * CORES * slots
                for who, from_far, out in zip((core, 1 - core), far, outs):
                    out[i, enc ^ d] = part[dx, at_rows(first + who * slots, slots), :]
                    out[i, enc ^ (2 * len(parts) + d)] = from_far[i, d]


def finish_kernel(mine, got, _, dk, dv, sems):
    core = core_of()
    pairs = []
    for half, ref in ((core, mine), (1 - core, got)):
        cols = at_cols(half * HALF_KCOLS, HALF_KCOLS, HALF_KCOLS)
        for i, out in enumerate((dk, dv)):
            pairs.append((ref.at[i], out.at[:, :, cols]))
    run_copies(pairs, sems)


def split_rows_kernel(whole, *refs):
    outs = refs[-DQ_PARTS:]
    rows = outs[0].shape[0]
    for i, out in enumerate(outs):
        out[...] = whole[i * rows : (i + 1) * rows, :]


def finish_text_kernel(mine, *refs):
    got, (out, token, sems) = refs[:-3], refs[-3:]
    core = core_of()
    token[...] = jnp.zeros_like(token)
    own_cols = at_cols(core * HALF_QCOLS, HALF_QCOLS, HALF_QCOLS)
    got_cols = at_cols((1 - core) * HALF_QCOLS, HALF_QCOLS, HALF_QCOLS)
    pairs = [(mine, out.at[0, :, own_cols])]
    rows = got[0].shape[0]
    for i, ref in enumerate(got):
        pairs.append((ref, out.at[0, i * rows : (i + 1) * rows, got_cols]))
    run_copies(pairs, sems)


def blocks_with(sample, q_own, got):
    tokens = q_own.shape[0] - SAMP_ROWS
    rows = (q_own[tokens : tokens + 1, :tokens], got[2 * tokens : 2 * tokens + 1, :tokens])
    rows = [row.astype(F32) for row in rows]
    wanted = sample.astype(F32)
    return rows, [jnp.max(jnp.where(row == wanted, 1.0, 0.0)) > 0.5 for row in rows]


def key_rows(kvs, block_rows, first, h):
    parts = []
    for kv in kvs:
        for at in range(first, kv.shape[0], 2 * block_rows):
            parts.append(kv[at : at + block_rows, h * HD : (h + 1) * HD])
    return jnp.concatenate(parts, axis=0)


def choose(flags, branch):
    for which in ((0, 1), (0,), (1,), ()):
        wants = [flags[t] if t in which else jnp.logical_not(flags[t]) for t in range(2)]

        @pl.when(wants[0] & wants[1])
        def _():
            branch(which)


def pass_kernel(role, n_blocks, n_kv, n_grads, where, bias, q_a, g_a, got, *rest):
    kvs, (ds_out, *grads) = rest[:n_kv], rest[-1 - n_grads :]
    sample = where()[0] ^ role
    tokens = g_a.shape[0]
    block_rows = SLOT_ROWS // n_blocks
    rows, present = blocks_with(sample, q_a, got)
    sources = ((q_a, 0, g_a, 0), (got, 0, got, tokens))

    def one_pass(which):
        if not which:
            for out in grads:
                out[...] = jnp.zeros_like(out)
            return
        mine = jnp.concatenate([rows[t] for t in which for _ in range(RATIO)], axis=1)
        mine = mine == sample.astype(F32)
        masks = bias[role]
        ones = jnp.ones((len(which) * RATIO * tokens, HD), BF16)

        def products(h):
            def stacked(part):
                parts = []
                for t in which:
                    ref, first = sources[t][part : part + 2]
                    for r in range(RATIO):
                        at = h * WIDE + r * HD
                        parts.append(ref[first : first + tokens, at : at + HD])
                return jnp.concatenate(parts, axis=0)

            q, g = stacked(0), stacked(2)
            k, v = (key_rows(kvs, block_rows, first, h) for first in (0, block_rows))
            s = lax.dot_general(
                jnp.concatenate([k, masks], axis=1),
                jnp.concatenate([q, ones], axis=1),
                NT,
                preferred_element_type=F32,
            )
            gp = lax.dot_general(v, g, NT, preferred_element_type=F32)
            return q, g, s, gp

        early = len(which) == 1
        ahead = products(0)
        for h in range(HALF_KV):
            q, g, s, gp = ahead
            if early and h + 1 < HALF_KV:
                ahead = products(h + 1)
            top = jnp.max(s, axis=0, keepdims=True)
            e = jnp.exp2((s - top) * (SCALE * LOG2E))
            total = jnp.sum(e, axis=0, keepdims=True)
            p = e * jnp.where(mine, 1.0 / total, 0.0)
            row_dot = jnp.sum(p * gp, axis=0, keepdims=True)
            ph = p.astype(BF16)
            ds = ph * (gp - row_dot).astype(BF16)
            dv = jnp.dot(ph, g, preferred_element_type=F32)
            dk = jnp.dot(ds, q, preferred_element_type=F32) * SCALE
            wide = RATIO * tokens
            for i, t in enumerate(which):
                ds_out[h, :, t * wide : (t + 1) * wide] = ds[:, i * wide : (i + 1) * wide]
            cols = slice(h * HD, (h + 1) * HD)
            for b in range(n_blocks):
                block = slice(b * block_rows, (b + 1) * block_rows)
                dx, at = block_place(b, len(grads))
                out, first = grads[dx], at * 2 * block_rows
                out[first : first + block_rows, cols] = dk[block].astype(out.dtype)
                out[first + block_rows : first + 2 * block_rows, cols] = dv[block].astype(out.dtype)
            if not early and h + 1 < HALF_KV:
                ahead = products(h + 1)

    choose(present, one_pass)


def dq_kernel(n_blocks, n_kv, where, q_a, got, *rest):
    keys = rest[:n_kv], rest[n_kv : 2 * n_kv]
    ds, dqs = rest[2 * n_kv : 2 * n_kv + 2], rest[-2:]
    tokens = dqs[0].shape[0]
    block_rows = SLOT_ROWS // n_blocks
    first = where()[0]
    present = [blocks_with(first ^ role, q_a, got)[1] for role in range(SAMP)]
    wide = RATIO * tokens
    for t, dq_ref in enumerate(dqs):

        def one_block(roles):
            for h in range(HALF_KV):
                total = 0.0
                for role in roles:
                    k = key_rows(keys[role], block_rows, 0, h)
                    part = ds[role][h, :, t * wide : (t + 1) * wide]
                    total += lax.dot_general(part, k, TN, preferred_element_type=F32)
                if roles:
                    for r in range(RATIO):
                        at = h * WIDE + r * HD
                        rows = total[r * tokens : (r + 1) * tokens] * SCALE
                        dq_ref[:, at : at + HD] = rows.astype(dq_ref.dtype)

        choose([present[role][t] for role in range(SAMP)], one_block)


def sample_pass(where, role, n_blocks, bias, text, kvs, grads, after=()):
    tokens = text[1].shape[0]
    ds = ((HALF_KV, SLOT_ROWS, CORES * RATIO * tokens), BF16)
    return in_vmem(
        functools.partial(pass_kernel, role, n_blocks, len(kvs), len(grads), where),
        [ds, *grads],
        flops=8 * tokens * WIDE * SLOT_ROWS * CORES * HALF_KV,
        moved=16 * 2**20,
    )(bias, *text, *kvs, *after)


def text_grads(where, n_blocks, text, keys, ds):
    tokens = text[1].shape[0]
    return in_vmem(
        functools.partial(dq_kernel, n_blocks, len(keys[0]), where),
        [((tokens, HALF_QCOLS), BF16)] * 2,
        flops=4 * tokens * WIDE * SLOT_ROWS * CORES * HALF_KV,
        moved=8 * 2**20,
    )(text[0], text[2], *keys[0], *keys[1], *ds)


def shards(n_ctx, n_enc, queries, d_out, text_sample, tiles, img_k, img_v):
    n_y = n_ctx // CORES
    slots = img_k.shape[1]
    tokens = queries.shape[1]
    swap_core = [(i, i ^ 1) for i in range(n_ctx)]
    near = n_y == SAMP and slots % 16 == 0 and n_enc == 8
    text_outs = [
        ((2 * tokens + SAMP_ROWS, HALF_QCOLS), BF16, IN_VMEM),
        ((tokens + SAMP_ROWS, HALF_QCOLS), BF16, IN_VMEM),
        ((tokens, HALF_QCOLS), BF16, IN_VMEM),
        ((SAMP, SLOT_ROWS, HD), BF16, IN_VMEM),
    ]

    def split_the_text(n_blocks, pieces, where):
        return local_call(
            functools.partial(split_text, n_blocks, pieces, where),
            [IN_HBM] * 4,
            text_outs,
            [
                pltpu.VMEM(text_sample.shape, jnp.int32),
                pltpu.VMEM(tiles.shape, jnp.int32),
                pltpu.SemaphoreType.DMA((6,)),
            ],
            moved=4 * 2**20,
        )(*in_hbm(queries, d_out, text_sample, tiles))

    if near:
        swap_y = [(i, (i + CORES) % n_ctx) for i in range(n_ctx)]
        n_z = n_enc // 2
        block_rows = 2 * CORES * slots
        pair = (2, block_rows, HALF_KCOLS)
        quarter = (2 * block_rows, HALF_KCOLS)
        whole = (SLOT_ROWS, HALF_KCOLS)
        kv_halves = (2, n_enc, slots, HALF_KCOLS)
        swap_x = [(i, i ^ 1) for i in range(n_enc)]
        swap_xy = [
            (i * n_enc + e, (i + CORES) % n_ctx * n_enc + (e ^ 1))
            for i in range(n_ctx)
            for e in range(n_enc)
        ]

        def along_z(part, dz):
            return lax.ppermute(part, "enc", [(i, i ^ (2 * dz)) for i in range(n_enc)]) if dz else part

        def along_x(part):
            return lax.ppermute(part, "enc", swap_x)

        def along_y(part):
            return lax.ppermute(part, "ctx", swap_y)

        def along_xy(part):
            return lax.ppermute(part, ("ctx", "enc"), swap_xy)

        mine, for_peer = local_call(
            split_kernel,
            [IN_HBM] * 2,
            [(kv_halves, BF16, IN_VMEM)] * 2,
            [pltpu.SemaphoreType.DMA((4,))],
        )(*in_hbm(img_k, img_v))
        text_peer, q_own, g_own, bias = split_the_text(n_enc, CORES, near_place)
        *carry, text_peer = in_vmem(
            functools.partial(carry_kernel, slots),
            [(pair, BF16)] * n_z + [(text_peer.shape, BF16)],
            aliases={2: n_z},
        )(mine, lax.ppermute(for_peer, "ctx", swap_core), text_peer)
        text = (q_own, g_own, lax.ppermute(text_peer, "ctx", swap_core))

        came = [along_z(part, dz) for dz, part in enumerate(carry)]
        own, far = [], []
        for z in (0, 2):
            here, beside = in_vmem(join_kernel, [(quarter, BF16)] * 2)(
                *came[z : z + 2], text[2], *far
            )
            own += [here, along_x(beside)]
            far += [along_y(here), along_xy(beside)]
        own_ds, own_here, *own_beside = sample_pass(
            near_place, 0, n_enc, bias, text, own, [(whole, F32)] + [(quarter, BF16)] * 2
        )
        far_ds, *far_grads = sample_pass(
            near_place, 1, n_enc, bias, text, far, [(quarter, BF16)] * 4, (own_here,)
        )
        dq = text_grads(near_place, n_enc, text, (own, far), (own_ds, far_ds))
        returned = [None] * n_z
        for z in (2, 0):
            here, beside = far_grads[z : z + 2]
            (own_part,) = hand_on(own_beside[z // 2], far_ds)
            back_y, back_xy, back_x = along_y(here), along_xy(beside), along_x(own_part)
            totals = in_vmem(functools.partial(add_kernel, z), [(pair, BF16)] * 2)(
                own_here, back_y, back_xy, back_x
            )
            for dz, total in enumerate(totals, z):
                returned[dz] = along_z(total, dz)
            if z:
                sent = totals[0]
        dq_parts = in_vmem(split_rows_kernel, [((tokens // DQ_PARTS, HALF_QCOLS), BF16)] * DQ_PARTS)(
            dq[1], sent, totals[0]
        )
        dq_got = [lax.ppermute(part, "ctx", swap_core) for part in dq_parts]
    else:
        both = ("ctx", "enc")
        same_y = [
            [yy * CORES * n_enc + i for i in range(CORES * n_enc)] for yy in range(n_y)
        ]
        same_column = [
            [(yy * CORES + c) * n_enc + e for yy in range(n_y)]
            for c in range(CORES)
            for e in range(n_enc)
        ]
        core = core_of()

        def exchange(parts):
            return lax.all_to_all(
                parts, both, split_axis=0, concat_axis=0, axis_index_groups=same_y, tiled=True
            )

        def to_groups(owned):
            parts = owned.reshape(n_enc, slots, CORES, HALF_KCOLS).transpose(2, 0, 1, 3)
            got = exchange(parts.reshape(CORES * n_enc, slots, HALF_KCOLS))
            got = got.reshape(CORES * n_enc * slots, HALF_KCOLS)
            return lax.all_gather(got, both, axis=0, axis_index_groups=same_column, tiled=True)

        def to_owners(grads):
            grads = lax.psum_scatter(
                grads, both, scatter_dimension=0, axis_index_groups=same_column, tiled=True
            )
            got = exchange(grads.reshape(CORES * n_enc, slots, HALF_KCOLS))
            got = got.reshape(CORES, n_enc, slots, HALF_KCOLS).transpose(1, 2, 0, 3)
            return got.reshape(n_enc, slots, CORES * HALF_KCOLS)

        def no_place():
            return jnp.int32(0), jnp.int32(0)

        all_k = to_groups(img_k)
        all_v = to_groups(img_v)
        text_peer, q_own, g_own, bias = split_the_text(1, 1, no_place)
        text = (q_own, g_own, lax.ppermute(text_peer, "ctx", swap_core))
        kvs = [
            jnp.concatenate([part[s * SLOT_ROWS : (s + 1) * SLOT_ROWS] for part in (all_k, all_v)], axis=0)
            for s in range(SAMP)
        ]
        all_ds, grads = [], []
        for sample, kv in enumerate(kvs):
            ds, grad = sample_pass(no_place, sample, 1, bias, text, [kv], [(kv.shape, BF16)])
            all_ds.append(ds)
            grads.append(grad)
        dq = text_grads(no_place, 1, text, [[kv] for kv in kvs], all_ds)
        d_img_k = to_owners(jnp.concatenate([g[:SLOT_ROWS] for g in grads], axis=0))
        d_img_v = to_owners(jnp.concatenate([g[SLOT_ROWS:] for g in grads], axis=0))
        dq_got = [lax.ppermute(dq[1], "ctx", swap_core)]

    d_queries, token = local_call(
        finish_text_kernel,
        [IN_VMEM] * (1 + len(dq_got)),
        [(queries.shape, BF16, IN_HBM), ((8, HD), F32, IN_VMEM)],
        [pltpu.SemaphoreType.DMA((1 + len(dq_got),))],
    )(dq[0], *dq_got)
    if near:
        far_rows = in_vmem(
            functools.partial(far_rows_kernel, slots),
            [((2, n_enc // 2, slots, HALF_KCOLS), BF16)] * 2,
        )(*returned[2:])
        mine, for_peer = in_vmem(
            functools.partial(owner_rows_kernel, slots),
            [(kv_halves, BF16)] * 2,
        )(*returned[:2], *far_rows)
        d_img_k, d_img_v = local_call(
            finish_kernel,
            [IN_VMEM] * 3,
            [(img_k.shape, BF16, IN_HBM)] * 2,
            [pltpu.SemaphoreType.DMA((4,))],
        )(mine, lax.ppermute(for_peer, "ctx", swap_core), token)
    return (d_queries, d_img_k, d_img_v)


def solution(mesh):
    in_specs = (
        P("enc", "ctx", None),
        P("enc", "ctx", None),
        P("enc", "ctx"),
        P("enc", None),
        P(None, ("ctx", "enc"), None),
        P(None, ("ctx", "enc"), None),
    )
    out_specs = (
        P("enc", "ctx", None),
        P(None, ("ctx", "enc"), None),
        P(None, ("ctx", "enc"), None),
    )
    body = functools.partial(shards, mesh.shape["ctx"], mesh.shape["enc"])
    return jax.shard_map(body, mesh=mesh, in_specs=in_specs, out_specs=out_specs, check_vma=False)
```

```python
import functools

import jax
import jax.numpy as jnp
from jax import lax
from jax.experimental import pallas as pl
from jax.experimental.pallas import tpu as pltpu
from jax.sharding import PartitionSpec as P

H = 32
KVH = 8
HD = 128
SAMP = 2
MAX_TILES = 4
TILE_TOK = 64
RATIO = H // KVH
CORES = 2
SLOT_ROWS = MAX_TILES * TILE_TOK
HALF_KV = KVH // CORES
HALF_KCOLS = HALF_KV * HD
HALF_QCOLS = HALF_KCOLS * RATIO
WIDE = RATIO * HD
SAMP_ROWS = 16
DQ_PARTS = 2
SCALE = HD ** (-0.5)
LOG2E = 1.4426950408889634
BIG_NEGATIVE = -1e30
NT = (((1,), (1,)), ((), ()))
TN = (((0,), (0,)), ((), ()))
BF16 = jnp.bfloat16
F32 = jnp.float32

IN_VMEM = pl.BlockSpec(memory_space=pltpu.VMEM)
IN_HBM = pl.BlockSpec(memory_space=pltpu.HBM)


def local_call(body, ins, outs, scratch=(), flops=0, moved=2**19, aliases={}):
    return pl.pallas_call(
        body,
        in_specs=ins,
        out_specs=[spec for _, _, spec in outs],
        out_shape=[jax.ShapeDtypeStruct(s, d) for s, d, _ in outs],
        scratch_shapes=list(scratch),
        compiler_params=pltpu.CompilerParams(vmem_limit_bytes=8 * 2**20),
        input_output_aliases=aliases,
        cost_estimate=pl.CostEstimate(
            flops=flops, bytes_accessed=moved, transcendentals=flops // 1280
        ),
    )


def in_vmem(body, outs, **more):
    def call(*args):
        spec = [(shape, dtype, IN_VMEM) for shape, dtype in outs]
        return local_call(body, [IN_VMEM] * len(args), spec, **more)(*args)

    return call


def core_of():
    return lax.rem(lax.axis_index("ctx"), CORES)


def at_rows(first, count):
    return pl.ds(pl.multiple_of(first, count), count)


def at_cols(first, width, step):
    return pl.ds(pl.multiple_of(first, step), width)


def start_copies(pairs, sems):
    copies = [pltpu.make_async_copy(src, dst, sems.at[i]) for i, (src, dst) in enumerate(pairs)]
    for copy in copies:
        copy.start()
    return copies


def run_copies(pairs, sems):
    for copy in start_copies(pairs, sems):
        copy.wait()


def in_hbm(*arrays):
    return [pltpu.with_memory_space_constraint(a, pltpu.HBM) for a in arrays]


def split_kernel(k_ref, v_ref, mine, peer, sems):
    core = core_of()
    pairs = []
    for half, out in ((1 - core, peer), (core, mine)):
        cols = at_cols(half * HALF_KCOLS, HALF_KCOLS, HALF_KCOLS)
        for i, ref in enumerate((k_ref, v_ref)):
            pairs.append((ref.at[:, :, cols], out.at[i]))
    run_copies(pairs, sems)


def near_place():
    return lax.div(lax.axis_index("ctx"), CORES), lax.axis_index("enc")


def split_text(n_blocks, pieces, where, q_ref, g_ref, samp_hbm, tiles_hbm, peer, q_own, g_own, bias, samp, tiles, sems):
    core = core_of()
    tokens = q_ref.shape[1]
    own_cols = at_cols(core * HALF_QCOLS, HALF_QCOLS, HALF_QCOLS)
    peer_cols = at_cols((1 - core) * HALF_QCOLS, HALF_QCOLS, HALF_QCOLS)
    copies = start_copies(
        [
            (samp_hbm, samp),
            (tiles_hbm, tiles),
            (q_ref.at[0, :, peer_cols], peer.at[:tokens]),
            (g_ref.at[0, :, peer_cols], peer.at[tokens : 2 * tokens]),
            (q_ref.at[0, :, own_cols], q_own.at[:tokens]),
            (g_ref.at[0, :, own_cols], g_own),
        ],
        sems,
    )
    for copy in copies[:2]:
        copy.wait()
    row = jnp.broadcast_to(samp[...].astype(F32), (SAMP_ROWS, tokens)).astype(BF16)
    for out, first in ((q_own, tokens), (peer, 2 * tokens)):
        out[first:, :] = jnp.zeros((SAMP_ROWS, HALF_QCOLS), BF16)
        out[first:, :tokens] = row

    sample, enc = where()
    block_rows = SLOT_ROWS // n_blocks
    slots = block_rows // pieces
    line = lax.broadcasted_iota(jnp.int32, (SLOT_ROWS, HD), 0)
    block = lax.div(line, block_rows)
    if n_blocks > 1:
        low, high = block & 1, lax.div(block, 2) & 1
        block = block - low - 2 * high + 2 * low + high
    owner = block ^ enc
    piece = lax.rem(lax.div(line, slots), pieces)
    slot = piece * (SLOT_ROWS // pieces) + owner * slots + lax.rem(line, slots)
    for i in range(SAMP):
        count = jnp.where((sample ^ i) == 0, tiles[0:1, 0:1], tiles[0:1, 1:2])
        masked = jnp.where(slot < count * TILE_TOK, 0.0, BIG_NEGATIVE)
        first = lax.broadcasted_iota(jnp.int32, masked.shape, 1) == 0
        bias[i] = jnp.where(first, masked, 0.0).astype(BF16)
    for copy in copies[2:]:
        copy.wait()


def carry_kernel(slots, own, got, text, *outs):
    core = core_of()
    enc = lax.axis_index("enc")
    for dz, out in enumerate(outs[:-1]):
        for dx in range(2):
            group = enc ^ (2 * dz + dx)
            for i in range(2):
                first = i * CORES * slots
                out[dx, at_rows(first + core * slots, slots), :] = own[i, group]
                out[dx, at_rows(first + (1 - core) * slots, slots), :] = got[i, group]


def join_kernel(*refs):
    parts, outs = refs[:2], refs[-2:]
    rows = parts[0].shape[1]
    for dx, out in enumerate(outs):
        for dz, part in enumerate(parts):
            out[dz * rows : (dz + 1) * rows, :] = part[dx]


def block_place(b, n_outs):
    half, x, z = b // 4, b // 2 % 2, b % 2
    whole = 2 * half + z
    return {1: (0, b), 3: (1 + half, z) if x else (0, whole), 4: (2 * half + x, z)}[n_outs]


def add_kernel(z, own, back_y, back_xy, back_x, *outs):
    rows = outs[0].shape[1]
    for dz, out in enumerate(outs):
        whole = slice((z + dz) * rows, (z + dz + 1) * rows)
        part = slice(dz * rows, (dz + 1) * rows)
        out[0] = (own[whole, :] + back_y[part, :].astype(F32)).astype(out.dtype)
        out[1] = (back_x[part, :].astype(F32) + back_xy[part, :].astype(F32)).astype(out.dtype)


def nothing_kernel(*refs):
    pass


def hand_on(array, *after):
    return in_vmem(nothing_kernel, [(array.shape, array.dtype)], aliases={0: 0})(array, *after)


def far_rows_kernel(slots, *refs):
    core = core_of()
    parts, outs = refs[:2], refs[-2:]
    for dz, part in enumerate(parts):
        for dx in range(2):
            for i in range(2):
                first = i * CORES * slots
                for who, out in zip((core, 1 - core), outs):
                    out[i, 2 * dz + dx] = part[dx, at_rows(first + who * slots, slots), :]


def owner_rows_kernel(slots, *refs):
    core = core_of()
    enc = lax.axis_index("enc")
    parts, far, outs = refs[:2], refs[2:4], refs[4:]
    for dz, part in enumerate(parts):
        for dx in range(2):
            d = 2 * dz + dx
            for i in range(2):
                first = i * CORES * slots
                for who, from_far, out in zip((core, 1 - core), far, outs):
                    out[i, enc ^ d] = part[dx, at_rows(first + who * slots, slots), :]
                    out[i, enc ^ (2 * len(parts) + d)] = from_far[i, d]


def finish_kernel(mine, got, _, dk, dv, sems):
    core = core_of()
    pairs = []
    for half, ref in ((core, mine), (1 - core, got)):
        cols = at_cols(half * HALF_KCOLS, HALF_KCOLS, HALF_KCOLS)
        for i, out in enumerate((dk, dv)):
            pairs.append((ref.at[i], out.at[:, :, cols]))
    run_copies(pairs, sems)


def split_rows_kernel(whole, *refs):
    outs = refs[-DQ_PARTS:]
    rows = outs[0].shape[0]
    for i, out in enumerate(outs):
        out[...] = whole[i * rows : (i + 1) * rows, :]


def finish_text_kernel(mine, *refs):
    got, (out, token, sems) = refs[:-3], refs[-3:]
    core = core_of()
    token[...] = jnp.zeros_like(token)
    own_cols = at_cols(core * HALF_QCOLS, HALF_QCOLS, HALF_QCOLS)
    got_cols = at_cols((1 - core) * HALF_QCOLS, HALF_QCOLS, HALF_QCOLS)
    pairs = [(mine, out.at[0, :, own_cols])]
    rows = got[0].shape[0]
    for i, ref in enumerate(got):
        pairs.append((ref, out.at[0, i * rows : (i + 1) * rows, got_cols]))
    run_copies(pairs, sems)


def blocks_with(sample, q_own, got):
    tokens = q_own.shape[0] - SAMP_ROWS
    rows = (q_own[tokens : tokens + 1, :tokens], got[2 * tokens : 2 * tokens + 1, :tokens])
    rows = [row.astype(F32) for row in rows]
    wanted = sample.astype(F32)
    return rows, [jnp.max(jnp.where(row == wanted, 1.0, 0.0)) > 0.5 for row in rows]


def key_rows(kvs, block_rows, first, h):
    parts = []
    for kv in kvs:
        for at in range(first, kv.shape[0], 2 * block_rows):
            parts.append(kv[at : at + block_rows, h * HD : (h + 1) * HD])
    return jnp.concatenate(parts, axis=0)


def choose(flags, branch):
    for which in ((0, 1), (0,), (1,), ()):
        wants = [flags[t] if t in which else jnp.logical_not(flags[t]) for t in range(2)]

        @pl.when(wants[0] & wants[1])
        def _():
            branch(which)


def pass_kernel(role, n_blocks, n_kv, n_grads, where, bias, q_a, g_a, got, *rest):
    kvs, (ds_out, *grads) = rest[:n_kv], rest[-1 - n_grads :]
    sample = where()[0] ^ role
    tokens = g_a.shape[0]
    block_rows = SLOT_ROWS // n_blocks
    rows, present = blocks_with(sample, q_a, got)
    sources = ((q_a, 0, g_a, 0), (got, 0, got, tokens))

    def one_pass(which):
        if not which:
            for out in grads:
                out[...] = jnp.zeros_like(out)
            return
        mine = jnp.concatenate([rows[t] for t in which for _ in range(RATIO)], axis=1)
        mine = mine == sample.astype(F32)
        masks = bias[role]
        ones = jnp.ones((len(which) * RATIO * tokens, HD), BF16)

        def products(h):
            def stacked(part):
                parts = []
                for t in which:
                    ref, first = sources[t][part : part + 2]
                    for r in range(RATIO):
                        at = h * WIDE + r * HD
                        parts.append(ref[first : first + tokens, at : at + HD])
                return jnp.concatenate(parts, axis=0)

            q, g = stacked(0), stacked(2)
            k, v = (key_rows(kvs, block_rows, first, h) for first in (0, block_rows))
            s = lax.dot_general(
                jnp.concatenate([k, masks], axis=1),
                jnp.concatenate([q, ones], axis=1),
                NT,
                preferred_element_type=F32,
            )
            gp = lax.dot_general(v, g, NT, preferred_element_type=F32)
            return q, g, s, gp

        ahead = products(0)
        for h in range(HALF_KV):
            q, g, s, gp = ahead
            if h + 1 < HALF_KV:
                ahead = products(h + 1)
            top = jnp.max(s, axis=0, keepdims=True)
            e = jnp.exp2((s - top) * (SCALE * LOG2E))
            total = jnp.sum(e, axis=0, keepdims=True)
            p = e * jnp.where(mine, 1.0 / total, 0.0)
            row_dot = jnp.sum(p * gp, axis=0, keepdims=True)
            ph = p.astype(BF16)
            ds = ph * (gp - row_dot).astype(BF16)
            dv = jnp.dot(ph, g, preferred_element_type=F32)
            dk = jnp.dot(ds, q, preferred_element_type=F32) * SCALE
            wide = RATIO * tokens
            for i, t in enumerate(which):
                ds_out[h, :, t * wide : (t + 1) * wide] = ds[:, i * wide : (i + 1) * wide]
            cols = slice(h * HD, (h + 1) * HD)
            for b in range(n_blocks):
                block = slice(b * block_rows, (b + 1) * block_rows)
                dx, at = block_place(b, len(grads))
                out, first = grads[dx], at * 2 * block_rows
                out[first : first + block_rows, cols] = dk[block].astype(out.dtype)
                out[first + block_rows : first + 2 * block_rows, cols] = dv[block].astype(out.dtype)

    choose(present, one_pass)


def dq_kernel(n_blocks, n_kv, where, q_a, got, *rest):
    keys = rest[:n_kv], rest[n_kv : 2 * n_kv]
    ds, dqs = rest[2 * n_kv : 2 * n_kv + 2], rest[-2:]
    tokens = dqs[0].shape[0]
    block_rows = SLOT_ROWS // n_blocks
    first = where()[0]
    present = [blocks_with(first ^ role, q_a, got)[1] for role in range(SAMP)]
    wide = RATIO * tokens
    for t, dq_ref in enumerate(dqs):

        def one_block(roles):
            for h in range(HALF_KV):
                total = 0.0
                for role in roles:
                    k = key_rows(keys[role], block_rows, 0, h)
                    part = ds[role][h, :, t * wide : (t + 1) * wide]
                    total += lax.dot_general(part, k, TN, preferred_element_type=F32)
                if roles:
                    for r in range(RATIO):
                        at = h * WIDE + r * HD
                        rows = total[r * tokens : (r + 1) * tokens] * SCALE
                        dq_ref[:, at : at + HD] = rows.astype(dq_ref.dtype)

        choose([present[role][t] for role in range(SAMP)], one_block)


def sample_pass(where, role, n_blocks, bias, text, kvs, grads, after=()):
    tokens = text[1].shape[0]
    ds = ((HALF_KV, SLOT_ROWS, CORES * RATIO * tokens), BF16)
    return in_vmem(
        functools.partial(pass_kernel, role, n_blocks, len(kvs), len(grads), where),
        [ds, *grads],
        flops=8 * tokens * WIDE * SLOT_ROWS * CORES * HALF_KV,
        moved=16 * 2**20,
    )(bias, *text, *kvs, *after)


def text_grads(where, n_blocks, text, keys, ds):
    tokens = text[1].shape[0]
    return in_vmem(
        functools.partial(dq_kernel, n_blocks, len(keys[0]), where),
        [((tokens, HALF_QCOLS), BF16)] * 2,
        flops=4 * tokens * WIDE * SLOT_ROWS * CORES * HALF_KV,
        moved=8 * 2**20,
    )(text[0], text[2], *keys[0], *keys[1], *ds)


def shards(n_ctx, n_enc, queries, d_out, text_sample, tiles, img_k, img_v):
    n_y = n_ctx // CORES
    slots = img_k.shape[1]
    tokens = queries.shape[1]
    swap_core = [(i, i ^ 1) for i in range(n_ctx)]
    near = n_y == SAMP and slots % 16 == 0 and n_enc == 8
    text_outs = [
        ((2 * tokens + SAMP_ROWS, HALF_QCOLS), BF16, IN_VMEM),
        ((tokens + SAMP_ROWS, HALF_QCOLS), BF16, IN_VMEM),
        ((tokens, HALF_QCOLS), BF16, IN_VMEM),
        ((SAMP, SLOT_ROWS, HD), BF16, IN_VMEM),
    ]

    def split_the_text(n_blocks, pieces, where):
        return local_call(
            functools.partial(split_text, n_blocks, pieces, where),
            [IN_HBM] * 4,
            text_outs,
            [
                pltpu.VMEM(text_sample.shape, jnp.int32),
                pltpu.VMEM(tiles.shape, jnp.int32),
                pltpu.SemaphoreType.DMA((6,)),
            ],
            moved=4 * 2**20,
        )(*in_hbm(queries, d_out, text_sample, tiles))

    if near:
        swap_y = [(i, (i + CORES) % n_ctx) for i in range(n_ctx)]
        n_z = n_enc // 2
        block_rows = 2 * CORES * slots
        pair = (2, block_rows, HALF_KCOLS)
        quarter = (2 * block_rows, HALF_KCOLS)
        whole = (SLOT_ROWS, HALF_KCOLS)
        kv_halves = (2, n_enc, slots, HALF_KCOLS)
        swap_x = [(i, i ^ 1) for i in range(n_enc)]
        swap_xy = [
            (i * n_enc + e, (i + CORES) % n_ctx * n_enc + (e ^ 1))
            for i in range(n_ctx)
            for e in range(n_enc)
        ]

        def along_z(part, dz):
            return lax.ppermute(part, "enc", [(i, i ^ (2 * dz)) for i in range(n_enc)]) if dz else part

        def along_x(part):
            return lax.ppermute(part, "enc", swap_x)

        def along_y(part):
            return lax.ppermute(part, "ctx", swap_y)

        def along_xy(part):
            return lax.ppermute(part, ("ctx", "enc"), swap_xy)

        mine, for_peer = local_call(
            split_kernel,
            [IN_HBM] * 2,
            [(kv_halves, BF16, IN_VMEM)] * 2,
            [pltpu.SemaphoreType.DMA((4,))],
        )(*in_hbm(img_k, img_v))
        text_peer, q_own, g_own, bias = split_the_text(n_enc, CORES, near_place)
        *carry, text_peer = in_vmem(
            functools.partial(carry_kernel, slots),
            [(pair, BF16)] * n_z + [(text_peer.shape, BF16)],
            aliases={2: n_z},
        )(mine, lax.ppermute(for_peer, "ctx", swap_core), text_peer)
        text = (q_own, g_own, lax.ppermute(text_peer, "ctx", swap_core))

        came = [along_z(part, dz) for dz, part in enumerate(carry)]
        own, far = [], []
        for z in (0, 2):
            here, beside = in_vmem(join_kernel, [(quarter, BF16)] * 2)(
                *came[z : z + 2], text[2], *far
            )
            own += [here, along_x(beside)]
            far += [along_y(here), along_xy(beside)]
        own_ds, own_here, *own_beside = sample_pass(
            near_place, 0, n_enc, bias, text, own, [(whole, F32)] + [(quarter, BF16)] * 2
        )
        far_ds, *far_grads = sample_pass(
            near_place, 1, n_enc, bias, text, far, [(quarter, BF16)] * 4, (own_here,)
        )
        dq = text_grads(near_place, n_enc, text, (own, far), (own_ds, far_ds))
        returned = [None] * n_z
        for z in (2, 0):
            here, beside = far_grads[z : z + 2]
            (own_part,) = hand_on(own_beside[z // 2], far_ds)
            back_y, back_xy, back_x = along_y(here), along_xy(beside), along_x(own_part)
            totals = in_vmem(functools.partial(add_kernel, z), [(pair, BF16)] * 2)(
                own_here, back_y, back_xy, back_x
            )
            for dz, total in enumerate(totals, z):
                returned[dz] = along_z(total, dz)
            if z:
                sent = totals[0]
        dq_parts = in_vmem(split_rows_kernel, [((tokens // DQ_PARTS, HALF_QCOLS), BF16)] * DQ_PARTS)(
            dq[1], sent, totals[0]
        )
        dq_got = [lax.ppermute(part, "ctx", swap_core) for part in dq_parts]
    else:
        both = ("ctx", "enc")
        same_y = [
            [yy * CORES * n_enc + i for i in range(CORES * n_enc)] for yy in range(n_y)
        ]
        same_column = [
            [(yy * CORES + c) * n_enc + e for yy in range(n_y)]
            for c in range(CORES)
            for e in range(n_enc)
        ]
        core = core_of()

        def exchange(parts):
            return lax.all_to_all(
                parts, both, split_axis=0, concat_axis=0, axis_index_groups=same_y, tiled=True
            )

        def to_groups(owned):
            parts = owned.reshape(n_enc, slots, CORES, HALF_KCOLS).transpose(2, 0, 1, 3)
            got = exchange(parts.reshape(CORES * n_enc, slots, HALF_KCOLS))
            got = got.reshape(CORES * n_enc * slots, HALF_KCOLS)
            return lax.all_gather(got, both, axis=0, axis_index_groups=same_column, tiled=True)

        def to_owners(grads):
            grads = lax.psum_scatter(
                grads, both, scatter_dimension=0, axis_index_groups=same_column, tiled=True
            )
            got = exchange(grads.reshape(CORES * n_enc, slots, HALF_KCOLS))
            got = got.reshape(CORES, n_enc, slots, HALF_KCOLS).transpose(1, 2, 0, 3)
            return got.reshape(n_enc, slots, CORES * HALF_KCOLS)

        def no_place():
            return jnp.int32(0), jnp.int32(0)

        all_k = to_groups(img_k)
        all_v = to_groups(img_v)
        text_peer, q_own, g_own, bias = split_the_text(1, 1, no_place)
        text = (q_own, g_own, lax.ppermute(text_peer, "ctx", swap_core))
        kvs = [
            jnp.concatenate([part[s * SLOT_ROWS : (s + 1) * SLOT_ROWS] for part in (all_k, all_v)], axis=0)
            for s in range(SAMP)
        ]
        all_ds, grads = [], []
        for sample, kv in enumerate(kvs):
            ds, grad = sample_pass(no_place, sample, 1, bias, text, [kv], [(kv.shape, BF16)])
            all_ds.append(ds)
            grads.append(grad)
        dq = text_grads(no_place, 1, text, [[kv] for kv in kvs], all_ds)
        d_img_k = to_owners(jnp.concatenate([g[:SLOT_ROWS] for g in grads], axis=0))
        d_img_v = to_owners(jnp.concatenate([g[SLOT_ROWS:] for g in grads], axis=0))
        dq_got = [lax.ppermute(dq[1], "ctx", swap_core)]

    d_queries, token = local_call(
        finish_text_kernel,
        [IN_VMEM] * (1 + len(dq_got)),
        [(queries.shape, BF16, IN_HBM), ((8, HD), F32, IN_VMEM)],
        [pltpu.SemaphoreType.DMA((1 + len(dq_got),))],
    )(dq[0], *dq_got)
    if near:
        far_rows = in_vmem(
            functools.partial(far_rows_kernel, slots),
            [((2, n_enc // 2, slots, HALF_KCOLS), BF16)] * 2,
        )(*returned[2:])
        mine, for_peer = in_vmem(
            functools.partial(owner_rows_kernel, slots),
            [(kv_halves, BF16)] * 2,
        )(*returned[:2], *far_rows)
        d_img_k, d_img_v = local_call(
            finish_kernel,
            [IN_VMEM] * 3,
            [(img_k.shape, BF16, IN_HBM)] * 2,
            [pltpu.SemaphoreType.DMA((4,))],
        )(mine, lax.ppermute(for_peer, "ctx", swap_core), token)
    return (d_queries, d_img_k, d_img_v)


def solution(mesh):
    in_specs = (
        P("enc", "ctx", None),
        P("enc", "ctx", None),
        P("enc", "ctx"),
        P("enc", None),
        P(None, ("ctx", "enc"), None),
        P(None, ("ctx", "enc"), None),
    )
    out_specs = (
        P("enc", "ctx", None),
        P(None, ("ctx", "enc"), None),
        P(None, ("ctx", "enc"), None),
    )
    body = functools.partial(shards, mesh.shape["ctx"], mesh.shape["enc"])
    return jax.shard_map(body, mesh=mesh, in_specs=in_specs, out_specs=out_specs, check_vma=False)
```

```python
import functools

import jax
import jax.numpy as jnp
from jax import lax
from jax.experimental import pallas as pl
from jax.experimental.pallas import tpu as pltpu
from jax.sharding import PartitionSpec as P

H = 32
KVH = 8
HD = 128
SAMP = 2
MAX_TILES = 4
TILE_TOK = 64
RATIO = H // KVH
CORES = 2
SLOT_ROWS = MAX_TILES * TILE_TOK
HALF_KV = KVH // CORES
HALF_KCOLS = HALF_KV * HD
HALF_QCOLS = HALF_KCOLS * RATIO
WIDE = RATIO * HD
SAMP_ROWS = 16
DQ_PARTS = 2
SCALE = HD ** (-0.5)
LOG2E = 1.4426950408889634
BIG_NEGATIVE = -1e30
NT = (((1,), (1,)), ((), ()))
TN = (((0,), (0,)), ((), ()))
BF16 = jnp.bfloat16
F32 = jnp.float32

IN_VMEM = pl.BlockSpec(memory_space=pltpu.VMEM)
IN_HBM = pl.BlockSpec(memory_space=pltpu.HBM)


def local_call(body, ins, outs, scratch=(), flops=0, moved=2**19, aliases={}):
    return pl.pallas_call(
        body,
        in_specs=ins,
        out_specs=[spec for _, _, spec in outs],
        out_shape=[jax.ShapeDtypeStruct(s, d) for s, d, _ in outs],
        scratch_shapes=list(scratch),
        compiler_params=pltpu.CompilerParams(vmem_limit_bytes=8 * 2**20),
        input_output_aliases=aliases,
        cost_estimate=pl.CostEstimate(
            flops=flops, bytes_accessed=moved, transcendentals=flops // 1280
        ),
    )


def in_vmem(body, outs, **more):
    def call(*args):
        spec = [(shape, dtype, IN_VMEM) for shape, dtype in outs]
        return local_call(body, [IN_VMEM] * len(args), spec, **more)(*args)

    return call


def core_of():
    return lax.rem(lax.axis_index("ctx"), CORES)


def at_rows(first, count):
    return pl.ds(pl.multiple_of(first, count), count)


def at_cols(first, width, step):
    return pl.ds(pl.multiple_of(first, step), width)


def start_copies(pairs, sems):
    copies = [pltpu.make_async_copy(src, dst, sems.at[i]) for i, (src, dst) in enumerate(pairs)]
    for copy in copies:
        copy.start()
    return copies


def run_copies(pairs, sems):
    for copy in start_copies(pairs, sems):
        copy.wait()


def in_hbm(*arrays):
    return [pltpu.with_memory_space_constraint(a, pltpu.HBM) for a in arrays]


def split_kernel(k_ref, v_ref, mine, peer, sems):
    core = core_of()
    pairs = []
    for half, out in ((1 - core, peer), (core, mine)):
        cols = at_cols(half * HALF_KCOLS, HALF_KCOLS, HALF_KCOLS)
        for i, ref in enumerate((k_ref, v_ref)):
            pairs.append((ref.at[:, :, cols], out.at[i]))
    run_copies(pairs, sems)


def near_place():
    return lax.div(lax.axis_index("ctx"), CORES), lax.axis_index("enc")


def split_text(n_blocks, pieces, where, q_ref, g_ref, samp_hbm, tiles_hbm, peer, q_own, g_own, bias, samp, tiles, sems):
    core = core_of()
    tokens = q_ref.shape[1]
    own_cols = at_cols(core * HALF_QCOLS, HALF_QCOLS, HALF_QCOLS)
    peer_cols = at_cols((1 - core) * HALF_QCOLS, HALF_QCOLS, HALF_QCOLS)
    copies = start_copies(
        [
            (samp_hbm, samp),
            (tiles_hbm, tiles),
            (q_ref.at[0, :, peer_cols], peer.at[:tokens]),
            (g_ref.at[0, :, peer_cols], peer.at[tokens : 2 * tokens]),
            (q_ref.at[0, :, own_cols], q_own.at[:tokens]),
            (g_ref.at[0, :, own_cols], g_own),
        ],
        sems,
    )
    for copy in copies[:2]:
        copy.wait()
    row = jnp.broadcast_to(samp[...].astype(F32), (SAMP_ROWS, tokens)).astype(BF16)
    for out, first in ((q_own, tokens), (peer, 2 * tokens)):
        out[first:, :] = jnp.zeros((SAMP_ROWS, HALF_QCOLS), BF16)
        out[first:, :tokens] = row

    sample, enc = where()
    block_rows = SLOT_ROWS // n_blocks
    slots = block_rows // pieces
    line = lax.broadcasted_iota(jnp.int32, (SLOT_ROWS, HD), 0)
    block = lax.div(line, block_rows)
    if n_blocks > 1:
        low, high = block & 1, lax.div(block, 2) & 1
        block = block - low - 2 * high + 2 * low + high
    owner = block ^ enc
    piece = lax.rem(lax.div(line, slots), pieces)
    slot = piece * (SLOT_ROWS // pieces) + owner * slots + lax.rem(line, slots)
    for i in range(SAMP):
        count = jnp.where((sample ^ i) == 0, tiles[0:1, 0:1], tiles[0:1, 1:2])
        masked = jnp.where(slot < count * TILE_TOK, 0.0, BIG_NEGATIVE)
        first = lax.broadcasted_iota(jnp.int32, masked.shape, 1) == 0
        bias[i] = jnp.where(first, masked, 0.0).astype(BF16)
    for copy in copies[2:]:
        copy.wait()


def carry_kernel(slots, own, got, text, *outs):
    core = core_of()
    enc = lax.axis_index("enc")
    for dz, out in enumerate(outs[:-1]):
        for dx in range(2):
            group = enc ^ (2 * dz + dx)
            for i in range(2):
                first = i * CORES * slots
                out[dx, at_rows(first + core * slots, slots), :] = own[i, group]
                out[dx, at_rows(first + (1 - core) * slots, slots), :] = got[i, group]


def join_kernel(*refs):
    parts, outs = refs[:2], refs[-2:]
    rows = parts[0].shape[1]
    for dx, out in enumerate(outs):
        for dz, part in enumerate(parts):
            out[dz * rows : (dz + 1) * rows, :] = part[dx]


def block_place(b, n_outs):
    half, x, z = b // 4, b // 2 % 2, b % 2
    whole = 2 * half + z
    return {1: (0, b), 3: (1 + half, z) if x else (0, whole), 4: (2 * half + x, z)}[n_outs]


def add_kernel(z, own, back_y, back_xy, back_x, *outs):
    rows = outs[0].shape[1]
    for dz, out in enumerate(outs):
        whole = slice((z + dz) * rows, (z + dz + 1) * rows)
        part = slice(dz * rows, (dz + 1) * rows)
        out[0] = (own[whole, :] + back_y[part, :].astype(F32)).astype(out.dtype)
        out[1] = (back_x[part, :].astype(F32) + back_xy[part, :].astype(F32)).astype(out.dtype)


def nothing_kernel(*refs):
    pass


def hand_on(array, *after):
    return in_vmem(nothing_kernel, [(array.shape, array.dtype)], aliases={0: 0})(array, *after)


def far_rows_kernel(slots, *refs):
    core = core_of()
    parts, outs = refs[:2], refs[-2:]
    for dz, part in enumerate(parts):
        for dx in range(2):
            for i in range(2):
                first = i * CORES * slots
                for who, out in zip((core, 1 - core), outs):
                    out[i, 2 * dz + dx] = part[dx, at_rows(first + who * slots, slots), :]


def owner_rows_kernel(slots, *refs):
    core = core_of()
    enc = lax.axis_index("enc")
    parts, far, outs = refs[:2], refs[2:4], refs[4:]
    for dz, part in enumerate(parts):
        for dx in range(2):
            d = 2 * dz + dx
            for i in range(2):
                first = i * CORES * slots
                for who, from_far, out in zip((core, 1 - core), far, outs):
                    out[i, enc ^ d] = part[dx, at_rows(first + who * slots, slots), :]
                    out[i, enc ^ (2 * len(parts) + d)] = from_far[i, d]


def finish_kernel(mine, got, _, dk, dv, sems):
    core = core_of()
    pairs = []
    for half, ref in ((core, mine), (1 - core, got)):
        cols = at_cols(half * HALF_KCOLS, HALF_KCOLS, HALF_KCOLS)
        for i, out in enumerate((dk, dv)):
            pairs.append((ref.at[i], out.at[:, :, cols]))
    run_copies(pairs, sems)


def split_rows_kernel(whole, *refs):
    outs = refs[-DQ_PARTS:]
    rows = outs[0].shape[0]
    for i, out in enumerate(outs):
        out[...] = whole[i * rows : (i + 1) * rows, :]


def finish_text_kernel(mine, *refs):
    got, (out, token, sems) = refs[:-3], refs[-3:]
    core = core_of()
    token[...] = jnp.zeros_like(token)
    own_cols = at_cols(core * HALF_QCOLS, HALF_QCOLS, HALF_QCOLS)
    got_cols = at_cols((1 - core) * HALF_QCOLS, HALF_QCOLS, HALF_QCOLS)
    pairs = [(mine, out.at[0, :, own_cols])]
    rows = got[0].shape[0]
    for i, ref in enumerate(got):
        pairs.append((ref, out.at[0, i * rows : (i + 1) * rows, got_cols]))
    run_copies(pairs, sems)


def blocks_with(sample, q_own, got):
    tokens = q_own.shape[0] - SAMP_ROWS
    rows = (q_own[tokens : tokens + 1, :tokens], got[2 * tokens : 2 * tokens + 1, :tokens])
    rows = [row.astype(F32) for row in rows]
    wanted = sample.astype(F32)
    return rows, [jnp.max(jnp.where(row == wanted, 1.0, 0.0)) > 0.5 for row in rows]


def key_rows(kvs, block_rows, first, h):
    parts = []
    for kv in kvs:
        for at in range(first, kv.shape[0], 2 * block_rows):
            parts.append(kv[at : at + block_rows, h * HD : (h + 1) * HD])
    return jnp.concatenate(parts, axis=0)


def choose(flags, branch):
    for which in ((0, 1), (0,), (1,), ()):
        wants = [flags[t] if t in which else jnp.logical_not(flags[t]) for t in range(2)]

        @pl.when(wants[0] & wants[1])
        def _():
            branch(which)


def pass_kernel(role, n_blocks, n_kv, n_grads, where, bias, q_a, g_a, got, *rest):
    kvs, (ds_out, *grads) = rest[:n_kv], rest[-1 - n_grads :]
    sample = where()[0] ^ role
    tokens = g_a.shape[0]
    block_rows = SLOT_ROWS // n_blocks
    rows, present = blocks_with(sample, q_a, got)
    sources = ((q_a, 0, g_a, 0), (got, 0, got, tokens))

    def one_pass(which):
        if not which:
            for out in grads:
                out[...] = jnp.zeros_like(out)
            return
        mine = jnp.concatenate([rows[t] for t in which for _ in range(RATIO)], axis=1)
        mine = mine == sample.astype(F32)
        masks = bias[role]
        ones = jnp.ones((len(which) * RATIO * tokens, HD), BF16)

        def products(h):
            def stacked(part):
                parts = []
                for t in which:
                    ref, first = sources[t][part : part + 2]
                    for r in range(RATIO):
                        at = h * WIDE + r * HD
                        parts.append(ref[first : first + tokens, at : at + HD])
                return jnp.concatenate(parts, axis=0)

            q, g = stacked(0), stacked(2)
            k, v = (key_rows(kvs, block_rows, first, h) for first in (0, block_rows))
            s = lax.dot_general(
                jnp.concatenate([k, masks], axis=1),
                jnp.concatenate([q, ones], axis=1),
                NT,
                preferred_element_type=F32,
            )
            gp = lax.dot_general(v, g, NT, preferred_element_type=F32)
            return q, g, s, gp

        ahead = products(0)
        for h in range(HALF_KV):
            q, g, s, gp = ahead
            if h + 1 < HALF_KV:
                ahead = products(h + 1)
            top = jnp.max(s, axis=0, keepdims=True)
            e = jnp.exp2((s - top) * (SCALE * LOG2E))
            total = jnp.sum(e, axis=0, keepdims=True)
            p = e * jnp.where(mine, 1.0 / total, 0.0)
            row_dot = jnp.sum(p * gp, axis=0, keepdims=True)
            ph = p.astype(BF16)
            ds = ph * (gp - row_dot).astype(BF16)
            dv = jnp.dot(ph, g, preferred_element_type=F32)
            dk = jnp.dot(ds, q, preferred_element_type=F32) * SCALE
            wide = RATIO * tokens
            for i, t in enumerate(which):
                ds_out[h, :, t * wide : (t + 1) * wide] = ds[:, i * wide : (i + 1) * wide]
            cols = slice(h * HD, (h + 1) * HD)
            for b in range(n_blocks):
                block = slice(b * block_rows, (b + 1) * block_rows)
                dx, at = block_place(b, len(grads))
                out, first = grads[dx], at * 2 * block_rows
                out[first : first + block_rows, cols] = dk[block].astype(out.dtype)
                out[first + block_rows : first + 2 * block_rows, cols] = dv[block].astype(out.dtype)

    choose(present, one_pass)


def dq_kernel(n_blocks, n_kv, where, q_a, got, *rest):
    keys = rest[:n_kv], rest[n_kv : 2 * n_kv]
    ds, dqs = rest[2 * n_kv : 2 * n_kv + 2], rest[-2:]
    tokens = dqs[0].shape[0]
    block_rows = SLOT_ROWS // n_blocks
    first = where()[0]
    present = [blocks_with(first ^ role, q_a, got)[1] for role in range(SAMP)]
    wide = RATIO * tokens
    for t, dq_ref in enumerate(dqs):

        def one_block(roles):
            for h in range(HALF_KV):
                total = 0.0
                for role in roles:
                    k = key_rows(keys[role], block_rows, 0, h)
                    part = ds[role][h, :, t * wide : (t + 1) * wide]
                    total += lax.dot_general(part, k, TN, preferred_element_type=F32)
                if roles:
                    for r in range(RATIO):
                        at = h * WIDE + r * HD
                        rows = total[r * tokens : (r + 1) * tokens] * SCALE
                        dq_ref[:, at : at + HD] = rows.astype(dq_ref.dtype)

        choose([present[role][t] for role in range(SAMP)], one_block)


def sample_pass(where, role, n_blocks, bias, text, kvs, grads, after=()):
    tokens = text[1].shape[0]
    ds = ((HALF_KV, SLOT_ROWS, CORES * RATIO * tokens), BF16)
    return in_vmem(
        functools.partial(pass_kernel, role, n_blocks, len(kvs), len(grads), where),
        [ds, *grads],
        flops=8 * tokens * WIDE * SLOT_ROWS * CORES * HALF_KV,
        moved=16 * 2**20,
    )(bias, *text, *kvs, *after)


def text_grads(where, n_blocks, text, keys, ds):
    tokens = text[1].shape[0]
    return in_vmem(
        functools.partial(dq_kernel, n_blocks, len(keys[0]), where),
        [((tokens, HALF_QCOLS), BF16)] * 2,
        flops=4 * tokens * WIDE * SLOT_ROWS * CORES * HALF_KV,
        moved=8 * 2**20,
    )(text[0], text[2], *keys[0], *keys[1], *ds)


def shards(n_ctx, n_enc, queries, d_out, text_sample, tiles, img_k, img_v):
    n_y = n_ctx // CORES
    slots = img_k.shape[1]
    tokens = queries.shape[1]
    swap_core = [(i, i ^ 1) for i in range(n_ctx)]
    near = n_y == SAMP and slots % 16 == 0 and n_enc == 8
    text_outs = [
        ((2 * tokens + SAMP_ROWS, HALF_QCOLS), BF16, IN_VMEM),
        ((tokens + SAMP_ROWS, HALF_QCOLS), BF16, IN_VMEM),
        ((tokens, HALF_QCOLS), BF16, IN_VMEM),
        ((SAMP, SLOT_ROWS, HD), BF16, IN_VMEM),
    ]

    def split_the_text(n_blocks, pieces, where):
        return local_call(
            functools.partial(split_text, n_blocks, pieces, where),
            [IN_HBM] * 4,
            text_outs,
            [
                pltpu.VMEM(text_sample.shape, jnp.int32),
                pltpu.VMEM(tiles.shape, jnp.int32),
                pltpu.SemaphoreType.DMA((6,)),
            ],
            moved=4 * 2**20,
        )(*in_hbm(queries, d_out, text_sample, tiles))

    if near:
        swap_y = [(i, (i + CORES) % n_ctx) for i in range(n_ctx)]
        n_z = n_enc // 2
        block_rows = 2 * CORES * slots
        pair = (2, block_rows, HALF_KCOLS)
        quarter = (2 * block_rows, HALF_KCOLS)
        whole = (SLOT_ROWS, HALF_KCOLS)
        kv_halves = (2, n_enc, slots, HALF_KCOLS)
        swap_x = [(i, i ^ 1) for i in range(n_enc)]
        swap_xy = [
            (i * n_enc + e, (i + CORES) % n_ctx * n_enc + (e ^ 1))
            for i in range(n_ctx)
            for e in range(n_enc)
        ]

        def along_z(part, dz):
            return lax.ppermute(part, "enc", [(i, i ^ (2 * dz)) for i in range(n_enc)]) if dz else part

        def along_x(part):
            return lax.ppermute(part, "enc", swap_x)

        def along_y(part):
            return lax.ppermute(part, "ctx", swap_y)

        def along_xy(part):
            return lax.ppermute(part, ("ctx", "enc"), swap_xy)

        mine, for_peer = local_call(
            split_kernel,
            [IN_HBM] * 2,
            [(kv_halves, BF16, IN_VMEM)] * 2,
            [pltpu.SemaphoreType.DMA((4,))],
        )(*in_hbm(img_k, img_v))
        text_peer, q_own, g_own, bias = split_the_text(n_enc, CORES, near_place)
        *carry, text_peer = in_vmem(
            functools.partial(carry_kernel, slots),
            [(pair, BF16)] * n_z + [(text_peer.shape, BF16)],
            aliases={2: n_z},
        )(mine, lax.ppermute(for_peer, "ctx", swap_core), text_peer)
        text = (q_own, g_own, lax.ppermute(text_peer, "ctx", swap_core))

        came = [along_z(part, dz) for dz, part in enumerate(carry)]
        own, far = [], []
        for z in (0, 2):
            here, beside = in_vmem(join_kernel, [(quarter, BF16)] * 2)(
                *came[z : z + 2], text[2], *far
            )
            own += [here, along_x(beside)]
            far += [along_y(here), along_xy(beside)]
        own_ds, own_here, *own_beside = sample_pass(
            near_place, 0, n_enc, bias, text, own, [(whole, F32)] + [(quarter, BF16)] * 2
        )
        far_ds, *far_grads = sample_pass(
            near_place, 1, n_enc, bias, text, far, [(quarter, BF16)] * 4, (own_here,)
        )
        dq = text_grads(near_place, n_enc, text, (own, far), (own_ds, far_ds))
        returned = [None] * n_z
        for z in (2, 0):
            here, beside = far_grads[z : z + 2]
            (own_part,) = hand_on(own_beside[z // 2], far_ds)
            back_x = along_x(own_part)
            if not z:
                (here,), (beside,) = hand_on(here, before), hand_on(beside, before)
            before = back_x
            back_y, back_xy = along_y(here), along_xy(beside)
            totals = in_vmem(functools.partial(add_kernel, z), [(pair, BF16)] * 2)(
                own_here, back_y, back_xy, back_x
            )
            for dz, total in enumerate(totals, z):
                returned[dz] = along_z(total, dz)
            if z:
                sent = totals[0]
        dq_parts = in_vmem(split_rows_kernel, [((tokens // DQ_PARTS, HALF_QCOLS), BF16)] * DQ_PARTS)(
            dq[1], sent, totals[0]
        )
        dq_got = [lax.ppermute(part, "ctx", swap_core) for part in dq_parts]
    else:
        both = ("ctx", "enc")
        same_y = [
            [yy * CORES * n_enc + i for i in range(CORES * n_enc)] for yy in range(n_y)
        ]
        same_column = [
            [(yy * CORES + c) * n_enc + e for yy in range(n_y)]
            for c in range(CORES)
            for e in range(n_enc)
        ]
        core = core_of()

        def exchange(parts):
            return lax.all_to_all(
                parts, both, split_axis=0, concat_axis=0, axis_index_groups=same_y, tiled=True
            )

        def to_groups(owned):
            parts = owned.reshape(n_enc, slots, CORES, HALF_KCOLS).transpose(2, 0, 1, 3)
            got = exchange(parts.reshape(CORES * n_enc, slots, HALF_KCOLS))
            got = got.reshape(CORES * n_enc * slots, HALF_KCOLS)
            return lax.all_gather(got, both, axis=0, axis_index_groups=same_column, tiled=True)

        def to_owners(grads):
            grads = lax.psum_scatter(
                grads, both, scatter_dimension=0, axis_index_groups=same_column, tiled=True
            )
            got = exchange(grads.reshape(CORES * n_enc, slots, HALF_KCOLS))
            got = got.reshape(CORES, n_enc, slots, HALF_KCOLS).transpose(1, 2, 0, 3)
            return got.reshape(n_enc, slots, CORES * HALF_KCOLS)

        def no_place():
            return jnp.int32(0), jnp.int32(0)

        all_k = to_groups(img_k)
        all_v = to_groups(img_v)
        text_peer, q_own, g_own, bias = split_the_text(1, 1, no_place)
        text = (q_own, g_own, lax.ppermute(text_peer, "ctx", swap_core))
        kvs = [
            jnp.concatenate([part[s * SLOT_ROWS : (s + 1) * SLOT_ROWS] for part in (all_k, all_v)], axis=0)
            for s in range(SAMP)
        ]
        all_ds, grads = [], []
        for sample, kv in enumerate(kvs):
            ds, grad = sample_pass(no_place, sample, 1, bias, text, [kv], [(kv.shape, BF16)])
            all_ds.append(ds)
            grads.append(grad)
        dq = text_grads(no_place, 1, text, [[kv] for kv in kvs], all_ds)
        d_img_k = to_owners(jnp.concatenate([g[:SLOT_ROWS] for g in grads], axis=0))
        d_img_v = to_owners(jnp.concatenate([g[SLOT_ROWS:] for g in grads], axis=0))
        dq_got = [lax.ppermute(dq[1], "ctx", swap_core)]

    d_queries, token = local_call(
        finish_text_kernel,
        [IN_VMEM] * (1 + len(dq_got)),
        [(queries.shape, BF16, IN_HBM), ((8, HD), F32, IN_VMEM)],
        [pltpu.SemaphoreType.DMA((1 + len(dq_got),))],
    )(dq[0], *dq_got)
    if near:
        far_rows = in_vmem(
            functools.partial(far_rows_kernel, slots),
            [((2, n_enc // 2, slots, HALF_KCOLS), BF16)] * 2,
        )(*returned[2:])
        mine, for_peer = in_vmem(
            functools.partial(owner_rows_kernel, slots),
            [(kv_halves, BF16)] * 2,
        )(*returned[:2], *far_rows)
        d_img_k, d_img_v = local_call(
            finish_kernel,
            [IN_VMEM] * 3,
            [(img_k.shape, BF16, IN_HBM)] * 2,
            [pltpu.SemaphoreType.DMA((4,))],
        )(mine, lax.ppermute(for_peer, "ctx", swap_core), token)
    return (d_queries, d_img_k, d_img_v)


def solution(mesh):
    in_specs = (
        P("enc", "ctx", None),
        P("enc", "ctx", None),
        P("enc", "ctx"),
        P("enc", None),
        P(None, ("ctx", "enc"), None),
        P(None, ("ctx", "enc"), None),
    )
    out_specs = (
        P("enc", "ctx", None),
        P(None, ("ctx", "enc"), None),
        P(None, ("ctx", "enc"), None),
    )
    body = functools.partial(shards, mesh.shape["ctx"], mesh.shape["enc"])
    return jax.shard_map(body, mesh=mesh, in_specs=in_specs, out_specs=out_specs, check_vma=False)
```

```python
import functools

import jax
import jax.numpy as jnp
from jax import lax
from jax.experimental import pallas as pl
from jax.experimental.pallas import tpu as pltpu
from jax.sharding import PartitionSpec as P

H = 32
KVH = 8
HD = 128
SAMP = 2
MAX_TILES = 4
TILE_TOK = 64
RATIO = H // KVH
CORES = 2
SLOT_ROWS = MAX_TILES * TILE_TOK
HALF_KV = KVH // CORES
HALF_KCOLS = HALF_KV * HD
HALF_QCOLS = HALF_KCOLS * RATIO
WIDE = RATIO * HD
SAMP_ROWS = 16
DQ_PARTS = 2
SCALE = HD ** (-0.5)
LOG2E = 1.4426950408889634
BIG_NEGATIVE = -1e30
NT = (((1,), (1,)), ((), ()))
TN = (((0,), (0,)), ((), ()))
BF16 = jnp.bfloat16
F32 = jnp.float32

IN_VMEM = pl.BlockSpec(memory_space=pltpu.VMEM)
IN_HBM = pl.BlockSpec(memory_space=pltpu.HBM)


def local_call(body, ins, outs, scratch=(), flops=0, moved=2**19, aliases={}):
    return pl.pallas_call(
        body,
        in_specs=ins,
        out_specs=[spec for _, _, spec in outs],
        out_shape=[jax.ShapeDtypeStruct(s, d) for s, d, _ in outs],
        scratch_shapes=list(scratch),
        compiler_params=pltpu.CompilerParams(vmem_limit_bytes=8 * 2**20),
        input_output_aliases=aliases,
        cost_estimate=pl.CostEstimate(
            flops=flops, bytes_accessed=moved, transcendentals=flops // 1280
        ),
    )


def in_vmem(body, outs, **more):
    def call(*args):
        spec = [(shape, dtype, IN_VMEM) for shape, dtype in outs]
        return local_call(body, [IN_VMEM] * len(args), spec, **more)(*args)

    return call


def core_of():
    return lax.rem(lax.axis_index("ctx"), CORES)


def at_rows(first, count):
    return pl.ds(pl.multiple_of(first, count), count)


def at_cols(first, width, step):
    return pl.ds(pl.multiple_of(first, step), width)


def start_copies(pairs, sems):
    copies = [pltpu.make_async_copy(src, dst, sems.at[i]) for i, (src, dst) in enumerate(pairs)]
    for copy in copies:
        copy.start()
    return copies


def run_copies(pairs, sems):
    for copy in start_copies(pairs, sems):
        copy.wait()


def in_hbm(*arrays):
    return [pltpu.with_memory_space_constraint(a, pltpu.HBM) for a in arrays]


def split_kernel(k_ref, v_ref, mine, peer, sems):
    core = core_of()
    pairs = []
    for half, out in ((1 - core, peer), (core, mine)):
        cols = at_cols(half * HALF_KCOLS, HALF_KCOLS, HALF_KCOLS)
        for i, ref in enumerate((k_ref, v_ref)):
            pairs.append((ref.at[:, :, cols], out.at[i]))
    run_copies(pairs, sems)


def near_place():
    return lax.div(lax.axis_index("ctx"), CORES), lax.axis_index("enc")


def split_text(n_blocks, pieces, where, q_ref, g_ref, samp_hbm, tiles_hbm, peer, q_own, g_own, bias, samp, tiles, sems):
    core = core_of()
    tokens = q_ref.shape[1]
    own_cols = at_cols(core * HALF_QCOLS, HALF_QCOLS, HALF_QCOLS)
    peer_cols = at_cols((1 - core) * HALF_QCOLS, HALF_QCOLS, HALF_QCOLS)
    copies = start_copies(
        [
            (samp_hbm, samp),
            (tiles_hbm, tiles),
            (q_ref.at[0, :, peer_cols], peer.at[:tokens]),
            (g_ref.at[0, :, peer_cols], peer.at[tokens : 2 * tokens]),
            (q_ref.at[0, :, own_cols], q_own.at[:tokens]),
            (g_ref.at[0, :, own_cols], g_own),
        ],
        sems,
    )
    for copy in copies[:2]:
        copy.wait()
    row = jnp.broadcast_to(samp[...].astype(F32), (SAMP_ROWS, tokens)).astype(BF16)
    for out, first in ((q_own, tokens), (peer, 2 * tokens)):
        out[first:, :] = jnp.zeros((SAMP_ROWS, HALF_QCOLS), BF16)
        out[first:, :tokens] = row

    sample, enc = where()
    block_rows = SLOT_ROWS // n_blocks
    slots = block_rows // pieces
    line = lax.broadcasted_iota(jnp.int32, (SLOT_ROWS, HD), 0)
    block = lax.div(line, block_rows)
    if n_blocks > 1:
        low, high = block & 1, lax.div(block, 2) & 1
        block = block - low - 2 * high + 2 * low + high
    owner = block ^ enc
    piece = lax.rem(lax.div(line, slots), pieces)
    slot = piece * (SLOT_ROWS // pieces) + owner * slots + lax.rem(line, slots)
    for i in range(SAMP):
        count = jnp.where((sample ^ i) == 0, tiles[0:1, 0:1], tiles[0:1, 1:2])
        masked = jnp.where(slot < count * TILE_TOK, 0.0, BIG_NEGATIVE)
        first = lax.broadcasted_iota(jnp.int32, masked.shape, 1) == 0
        bias[i] = jnp.where(first, masked, 0.0).astype(BF16)
    for copy in copies[2:]:
        copy.wait()


def carry_kernel(slots, own, got, text, *outs):
    core = core_of()
    enc = lax.axis_index("enc")
    for dz, out in enumerate(outs[:-1]):
        for dx in range(2):
            group = enc ^ (2 * dz + dx)
            for i in range(2):
                first = i * CORES * slots
                out[dx, at_rows(first + core * slots, slots), :] = own[i, group]
                out[dx, at_rows(first + (1 - core) * slots, slots), :] = got[i, group]


def join_kernel(*refs):
    parts, outs = refs[:2], refs[-2:]
    rows = parts[0].shape[1]
    for dx, out in enumerate(outs):
        for dz, part in enumerate(parts):
            out[dz * rows : (dz + 1) * rows, :] = part[dx]


def block_place(b, n_outs):
    half, x, z = b // 4, b // 2 % 2, b % 2
    whole = 2 * half + z
    return {1: (0, b), 3: (1 + half, z) if x else (0, whole), 4: (2 * half + x, z)}[n_outs]


def add_kernel(z, own, back_y, back_xy, back_x, *outs):
    rows = outs[0].shape[1]
    for dz, out in enumerate(outs):
        whole = slice((z + dz) * rows, (z + dz + 1) * rows)
        part = slice(dz * rows, (dz + 1) * rows)
        out[0] = (own[whole, :] + back_y[part, :].astype(F32)).astype(out.dtype)
        out[1] = (back_x[part, :].astype(F32) + back_xy[part, :].astype(F32)).astype(out.dtype)


def nothing_kernel(*refs):
    pass


def hand_on(array, *after):
    return in_vmem(nothing_kernel, [(array.shape, array.dtype)], aliases={0: 0})(array, *after)


def far_rows_kernel(slots, *refs):
    core = core_of()
    parts, outs = refs[:2], refs[-2:]
    for dz, part in enumerate(parts):
        for dx in range(2):
            for i in range(2):
                first = i * CORES * slots
                for who, out in zip((core, 1 - core), outs):
                    out[i, 2 * dz + dx] = part[dx, at_rows(first + who * slots, slots), :]


def owner_rows_kernel(slots, *refs):
    core = core_of()
    enc = lax.axis_index("enc")
    parts, far, outs = refs[:2], refs[2:4], refs[4:]
    for dz, part in enumerate(parts):
        for dx in range(2):
            d = 2 * dz + dx
            for i in range(2):
                first = i * CORES * slots
                for who, from_far, out in zip((core, 1 - core), far, outs):
                    out[i, enc ^ d] = part[dx, at_rows(first + who * slots, slots), :]
                    out[i, enc ^ (2 * len(parts) + d)] = from_far[i, d]


def finish_kernel(mine, got, _, dk, dv, sems):
    core = core_of()
    pairs = []
    for half, ref in ((core, mine), (1 - core, got)):
        cols = at_cols(half * HALF_KCOLS, HALF_KCOLS, HALF_KCOLS)
        for i, out in enumerate((dk, dv)):
            pairs.append((ref.at[i], out.at[:, :, cols]))
    run_copies(pairs, sems)


def split_rows_kernel(whole, *refs):
    outs = refs[-DQ_PARTS:]
    rows = outs[0].shape[0]
    for i, out in enumerate(outs):
        out[...] = whole[i * rows : (i + 1) * rows, :]


def finish_text_kernel(mine, *refs):
    got, (out, token, sems) = refs[:-3], refs[-3:]
    core = core_of()
    token[...] = jnp.zeros_like(token)
    own_cols = at_cols(core * HALF_QCOLS, HALF_QCOLS, HALF_QCOLS)
    got_cols = at_cols((1 - core) * HALF_QCOLS, HALF_QCOLS, HALF_QCOLS)
    pairs = [(mine, out.at[0, :, own_cols])]
    rows = got[0].shape[0]
    for i, ref in enumerate(got):
        pairs.append((ref, out.at[0, i * rows : (i + 1) * rows, got_cols]))
    run_copies(pairs, sems)


def blocks_with(sample, q_own, got):
    tokens = q_own.shape[0] - SAMP_ROWS
    rows = (q_own[tokens : tokens + 1, :tokens], got[2 * tokens : 2 * tokens + 1, :tokens])
    rows = [row.astype(F32) for row in rows]
    wanted = sample.astype(F32)
    return rows, [jnp.max(jnp.where(row == wanted, 1.0, 0.0)) > 0.5 for row in rows]


def key_rows(kvs, block_rows, first, h):
    parts = []
    for kv in kvs:
        for at in range(first, kv.shape[0], 2 * block_rows):
            parts.append(kv[at : at + block_rows, h * HD : (h + 1) * HD])
    return jnp.concatenate(parts, axis=0)


def choose(flags, branch):
    for which in ((0, 1), (0,), (1,), ()):
        wants = [flags[t] if t in which else jnp.logical_not(flags[t]) for t in range(2)]

        @pl.when(wants[0] & wants[1])
        def _():
            branch(which)


def pass_kernel(role, n_blocks, n_kv, n_grads, where, bias, q_a, g_a, got, *rest):
    kvs, (ds_out, *grads) = rest[:n_kv], rest[-1 - n_grads :]
    sample = where()[0] ^ role
    tokens = g_a.shape[0]
    block_rows = SLOT_ROWS // n_blocks
    rows, present = blocks_with(sample, q_a, got)
    sources = ((q_a, 0, g_a, 0), (got, 0, got, tokens))

    def one_pass(which):
        if not which:
            for out in grads:
                out[...] = jnp.zeros_like(out)
            return
        mine = jnp.concatenate([rows[t] for t in which for _ in range(RATIO)], axis=1)
        mine = mine == sample.astype(F32)
        masks = bias[role]
        ones = jnp.ones((len(which) * RATIO * tokens, HD), BF16)

        def products(h):
            def stacked(part):
                parts = []
                for t in which:
                    ref, first = sources[t][part : part + 2]
                    for r in range(RATIO):
                        at = h * WIDE + r * HD
                        parts.append(ref[first : first + tokens, at : at + HD])
                return jnp.concatenate(parts, axis=0)

            q, g = stacked(0), stacked(2)
            k, v = (key_rows(kvs, block_rows, first, h) for first in (0, block_rows))
            s = lax.dot_general(
                jnp.concatenate([k, masks], axis=1),
                jnp.concatenate([q, ones], axis=1),
                NT,
                preferred_element_type=F32,
            )
            gp = lax.dot_general(v, g, NT, preferred_element_type=F32)
            return q, g, s, gp

        ahead = products(0)
        for h in range(HALF_KV):
            q, g, s, gp = ahead
            if h + 1 < HALF_KV:
                ahead = products(h + 1)
            top = jnp.max(s, axis=0, keepdims=True)
            e = jnp.exp2((s - top) * (SCALE * LOG2E))
            total = jnp.sum(e, axis=0, keepdims=True)
            p = e * jnp.where(mine, 1.0 / total, 0.0)
            ph = p.astype(BF16)
            dv = jnp.dot(ph, g, preferred_element_type=F32)
            row_dot = jnp.sum(p * gp, axis=0, keepdims=True)
            ds = ph * (gp - row_dot).astype(BF16)
            dk = jnp.dot(ds, q, preferred_element_type=F32) * SCALE
            wide = RATIO * tokens
            for i, t in enumerate(which):
                ds_out[h, :, t * wide : (t + 1) * wide] = ds[:, i * wide : (i + 1) * wide]
            cols = slice(h * HD, (h + 1) * HD)
            for b in range(n_blocks):
                block = slice(b * block_rows, (b + 1) * block_rows)
                dx, at = block_place(b, len(grads))
                out, first = grads[dx], at * 2 * block_rows
                out[first : first + block_rows, cols] = dk[block].astype(out.dtype)
                out[first + block_rows : first + 2 * block_rows, cols] = dv[block].astype(out.dtype)

    choose(present, one_pass)


def dq_kernel(n_blocks, n_kv, where, q_a, got, *rest):
    keys = rest[:n_kv], rest[n_kv : 2 * n_kv]
    ds, dqs = rest[2 * n_kv : 2 * n_kv + 2], rest[-2:]
    tokens = dqs[0].shape[0]
    block_rows = SLOT_ROWS // n_blocks
    first = where()[0]
    present = [blocks_with(first ^ role, q_a, got)[1] for role in range(SAMP)]
    wide = RATIO * tokens
    for t, dq_ref in enumerate(dqs):

        def one_block(roles):
            for h in range(HALF_KV):
                total = 0.0
                for role in roles:
                    k = key_rows(keys[role], block_rows, 0, h)
                    part = ds[role][h, :, t * wide : (t + 1) * wide]
                    total += lax.dot_general(part, k, TN, preferred_element_type=F32)
                if roles:
                    for r in range(RATIO):
                        at = h * WIDE + r * HD
                        rows = total[r * tokens : (r + 1) * tokens] * SCALE
                        dq_ref[:, at : at + HD] = rows.astype(dq_ref.dtype)

        choose([present[role][t] for role in range(SAMP)], one_block)


def sample_pass(where, role, n_blocks, bias, text, kvs, grads, after=()):
    tokens = text[1].shape[0]
    ds = ((HALF_KV, SLOT_ROWS, CORES * RATIO * tokens), BF16)
    return in_vmem(
        functools.partial(pass_kernel, role, n_blocks, len(kvs), len(grads), where),
        [ds, *grads],
        flops=8 * tokens * WIDE * SLOT_ROWS * CORES * HALF_KV,
        moved=16 * 2**20,
    )(bias, *text, *kvs, *after)


def text_grads(where, n_blocks, text, keys, ds):
    tokens = text[1].shape[0]
    return in_vmem(
        functools.partial(dq_kernel, n_blocks, len(keys[0]), where),
        [((tokens, HALF_QCOLS), BF16)] * 2,
        flops=4 * tokens * WIDE * SLOT_ROWS * CORES * HALF_KV,
        moved=8 * 2**20,
    )(text[0], text[2], *keys[0], *keys[1], *ds)


def shards(n_ctx, n_enc, queries, d_out, text_sample, tiles, img_k, img_v):
    n_y = n_ctx // CORES
    slots = img_k.shape[1]
    tokens = queries.shape[1]
    swap_core = [(i, i ^ 1) for i in range(n_ctx)]
    near = n_y == SAMP and slots % 16 == 0 and n_enc == 8
    text_outs = [
        ((2 * tokens + SAMP_ROWS, HALF_QCOLS), BF16, IN_VMEM),
        ((tokens + SAMP_ROWS, HALF_QCOLS), BF16, IN_VMEM),
        ((tokens, HALF_QCOLS), BF16, IN_VMEM),
        ((SAMP, SLOT_ROWS, HD), BF16, IN_VMEM),
    ]

    def split_the_text(n_blocks, pieces, where):
        return local_call(
            functools.partial(split_text, n_blocks, pieces, where),
            [IN_HBM] * 4,
            text_outs,
            [
                pltpu.VMEM(text_sample.shape, jnp.int32),
                pltpu.VMEM(tiles.shape, jnp.int32),
                pltpu.SemaphoreType.DMA((6,)),
            ],
            moved=4 * 2**20,
        )(*in_hbm(queries, d_out, text_sample, tiles))

    if near:
        swap_y = [(i, (i + CORES) % n_ctx) for i in range(n_ctx)]
        n_z = n_enc // 2
        block_rows = 2 * CORES * slots
        pair = (2, block_rows, HALF_KCOLS)
        quarter = (2 * block_rows, HALF_KCOLS)
        whole = (SLOT_ROWS, HALF_KCOLS)
        kv_halves = (2, n_enc, slots, HALF_KCOLS)
        swap_x = [(i, i ^ 1) for i in range(n_enc)]
        swap_xy = [
            (i * n_enc + e, (i + CORES) % n_ctx * n_enc + (e ^ 1))
            for i in range(n_ctx)
            for e in range(n_enc)
        ]

        def along_z(part, dz):
            return lax.ppermute(part, "enc", [(i, i ^ (2 * dz)) for i in range(n_enc)]) if dz else part

        def along_x(part):
            return lax.ppermute(part, "enc", swap_x)

        def along_y(part):
            return lax.ppermute(part, "ctx", swap_y)

        def along_xy(part):
            return lax.ppermute(part, ("ctx", "enc"), swap_xy)

        mine, for_peer = local_call(
            split_kernel,
            [IN_HBM] * 2,
            [(kv_halves, BF16, IN_VMEM)] * 2,
            [pltpu.SemaphoreType.DMA((4,))],
        )(*in_hbm(img_k, img_v))
        text_peer, q_own, g_own, bias = split_the_text(n_enc, CORES, near_place)
        *carry, text_peer = in_vmem(
            functools.partial(carry_kernel, slots),
            [(pair, BF16)] * n_z + [(text_peer.shape, BF16)],
            aliases={2: n_z},
        )(mine, lax.ppermute(for_peer, "ctx", swap_core), text_peer)
        text = (q_own, g_own, lax.ppermute(text_peer, "ctx", swap_core))

        came = [along_z(part, dz) for dz, part in enumerate(carry)]
        own, far = [], []
        for z in (0, 2):
            here, beside = in_vmem(join_kernel, [(quarter, BF16)] * 2)(
                *came[z : z + 2], text[2], *far
            )
            own += [here, along_x(beside)]
            far += [along_y(here), along_xy(beside)]
        own_ds, own_here, *own_beside = sample_pass(
            near_place, 0, n_enc, bias, text, own, [(whole, F32)] + [(quarter, BF16)] * 2
        )
        far_ds, *far_grads = sample_pass(
            near_place, 1, n_enc, bias, text, far, [(quarter, BF16)] * 4, (own_here,)
        )
        dq = text_grads(near_place, n_enc, text, (own, far), (own_ds, far_ds))
        returned = [None] * n_z
        for z in (2, 0):
            here, beside = far_grads[z : z + 2]
            (own_part,) = hand_on(own_beside[z // 2], far_ds)
            back_y, back_xy, back_x = along_y(here), along_xy(beside), along_x(own_part)
            totals = in_vmem(functools.partial(add_kernel, z), [(pair, BF16)] * 2)(
                own_here, back_y, back_xy, back_x
            )
            for dz, total in enumerate(totals, z):
                returned[dz] = along_z(total, dz)
            if z:
                sent = totals[0]
        dq_parts = in_vmem(split_rows_kernel, [((tokens // DQ_PARTS, HALF_QCOLS), BF16)] * DQ_PARTS)(
            dq[1], sent, totals[0]
        )
        dq_got = [lax.ppermute(part, "ctx", swap_core) for part in dq_parts]
    else:
        both = ("ctx", "enc")
        same_y = [
            [yy * CORES * n_enc + i for i in range(CORES * n_enc)] for yy in range(n_y)
        ]
        same_column = [
            [(yy * CORES + c) * n_enc + e for yy in range(n_y)]
            for c in range(CORES)
            for e in range(n_enc)
        ]
        core = core_of()

        def exchange(parts):
            return lax.all_to_all(
                parts, both, split_axis=0, concat_axis=0, axis_index_groups=same_y, tiled=True
            )

        def to_groups(owned):
            parts = owned.reshape(n_enc, slots, CORES, HALF_KCOLS).transpose(2, 0, 1, 3)
            got = exchange(parts.reshape(CORES * n_enc, slots, HALF_KCOLS))
            got = got.reshape(CORES * n_enc * slots, HALF_KCOLS)
            return lax.all_gather(got, both, axis=0, axis_index_groups=same_column, tiled=True)

        def to_owners(grads):
            grads = lax.psum_scatter(
                grads, both, scatter_dimension=0, axis_index_groups=same_column, tiled=True
            )
            got = exchange(grads.reshape(CORES * n_enc, slots, HALF_KCOLS))
            got = got.reshape(CORES, n_enc, slots, HALF_KCOLS).transpose(1, 2, 0, 3)
            return got.reshape(n_enc, slots, CORES * HALF_KCOLS)

        def no_place():
            return jnp.int32(0), jnp.int32(0)

        all_k = to_groups(img_k)
        all_v = to_groups(img_v)
        text_peer, q_own, g_own, bias = split_the_text(1, 1, no_place)
        text = (q_own, g_own, lax.ppermute(text_peer, "ctx", swap_core))
        kvs = [
            jnp.concatenate([part[s * SLOT_ROWS : (s + 1) * SLOT_ROWS] for part in (all_k, all_v)], axis=0)
            for s in range(SAMP)
        ]
        all_ds, grads = [], []
        for sample, kv in enumerate(kvs):
            ds, grad = sample_pass(no_place, sample, 1, bias, text, [kv], [(kv.shape, BF16)])
            all_ds.append(ds)
            grads.append(grad)
        dq = text_grads(no_place, 1, text, [[kv] for kv in kvs], all_ds)
        d_img_k = to_owners(jnp.concatenate([g[:SLOT_ROWS] for g in grads], axis=0))
        d_img_v = to_owners(jnp.concatenate([g[SLOT_ROWS:] for g in grads], axis=0))
        dq_got = [lax.ppermute(dq[1], "ctx", swap_core)]

    d_queries, token = local_call(
        finish_text_kernel,
        [IN_VMEM] * (1 + len(dq_got)),
        [(queries.shape, BF16, IN_HBM), ((8, HD), F32, IN_VMEM)],
        [pltpu.SemaphoreType.DMA((1 + len(dq_got),))],
    )(dq[0], *dq_got)
    if near:
        far_rows = in_vmem(
            functools.partial(far_rows_kernel, slots),
            [((2, n_enc // 2, slots, HALF_KCOLS), BF16)] * 2,
        )(*returned[2:])
        mine, for_peer = in_vmem(
            functools.partial(owner_rows_kernel, slots),
            [(kv_halves, BF16)] * 2,
        )(*returned[:2], *far_rows)
        d_img_k, d_img_v = local_call(
            finish_kernel,
            [IN_VMEM] * 3,
            [(img_k.shape, BF16, IN_HBM)] * 2,
            [pltpu.SemaphoreType.DMA((4,))],
        )(mine, lax.ppermute(for_peer, "ctx", swap_core), token)
    return (d_queries, d_img_k, d_img_v)


def solution(mesh):
    in_specs = (
        P("enc", "ctx", None),
        P("enc", "ctx", None),
        P("enc", "ctx"),
        P("enc", None),
        P(None, ("ctx", "enc"), None),
        P(None, ("ctx", "enc"), None),
    )
    out_specs = (
        P("enc", "ctx", None),
        P(None, ("ctx", "enc"), None),
        P(None, ("ctx", "enc"), None),
    )
    body = functools.partial(shards, mesh.shape["ctx"], mesh.shape["enc"])
    return jax.shard_map(body, mesh=mesh, in_specs=in_specs, out_specs=out_specs, check_vma=False)
```
